32 devices in a mesh: dp: 8 (over z, y), seq: 4 (over x, core).
Axes of the slice: x: 2, y: 2, z: 4, core: 2. Of those that a mesh axis runs over, the one named last changes fastest.
Arguments:
- tokens: bfloat16 [8, 1024, 896], P('dp', 'seq'), may hold values from -6 to 6
- cotangent: bfloat16 [8, 1024, 896], P('dp', 'seq'), may hold values from -6 to 6
- span_order: int32 [8, 4], P('dp'), may hold values from 0 to 3, each once within a row
- attn_gain: bfloat16 [2, 896], P(None, ('dp', 'seq')), may hold values from 0.099609375 to 1.8984375
- joined_weight: bfloat16 [2, 896, 1152], P(None, ('dp', 'seq')), may hold values from -0.1875 to 0.1875
- joined_bias: bfloat16 [2, 1152], P(None, ('dp', 'seq')), may hold values from -3 to 3
- out_weight: bfloat16 [2, 896, 896], P(None, ('dp', 'seq')), may hold values from -1 to 1
- mlp_gain: bfloat16 [2, 896], P(None, ('dp', 'seq')), may hold values from 0.099609375 to 1.8984375
- gate_up_weight: bfloat16 [2, 896, 9728], P(None, ('dp', 'seq')), may hold values from -0.1875 to 0.1875
- down_weight: bfloat16 [2, 4864, 896], P(None, ('dp', 'seq')), may hold values from -0.125 to 0.125
Outputs:
- activations: bfloat16 [8, 1024, 896], P('dp', 'seq')
- input_grad: float32 [8, 1024, 896], P('dp', 'seq')
- attn_gain_grad: float32 [2, 896], P(None, ('dp', 'seq'))
- joined_weight_grad: float32 [2, 896, 1152], P(None, ('dp', 'seq'))
- joined_bias_grad: float32 [2, 1024], P(None, ('dp', 'seq'))
- value_bias_grad: float32 [2, 128], P(None, ('dp', 'seq'))
- out_weight_grad: float32 [2, 896, 896], P(None, ('dp', 'seq'))
- mlp_gain_grad: float32 [2, 896], P(None, ('dp', 'seq'))
- gate_up_grad: float32 [2, 896, 9728], P(None, ('dp', 'seq'))
- down_grad: float32 [2, 4864, 896], P(None, ('dp', 'seq'))
The draws below stay inside these ranges and needn't reach their ends.
Inputs may be any that keep to these rules, and one draw needn't show every extreme that they name: Each row of span_order holds every number below 4 once.
All inputs are finite; a program needn't handle non-finite values.
Results may differ from the reference program's by a relative error of at most 0.023.
Values may be sent and summed in bfloat16 or wider, within the bound.
No kernel may reach another device: no remote copies, remote signals or barrier semaphores. Data moves between devices by JAX's collectives and lax.ppermute only.
A program may use at most 256 MiB of HBM per device.

```python
import jax
import jax.numpy as jnp
from jax import lax

D = 896
HEADS = 14
KV_HEADS = 2
HEAD = 64
FF = 4864
LAYERS = 2
SEQ_LEN = 1024
SEQS = 1
SEQUENCES = 8
JOINED = 1152
N_DP = 8
N_SEQ = 4


def levels(own_key, extent, pieces, low, top_value):
    loudness = 1.0
    for dim, shards_of in pieces:
        draws = jax.random.uniform(jax.random.fold_in(jax.random.fold_in(own_key, 6), dim), (shards_of,), jnp.float32, low / len(pieces), top_value / len(pieces))
        loudness = loudness * jnp.repeat(jnp.exp(draws), extent[dim] // shards_of).reshape((-1,) + (1,) * (len(extent) - 1 - dim))
    return loudness


def bell_draw(stream_key, dims, deviation, reach, cuts=(), kind=jnp.bfloat16):
    drawn = jax.random.normal(stream_key, dims, jnp.float32) * deviation
    if len(cuts) > 0:
        drawn = levels(stream_key, dims, cuts, -0.22, 0.18) * drawn
    return jnp.clip(drawn, min=-reach, max=reach).astype(kind)


def setup_inputs(seed: int = 0) -> dict:
    key_list = jax.random.split(jax.random.key(seed), 11)
    tokens = bell_draw(key_list[0], (SEQUENCES, SEQ_LEN, D), 1.0, 6.0, ((0, 8), (1, 4)))
    cotangent = bell_draw(key_list[1], (SEQUENCES, SEQ_LEN, D), 1.0, 6.0, ((0, 8), (1, 4)))
    span_order = jax.vmap(lambda own: jax.random.permutation(own, N_SEQ))(jax.random.split(key_list[2], SEQUENCES)).reshape((SEQUENCES, N_SEQ)).astype(jnp.int32)
    attn_gain = jnp.clip(1.0 + 0.18 * jax.random.normal(key_list[3], (LAYERS, D), jnp.float32), 0.099609375, 1.8984375).astype(jnp.bfloat16)
    joined_weight = bell_draw(key_list[4], (LAYERS, D, JOINED), D ** -0.5, 0.1875, ((1, 32),))
    joined_bias = bell_draw(key_list[5], (LAYERS, JOINED), 0.5, 3.0, ((1, 32),))
    out_weight = bell_draw(key_list[6], (LAYERS, D, D), (D // 32) ** -0.5, 1.0, ((1, 32),))
    mlp_gain = jnp.clip(1.0 + 0.18 * jax.random.normal(key_list[7], (LAYERS, D), jnp.float32), 0.099609375, 1.8984375).astype(jnp.bfloat16)
    gate_up_weight = bell_draw(key_list[8], (LAYERS, D, 2 * FF), D ** -0.5, 0.1875, ((1, 32),))
    down_weight = bell_draw(key_list[9], (LAYERS, FF, D), (FF // 2) ** -0.5, 0.125, ((1, 32),))
    return {"tokens": tokens, "cotangent": cotangent, "span_order": span_order, "attn_gain": attn_gain, "joined_weight": joined_weight, "joined_bias": joined_bias, "out_weight": out_weight, "mlp_gain": mlp_gain, "gate_up_weight": gate_up_weight, "down_weight": down_weight}


EPS = 1e-06
THETA = 1000000.0
NEGATIVE = -1e+30
PRECISE = lax.Precision.HIGHEST

@jax.custom_vjp
def low(v):
    return lax.optimization_barrier(v.astype(jnp.bfloat16)).astype(jnp.float32)

@jax.custom_vjp
def low_back(v):
    return v

def low_keep(v):
    return (low(v), None)

def low_pass(kept, grad):
    return (grad,)

def back_keep(v):
    return (v, None)

def back_low(kept, grad):
    return (low(grad),)
low.defvjp(low_keep, low_pass)
low_back.defvjp(back_keep, back_low)

def token_places(order_cols, span_len, num_devices):
    inside = jnp.arange(2 * span_len, dtype=jnp.int32)
    lower_part = inside < span_len
    offsets = jnp.where(lower_part, inside, inside - span_len)
    picked = jnp.where(lower_part[None, None, :], order_cols[..., None], 2 * num_devices - 1 - order_cols[..., None])
    return (picked * span_len + offsets[None, None, :]).reshape(order_cols.shape[0], -1)

def rotary_tables(positions):
    half_head = HEAD // 2
    frequency = THETA ** (-2.0 * jnp.arange(half_head, dtype=jnp.float32) / HEAD)
    angles = positions.astype(jnp.float32)[..., None] * frequency
    return (jnp.cos(angles), jnp.sin(angles))

def rotate(values_in, cos_table, sin_table):
    half_head = HEAD // 2
    upper_half = values_in[..., :half_head]
    lower_half = values_in[..., half_head:]
    cos_part = cos_table[..., None, :]
    sin_part = sin_table[..., None, :]
    return jnp.concatenate([upper_half * cos_part - lower_half * sin_part, lower_half * cos_part + upper_half * sin_part], axis=-1)

def rms_norm(residual, gain_row):
    inv_root = lax.rsqrt(lax.optimization_barrier(jnp.mean(residual * residual, axis=-1, keepdims=True)) + EPS)
    return residual * inv_root * gain_row

def project(left, right):
    return jnp.matmul(left, right, precision=PRECISE)

def attend_one(parts):
    queries, key_rows, value_rows, positions = parts
    group_size = HEADS // KV_HEADS
    grouped = queries.reshape(SEQ_LEN, KV_HEADS, group_size, HEAD)
    scores = low_back(jnp.einsum('qkgd,tkd->kgqt', grouped, key_rows, precision=PRECISE) * HEAD ** (-0.5))
    allowed = positions[:, None] >= positions[None, :]
    scores = jnp.where(allowed[None, None], scores, NEGATIVE)
    weights = low(jax.nn.softmax(scores, axis=-1))
    mixed = jnp.einsum('kgqt,tkd->qkgd', weights, value_rows, precision=PRECISE)
    return mixed.reshape(SEQ_LEN, D)

def layer_forward(residual, layer_params, cos_table, sin_table, positions):
    attn_gain, joined_weight, joined_bias, out_weight, mlp_gain, gate_up_weight, down_weight = layer_params
    kv_width = KV_HEADS * HEAD
    normed = low(rms_norm(residual, attn_gain))
    joined_proj = low_back(project(normed, joined_weight) + joined_bias)
    queries = low(rotate(joined_proj[..., :D].reshape(SEQS, SEQ_LEN, HEADS, HEAD), cos_table, sin_table))
    key_rows = low(rotate(joined_proj[..., D:D + kv_width].reshape(SEQS, SEQ_LEN, KV_HEADS, HEAD), cos_table, sin_table))
    value_rows = low(joined_proj[..., D + kv_width:].reshape(SEQS, SEQ_LEN, KV_HEADS, HEAD))
    mixed = lax.map(jax.checkpoint(attend_one), (queries, key_rows, value_rows, positions))
    mixed = low(low_back(mixed))
    middle = residual + low_back(project(mixed, out_weight))
    normed_two = low(rms_norm(middle, mlp_gain))
    gate_up = low_back(project(normed_two, gate_up_weight))
    hidden = low(jax.nn.silu(gate_up[..., :FF]) * gate_up[..., FF:])
    return middle + low_back(project(hidden, down_weight))

def reference(tokens, cotangent, span_order, attn_gain, joined_weight, joined_bias, out_weight, mlp_gain, gate_up_weight, down_weight):
    weights = tuple((tensor.astype(jnp.float32) for tensor in (attn_gain, joined_weight, joined_bias, out_weight, mlp_gain, gate_up_weight, down_weight)))
    group_tokens = tokens.reshape(N_DP, SEQS, SEQ_LEN, D)
    group_cotan = cotangent.reshape(N_DP, SEQS, SEQ_LEN, D)
    group_order = span_order.reshape(N_DP, SEQS, N_SEQ)
    span_len = SEQ_LEN // (2 * N_SEQ)
    split_col = D + KV_HEADS * HEAD

    def group_step(totals, batch):
        token_rows, cotan_rows, order_rows = batch
        positions = token_places(order_rows, span_len, N_SEQ)
        cos_table, sin_table = rotary_tables(positions)

        def forward(residual, params):
            for layer_index in range(LAYERS):
                layer_params = tuple((tensor[layer_index] for tensor in params))
                residual = layer_forward(residual, layer_params, cos_table, sin_table, positions)
            return residual
        result, pullback = jax.vjp(forward, token_rows.astype(jnp.float32), weights)
        input_grad, weight_grads = pullback(cotan_rows.astype(jnp.float32))
        totals = jax.tree.map(jnp.add, totals, weight_grads)
        return (totals, (result.astype(jnp.bfloat16), input_grad))
    zeros = jax.tree.map(jnp.zeros_like, weights)
    totals, (outputs, input_grads) = lax.scan(group_step, zeros, (group_tokens, group_cotan, group_order))
    return (outputs.reshape(SEQUENCES, SEQ_LEN, D), input_grads.reshape(SEQUENCES, SEQ_LEN, D), totals[0], totals[1], totals[2][:, :split_col], totals[2][:, split_col:], totals[3], totals[4], totals[5], totals[6])
```

```python
import jax
import jax.numpy as jnp
from jax import lax
from jax.experimental import pallas as pl
from jax.experimental.pallas import tpu as pltpu
from jax.sharding import PartitionSpec as P

D = 896
HEADS = 14
KV_HEADS = 2
HEAD = 64
LAYERS = 2


EPS = 1e-06
THETA = 1000000.0
NEGATIVE = -1e30


def rotary_tables(positions):
    half_head = HEAD // 2
    frequency = THETA ** (-2.0 * jnp.arange(half_head, dtype=jnp.float32) / HEAD)
    angles = positions.astype(jnp.float32)[..., None] * frequency
    return (jnp.cos(angles), jnp.sin(angles))


NT = (((1,), (1,)), ((), ()))
TN = (((0,), (0,)), ((), ()))
FULL = pl.BlockSpec(memory_space=pltpu.VMEM)
SCALE = HEAD ** (-0.5)
GROUP = HEADS // KV_HEADS
KV_WIDTH = KV_HEADS * HEAD
SPLIT = D + KV_WIDTH
TILE = 384


def dot(left, right, dims=(((1,), (0,)), ((), ()))):
    return lax.dot_general(left, right, dims, preferred_element_type=jnp.float32)


def call(kernel, outs, micros, scratch=(), limit=40, **grid):
    return pl.pallas_call(
        kernel,
        out_shape=[jax.ShapeDtypeStruct(shape, kind) for shape, kind in outs],
        scratch_shapes=list(scratch),
        compiler_params=pltpu.CompilerParams(vmem_limit_bytes=limit * 2**20),
        name=kernel.__qualname__.split(".")[0],
        cost_estimate=pl.CostEstimate(
            flops=0, bytes_accessed=int(micros * 4e5), transcendentals=0
        ),
        **grid,
    )


def turn(block, cos_wide, sin_wide):
    lane = lax.broadcasted_iota(jnp.int32, block.shape, 1)
    width = block.shape[1]
    partner = jnp.where(
        lane % HEAD < HEAD // 2,
        pltpu.roll(block, width - HEAD // 2, 1),
        pltpu.roll(block, HEAD // 2, 1),
    )
    return block * cos_wide + partner * sin_wide


def inverse_root(rows):
    return lax.rsqrt(jnp.mean(rows * rows, axis=-1, keepdims=True) + EPS)


def before_attention(terms, gain, first_full, second_full, bias_first, bias_second, cos_wide, sin_wide):
    count = len(terms)
    rows = terms[0].shape[0]
    span = rows // 2

    def kernel(*refs):
        parts = refs[:count]
        gain_ref, first_ref, second_ref, bias_one, bias_two, cos_ref, sin_ref = refs[count : count + 7]
        x_ref, n_ref, q_ref, kv_ref = refs[count + 7 :]
        x = parts[0][...].astype(jnp.float32)
        for part in parts[1:]:
            x = x + part[...].astype(jnp.float32)
        x_ref[...] = x
        normed = (x * inverse_root(x) * gain_ref[...]).astype(jnp.bfloat16)
        n_ref[...] = normed
        cos_w, sin_w = cos_ref[...], sin_ref[...]
        for tile in range(SPLIT // 128):
            lanes = slice(tile * 128, tile * 128 + 128)
            block = dot(normed, first_ref[:, lanes]) + bias_one[:, lanes]
            turned = turn(block, cos_w, sin_w)
            if tile * 128 < D:
                for part in range(2):
                    head = 2 * tile + part
                    piece = turned[:, part * HEAD : part * HEAD + HEAD].astype(jnp.bfloat16)
                    place = (head % GROUP) * span
                    for half in range(2):
                        q_ref[head // GROUP, half, place : place + span, :] = piece[
                            half * span : half * span + span
                        ]
            else:
                kv_ref[:, :KV_WIDTH] = turned.astype(jnp.bfloat16)
        kv_ref[:, KV_WIDTH:] = (
            dot(normed, second_ref[:, :KV_WIDTH]) + bias_two[...]
        ).astype(jnp.bfloat16)

    return call(
        kernel,
        [
            ((rows, D), jnp.float32),
            ((rows, D), jnp.bfloat16),
            ((KV_HEADS, 2, GROUP * span, HEAD), jnp.bfloat16),
            ((rows, 2 * KV_WIDTH), jnp.bfloat16),
        ],
        4.0,
    )(*terms, gain, first_full, second_full, bias_first, bias_second, cos_wide, sin_wide)


def key_part(kv_refs, half, lanes):
    span = kv_refs[0].shape[0] // 2
    return jnp.concatenate(
        [ref[half * span : half * span + span, lanes] for ref in kv_refs], axis=0
    )


def attention(queries, kv_blocks, biases, x, second_full, gain):
    rows = x.shape[0]
    span = rows // 2

    def kernel(q_ref, kv0, kv1, kv2, kv3, bias_ref, x_ref, w_ref, gain_ref, mixed_ref, mid_ref, n_ref):
        kvs = (kv0, kv1, kv2, kv3)
        for group in range(KV_HEADS):
            key_lanes = slice(group * HEAD, group * HEAD + HEAD)
            value_lanes = slice(KV_WIDTH + group * HEAD, KV_WIDTH + group * HEAD + HEAD)
            keys = [key_part(kvs, half, key_lanes) for half in range(2)]
            values = []
            for half in range(2):
                block = key_part(kvs, half, value_lanes)
                values.append(jnp.concatenate([block, jnp.ones_like(block)], axis=1))
            for half in range(2):
                bias = bias_ref[half]
                for member in range(GROUP):
                    query = q_ref[group, half, member * span : member * span + span, :] * jnp.bfloat16(SCALE)
                    near = dot(query, keys[half], NT) + bias
                    top = jnp.max(near, axis=-1, keepdims=True)
                    if half == 1:
                        far = dot(query, keys[0], NT)
                        top = jnp.maximum(top, jnp.max(far, axis=-1, keepdims=True))
                    total = dot(jnp.exp(near - top).astype(jnp.bfloat16), values[half])
                    if half == 1:
                        total = total + dot(jnp.exp(far - top).astype(jnp.bfloat16), values[0])
                    out = total[:, :HEAD] / total[:, HEAD : 2 * HEAD]
                    head = group * GROUP + member
                    mixed_ref[half * span : half * span + span, head * HEAD : head * HEAD + HEAD] = (
                        out.astype(jnp.bfloat16)
                    )
        middle = x_ref[...] + dot(mixed_ref[...], w_ref[:, KV_WIDTH:])
        mid_ref[...] = middle
        n_ref[...] = (middle * inverse_root(middle) * gain_ref[...]).astype(jnp.bfloat16)

    return call(
        kernel,
        [((rows, D), jnp.bfloat16), ((rows, D), jnp.float32), ((rows, D), jnp.bfloat16)],
        10.5,
    )(queries, *kv_blocks, biases, x, second_full, gain)


def feed_forward(parts, gate_up_full, down_full):
    count = len(parts)
    part_rows = parts[0].shape[0]
    rows = count * part_rows
    units = down_full.shape[0]
    steps = pl.cdiv(units, TILE)
    last = units - (steps - 1) * TILE

    def kernel(*refs):
        part_refs = refs[:count]
        w_ref, d_ref, gu_ref = refs[count : count + 3]
        out_refs, total = refs[count + 3 : -1], refs[-1]
        step = pl.program_id(0)
        n2 = jnp.concatenate([ref[...] for ref in part_refs], axis=0)

        @pl.when(step == 0)
        def _():
            total[...] = jnp.zeros_like(total)

        @pl.when(step < steps - 1)
        def _():
            both = dot(n2, w_ref[...])
            gu_ref[...] = both.astype(jnp.bfloat16)
            gate, up = both[:, :TILE], both[:, TILE:]
            hidden = (gate * jax.nn.sigmoid(gate) * up).astype(jnp.bfloat16)
            total[...] += dot(hidden, d_ref[...])

        @pl.when(step == steps - 1)
        def _():
            both = dot(n2, w_ref[:, : 2 * last])
            gu_ref[:, : 2 * last] = both.astype(jnp.bfloat16)
            gate, up = both[:, :last], both[:, last:]
            hidden = (gate * jax.nn.sigmoid(gate) * up).astype(jnp.bfloat16)
            summed = (total[...] + dot(hidden, d_ref[:last, :])).astype(jnp.bfloat16)
            for place in range(count):
                out_refs[place][...] = summed[place * part_rows : place * part_rows + part_rows]

    whole = lambda step: (0, 0)
    return call(
        kernel,
        [((rows, 2 * units), jnp.bfloat16)] + [((part_rows, D), jnp.bfloat16)] * count,
        9.0,
        [pltpu.VMEM((rows, D), jnp.float32)],
        grid=(steps,),
        in_specs=[pl.BlockSpec((part_rows, D), whole)] * count
        + [
            pl.BlockSpec((D, 2 * TILE), lambda step: (0, step)),
            pl.BlockSpec((TILE, D), lambda step: (step, 0)),
        ],
        out_specs=[
            pl.BlockSpec((rows, 2 * TILE), lambda step: (0, step)),
        ]
        + [pl.BlockSpec((part_rows, D), whole)] * count,
    )(*parts, gate_up_full, down_full)


def feed_back(gz_parts, n2_parts, gu_parts, gate_up_full, down_full, dp_place, group_count):
    line = group_count // 2
    half = line // 2
    chunk = D // group_count
    count = len(gz_parts)
    gu_count = len(gu_parts)
    part_rows = gz_parts[0].shape[0]
    rows = count * part_rows
    units = down_full.shape[0]
    steps = pl.cdiv(units, TILE)
    last = units - (steps - 1) * TILE

    def kernel(*refs):
        place_ref, *refs = refs
        gz_refs = refs[:count]
        n2_refs = refs[count : 2 * count]
        gu_refs = refs[2 * count : 2 * count + gu_count]
        w_ref, d_ref = refs[2 * count + gu_count : 2 * count + gu_count + 2]
        keep_near, keep_far, send_near, send_far, down_ref, own_ref, across_ref, pair_ref = refs[
            2 * count + gu_count + 2 : 2 * count + gu_count + 10
        ]
        total, gz, n2t = refs[-3:]
        side, mine = place_ref[0] % 2, place_ref[0] // 2
        step = pl.program_id(0)

        @pl.when(step == 0)
        def _():
            total[...] = jnp.zeros_like(total)
            for place in range(count):
                here = slice(place * part_rows, place * part_rows + part_rows)
                gz[here, :] = gz_refs[place][...]
                n2t[:, here] = n2_refs[place][...].T

        def work(width):
            gu = jnp.concatenate([ref[:, : 2 * width] for ref in gu_refs], axis=0).astype(jnp.float32)
            gate, up = gu[:, :width], gu[:, width:]
            sig = jax.nn.sigmoid(gate)
            act = gate * sig
            hidden = (act * up).astype(jnp.bfloat16)
            down_ref[:width, :] = dot(hidden, gz[...], TN).astype(jnp.bfloat16)
            grad = dot(gz[...], d_ref[:width, :], NT)
            d_gate = grad * up * (sig + act * (1.0 - sig))
            d_up = grad * act
            both = jnp.concatenate([d_gate, d_up], axis=1).astype(jnp.bfloat16)
            part = dot(n2t[...], both)
            for spot in range(line):
                even = part[2 * spot * chunk : (2 * spot + 1) * chunk].astype(jnp.bfloat16)
                odd = part[(2 * spot + 1) * chunk : (2 * spot + 2) * chunk].astype(jnp.bfloat16)
                keep = jnp.where(side == 0, even, odd)
                send = jnp.where(side == 0, odd, even)
                slot = mine ^ spot

                @pl.when(slot < half)
                def _():
                    keep_near[slot, :, : 2 * width] = keep
                    send_near[slot, :, : 2 * width] = send

                @pl.when(slot >= half)
                def _():
                    keep_far[slot - half, :, : 2 * width] = keep
                    send_far[slot - half, :, : 2 * width] = send

            return dot(both, w_ref[:, : 2 * width], NT)

        @pl.when(step < steps - 1)
        def _():
            total[...] += work(TILE)

        @pl.when(step == steps - 1)
        def _():
            summed = (total[...] + work(last)).astype(jnp.bfloat16)
            own_ref[...] = summed[:part_rows]
            pair_ref[0] = summed[part_rows : 2 * part_rows]
            across_ref[...] = summed[2 * part_rows : 3 * part_rows]
            pair_ref[1] = summed[3 * part_rows :]

    whole = lambda step: (0, 0)
    return call(
        kernel,
        [
            ((half, chunk, 2 * units), jnp.bfloat16),
            ((half, chunk, 2 * units), jnp.bfloat16),
            ((half, chunk, 2 * units), jnp.bfloat16),
            ((half, chunk, 2 * units), jnp.bfloat16),
            ((units, D), jnp.bfloat16),
            ((part_rows, D), jnp.bfloat16),
            ((part_rows, D), jnp.bfloat16),
            ((2, part_rows, D), jnp.bfloat16),
        ],
        25.0,
        [
            pltpu.VMEM((rows, D), jnp.float32),
            pltpu.VMEM((rows, D), jnp.bfloat16),
            pltpu.VMEM((D, rows), jnp.bfloat16),
        ],
        limit=56,
        grid=(steps,),
        in_specs=[pl.BlockSpec(memory_space=pltpu.SMEM)]
        + [pl.BlockSpec((part_rows, D), whole)] * (2 * count)
        + [pl.BlockSpec((rows // gu_count, 2 * TILE), lambda step: (0, step))] * gu_count
        + [
            pl.BlockSpec((D, 2 * TILE), lambda step: (0, step)),
            pl.BlockSpec((TILE, D), lambda step: (step, 0)),
        ],
        out_specs=[
            pl.BlockSpec((half, chunk, 2 * TILE), lambda step: (0, 0, step)),
            pl.BlockSpec((half, chunk, 2 * TILE), lambda step: (0, 0, step)),
            pl.BlockSpec((half, chunk, 2 * TILE), lambda step: (0, 0, step)),
            pl.BlockSpec((half, chunk, 2 * TILE), lambda step: (0, 0, step)),
            pl.BlockSpec((TILE, D), lambda step: (step, 0)),
            pl.BlockSpec((part_rows, D), whole),
            pl.BlockSpec((part_rows, D), whole),
            pl.BlockSpec((2, part_rows, D), lambda step: (0, 0, 0)),
        ],
    )(dp_place.reshape(1).astype(jnp.int32), *gz_parts, *n2_parts, *gu_parts, gate_up_full, down_full)


def norm_back(rows, gain, grad):
    inv_root = inverse_root(rows)
    normal = rows * inv_root
    gain_part = jnp.sum(grad * normal, axis=0, keepdims=True)
    weighted = grad * gain
    inner = jnp.mean(weighted * normal, axis=-1, keepdims=True)
    return gain_part, inv_root * (weighted - normal * inner)


def attention_back(upstream, middle, gain, terms, second_full, queries, kv_blocks, biases, cos_wide, sin_wide):
    count = len(terms)
    rows = middle.shape[0]
    span = rows // 2
    wide = GROUP * span

    def kernel(*refs):
        up_ref, mid_ref, gain_ref = refs[:3]
        term_refs = refs[3 : 3 + count]
        w_ref, q_ref, kv0, kv1, kv2, kv3, bias_ref, cos_ref, sin_ref = refs[3 + count : 12 + count]
        gm_ref, gy_ref, dgain_ref, gq_ref, own_ref, d1, d2, d3, go_ref, dkv = refs[12 + count :]
        kvs = (kv0, kv1, kv2, kv3)
        grad = term_refs[0][...].astype(jnp.float32)
        for term in term_refs[1:]:
            grad = grad + term[...].astype(jnp.float32)
        gain_part, back = norm_back(mid_ref[...], gain_ref[...], grad)
        dgain_ref[...] = gain_part
        grad_middle = up_ref[...].astype(jnp.float32) + back
        gm_ref[...] = grad_middle
        grad_low = grad_middle.astype(jnp.bfloat16)
        gy_ref[...] = grad_low
        for tile in range(D // 128):
            start = KV_WIDTH
            block = dot(grad_low, w_ref[tile * 128 : tile * 128 + 128, start:], NT).astype(jnp.bfloat16)
            for part in range(2):
                head = 2 * tile + part
                place = (head % GROUP) * span
                for half in range(2):
                    go_ref[head // GROUP, half, place : place + span, :] = block[
                        half * span : half * span + span, part * HEAD : part * HEAD + HEAD
                    ]
        for group in range(KV_HEADS):
            key_lanes = slice(group * HEAD, group * HEAD + HEAD)
            value_lanes = slice(KV_WIDTH + group * HEAD, KV_WIDTH + group * HEAD + HEAD)
            keys = [key_part(kvs, half, key_lanes) for half in range(2)]
            values = [key_part(kvs, half, value_lanes) for half in range(2)]
            for half in range(2):
                query = q_ref[group, half] * jnp.bfloat16(SCALE)
                grad_out = go_ref[group, half]
                bias = jnp.concatenate([bias_ref[half]] * GROUP, axis=1)
                use = [half] if half == 0 else [1, 0]
                scores = []
                top = None
                for which in use:
                    score = dot(keys[which], query, NT)
                    if which == half:
                        score = score + bias
                    scores.append(score)
                    best = jnp.max(score, axis=0, keepdims=True)
                    top = best if top is None else jnp.maximum(top, best)
                weights = [jnp.exp(score - top) for score in scores]
                total = sum(jnp.sum(weight, axis=0, keepdims=True) for weight in weights)
                scale = 1.0 / total
                probs = [weight * scale for weight in weights]
                grads = [dot(values[which], grad_out, NT) for which in use]
                inner = sum(
                    jnp.sum(prob * grad_prob, axis=0, keepdims=True)
                    for prob, grad_prob in zip(probs, grads)
                )
                grad_query = None
                for which, prob, grad_prob in zip(use, probs, grads):
                    grad_score = (prob * (grad_prob - inner)).astype(jnp.bfloat16)
                    value_grad = dot(prob.astype(jnp.bfloat16), grad_out)
                    key_grad = dot(grad_score, query)
                    if half == 0:
                        dkv[group, which] = key_grad
                        dkv[KV_HEADS + group, which] = value_grad
                    elif which == 0:
                        dkv[group, which] += key_grad
                        dkv[KV_HEADS + group, which] += value_grad
                    else:
                        dkv[group, which] = key_grad
                        dkv[KV_HEADS + group, which] = value_grad
                    term = dot(keys[which].T, grad_score)
                    grad_query = term if grad_query is None else grad_query + term
                grad_query = grad_query * SCALE
                cos_w = cos_ref[half * span : half * span + span, :]
                sin_w = sin_ref[half * span : half * span + span, :]
                for member in range(GROUP):
                    head = group * GROUP + member
                    piece = grad_query[:, member * span : member * span + span].T
                    pair = jnp.concatenate([piece, piece], axis=1)
                    turned = turn(pair, cos_w, -sin_w)[:, :HEAD]
                    gq_ref[half * span : half * span + span, head * HEAD : head * HEAD + HEAD] = (
                        turned.astype(jnp.bfloat16)
                    )
        for place, out in enumerate((own_ref, d1, d2, d3)):
            for half in range(2):
                block = jnp.concatenate(
                    [dkv[lane, half, place * span : place * span + span, :] for lane in range(2 * KV_HEADS)],
                    axis=1,
                )
                out[half * span : half * span + span, :] = block.astype(out.dtype)

    return call(
        kernel,
        [
            ((rows, D), jnp.float32),
            ((rows, D), jnp.bfloat16),
            ((1, D), jnp.float32),
            ((rows, D), jnp.bfloat16),
            ((rows, 2 * KV_WIDTH), jnp.float32),
        ]
        + [((rows, 2 * KV_WIDTH), jnp.bfloat16)] * 3,
        13.0,
        [
            pltpu.VMEM((KV_HEADS, 2, wide, HEAD), jnp.bfloat16),
            pltpu.VMEM((2 * KV_HEADS, 2, 4 * span, HEAD), jnp.float32),
        ],
    )(upstream, middle, gain, *terms, second_full, queries, *kv_blocks, biases, cos_wide, sin_wide)


def before_back(kv_terms, gq, x, gain, grad_middle, first_full, second_full, cos_wide, sin_wide):
    rows = x.shape[0]
    count = len(kv_terms)

    def kernel(*refs):
        kv_refs = refs[:count]
        gq_ref, x_ref, gain_ref, gm_ref, w1_ref, w2_ref, cos_ref, sin_ref = refs[count : count + 8]
        up_ref, low_ref, gkv_ref, dgain_ref, bias_one, bias_two = refs[count + 8 :]
        grad = kv_refs[0][...].astype(jnp.float32)
        for ref in kv_refs[1:]:
            grad = grad + ref[...].astype(jnp.float32)
        grad_key = turn(grad[:, :KV_WIDTH], cos_ref[...], -sin_ref[...]).astype(jnp.bfloat16)
        grad_value = grad[:, KV_WIDTH:].astype(jnp.bfloat16)
        gkv_ref[:, :KV_WIDTH] = grad_key
        gkv_ref[:, KV_WIDTH:] = grad_value
        grad_query = gq_ref[...]
        bias_one[:, :D] = jnp.sum(grad_query.astype(jnp.float32), axis=0, keepdims=True)
        bias_one[:, D:] = jnp.sum(grad_key.astype(jnp.float32), axis=0, keepdims=True)
        bias_two[...] = jnp.sum(grad_value.astype(jnp.float32), axis=0, keepdims=True)
        grad_normed = (
            dot(grad_query, w1_ref[:, :D], NT)
            + dot(grad_key, w1_ref[:, D:], NT)
            + dot(grad_value, w2_ref[:, :KV_WIDTH], NT)
        )
        gain_part, back = norm_back(x_ref[...], gain_ref[...], grad_normed)
        dgain_ref[...] = gain_part
        upstream = gm_ref[...] + back
        up_ref[...] = upstream
        low_ref[...] = upstream.astype(jnp.bfloat16)

    return call(
        kernel,
        [
            ((rows, D), jnp.float32),
            ((rows, D), jnp.bfloat16),
            ((rows, 2 * KV_WIDTH), jnp.bfloat16),
            ((1, D), jnp.float32),
            ((1, SPLIT), jnp.float32),
            ((1, KV_WIDTH), jnp.float32),
        ],
        2.4,
    )(*kv_terms, gq, x, gain, grad_middle, first_full, second_full, cos_wide, sin_wide)


def unit_pieces(unit_rows, group_count, seq_devices):
    units = unit_rows * group_count
    steps = pl.cdiv(units, TILE)
    pieces = []
    for owner in range(seq_devices):
        for kind in range(2):
            for group in range(group_count):
                unit = group * unit_rows
                stop = unit + unit_rows
                column = kind * units * seq_devices + (group * seq_devices + owner) * unit_rows
                while unit < stop:
                    step = unit // TILE
                    end = min(stop, (step + 1) * TILE)
                    width = TILE if step < steps - 1 else units - (steps - 1) * TILE
                    inside = 2 * step * TILE + kind * width + unit - step * TILE
                    pieces.append((owner, inside, column, end - unit))
                    column += end - unit
                    unit = end
    return pieces


def spread_columns(weight, place, unit_rows, group_count, seq_devices):
    layers, rows, columns = weight.shape
    quarter = columns // seq_devices
    pieces = unit_pieces(unit_rows, group_count, seq_devices)

    def kernel(place_ref, w_ref, *refs):
        outs, wide, narrow = refs[:seq_devices], refs[-2], refs[-1]
        for layer in range(layers):
            wide[...] = w_ref[layer].astype(jnp.float32)
            for owner in range(seq_devices):
                for who, inside, column, width in pieces:
                    if who == owner:
                        narrow[:, inside : inside + width] = wide[:, column : column + width]
                block = narrow[...].astype(jnp.bfloat16)
                for bit in range(seq_devices):

                    @pl.when(place_ref[0] == owner ^ bit)
                    def _():
                        outs[bit][layer] = block

    return call(
        kernel,
        [((layers, rows, quarter), jnp.bfloat16)] * seq_devices,
        2.5,
        [pltpu.VMEM((rows, columns), jnp.float32), pltpu.VMEM((rows, quarter), jnp.float32)],
        in_specs=[pl.BlockSpec(memory_space=pltpu.SMEM), FULL],
        out_specs=[FULL] * seq_devices,
    )(place.reshape(1).astype(jnp.int32), weight)


def collect_columns(blocks, place, unit_rows, group_count):
    count = len(blocks)
    rows, quarter = blocks[0].shape
    pieces = unit_pieces(unit_rows, group_count, count)

    def kernel(place_ref, *refs):
        out_ref, narrow = refs[count:]
        me = place_ref[0]
        for owner in range(count):
            for bit in range(count):

                @pl.when(me == owner ^ bit)
                def _():
                    narrow[...] = refs[bit][...].astype(jnp.float32)

            for who, inside, column, width in pieces:
                if who == owner:
                    out_ref[:, column : column + width] = narrow[:, inside : inside + width]

    return call(
        kernel,
        [((rows, count * quarter), jnp.float32)],
        1.5,
        [pltpu.VMEM((rows, quarter), jnp.float32)],
        in_specs=[pl.BlockSpec(memory_space=pltpu.SMEM)] + [FULL] * count,
        out_specs=[FULL],
    )(place.reshape(1).astype(jnp.int32), *blocks)[0]


def join_rows(blocks, place):
    owners = len(blocks)
    layers, rows, columns = blocks[0].shape

    def kernel(place_ref, *refs):
        ins, outs = refs[:owners], refs[owners:]
        for layer in range(layers):
            parts = []
            for owner in range(owners):
                part = ins[0][layer].astype(jnp.float32)
                for bit in range(1, owners):
                    part = jnp.where(
                        place_ref[0] == owner ^ bit, ins[bit][layer].astype(jnp.float32), part
                    )
                parts.append(part)
            outs[layer][0] = jnp.concatenate(parts, axis=0).astype(jnp.bfloat16)

    return call(
        kernel,
        [((1, owners * rows, columns), jnp.bfloat16)] * layers,
        2.0,
        in_specs=[pl.BlockSpec(memory_space=pltpu.SMEM)] + [FULL] * owners,
        out_specs=[FULL] * layers,
    )(place.reshape(1).astype(jnp.int32), *blocks)


def split_rows(terms, place, count):
    number, total_rows, columns = terms.shape
    rows = total_rows // count

    def kernel(place_ref, in_ref, *outs):
        total = in_ref[0].astype(jnp.float32)
        for k in range(1, number):
            total = total + in_ref[k].astype(jnp.float32)
        for owner in range(count):
            block = total[owner * rows : owner * rows + rows].astype(jnp.bfloat16)
            for bit in range(count):

                @pl.when(place_ref[0] == owner ^ bit)
                def _():
                    outs[bit][...] = block

    return call(
        kernel,
        [((rows, columns), jnp.bfloat16)] * count,
        2.0,
        in_specs=[pl.BlockSpec(memory_space=pltpu.SMEM), FULL],
        out_specs=[FULL] * count,
    )(place.reshape(1).astype(jnp.int32), terms)


def lay_out(blocks, places):
    total = len(places)
    shape = blocks[0].shape[-2:]
    count = len(blocks)

    def kernel(place_ref, *refs):
        ins, out, sems = refs[:count], refs[count], refs[-1]
        copies = []
        spot = 0
        for which in range(count):
            many = blocks[which].shape[0] if blocks[which].ndim == 3 else 1
            for k in range(many):
                source = ins[which].at[k] if blocks[which].ndim == 3 else ins[which]
                copies.append(
                    pltpu.make_async_copy(source, out.at[place_ref[spot]], sems.at[spot])
                )
                spot += 1
        for copy in copies:
            copy.start()
        for copy in copies:
            copy.wait()

    outside = pl.BlockSpec(memory_space=pltpu.HBM)
    return call(
        kernel,
        [((total,) + shape, blocks[0].dtype)],
        2.5,
        [pltpu.SemaphoreType.DMA((total,))],
        in_specs=[pl.BlockSpec(memory_space=pltpu.SMEM)] + [outside] * count,
        out_specs=[outside],
    )(jnp.stack(places).astype(jnp.int32), *blocks)[0]


def assemble(parts, places, chip_rows):
    line, rows, width = parts[0].shape

    def kernel(place_ref, *refs):
        ins = refs[:8]
        first_ref, second_ref, small_ref = refs[8:]
        here, chip, side = place_ref[0] == 0, place_ref[1] == 0, place_ref[2] % 2 == 0
        mine = place_ref[2] // 2
        small = jnp.zeros((rows - chip_rows, width), jnp.float32)
        for spot in range(line):
            halves = []
            for half in range(2):
                pieces = []
                blocks = [ins[4 * half + k][spot].astype(jnp.float32) for k in range(4)]
                for block in blocks:
                    small = small + block[chip_rows:]
                lower = [jnp.where(side, blocks[2 * x], blocks[2 * x + 1]) for x in range(2)]
                upper = [jnp.where(side, blocks[2 * x + 1], blocks[2 * x]) for x in range(2)]
                for pair in (lower, upper):
                    pieces.append(jnp.where(chip, pair[0], pair[1])[:chip_rows])
                    pieces.append(jnp.where(chip, pair[1], pair[0])[:chip_rows])
                halves.append(jnp.concatenate(pieces, axis=0).astype(jnp.bfloat16))
            first_ref[mine ^ spot] = jnp.where(here, halves[0], halves[1])
            second_ref[mine ^ spot] = jnp.where(here, halves[1], halves[0])
        small_ref[...] = small

    first, second, small = call(
        kernel,
        [
            ((line, 4 * chip_rows, width), jnp.bfloat16),
            ((line, 4 * chip_rows, width), jnp.bfloat16),
            ((rows - chip_rows, width), jnp.float32),
        ],
        4.0,
        in_specs=[pl.BlockSpec(memory_space=pltpu.SMEM)] + [FULL] * 8,
        out_specs=[FULL] * 3,
    )(jnp.stack(places).astype(jnp.int32), *parts)
    return first.reshape(-1, width), second.reshape(-1, width), small


def projection_grads(normed, grad_query, grad_kv, mixed, grad_low, gain_one, gain_two, bias_one, bias_two, places, chip_rows, line):
    width = SPLIT

    def kernel(place_ref, n_ref, gq_ref, gkv_ref, mixed_ref, gy_ref, g1_ref, g2_ref, b1_ref, b2_ref, keep0, keep1, send0, send1, pad):
        here, chip, side = place_ref[0] == 0, place_ref[1] == 0, place_ref[2] % 2
        mine = place_ref[2] // 2
        turned = n_ref[...].T
        pad[...] = jnp.zeros_like(pad)
        pad[0:1, :D] = g1_ref[...]
        pad[1:2, :D] = g2_ref[...]
        pad[2:3, :] = b1_ref[...]
        pad[3:4, :KV_WIDTH] = b2_ref[...]
        small = pad[...]
        first = jnp.concatenate(
            [dot(turned, gq_ref[...]), dot(turned, gkv_ref[:, :KV_WIDTH])], axis=1
        )
        second = jnp.concatenate(
            [dot(turned, gkv_ref[:, KV_WIDTH:]), dot(mixed_ref[...], gy_ref[...], TN)], axis=1
        )

        def chunk(part, number):
            rows = part[number * chip_rows : (number + 1) * chip_rows]
            return jnp.concatenate([rows, small], axis=0).astype(jnp.bfloat16)

        for spot in range(line):
            for pair in range(2):
                slot = side ^ pair
                firsts = [chunk(first, 4 * spot + 2 * pair + x) for x in range(2)]
                seconds = [chunk(second, 4 * spot + 2 * pair + x) for x in range(2)]
                keeps = [jnp.where(here, one, two) for one, two in zip(firsts, seconds)]
                sends = [jnp.where(here, two, one) for one, two in zip(firsts, seconds)]
                keep0[slot, mine ^ spot] = jnp.where(chip, keeps[0], keeps[1])
                keep1[slot, mine ^ spot] = jnp.where(chip, keeps[1], keeps[0])
                send0[slot, mine ^ spot] = jnp.where(chip, sends[0], sends[1])
                send1[slot, mine ^ spot] = jnp.where(chip, sends[1], sends[0])

    return call(
        kernel,
        [((2, line, chip_rows + 8, width), jnp.bfloat16)] * 4,
        6.0,
        [pltpu.VMEM((8, width), jnp.float32)],
        in_specs=[pl.BlockSpec(memory_space=pltpu.SMEM)] + [FULL] * 9,
        out_specs=[FULL] * 4,
    )(
        jnp.stack(places).astype(jnp.int32),
        normed,
        grad_query,
        grad_kv,
        mixed,
        grad_low,
        gain_one,
        gain_two,
        bias_one,
        bias_two,
    )


def swap(values, axis, bit):
    size = lax.axis_size(axis)
    return lax.ppermute(values, axis, [(i, i ^ bit) for i in range(size)])


def after(values, *others):
    return lax.optimization_barrier((values,) + tuple(others))[0]


def line_bits():
    bits = [1]
    while 4 * bits[-1] < lax.axis_size("dp"):
        bits.append(2 * bits[-1])
    return bits


def line_gather(values, bits):
    for bit in bits:
        values = jnp.concatenate([values, swap(values, "dp", 2 * bit)], axis=0)
    return values


def line_scatter(values, bits):
    for bit in bits[:0:-1]:
        values = add_low(values[:bit], swap(values[bit:], "dp", 2 * bit))
    return [values[0], swap(values[1], "dp", 2)]


def add_low(left, right):
    return (left.astype(jnp.float32) + right.astype(jnp.float32)).astype(jnp.bfloat16)


def group_rows(values):
    beside = swap(values, "seq", 1)
    across = swap(values, "seq", 2)
    return [values, beside, across, swap(across, "seq", 1)]


def placed(values, offset, width):
    return lax.dynamic_update_slice(jnp.zeros((width,), values.dtype), values, (offset,))


def body(
    tokens,
    cotangent,
    span_order,
    attn_gain,
    joined_weight,
    joined_bias,
    out_weight,
    mlp_gain,
    gate_up_weight,
    down_weight,
):
    seq_count, tok_len, model_width = tokens.shape
    span_len = tok_len // 2
    group_count = lax.axis_size("dp")
    seq_devices = lax.axis_size("seq")
    unit_rows = down_weight.shape[1]
    width_rows = gate_up_weight.shape[1]
    units = group_count * unit_rows
    dp_place = lax.axis_index("dp")
    seq_place = lax.axis_index("seq")
    core = seq_place % 2
    chip_x = seq_place // 2
    device = dp_place * seq_devices + seq_place
    chip_rows = 2 * width_rows
    line = group_count // 2
    side = dp_place % 2

    order = [lax.dynamic_slice(span_order, (0, seq_place ^ bit), (1, 1))[0, 0] for bit in range(4)]
    inside = jnp.arange(span_len, dtype=jnp.int32)
    own_places = jnp.concatenate(
        [order[0] * span_len + inside, (2 * seq_devices - 1 - order[0]) * span_len + inside]
    )
    half_biases = []
    for half in range(2):
        blocks = []
        for bit in range(4):
            ahead = order[bit] < order[0] if half == 0 else order[bit] > order[0]
            allowed = ahead | ((order[bit] == order[0]) & (inside[:, None] >= inside[None, :]))
            blocks.append(jnp.where(allowed, 0.0, NEGATIVE).astype(jnp.float32))
        half_biases.append(jnp.concatenate(blocks, axis=1))
    biases = jnp.stack(half_biases)
    biases_turned = jnp.swapaxes(biases, 1, 2)
    cos_table, sin_table = rotary_tables(own_places)
    cos_wide = jnp.concatenate([cos_table] * 4, axis=1)
    sin_wide = jnp.concatenate([-sin_table, sin_table] * 2, axis=1)

    def attn_shard(layer):
        first = joined_weight[layer][:, :SPLIT]
        second = jnp.concatenate([joined_weight[layer][:, SPLIT:], out_weight[layer]], axis=1)
        got = swap(jnp.where(core == 0, second, first), "seq", 1)
        mine = jnp.where(core == 0, first, second)
        rows = jnp.where(core == 0, jnp.stack([mine, got]), jnp.stack([got, mine])).reshape(
            chip_rows, -1
        )
        bias_all = placed(joined_bias[layer], device * joined_bias.shape[1], SPLIT + KV_WIDTH)
        extra = jnp.zeros((8, SPLIT), jnp.bfloat16)
        extra = extra.at[0].set(placed(attn_gain[layer], device * width_rows, SPLIT))
        extra = extra.at[1].set(placed(mlp_gain[layer], device * width_rows, SPLIT))
        extra = extra.at[2].set(bias_all[:SPLIT])
        extra = extra.at[3, :KV_WIDTH].set(bias_all[SPLIT:])
        return jnp.concatenate([rows, extra], axis=0)

    def attn_finish(near):
        far = swap(near, "dp", 1)
        across = swap(near, "seq", 2)
        parts = [near, far, across, swap(far, "seq", 2)]
        parts = parts + [swap(part, "seq", 1) for part in parts]
        first_full, second_full, small = assemble(parts, [core, chip_x, dp_place], chip_rows)
        return (
            first_full,
            second_full,
            small[0:1, :model_width],
            small[1:2, :model_width],
            small[2:3],
            small[3:4, :KV_WIDTH],
        )

    bits = line_bits()
    spread = spread_columns(gate_up_weight, seq_place, unit_rows, group_count, seq_devices)
    shards = [attn_shard(layer)[None] for layer in range(LAYERS)]
    down_full = [
        lax.all_gather(down_weight[layer], "dp", axis=0, tiled=True) for layer in range(LAYERS)
    ]
    gate_blocks = [spread[0]] + [swap(spread[bit], "seq", bit) for bit in range(1, 4)]
    gate_shards = join_rows(gate_blocks, seq_place)
    attn_near = [line_gather(after(shards[0], *spread), bits)]
    attn_near.append(line_gather(after(shards[1], attn_near[0]), bits))
    gate_near = []
    gate_far = []
    gate_near_pair = []
    started = attn_near[0]
    for layer in range(LAYERS):
        gate_near.append(line_gather(after(gate_shards[layer], started), bits[:-1]))
        gate_far.append(swap(gate_near[layer], "dp", 2 * bits[-1]))
        gate_near_pair.append(swap(gate_near[layer], "dp", 1))
        started = gate_far[layer]
    attn_sets = [attn_finish(after(attn_near[0], *gate_shards)), attn_finish(attn_near[1])]
    half = line // 2
    offsets = [dp_place ^ (2 * k) for k in range(line)]
    places = offsets + [offset ^ 1 for offset in offsets]

    def gate_finish(layer):
        far_pair = swap(gate_far[layer], "dp", 1)
        blocks = [gate_near[layer], gate_far[layer], gate_near_pair[layer], far_pair]
        return lay_out(blocks, places).reshape(model_width, 2 * units)

    terms = [tokens.reshape(tok_len, model_width)]
    kept_state = []
    gate_up_full = []
    for layer in range(LAYERS):
        first_full, second_full, gain_full, mlp_gain_full, bias_first, bias_second = attn_sets[layer]
        x, normed, queries, own_kv = before_attention(
            terms,
            after(gain_full, gate_near[0], attn_near[1]) if layer == 0 else after(gain_full, gate_far[1]),
            first_full,
            second_full,
            bias_first,
            bias_second,
            cos_wide,
            sin_wide,
        )
        kv_blocks = [own_kv] + [swap(own_kv, "seq", bit) for bit in range(1, 4)]
        waited = (gate_near_pair[layer],)
        mixed, middle, n2 = attention(
            queries, kv_blocks, biases, x, second_full, after(mlp_gain_full, *waited)
        )
        n2_parts = group_rows(n2)
        gate_up_full.append(gate_finish(layer))
        gu_near, *outs_near = feed_forward(n2_parts[:2], gate_up_full[layer], down_full[layer])
        gu_far, *outs_far = feed_forward(n2_parts[2:], gate_up_full[layer], down_full[layer])
        far = add_low(outs_far[0], swap(outs_far[1], "seq", 1))
        terms = [middle, outs_near[0], swap(outs_near[1], "seq", 1), swap(far, "seq", 2)]
        kept_state.append((x, normed, queries, kv_blocks, mixed, middle, n2_parts, [gu_near, gu_far]))
    activations = sum(term.astype(jnp.float32) for term in terms).astype(jnp.bfloat16)
    upstream = cotangent.reshape(tok_len, model_width)
    upstream_low = upstream
    results = [None] * LAYERS
    before = None

    def send_attn(state, pair, *waited):
        near, far, got_near, got_far = state["attn_parts"]
        return swap(after(add_low(far[pair], got_far[pair]), *waited), "seq", 2)

    def sum_attn(state, arrived, *waited):
        near, far, got_near, got_far = state["attn_parts"]
        sums = [
            (
                near[pair].astype(jnp.float32)
                + got_near[pair].astype(jnp.float32)
                + after(arrived[pair], *waited).astype(jnp.float32)
            ).astype(jnp.bfloat16)
            for pair in range(2)
        ]
        return add_low(sums[0], swap(sums[1], "dp", 1))

    def sum_gate(state, *waited):
        near = add_low(state["keep_near"], after(state["near_got"], *waited))
        return add_low(near, after(state["gate_got"], *waited))

    def finish(state, gate_sum, attn_sum, *waited):
        gate_terms = jnp.stack(line_scatter(gate_sum, bits[:-1]))
        gate_rows = split_rows(after(gate_terms, *waited), seq_place, seq_devices)
        gate_owned = collect_columns(
            [gate_rows[0]] + [swap(gate_rows[bit], "seq", bit) for bit in range(1, 4)],
            seq_place,
            unit_rows,
            group_count,
        )
        owned = sum(
            term.astype(jnp.float32) for term in line_scatter(attn_sum, bits)
        )
        extra = owned[chip_rows:]
        halves = owned[:chip_rows].reshape(2, width_rows, -1)
        mine = lax.dynamic_index_in_dim(halves, core, 0, keepdims=False)
        theirs = swap(
            lax.dynamic_index_in_dim(halves, 1 - core, 0, keepdims=False), "seq", 1
        )
        first_own = jnp.where(core == 0, mine, theirs)
        second_own = jnp.where(core == 0, theirs, mine)

        def cut(row, width, stop):
            return lax.dynamic_slice(extra[row, :stop], (device * width,), (width,))

        results[state["layer"]] = (
            cut(0, width_rows, model_width),
            jnp.concatenate([first_own, second_own[:, :KV_WIDTH]], axis=1),
            cut(2, SPLIT // (group_count * seq_devices), SPLIT),
            cut(3, KV_WIDTH // (group_count * seq_devices), KV_WIDTH),
            second_own[:, KV_WIDTH:],
            cut(1, width_rows, model_width),
            gate_owned,
            state["down_sum"],
        )

    for layer in reversed(range(LAYERS)):
        x, normed, queries, kv_blocks, mixed, middle, n2_parts, gu_parts = kept_state[layer]
        first_full, second_full, gain_full, mlp_gain_full, _, _ = attn_sets[layer]
        low_parts = group_rows(upstream_low)
        if before is not None:
            low_parts[0] = after(low_parts[0], before["attn_parts"][3])
        keep_near, keep_far, send_near, send_far, down_part, own_out, across_out, pair_out = feed_back(
            low_parts,
            n2_parts,
            gu_parts,
            gate_up_full[layer],
            down_full[layer],
            dp_place,
            group_count,
        )
        got = swap(pair_out, "seq", 1)
        out_terms = [own_out, got[0], swap(add_low(across_out, got[1]), "seq", 2)]
        down_sum = lax.psum_scatter(down_part, "dp", scatter_dimension=0, tiled=True).astype(
            jnp.float32
        )
        got_far = swap(send_far, "dp", 1)
        gate_far_sum = add_low(keep_far, got_far)
        near_got = swap(after(send_near, got_far), "dp", 1)
        if before is not None:
            attn_far = send_attn(before, 1, out_terms[2])
            gate_before = sum_gate(before, own_out)
        grad_middle, grad_low, mlp_gain_part, grad_query, own_term, *kv_terms = attention_back(
            upstream,
            middle,
            mlp_gain_full,
            out_terms,
            second_full,
            queries,
            kv_blocks,
            biases_turned,
            cos_wide,
            sin_wide,
        )
        kv_terms = [own_term] + [swap(kv_terms[bit - 1], "seq", bit) for bit in range(1, 4)]
        if before is not None:
            attn_near_sent = send_attn(before, 0, *kv_terms[1:])
        upstream, upstream_low, grad_kv, attn_gain_part, bias_first, bias_second = before_back(
            kv_terms,
            grad_query,
            x,
            after(gain_full, gate_far_sum)
            if before is None
            else after(gain_full, gate_far_sum, gate_before),
            grad_middle,
            first_full,
            second_full,
            cos_wide,
            sin_wide,
        )
        near, far, near_other, far_other = projection_grads(
            normed,
            grad_query,
            grad_kv,
            mixed,
            grad_low,
            attn_gain_part,
            mlp_gain_part,
            bias_first,
            bias_second,
            [core, chip_x, dp_place],
            chip_rows,
            line,
        )
        got_far_other = swap(far_other, "seq", 1)
        got_near_other = swap(near_other, "seq", 1)
        state = {
            "layer": layer,
            "keep_near": keep_near,
            "near_got": near_got,
            "gate_got": swap(after(gate_far_sum, upstream_low), "dp", 2 * bits[-1]),
            "attn_parts": (near, far, got_near_other, got_far_other),
            "down_sum": down_sum,
        }
        if before is not None:
            attn_sum = sum_attn(before, [attn_near_sent, attn_far], grad_low)
            finish(before, gate_before, attn_sum, near)
        before = state
    arrived = [None, send_attn(before, 1)]
    arrived[0] = send_attn(before, 0)
    finish(before, sum_gate(before), sum_attn(before, arrived))
    return (
        activations.reshape(seq_count, tok_len, model_width),
        upstream.reshape(seq_count, tok_len, model_width),
    ) + tuple(jnp.stack([results[layer][k] for layer in range(LAYERS)]) for k in range(8))


def solution(mesh):
    in_specs = (
        P("dp", "seq", None),
        P("dp", "seq", None),
        P("dp", None),
        P(None, ("dp", "seq")),
        P(None, ("dp", "seq"), None),
        P(None, ("dp", "seq")),
        P(None, ("dp", "seq"), None),
        P(None, ("dp", "seq")),
        P(None, ("dp", "seq"), None),
        P(None, ("dp", "seq"), None),
    )
    out_specs = (
        P("dp", "seq", None),
        P("dp", "seq", None),
        P(None, ("dp", "seq")),
        P(None, ("dp", "seq"), None),
        P(None, ("dp", "seq")),
        P(None, ("dp", "seq")),
        P(None, ("dp", "seq"), None),
        P(None, ("dp", "seq")),
        P(None, ("dp", "seq"), None),
        P(None, ("dp", "seq"), None),
    )
    return jax.shard_map(body, mesh=mesh, in_specs=in_specs, out_specs=out_specs, check_vma=False)
```

```python
import jax
import jax.numpy as jnp
from jax import lax
from jax.experimental import pallas as pl
from jax.experimental.pallas import tpu as pltpu
from jax.sharding import PartitionSpec as P

D = 896
HEADS = 14
KV_HEADS = 2
HEAD = 64
LAYERS = 2


EPS = 1e-06
THETA = 1000000.0
NEGATIVE = -1e30


def rotary_tables(positions):
    half_head = HEAD // 2
    frequency = THETA ** (-2.0 * jnp.arange(half_head, dtype=jnp.float32) / HEAD)
    angles = positions.astype(jnp.float32)[..., None] * frequency
    return (jnp.cos(angles), jnp.sin(angles))


NT = (((1,), (1,)), ((), ()))
TN = (((0,), (0,)), ((), ()))
FULL = pl.BlockSpec(memory_space=pltpu.VMEM)
SCALE = HEAD ** (-0.5)
GROUP = HEADS // KV_HEADS
KV_WIDTH = KV_HEADS * HEAD
SPLIT = D + KV_WIDTH
TILE = 384


def dot(left, right, dims=(((1,), (0,)), ((), ()))):
    return lax.dot_general(left, right, dims, preferred_element_type=jnp.float32)


def call(kernel, outs, micros, scratch=(), limit=40, **grid):
    return pl.pallas_call(
        kernel,
        out_shape=[jax.ShapeDtypeStruct(shape, kind) for shape, kind in outs],
        scratch_shapes=list(scratch),
        compiler_params=pltpu.CompilerParams(vmem_limit_bytes=limit * 2**20),
        name=kernel.__qualname__.split(".")[0],
        cost_estimate=pl.CostEstimate(
            flops=0, bytes_accessed=int(micros * 4e3), transcendentals=0
        ),
        **grid,
    )


def turn(block, cos_wide, sin_wide):
    lane = lax.broadcasted_iota(jnp.int32, block.shape, 1)
    width = block.shape[1]
    partner = jnp.where(
        lane % HEAD < HEAD // 2,
        pltpu.roll(block, width - HEAD // 2, 1),
        pltpu.roll(block, HEAD // 2, 1),
    )
    return block * cos_wide + partner * sin_wide


def inverse_root(rows):
    return lax.rsqrt(jnp.mean(rows * rows, axis=-1, keepdims=True) + EPS)


def before_attention(terms, gain, first_full, second_full, bias_first, bias_second, cos_wide, sin_wide):
    count = len(terms)
    rows = terms[0].shape[0]
    span = rows // 2

    def kernel(*refs):
        parts = refs[:count]
        gain_ref, first_ref, second_ref, bias_one, bias_two, cos_ref, sin_ref = refs[count : count + 7]
        x_ref, n_ref, q_ref, kv_ref = refs[count + 7 :]
        x = parts[0][...].astype(jnp.float32)
        for part in parts[1:]:
            x = x + part[...].astype(jnp.float32)
        x_ref[...] = x
        normed = (x * inverse_root(x) * gain_ref[...]).astype(jnp.bfloat16)
        n_ref[...] = normed
        cos_w, sin_w = cos_ref[...], sin_ref[...]
        for tile in range(SPLIT // 128):
            lanes = slice(tile * 128, tile * 128 + 128)
            block = dot(normed, first_ref[:, lanes]) + bias_one[:, lanes]
            turned = turn(block, cos_w, sin_w)
            if tile * 128 < D:
                for part in range(2):
                    head = 2 * tile + part
                    piece = turned[:, part * HEAD : part * HEAD + HEAD].astype(jnp.bfloat16)
                    place = (head % GROUP) * span
                    for half in range(2):
                        q_ref[head // GROUP, half, place : place + span, :] = piece[
                            half * span : half * span + span
                        ]
            else:
                kv_ref[:, :KV_WIDTH] = turned.astype(jnp.bfloat16)
        kv_ref[:, KV_WIDTH:] = (
            dot(normed, second_ref[:, :KV_WIDTH]) + bias_two[...]
        ).astype(jnp.bfloat16)

    return call(
        kernel,
        [
            ((rows, D), jnp.float32),
            ((rows, D), jnp.bfloat16),
            ((KV_HEADS, 2, GROUP * span, HEAD), jnp.bfloat16),
            ((rows, 2 * KV_WIDTH), jnp.bfloat16),
        ],
        4.0,
    )(*terms, gain, first_full, second_full, bias_first, bias_second, cos_wide, sin_wide)


def key_part(kv_refs, half, lanes):
    span = kv_refs[0].shape[0] // 2
    return jnp.concatenate(
        [ref[half * span : half * span + span, lanes] for ref in kv_refs], axis=0
    )


def attention(queries, kv_blocks, biases, x, second_full, gain):
    rows = x.shape[0]
    span = rows // 2

    def kernel(q_ref, kv0, kv1, kv2, kv3, bias_ref, x_ref, w_ref, gain_ref, mixed_ref, mid_ref, n_ref):
        kvs = (kv0, kv1, kv2, kv3)
        for group in range(KV_HEADS):
            key_lanes = slice(group * HEAD, group * HEAD + HEAD)
            value_lanes = slice(KV_WIDTH + group * HEAD, KV_WIDTH + group * HEAD + HEAD)
            keys = [key_part(kvs, half, key_lanes) for half in range(2)]
            values = []
            for half in range(2):
                block = key_part(kvs, half, value_lanes)
                values.append(jnp.concatenate([block, jnp.ones_like(block)], axis=1))
            for half in range(2):
                bias = bias_ref[half]
                for member in range(GROUP):
                    query = q_ref[group, half, member * span : member * span + span, :] * jnp.bfloat16(SCALE)
                    near = dot(query, keys[half], NT) + bias
                    top = jnp.max(near, axis=-1, keepdims=True)
                    if half == 1:
                        far = dot(query, keys[0], NT)
                        top = jnp.maximum(top, jnp.max(far, axis=-1, keepdims=True))
                    total = dot(jnp.exp(near - top).astype(jnp.bfloat16), values[half])
                    if half == 1:
                        total = total + dot(jnp.exp(far - top).astype(jnp.bfloat16), values[0])
                    out = total[:, :HEAD] / total[:, HEAD : 2 * HEAD]
                    head = group * GROUP + member
                    mixed_ref[half * span : half * span + span, head * HEAD : head * HEAD + HEAD] = (
                        out.astype(jnp.bfloat16)
                    )
        middle = x_ref[...] + dot(mixed_ref[...], w_ref[:, KV_WIDTH:])
        mid_ref[...] = middle
        n_ref[...] = (middle * inverse_root(middle) * gain_ref[...]).astype(jnp.bfloat16)

    return call(
        kernel,
        [((rows, D), jnp.bfloat16), ((rows, D), jnp.float32), ((rows, D), jnp.bfloat16)],
        10.5,
    )(queries, *kv_blocks, biases, x, second_full, gain)


def feed_forward(parts, gate_up_full, down_full):
    count = len(parts)
    part_rows = parts[0].shape[0]
    rows = count * part_rows
    units = down_full.shape[0]
    steps = pl.cdiv(units, TILE)
    last = units - (steps - 1) * TILE

    def kernel(*refs):
        part_refs = refs[:count]
        w_ref, d_ref, gu_ref = refs[count : count + 3]
        out_refs, total = refs[count + 3 : -1], refs[-1]
        step = pl.program_id(0)
        n2 = jnp.concatenate([ref[...] for ref in part_refs], axis=0)

        @pl.when(step == 0)
        def _():
            total[...] = jnp.zeros_like(total)

        @pl.when(step < steps - 1)
        def _():
            both = dot(n2, w_ref[...])
            gu_ref[...] = both.astype(jnp.bfloat16)
            gate, up = both[:, :TILE], both[:, TILE:]
            hidden = (gate * jax.nn.sigmoid(gate) * up).astype(jnp.bfloat16)
            total[...] += dot(hidden, d_ref[...])

        @pl.when(step == steps - 1)
        def _():
            both = dot(n2, w_ref[:, : 2 * last])
            gu_ref[:, : 2 * last] = both.astype(jnp.bfloat16)
            gate, up = both[:, :last], both[:, last:]
            hidden = (gate * jax.nn.sigmoid(gate) * up).astype(jnp.bfloat16)
            summed = (total[...] + dot(hidden, d_ref[:last, :])).astype(jnp.bfloat16)
            for place in range(count):
                out_refs[place][...] = summed[place * part_rows : place * part_rows + part_rows]

    whole = lambda step: (0, 0)
    return call(
        kernel,
        [((rows, 2 * units), jnp.bfloat16)] + [((part_rows, D), jnp.bfloat16)] * count,
        9.0,
        [pltpu.VMEM((rows, D), jnp.float32)],
        limit=60,
        grid=(steps,),
        in_specs=[pl.BlockSpec((part_rows, D), whole)] * count
        + [
            pl.BlockSpec((D, 2 * TILE), lambda step: (0, step)),
            pl.BlockSpec((TILE, D), lambda step: (step, 0)),
        ],
        out_specs=[
            pl.BlockSpec((rows, 2 * TILE), lambda step: (0, step)),
        ]
        + [pl.BlockSpec((part_rows, D), whole)] * count,
    )(*parts, gate_up_full, down_full)


def far_slot(mine, place, line):
    if line == 4:
        return jnp.where(mine < 2, place - 2, 1 - place)
    return (mine ^ place) - line // 2


def feed_back(gz_parts, n2_parts, gu_parts, gate_up_full, down_full, dp_place, group_count):
    line = group_count // 2
    half = line // 2
    chunk = D // group_count
    count = len(gz_parts)
    gu_count = len(gu_parts)
    part_rows = gz_parts[0].shape[0]
    rows = count * part_rows
    units = down_full.shape[0]
    steps = pl.cdiv(units, TILE)
    last = units - (steps - 1) * TILE

    def kernel(*refs):
        place_ref, *refs = refs
        gz_refs = refs[:count]
        n2_refs = refs[count : 2 * count]
        gu_refs = refs[2 * count : 2 * count + gu_count]
        w_ref, d_ref = refs[2 * count + gu_count : 2 * count + gu_count + 2]
        keep_near, keep_far, send_near, send_far, down_ref, own_ref, across_ref, pair_ref = refs[
            2 * count + gu_count + 2 : 2 * count + gu_count + 10
        ]
        total, gz, n2t = refs[-3:]
        side, mine = place_ref[0] % 2, place_ref[0] // 2
        step = pl.program_id(0)

        @pl.when(step == 0)
        def _():
            total[...] = jnp.zeros_like(total)
            for place in range(count):
                here = slice(place * part_rows, place * part_rows + part_rows)
                gz[here, :] = gz_refs[place][...]
                n2t[:, here] = n2_refs[place][...].T

        def work(width):
            gu = jnp.concatenate([ref[:, : 2 * width] for ref in gu_refs], axis=0).astype(jnp.float32)
            gate, up = gu[:, :width], gu[:, width:]
            sig = jax.nn.sigmoid(gate)
            act = gate * sig
            hidden = (act * up).astype(jnp.bfloat16)
            down_ref[:width, :] = dot(hidden, gz[...], TN).astype(jnp.bfloat16)
            grad = dot(gz[...], d_ref[:width, :], NT)
            d_gate = grad * up * (sig + act * (1.0 - sig))
            d_up = grad * act
            both = jnp.concatenate([d_gate, d_up], axis=1).astype(jnp.bfloat16)
            part = dot(n2t[...], both)
            for spot in range(line):
                even = part[2 * spot * chunk : (2 * spot + 1) * chunk].astype(jnp.bfloat16)
                odd = part[(2 * spot + 1) * chunk : (2 * spot + 2) * chunk].astype(jnp.bfloat16)
                keep = jnp.where(side == 0, even, odd)
                send = jnp.where(side == 0, odd, even)
                slot = mine ^ spot
                beyond = far_slot(mine, spot, line)

                @pl.when(slot < half)
                def _():
                    keep_near[slot, :, : 2 * width] = keep
                    send_near[slot, :, : 2 * width] = send

                @pl.when(slot >= half)
                def _():
                    keep_far[beyond, :, : 2 * width] = keep
                    send_far[beyond, :, : 2 * width] = send

            return dot(both, w_ref[:, : 2 * width], NT)

        @pl.when(step < steps - 1)
        def _():
            total[...] += work(TILE)

        @pl.when(step == steps - 1)
        def _():
            summed = (total[...] + work(last)).astype(jnp.bfloat16)
            own_ref[...] = summed[:part_rows]
            pair_ref[0] = summed[part_rows : 2 * part_rows]
            across_ref[...] = summed[2 * part_rows : 3 * part_rows]
            pair_ref[1] = summed[3 * part_rows :]

    whole = lambda step: (0, 0)
    return call(
        kernel,
        [
            ((half, chunk, 2 * units), jnp.bfloat16),
            ((half, chunk, 2 * units), jnp.bfloat16),
            ((half, chunk, 2 * units), jnp.bfloat16),
            ((half, chunk, 2 * units), jnp.bfloat16),
            ((units, D), jnp.bfloat16),
            ((part_rows, D), jnp.bfloat16),
            ((part_rows, D), jnp.bfloat16),
            ((2, part_rows, D), jnp.bfloat16),
        ],
        25.0,
        [
            pltpu.VMEM((rows, D), jnp.float32),
            pltpu.VMEM((rows, D), jnp.bfloat16),
            pltpu.VMEM((D, rows), jnp.bfloat16),
        ],
        limit=56,
        grid=(steps,),
        in_specs=[pl.BlockSpec(memory_space=pltpu.SMEM)]
        + [pl.BlockSpec((part_rows, D), whole)] * (2 * count)
        + [pl.BlockSpec((rows // gu_count, 2 * TILE), lambda step: (0, step))] * gu_count
        + [
            pl.BlockSpec((D, 2 * TILE), lambda step: (0, step)),
            pl.BlockSpec((TILE, D), lambda step: (step, 0)),
        ],
        out_specs=[
            pl.BlockSpec((half, chunk, 2 * TILE), lambda step: (0, 0, step)),
            pl.BlockSpec((half, chunk, 2 * TILE), lambda step: (0, 0, step)),
            pl.BlockSpec((half, chunk, 2 * TILE), lambda step: (0, 0, step)),
            pl.BlockSpec((half, chunk, 2 * TILE), lambda step: (0, 0, step)),
            pl.BlockSpec((TILE, D), lambda step: (step, 0)),
            pl.BlockSpec((part_rows, D), whole),
            pl.BlockSpec((part_rows, D), whole),
            pl.BlockSpec((2, part_rows, D), lambda step: (0, 0, 0)),
        ],
    )(dp_place.reshape(1).astype(jnp.int32), *gz_parts, *n2_parts, *gu_parts, gate_up_full, down_full)


def norm_back(rows, gain, grad):
    inv_root = inverse_root(rows)
    normal = rows * inv_root
    gain_part = jnp.sum(grad * normal, axis=0, keepdims=True)
    weighted = grad * gain
    inner = jnp.mean(weighted * normal, axis=-1, keepdims=True)
    return gain_part, inv_root * (weighted - normal * inner)


def attention_back(upstream, middle, gain, terms, second_full, queries, kv_blocks, biases, cos_wide, sin_wide):
    count = len(terms)
    rows = middle.shape[0]
    span = rows // 2
    wide = GROUP * span

    def kernel(*refs):
        up_ref, mid_ref, gain_ref = refs[:3]
        term_refs = refs[3 : 3 + count]
        w_ref, q_ref, kv0, kv1, kv2, kv3, bias_ref, cos_ref, sin_ref = refs[3 + count : 12 + count]
        gm_ref, gy_ref, dgain_ref, gq_ref, own_ref, d1, d2, d3, go_ref, dkv = refs[12 + count :]
        kvs = (kv0, kv1, kv2, kv3)
        grad = term_refs[0][...].astype(jnp.float32)
        for term in term_refs[1:]:
            grad = grad + term[...].astype(jnp.float32)
        gain_part, back = norm_back(mid_ref[...], gain_ref[...], grad)
        dgain_ref[...] = gain_part
        grad_middle = up_ref[...].astype(jnp.float32) + back
        gm_ref[...] = grad_middle
        grad_low = grad_middle.astype(jnp.bfloat16)
        gy_ref[...] = grad_low
        for tile in range(D // 128):
            start = KV_WIDTH
            block = dot(grad_low, w_ref[tile * 128 : tile * 128 + 128, start:], NT).astype(jnp.bfloat16)
            for part in range(2):
                head = 2 * tile + part
                place = (head % GROUP) * span
                for half in range(2):
                    go_ref[head // GROUP, half, place : place + span, :] = block[
                        half * span : half * span + span, part * HEAD : part * HEAD + HEAD
                    ]
        for group in range(KV_HEADS):
            key_lanes = slice(group * HEAD, group * HEAD + HEAD)
            value_lanes = slice(KV_WIDTH + group * HEAD, KV_WIDTH + group * HEAD + HEAD)
            keys = [key_part(kvs, half, key_lanes) for half in range(2)]
            values = [key_part(kvs, half, value_lanes) for half in range(2)]
            for half in range(2):
                query = q_ref[group, half] * jnp.bfloat16(SCALE)
                grad_out = go_ref[group, half]
                bias = jnp.concatenate([bias_ref[half]] * GROUP, axis=1)
                use = [half] if half == 0 else [1, 0]
                scores = []
                top = None
                for which in use:
                    score = dot(keys[which], query, NT)
                    if which == half:
                        score = score + bias
                    scores.append(score)
                    best = jnp.max(score, axis=0, keepdims=True)
                    top = best if top is None else jnp.maximum(top, best)
                weights = [jnp.exp(score - top) for score in scores]
                total = sum(jnp.sum(weight, axis=0, keepdims=True) for weight in weights)
                scale = 1.0 / total
                probs = [weight * scale for weight in weights]
                grads = [dot(values[which], grad_out, NT) for which in use]
                inner = sum(
                    jnp.sum(prob * grad_prob, axis=0, keepdims=True)
                    for prob, grad_prob in zip(probs, grads)
                )
                grad_query = None
                for which, prob, grad_prob in zip(use, probs, grads):
                    grad_score = (prob * (grad_prob - inner)).astype(jnp.bfloat16)
                    value_grad = dot(prob.astype(jnp.bfloat16), grad_out)
                    key_grad = dot(grad_score, query)
                    if half == 0:
                        dkv[group, which] = key_grad
                        dkv[KV_HEADS + group, which] = value_grad
                    elif which == 0:
                        dkv[group, which] += key_grad
                        dkv[KV_HEADS + group, which] += value_grad
                    else:
                        dkv[group, which] = key_grad
                        dkv[KV_HEADS + group, which] = value_grad
                    term = dot(keys[which].T, grad_score)
                    grad_query = term if grad_query is None else grad_query + term
                grad_query = grad_query * SCALE
                cos_w = cos_ref[half * span : half * span + span, :]
                sin_w = sin_ref[half * span : half * span + span, :]
                for member in range(GROUP):
                    head = group * GROUP + member
                    piece = grad_query[:, member * span : member * span + span].T
                    pair = jnp.concatenate([piece, piece], axis=1)
                    turned = turn(pair, cos_w, -sin_w)[:, :HEAD]
                    gq_ref[half * span : half * span + span, head * HEAD : head * HEAD + HEAD] = (
                        turned.astype(jnp.bfloat16)
                    )
        for place, out in enumerate((own_ref, d1, d2, d3)):
            for half in range(2):
                block = jnp.concatenate(
                    [dkv[lane, half, place * span : place * span + span, :] for lane in range(2 * KV_HEADS)],
                    axis=1,
                )
                out[half * span : half * span + span, :] = block.astype(out.dtype)

    return call(
        kernel,
        [
            ((rows, D), jnp.float32),
            ((rows, D), jnp.bfloat16),
            ((1, D), jnp.float32),
            ((rows, D), jnp.bfloat16),
            ((rows, 2 * KV_WIDTH), jnp.float32),
        ]
        + [((rows, 2 * KV_WIDTH), jnp.bfloat16)] * 3,
        13.0,
        [
            pltpu.VMEM((KV_HEADS, 2, wide, HEAD), jnp.bfloat16),
            pltpu.VMEM((2 * KV_HEADS, 2, 4 * span, HEAD), jnp.float32),
        ],
    )(upstream, middle, gain, *terms, second_full, queries, *kv_blocks, biases, cos_wide, sin_wide)


def before_back(kv_terms, gq, x, gain, grad_middle, first_full, second_full, cos_wide, sin_wide):
    rows = x.shape[0]
    count = len(kv_terms)

    def kernel(*refs):
        kv_refs = refs[:count]
        gq_ref, x_ref, gain_ref, gm_ref, w1_ref, w2_ref, cos_ref, sin_ref = refs[count : count + 8]
        up_ref, low_ref, gkv_ref, dgain_ref, bias_one, bias_two = refs[count + 8 :]
        grad = kv_refs[0][...].astype(jnp.float32)
        for ref in kv_refs[1:]:
            grad = grad + ref[...].astype(jnp.float32)
        grad_key = turn(grad[:, :KV_WIDTH], cos_ref[...], -sin_ref[...]).astype(jnp.bfloat16)
        grad_value = grad[:, KV_WIDTH:].astype(jnp.bfloat16)
        gkv_ref[:, :KV_WIDTH] = grad_key
        gkv_ref[:, KV_WIDTH:] = grad_value
        grad_query = gq_ref[...]
        bias_one[:, :D] = jnp.sum(grad_query.astype(jnp.float32), axis=0, keepdims=True)
        bias_one[:, D:] = jnp.sum(grad_key.astype(jnp.float32), axis=0, keepdims=True)
        bias_two[...] = jnp.sum(grad_value.astype(jnp.float32), axis=0, keepdims=True)
        grad_normed = (
            dot(grad_query, w1_ref[:, :D], NT)
            + dot(grad_key, w1_ref[:, D:], NT)
            + dot(grad_value, w2_ref[:, :KV_WIDTH], NT)
        )
        gain_part, back = norm_back(x_ref[...], gain_ref[...], grad_normed)
        dgain_ref[...] = gain_part
        upstream = gm_ref[...] + back
        up_ref[...] = upstream
        low_ref[...] = upstream.astype(jnp.bfloat16)

    return call(
        kernel,
        [
            ((rows, D), jnp.float32),
            ((rows, D), jnp.bfloat16),
            ((rows, 2 * KV_WIDTH), jnp.bfloat16),
            ((1, D), jnp.float32),
            ((1, SPLIT), jnp.float32),
            ((1, KV_WIDTH), jnp.float32),
        ],
        2.4,
    )(*kv_terms, gq, x, gain, grad_middle, first_full, second_full, cos_wide, sin_wide)


def unit_pieces(unit_rows, group_count, seq_devices):
    units = unit_rows * group_count
    steps = pl.cdiv(units, TILE)
    pieces = []
    for owner in range(seq_devices):
        for kind in range(2):
            for group in range(group_count):
                unit = group * unit_rows
                stop = unit + unit_rows
                column = kind * units * seq_devices + (group * seq_devices + owner) * unit_rows
                while unit < stop:
                    step = unit // TILE
                    end = min(stop, (step + 1) * TILE)
                    width = TILE if step < steps - 1 else units - (steps - 1) * TILE
                    inside = 2 * step * TILE + kind * width + unit - step * TILE
                    pieces.append((owner, inside, column, end - unit))
                    column += end - unit
                    unit = end
    return pieces


def spread_columns(weight, place, unit_rows, group_count, seq_devices):
    layers, rows, columns = weight.shape
    quarter = columns // seq_devices
    pieces = unit_pieces(unit_rows, group_count, seq_devices)

    def kernel(place_ref, w_ref, *refs):
        outs, wide, narrow = refs[:seq_devices], refs[-2], refs[-1]
        for layer in range(layers):
            wide[...] = w_ref[layer].astype(jnp.float32)
            for owner in range(seq_devices):
                for who, inside, column, width in pieces:
                    if who == owner:
                        narrow[:, inside : inside + width] = wide[:, column : column + width]
                block = narrow[...].astype(jnp.bfloat16)
                for bit in range(seq_devices):

                    @pl.when(place_ref[0] == owner ^ bit)
                    def _():
                        outs[bit][layer] = block

    return call(
        kernel,
        [((layers, rows, quarter), jnp.bfloat16)] * seq_devices,
        2.5,
        [pltpu.VMEM((rows, columns), jnp.float32), pltpu.VMEM((rows, quarter), jnp.float32)],
        in_specs=[pl.BlockSpec(memory_space=pltpu.SMEM), FULL],
        out_specs=[FULL] * seq_devices,
    )(place.reshape(1).astype(jnp.int32), weight)


def collect_columns(blocks, place, unit_rows, group_count):
    count = len(blocks)
    layers, rows, quarter = blocks[0].shape
    pieces = unit_pieces(unit_rows, group_count, count)

    def kernel(place_ref, *refs):
        out_ref, narrow = refs[count:]
        me = place_ref[0]
        for layer in range(layers):
            for owner in range(count):
                for bit in range(count):

                    @pl.when(me == owner ^ bit)
                    def _():
                        narrow[...] = refs[bit][layer].astype(jnp.float32)

                for who, inside, column, width in pieces:
                    if who == owner:
                        out_ref[layer, :, column : column + width] = narrow[:, inside : inside + width]

    return call(
        kernel,
        [((layers, rows, count * quarter), jnp.float32)],
        1.5,
        [pltpu.VMEM((rows, quarter), jnp.float32)],
        in_specs=[pl.BlockSpec(memory_space=pltpu.SMEM)] + [FULL] * count,
        out_specs=[FULL],
    )(place.reshape(1).astype(jnp.int32), *blocks)[0]


def join_rows(blocks, place):
    owners = len(blocks)
    layers, rows, columns = blocks[0].shape

    def kernel(place_ref, *refs):
        ins, outs = refs[:owners], refs[owners:]
        for layer in range(layers):
            parts = []
            for owner in range(owners):
                part = ins[0][layer].astype(jnp.float32)
                for bit in range(1, owners):
                    part = jnp.where(
                        place_ref[0] == owner ^ bit, ins[bit][layer].astype(jnp.float32), part
                    )
                parts.append(part)
            outs[layer][0] = jnp.concatenate(parts, axis=0).astype(jnp.bfloat16)

    return call(
        kernel,
        [((1, owners * rows, columns), jnp.bfloat16)] * layers,
        2.0,
        in_specs=[pl.BlockSpec(memory_space=pltpu.SMEM)] + [FULL] * owners,
        out_specs=[FULL] * layers,
    )(place.reshape(1).astype(jnp.int32), *blocks)


def split_rows(terms, layers, place, count):
    number = len(terms)
    layer_rows = terms[0].shape[0] // layers
    columns = terms[0].shape[1]
    rows = layer_rows // count

    def kernel(place_ref, *refs):
        ins, outs = refs[:number], refs[number:]
        for layer in range(layers):
            here = slice(layer * layer_rows, (layer + 1) * layer_rows)
            total = ins[0][here, :].astype(jnp.float32)
            for ref in ins[1:]:
                total = total + ref[here, :].astype(jnp.float32)
            for owner in range(count):
                block = total[owner * rows : owner * rows + rows].astype(jnp.bfloat16)
                for bit in range(count):

                    @pl.when(place_ref[0] == owner ^ bit)
                    def _():
                        outs[bit][layer] = block

    return call(
        kernel,
        [((layers, rows, columns), jnp.bfloat16)] * count,
        2.0,
        in_specs=[pl.BlockSpec(memory_space=pltpu.SMEM)] + [FULL] * number,
        out_specs=[FULL] * count,
    )(place.reshape(1).astype(jnp.int32), *terms)


def lay_out(blocks, places):
    total = len(places)
    shape = blocks[0].shape[-2:]
    count = len(blocks)

    def kernel(place_ref, *refs):
        ins, out, sems = refs[:count], refs[count], refs[-1]
        copies = []
        spot = 0
        for which in range(count):
            many = blocks[which].shape[0] if blocks[which].ndim == 3 else 1
            for k in range(many):
                source = ins[which].at[k] if blocks[which].ndim == 3 else ins[which]
                copies.append(
                    pltpu.make_async_copy(source, out.at[place_ref[spot]], sems.at[spot])
                )
                spot += 1
        for copy in copies:
            copy.start()
        for copy in copies:
            copy.wait()

    outside = pl.BlockSpec(memory_space=pltpu.HBM)
    return call(
        kernel,
        [((total,) + shape, blocks[0].dtype)],
        2.5,
        [pltpu.SemaphoreType.DMA((total,))],
        in_specs=[pl.BlockSpec(memory_space=pltpu.SMEM)] + [outside] * count,
        out_specs=[outside],
    )(jnp.stack(places).astype(jnp.int32), *blocks)[0]


def assemble(parts, places, chip_rows):
    line, rows, width = parts[0].shape

    def kernel(place_ref, *refs):
        ins = refs[:8]
        first_ref, second_ref, small_ref = refs[8:]
        here, chip, side = place_ref[0] == 0, place_ref[1] == 0, place_ref[2] % 2 == 0
        mine = place_ref[2] // 2
        small = jnp.zeros((rows - chip_rows, width), jnp.float32)
        for spot in range(line):
            halves = []
            for half in range(2):
                pieces = []
                blocks = [ins[4 * half + k][spot].astype(jnp.float32) for k in range(4)]
                for block in blocks:
                    small = small + block[chip_rows:]
                lower = [jnp.where(side, blocks[2 * x], blocks[2 * x + 1]) for x in range(2)]
                upper = [jnp.where(side, blocks[2 * x + 1], blocks[2 * x]) for x in range(2)]
                for pair in (lower, upper):
                    pieces.append(jnp.where(chip, pair[0], pair[1])[:chip_rows])
                    pieces.append(jnp.where(chip, pair[1], pair[0])[:chip_rows])
                halves.append(jnp.concatenate(pieces, axis=0).astype(jnp.bfloat16))
            first_ref[mine ^ spot] = jnp.where(here, halves[0], halves[1])
            second_ref[mine ^ spot] = jnp.where(here, halves[1], halves[0])
        small_ref[...] = small

    first, second, small = call(
        kernel,
        [
            ((line, 4 * chip_rows, width), jnp.bfloat16),
            ((line, 4 * chip_rows, width), jnp.bfloat16),
            ((rows - chip_rows, width), jnp.float32),
        ],
        4.0,
        in_specs=[pl.BlockSpec(memory_space=pltpu.SMEM)] + [FULL] * 8,
        out_specs=[FULL] * 3,
    )(jnp.stack(places).astype(jnp.int32), *parts)
    return first.reshape(-1, width), second.reshape(-1, width), small


def projection_grads(normed, grad_query, grad_kv, mixed, grad_low, gain_one, gain_two, bias_one, bias_two, places, chip_rows, line):
    width = SPLIT

    def kernel(place_ref, n_ref, gq_ref, gkv_ref, mixed_ref, gy_ref, g1_ref, g2_ref, b1_ref, b2_ref, keep0, keep1, send0, send1, pad):
        here, chip, side = place_ref[0] == 0, place_ref[1] == 0, place_ref[2] % 2
        mine = place_ref[2] // 2
        turned = n_ref[...].T
        pad[...] = jnp.zeros_like(pad)
        pad[0:1, :D] = g1_ref[...]
        pad[1:2, :D] = g2_ref[...]
        pad[2:3, :] = b1_ref[...]
        pad[3:4, :KV_WIDTH] = b2_ref[...]
        small = pad[...]
        first = jnp.concatenate(
            [dot(turned, gq_ref[...]), dot(turned, gkv_ref[:, :KV_WIDTH])], axis=1
        )
        second = jnp.concatenate(
            [dot(turned, gkv_ref[:, KV_WIDTH:]), dot(mixed_ref[...], gy_ref[...], TN)], axis=1
        )

        def chunk(part, number):
            rows = part[number * chip_rows : (number + 1) * chip_rows]
            return jnp.concatenate([rows, small], axis=0).astype(jnp.bfloat16)

        for spot in range(line):
            for pair in range(2):
                slot = side ^ pair
                firsts = [chunk(first, 4 * spot + 2 * pair + x) for x in range(2)]
                seconds = [chunk(second, 4 * spot + 2 * pair + x) for x in range(2)]
                keeps = [jnp.where(here, one, two) for one, two in zip(firsts, seconds)]
                sends = [jnp.where(here, two, one) for one, two in zip(firsts, seconds)]
                keep0[slot, mine ^ spot] = jnp.where(chip, keeps[0], keeps[1])
                keep1[slot, mine ^ spot] = jnp.where(chip, keeps[1], keeps[0])
                send0[slot, mine ^ spot] = jnp.where(chip, sends[0], sends[1])
                send1[slot, mine ^ spot] = jnp.where(chip, sends[1], sends[0])

    return call(
        kernel,
        [((2, line, chip_rows + 8, width), jnp.bfloat16)] * 4,
        6.0,
        [pltpu.VMEM((8, width), jnp.float32)],
        in_specs=[pl.BlockSpec(memory_space=pltpu.SMEM)] + [FULL] * 9,
        out_specs=[FULL] * 4,
    )(
        jnp.stack(places).astype(jnp.int32),
        normed,
        grad_query,
        grad_kv,
        mixed,
        grad_low,
        gain_one,
        gain_two,
        bias_one,
        bias_two,
    )


def swap(values, axis, bit):
    size = lax.axis_size(axis)
    return lax.ppermute(values, axis, [(i, i ^ bit) for i in range(size)])


def after(values, *others):
    return lax.optimization_barrier((values,) + tuple(others))[0]


def line_bits():
    bits = [1]
    while 4 * bits[-1] < lax.axis_size("dp"):
        bits.append(2 * bits[-1])
    return bits


def line_gather(values, bits):
    for bit in bits:
        values = jnp.concatenate([values, swap(values, "dp", 2 * bit)], axis=0)
    return values


def line_steps(values, moves):
    return lax.ppermute(
        values, "dp", [(2 * here + side, 2 * there + side) for here, there in moves for side in range(2)]
    )


def cross_middle(values):
    line = lax.axis_size("dp") // 2
    if line == 4:
        return line_steps(values, [(1, 2), (2, 1)])
    return swap(values, "dp", line)


def line_scatter(values, bits):
    for bit in bits[:0:-1]:
        values = add_low(values[:bit], swap(values[bit:], "dp", 2 * bit))
    return [values[0], swap(values[1], "dp", 2)]


def add_low(left, right):
    return (left.astype(jnp.float32) + right.astype(jnp.float32)).astype(jnp.bfloat16)


def group_rows(values, *waited):
    beside = swap(values, "seq", 1)
    across = swap(values, "seq", 2)
    return [values, beside, across, swap(after(across, *waited), "seq", 1)]


def placed(values, offset, width):
    return lax.dynamic_update_slice(jnp.zeros((width,), values.dtype), values, (offset,))


def body(
    tokens,
    cotangent,
    span_order,
    attn_gain,
    joined_weight,
    joined_bias,
    out_weight,
    mlp_gain,
    gate_up_weight,
    down_weight,
):
    seq_count, tok_len, model_width = tokens.shape
    span_len = tok_len // 2
    group_count = lax.axis_size("dp")
    seq_devices = lax.axis_size("seq")
    unit_rows = down_weight.shape[1]
    width_rows = gate_up_weight.shape[1]
    units = group_count * unit_rows
    dp_place = lax.axis_index("dp")
    seq_place = lax.axis_index("seq")
    core = seq_place % 2
    chip_x = seq_place // 2
    device = dp_place * seq_devices + seq_place
    chip_rows = 2 * width_rows
    line = group_count // 2
    side = dp_place % 2
    line_place = dp_place // 2

    order = [lax.dynamic_slice(span_order, (0, seq_place ^ bit), (1, 1))[0, 0] for bit in range(4)]
    inside = jnp.arange(span_len, dtype=jnp.int32)
    own_places = jnp.concatenate(
        [order[0] * span_len + inside, (2 * seq_devices - 1 - order[0]) * span_len + inside]
    )
    half_biases = []
    for half in range(2):
        blocks = []
        for bit in range(4):
            ahead = order[bit] < order[0] if half == 0 else order[bit] > order[0]
            allowed = ahead | ((order[bit] == order[0]) & (inside[:, None] >= inside[None, :]))
            blocks.append(jnp.where(allowed, 0.0, NEGATIVE).astype(jnp.float32))
        half_biases.append(jnp.concatenate(blocks, axis=1))
    biases = jnp.stack(half_biases)
    biases_turned = jnp.swapaxes(biases, 1, 2)
    cos_table, sin_table = rotary_tables(own_places)
    cos_wide = jnp.concatenate([cos_table] * 4, axis=1)
    sin_wide = jnp.concatenate([-sin_table, sin_table] * 2, axis=1)

    def attn_shard(layer):
        first = joined_weight[layer][:, :SPLIT]
        second = jnp.concatenate([joined_weight[layer][:, SPLIT:], out_weight[layer]], axis=1)
        got = swap(jnp.where(core == 0, second, first), "seq", 1)
        mine = jnp.where(core == 0, first, second)
        rows = jnp.where(core == 0, jnp.stack([mine, got]), jnp.stack([got, mine])).reshape(
            chip_rows, -1
        )
        bias_all = placed(joined_bias[layer], device * joined_bias.shape[1], SPLIT + KV_WIDTH)
        extra = jnp.zeros((8, SPLIT), jnp.bfloat16)
        extra = extra.at[0].set(placed(attn_gain[layer], device * width_rows, SPLIT))
        extra = extra.at[1].set(placed(mlp_gain[layer], device * width_rows, SPLIT))
        extra = extra.at[2].set(bias_all[:SPLIT])
        extra = extra.at[3, :KV_WIDTH].set(bias_all[SPLIT:])
        return jnp.concatenate([rows, extra], axis=0)

    def attn_finish(own_side, other_side, *waited):
        parts = [own_side, other_side]
        parts = parts + [swap(after(part, *waited), "seq", 2) for part in parts]
        parts = parts + [swap(part, "seq", 1) for part in parts]
        first_full, second_full, small = assemble(parts, [core, chip_x, dp_place], chip_rows)
        return (
            first_full,
            second_full,
            small[0:1, :model_width],
            small[1:2, :model_width],
            small[2:3],
            small[3:4, :KV_WIDTH],
        )

    bits = line_bits()
    spread = spread_columns(gate_up_weight, seq_place, unit_rows, group_count, seq_devices)
    shards = [attn_shard(layer)[None] for layer in range(LAYERS)]
    gate_blocks = [spread[0]] + [swap(spread[bit], "seq", bit) for bit in range(1, 4)]
    gate_shards = join_rows(gate_blocks, seq_place)
    attn_line = line_gather(after(shards[0], *spread), bits)
    attn_other = swap(after(attn_line, *gate_shards), "dp", 1)
    near = [line_gather(after(gate_shards[0], attn_line), bits[:-1])]
    far = [swap(near[0], "dp", 2 * bits[-1])]
    near_pair = [swap(after(near[0], attn_other), "dp", 1)]
    down_full = [
        lax.all_gather(
            down_weight[layer] if layer == 0 else after(down_weight[layer], near_pair[0]),
            "dp",
            axis=0,
            tiled=True,
        )
        for layer in range(LAYERS)
    ]
    offsets = [dp_place ^ (2 * k) for k in range(line)]
    half = line // 2
    gate_places = offsets + [offset ^ 1 for offset in offsets]

    def mlp_finish(layer, *waited):
        far_pair = swap(after(far[layer], *waited), "dp", 1)
        blocks = [near[layer], far[layer], near_pair[layer], far_pair]
        gate_up = lay_out(blocks, gate_places).reshape(model_width, 2 * units)
        return gate_up, down_full[layer], far_pair

    terms = [tokens.reshape(tok_len, model_width)]
    kept_state = []
    mlp_sets = []
    attn_sets = [attn_finish(attn_line, attn_other)]
    for layer in range(LAYERS):
        first_full, second_full, gain_full, mlp_gain_full, bias_first, bias_second = attn_sets[layer]
        x, normed, queries, own_kv = before_attention(
            terms,
            after(gain_full, near[0]) if layer == 0 else gain_full,
            first_full,
            second_full,
            bias_first,
            bias_second,
            cos_wide,
            sin_wide,
        )
        kv_blocks = [own_kv] + [swap(own_kv, "seq", bit) for bit in range(1, 4)]
        waited = (near_pair[0],) if layer == 0 else ()
        mixed, middle, n2 = attention(
            queries, kv_blocks, biases, x, second_full, after(mlp_gain_full, *waited)
        )
        n2_parts = group_rows(n2 if layer == 0 else after(n2, mlp_sets[1][2]))
        if layer + 1 == LAYERS:
            low_parts = group_rows(after(cotangent.reshape(tok_len, model_width), n2_parts[3]))
        if layer == 0:
            second_line = line_gather(after(shards[1], own_kv), bits[:1])
            for bit in bits[1:]:
                second_line = line_gather(after(second_line, n2), [bit])
            second_other = swap(after(second_line, n2_parts[3]), "dp", 1)
            near.append(line_gather(after(gate_shards[1], n2), bits[:-1]))
            far.append(swap(after(near[1], n2_parts[3]), "dp", 2 * bits[-1]))
            near_pair.append(swap(after(near[1], n2_parts[3]), "dp", 1))
            mlp_sets.append(mlp_finish(0, n2))
            n2_parts[0] = after(n2_parts[0], near[1])
        gu_near, *outs_near = feed_forward(n2_parts[:2], *mlp_sets[layer][:2])
        gu_far, *outs_far = feed_forward(n2_parts[2:], *mlp_sets[layer][:2])
        if layer == 0:
            attn_sets.append(attn_finish(second_line, second_other, gu_near))
            mlp_sets.append(mlp_finish(1, outs_far[0]))
            outs_far[0] = after(outs_far[0], far[1], near_pair[1])
        across_sum = add_low(outs_far[0], swap(outs_far[1], "seq", 1))
        terms = [middle, outs_near[0], swap(outs_near[1], "seq", 1)]
        if layer + 1 < LAYERS:
            terms.append(swap(across_sum, "seq", 2))
        kept_state.append((x, normed, queries, kv_blocks, mixed, middle, n2_parts, [gu_near, gu_far]))
    upstream = cotangent.reshape(tok_len, model_width)
    states = [None] * LAYERS
    before = None

    def send_attn(state, pair, *waited):
        near, far, got_near, got_far = state["attn_parts"]
        return swap(after(add_low(far[pair], got_far[pair]), *waited), "seq", 2)

    def sum_attn(state, arrived, *waited):
        near, far, got_near, got_far = state["attn_parts"]
        return [
            (
                near[pair].astype(jnp.float32)
                + got_near[pair].astype(jnp.float32)
                + after(arrived[pair], *waited).astype(jnp.float32)
            ).astype(jnp.bfloat16)
            for pair in range(2)
        ]

    def half_of(values, which):
        count = values.shape[0] // 2
        return lax.dynamic_slice_in_dim(values, which * count, count, 0)

    def halve_down(values, bit):
        upper = (line_place // bit) % 2
        return half_of(values, upper), swap(half_of(values, 1 - upper), "dp", 2 * bit)

    def step_one(state, *waited):
        far_sum = state["far_sum"]
        if line == 4:
            far_sum = add_low(far_sum, after(state["inward"], *waited))
        state["crossed"] = cross_middle(far_sum)
        state["near_sum"] = add_low(state["keep_near"], after(state["near_got"], *waited))

    def step_two(state, *waited):
        state["near_sum"] = add_low(state["near_sum"], after(state["crossed"], *waited))

    def step_three(state, *waited):
        down = add_low(state["down_keep"], after(state["down_got"], *waited))
        state["down_kept"], state["down_got"] = halve_down(down, bits[-1])

    def finish(states):
        other_side = swap(jnp.concatenate([state["attn_sums"][1] for state in states], axis=1), "dp", 1)
        own_side = jnp.concatenate([state["attn_sums"][0] for state in states], axis=1)
        owned = sum(
            term.astype(jnp.float32) for term in line_scatter(add_low(own_side, other_side), bits)
        ).reshape(LAYERS, chip_rows + 8, -1)
        extra = owned[:, chip_rows:]
        halves = owned[:, :chip_rows].reshape(LAYERS, 2, width_rows, -1)
        mine = lax.dynamic_index_in_dim(halves, core, 1, keepdims=False)
        theirs = swap(
            lax.dynamic_index_in_dim(halves, 1 - core, 1, keepdims=False), "seq", 1
        )
        first_own = jnp.where(core == 0, mine, theirs)
        second_own = jnp.where(core == 0, theirs, mine)

        def cut(row, width, stop):
            start = (0, row, device * width)
            return lax.dynamic_slice(extra[:, :, :stop], start, (LAYERS, 1, width))[:, 0]

        near_sums = jnp.concatenate([state["near_sum"] for state in states], axis=1)
        gate_rows = split_rows(
            line_scatter(near_sums, bits[:-1]), len(states), seq_place, seq_devices
        )
        gate_owned = collect_columns(
            [gate_rows[0]] + [swap(gate_rows[bit], "seq", bit) for bit in range(1, 4)],
            seq_place,
            unit_rows,
            group_count,
        )
        down = jnp.concatenate(
            [add_low(state["down_kept"], state["down_got"]) for state in states], axis=1
        )
        for bit in bits[-2::-1]:
            kept, got = halve_down(down, bit)
            down = kept.astype(jnp.float32) + got.astype(jnp.float32)
            if bit > 1:
                down = down.astype(jnp.bfloat16)
        down_owned = down.reshape(len(states), unit_rows, model_width)
        return (
            cut(0, width_rows, model_width),
            jnp.concatenate([first_own, second_own[:, :, :KV_WIDTH]], axis=2),
            cut(2, SPLIT // (group_count * seq_devices), SPLIT),
            cut(3, KV_WIDTH // (group_count * seq_devices), KV_WIDTH),
            second_own[:, :, KV_WIDTH:],
            cut(1, width_rows, model_width),
            gate_owned,
            down_owned,
        )

    for layer in reversed(range(LAYERS)):
        x, normed, queries, kv_blocks, mixed, middle, n2_parts, gu_parts = kept_state[layer]
        first_full, second_full, gain_full, mlp_gain_full, _, _ = attn_sets[layer]
        if before is not None:
            low_parts = group_rows(upstream_low, before["near_got"])
            low_parts[0] = after(low_parts[0], *before["attn_parts"][2:])
            attn_sent = [send_attn(before, pair, low_parts[3]) for pair in range(2)]
            last_across = swap(after(across_sum, low_parts[3]), "seq", 2)
        keep_near, keep_far, send_near, send_far, down_part, own_out, across_out, pair_out = feed_back(
            low_parts,
            n2_parts,
            gu_parts,
            *mlp_sets[layer][:2],
            dp_place,
            group_count,
        )
        if before is not None:
            pair_out = after(pair_out, last_across, *attn_sent, before["down_got"])
        got = swap(pair_out, "seq", 1)
        out_terms = [own_out, got[0], swap(add_low(across_out, got[1]), "seq", 2)]
        got_far = swap(send_far, "dp", 1)
        near_got = swap(after(send_near, got), "dp", 1)
        if before is not None:
            step_one(before, own_out)
            before["attn_sums"] = sum_attn(before, attn_sent, own_out)
        grad_middle, grad_low, mlp_gain_part, grad_query, own_term, *kv_terms = attention_back(
            upstream,
            middle,
            mlp_gain_full,
            out_terms,
            second_full,
            queries,
            kv_blocks,
            biases_turned,
            cos_wide,
            sin_wide,
        )
        if before is not None:
            kv_terms[2] = after(kv_terms[2], before["crossed"])
        kv_terms = [own_term] + [swap(kv_terms[bit - 1], "seq", bit) for bit in range(1, 4)]
        far_sum = add_low(keep_far, after(got_far, grad_low))
        waited = (far_sum,)
        if before is not None:
            step_two(before, grad_low)
        state = {
            "layer": layer,
            "far_sum": far_sum,
            "keep_near": keep_near,
            "near_got": near_got,
        }
        if line == 4:
            state["inward"] = line_steps(far_sum, [(0, 1), (3, 2)])
        by_side = down_part.reshape(line, 2, unit_rows, model_width)
        down_send = lax.dynamic_index_in_dim(by_side, 1 - side, 1, keepdims=False)
        state["down_keep"] = lax.dynamic_index_in_dim(by_side, side, 1, keepdims=False)
        state["down_got"] = swap(
            after(down_send, *(out_terms[2:] if before is None else kv_terms[1:])), "dp", 1
        )
        upstream, upstream_low, grad_kv, attn_gain_part, bias_first, bias_second = before_back(
            kv_terms,
            grad_query,
            x,
            after(gain_full, *waited),
            grad_middle,
            first_full,
            second_full,
            cos_wide,
            sin_wide,
        )
        near_x, far_x, near_other, far_other = projection_grads(
            normed,
            grad_query,
            grad_kv,
            mixed,
            grad_low,
            attn_gain_part,
            mlp_gain_part,
            bias_first,
            bias_second,
            [core, chip_x, dp_place],
            chip_rows,
            line,
        )
        got_far_other = swap(far_other, "seq", 1)
        got_near_other = swap(near_other, "seq", 1)
        state["attn_parts"] = (near_x, far_x, got_near_other, got_far_other)
        if before is not None:
            step_three(before, upstream)
        states[layer] = before = state
    step_one(before)
    step_two(before)
    step_three(before)
    arrived = [None, send_attn(before, 1)]
    arrived[0] = send_attn(before, 0)
    before["attn_sums"] = sum_attn(before, arrived)
    grads = finish(states)
    terms.append(last_across)
    activations = sum(term.astype(jnp.float32) for term in terms).astype(jnp.bfloat16)
    return (
        activations.reshape(seq_count, tok_len, model_width),
        upstream.reshape(seq_count, tok_len, model_width),
    ) + grads


def solution(mesh):
    in_specs = (
        P("dp", "seq", None),
        P("dp", "seq", None),
        P("dp", None),
        P(None, ("dp", "seq")),
        P(None, ("dp", "seq"), None),
        P(None, ("dp", "seq")),
        P(None, ("dp", "seq"), None),
        P(None, ("dp", "seq")),
        P(None, ("dp", "seq"), None),
        P(None, ("dp", "seq"), None),
    )
    out_specs = (
        P("dp", "seq", None),
        P("dp", "seq", None),
        P(None, ("dp", "seq")),
        P(None, ("dp", "seq"), None),
        P(None, ("dp", "seq")),
        P(None, ("dp", "seq")),
        P(None, ("dp", "seq"), None),
        P(None, ("dp", "seq")),
        P(None, ("dp", "seq"), None),
        P(None, ("dp", "seq"), None),
    )
    return jax.shard_map(body, mesh=mesh, in_specs=in_specs, out_specs=out_specs, check_vma=False)
```

```python
import jax
import jax.numpy as jnp
from jax import lax
from jax.experimental import pallas as pl
from jax.experimental.pallas import tpu as pltpu
from jax.sharding import PartitionSpec as P

D = 896
HEADS = 14
KV_HEADS = 2
HEAD = 64
LAYERS = 2


EPS = 1e-06
THETA = 1000000.0
NEGATIVE = -1e30


def rotary_tables(positions):
    half_head = HEAD // 2
    frequency = THETA ** (-2.0 * jnp.arange(half_head, dtype=jnp.float32) / HEAD)
    angles = positions.astype(jnp.float32)[..., None] * frequency
    return (jnp.cos(angles), jnp.sin(angles))


NT = (((1,), (1,)), ((), ()))
TN = (((0,), (0,)), ((), ()))
FULL = pl.BlockSpec(memory_space=pltpu.VMEM)
SCALE = HEAD ** (-0.5)
GROUP = HEADS // KV_HEADS
KV_WIDTH = KV_HEADS * HEAD
SPLIT = D + KV_WIDTH
TILE = 384


def dot(left, right, dims=(((1,), (0,)), ((), ()))):
    return lax.dot_general(left, right, dims, preferred_element_type=jnp.float32)


def call(kernel, outs, micros, scratch=(), limit=40, **grid):
    return pl.pallas_call(
        kernel,
        out_shape=[jax.ShapeDtypeStruct(shape, kind) for shape, kind in outs],
        scratch_shapes=list(scratch),
        compiler_params=pltpu.CompilerParams(vmem_limit_bytes=limit * 2**20),
        name=kernel.__qualname__.split(".")[0],
        cost_estimate=pl.CostEstimate(
            flops=0, bytes_accessed=int(micros * 4e3), transcendentals=0
        ),
        **grid,
    )


def turn(block, cos_wide, sin_wide):
    lane = lax.broadcasted_iota(jnp.int32, block.shape, 1)
    width = block.shape[1]
    partner = jnp.where(
        lane % HEAD < HEAD // 2,
        pltpu.roll(block, width - HEAD // 2, 1),
        pltpu.roll(block, HEAD // 2, 1),
    )
    return block * cos_wide + partner * sin_wide


def inverse_root(rows):
    return lax.rsqrt(jnp.mean(rows * rows, axis=-1, keepdims=True) + EPS)


def before_attention(terms, gain, first_full, second_full, bias_first, bias_second, cos_wide, sin_wide):
    count = len(terms)
    rows = terms[0].shape[0]
    span = rows // 2

    def kernel(*refs):
        parts = refs[:count]
        gain_ref, first_ref, second_ref, bias_one, bias_two, cos_ref, sin_ref = refs[count : count + 7]
        x_ref, n_ref, q_ref, kv_ref = refs[count + 7 :]
        x = parts[0][...].astype(jnp.float32)
        for part in parts[1:]:
            x = x + part[...].astype(jnp.float32)
        x_ref[...] = x
        normed = (x * inverse_root(x) * gain_ref[...]).astype(jnp.bfloat16)
        n_ref[...] = normed
        cos_w, sin_w = cos_ref[...], sin_ref[...]
        for tile in range(SPLIT // 128):
            lanes = slice(tile * 128, tile * 128 + 128)
            block = dot(normed, first_ref[:, lanes]) + bias_one[:, lanes]
            turned = turn(block, cos_w, sin_w)
            if tile * 128 < D:
                for part in range(2):
                    head = 2 * tile + part
                    piece = turned[:, part * HEAD : part * HEAD + HEAD].astype(jnp.bfloat16)
                    place = (head % GROUP) * span
                    for half in range(2):
                        q_ref[head // GROUP, half, place : place + span, :] = piece[
                            half * span : half * span + span
                        ]
            else:
                kv_ref[:, :KV_WIDTH] = turned.astype(jnp.bfloat16)
        kv_ref[:, KV_WIDTH:] = (
            dot(normed, second_ref[:, :KV_WIDTH]) + bias_two[...]
        ).astype(jnp.bfloat16)

    return call(
        kernel,
        [
            ((rows, D), jnp.float32),
            ((rows, D), jnp.bfloat16),
            ((KV_HEADS, 2, GROUP * span, HEAD), jnp.bfloat16),
            ((rows, 2 * KV_WIDTH), jnp.bfloat16),
        ],
        4.0,
    )(*terms, gain, first_full, second_full, bias_first, bias_second, cos_wide, sin_wide)


def key_part(kv_refs, half, lanes):
    span = kv_refs[0].shape[0] // 2
    return jnp.concatenate(
        [ref[half * span : half * span + span, lanes] for ref in kv_refs], axis=0
    )


def attention(queries, kv_blocks, biases, x, second_full, gain):
    rows = x.shape[0]
    span = rows // 2

    def kernel(q_ref, kv0, kv1, kv2, kv3, bias_ref, x_ref, w_ref, gain_ref, mixed_ref, mid_ref, n_ref):
        kvs = (kv0, kv1, kv2, kv3)
        for group in range(KV_HEADS):
            key_lanes = slice(group * HEAD, group * HEAD + HEAD)
            value_lanes = slice(KV_WIDTH + group * HEAD, KV_WIDTH + group * HEAD + HEAD)
            keys = [key_part(kvs, half, key_lanes) for half in range(2)]
            values = []
            for half in range(2):
                block = key_part(kvs, half, value_lanes)
                values.append(jnp.concatenate([block, jnp.ones_like(block)], axis=1))
            for half in range(2):
                bias = bias_ref[half]
                for member in range(GROUP):
                    query = q_ref[group, half, member * span : member * span + span, :] * jnp.bfloat16(SCALE)
                    near = dot(query, keys[half], NT) + bias
                    top = jnp.max(near, axis=-1, keepdims=True)
                    if half == 1:
                        far = dot(query, keys[0], NT)
                        top = jnp.maximum(top, jnp.max(far, axis=-1, keepdims=True))
                    total = dot(jnp.exp(near - top).astype(jnp.bfloat16), values[half])
                    if half == 1:
                        total = total + dot(jnp.exp(far - top).astype(jnp.bfloat16), values[0])
                    out = total[:, :HEAD] / total[:, HEAD : 2 * HEAD]
                    head = group * GROUP + member
                    mixed_ref[half * span : half * span + span, head * HEAD : head * HEAD + HEAD] = (
                        out.astype(jnp.bfloat16)
                    )
        middle = x_ref[...] + dot(mixed_ref[...], w_ref[:, KV_WIDTH:])
        mid_ref[...] = middle
        n_ref[...] = (middle * inverse_root(middle) * gain_ref[...]).astype(jnp.bfloat16)

    return call(
        kernel,
        [((rows, D), jnp.bfloat16), ((rows, D), jnp.float32), ((rows, D), jnp.bfloat16)],
        10.5,
    )(queries, *kv_blocks, biases, x, second_full, gain)


def feed_forward(parts, gate_up_full, down_full):
    count = len(parts)
    part_rows = parts[0].shape[0]
    rows = count * part_rows
    units = down_full.shape[0]
    steps = pl.cdiv(units, TILE)
    last = units - (steps - 1) * TILE

    def kernel(*refs):
        part_refs = refs[:count]
        w_ref, d_ref, gu_ref = refs[count : count + 3]
        out_refs, total = refs[count + 3 : -1], refs[-1]
        step = pl.program_id(0)
        n2 = jnp.concatenate([ref[...] for ref in part_refs], axis=0)

        @pl.when(step == 0)
        def _():
            total[...] = jnp.zeros_like(total)

        @pl.when(step < steps - 1)
        def _():
            both = dot(n2, w_ref[...])
            gu_ref[...] = both.astype(jnp.bfloat16)
            gate, up = both[:, :TILE], both[:, TILE:]
            hidden = (gate * jax.nn.sigmoid(gate) * up).astype(jnp.bfloat16)
            total[...] += dot(hidden, d_ref[...])

        @pl.when(step == steps - 1)
        def _():
            both = dot(n2, w_ref[:, : 2 * last])
            gu_ref[:, : 2 * last] = both.astype(jnp.bfloat16)
            gate, up = both[:, :last], both[:, last:]
            hidden = (gate * jax.nn.sigmoid(gate) * up).astype(jnp.bfloat16)
            summed = (total[...] + dot(hidden, d_ref[:last, :])).astype(jnp.bfloat16)
            for place in range(count):
                out_refs[place][...] = summed[place * part_rows : place * part_rows + part_rows]

    whole = lambda step: (0, 0)
    return call(
        kernel,
        [((rows, 2 * units), jnp.bfloat16)] + [((part_rows, D), jnp.bfloat16)] * count,
        9.0,
        [pltpu.VMEM((rows, D), jnp.float32)],
        limit=60,
        grid=(steps,),
        in_specs=[pl.BlockSpec((part_rows, D), whole)] * count
        + [
            pl.BlockSpec((D, 2 * TILE), lambda step: (0, step)),
            pl.BlockSpec((TILE, D), lambda step: (step, 0)),
        ],
        out_specs=[
            pl.BlockSpec((rows, 2 * TILE), lambda step: (0, step)),
        ]
        + [pl.BlockSpec((part_rows, D), whole)] * count,
    )(*parts, gate_up_full, down_full)


def far_slot(mine, place, line):
    if line == 4:
        return jnp.where(mine < 2, place - 2, 1 - place)
    return (mine ^ place) - line // 2


def feed_back(gz_parts, n2_parts, gu_parts, gate_up_full, down_full, dp_place, group_count):
    line = group_count // 2
    half = line // 2
    chunk = D // group_count
    count = len(gz_parts)
    gu_count = len(gu_parts)
    part_rows = gz_parts[0].shape[0]
    rows = count * part_rows
    units = down_full.shape[0]
    unit_rows = units // group_count
    packed = chunk + unit_rows * D // (2 * units)
    once = pl.Buffered(1)
    steps = pl.cdiv(units, TILE)
    last = units - (steps - 1) * TILE

    def kernel(*refs):
        place_ref, *refs = refs
        gz_refs = refs[:count]
        n2_refs = refs[count : 2 * count]
        gu_refs = refs[2 * count : 2 * count + gu_count]
        w_ref, d_ref = refs[2 * count + gu_count : 2 * count + gu_count + 2]
        keep_near, keep_far, send_near, send_far, own_ref, across_ref, pair_ref = refs[
            2 * count + gu_count + 2 : 2 * count + gu_count + 9
        ]
        total, gz, n2t, down = refs[-4:]
        side, mine = place_ref[0] % 2, place_ref[0] // 2
        step = pl.program_id(0)

        @pl.when(step == 0)
        def _():
            total[...] = jnp.zeros_like(total)
            for place in range(count):
                here = slice(place * part_rows, place * part_rows + part_rows)
                gz[here, :] = gz_refs[place][...]
                n2t[:, here] = n2_refs[place][...].T

        def write(spot, even, odd, rows, lanes):
            keep = jnp.where(side == 0, even, odd)
            send = jnp.where(side == 0, odd, even)
            slot = mine ^ spot
            beyond = far_slot(mine, spot, line)

            @pl.when(slot < half)
            def _():
                keep_near[slot, rows, lanes] = keep
                send_near[slot, rows, lanes] = send

            @pl.when(slot >= half)
            def _():
                keep_far[beyond, rows, lanes] = keep
                send_far[beyond, rows, lanes] = send

        def work(width):
            gu = jnp.concatenate([ref[:, : 2 * width] for ref in gu_refs], axis=0).astype(jnp.float32)
            gate, up = gu[:, :width], gu[:, width:]
            sig = jax.nn.sigmoid(gate)
            act = gate * sig
            hidden = (act * up).astype(jnp.bfloat16)
            down[pl.ds(pl.multiple_of(step * TILE, 128), width), :] = dot(hidden, gz[...], TN)
            grad = dot(gz[...], d_ref[:width, :], NT)
            d_gate = grad * up * (sig + act * (1.0 - sig))
            d_up = grad * act
            both = jnp.concatenate([d_gate, d_up], axis=1).astype(jnp.bfloat16)
            part = dot(n2t[...], both)
            for spot in range(line):
                even = part[2 * spot * chunk : (2 * spot + 1) * chunk].astype(jnp.bfloat16)
                odd = part[(2 * spot + 1) * chunk : (2 * spot + 2) * chunk].astype(jnp.bfloat16)
                write(spot, even, odd, slice(0, chunk), pl.ds(pl.multiple_of(step * 2 * TILE, 128), 2 * width))

            return dot(both, w_ref[:, : 2 * width], NT)

        @pl.when(step < steps - 1)
        def _():
            total[...] += work(TILE)

        @pl.when(step == steps - 1)
        def _():
            summed = (total[...] + work(last)).astype(jnp.bfloat16)
            for spot in range(line):
                even, odd = (
                    fold(down[place * unit_rows : place * unit_rows + unit_rows, :], 2 * units).astype(
                        jnp.bfloat16
                    )
                    for place in (2 * spot, 2 * spot + 1)
                )
                write(spot, even, odd, slice(chunk, packed), slice(0, 2 * units))
            own_ref[...] = summed[:part_rows]
            pair_ref[0] = summed[part_rows : 2 * part_rows]
            across_ref[...] = summed[2 * part_rows : 3 * part_rows]
            pair_ref[1] = summed[3 * part_rows :]

    whole = lambda step: (0, 0)
    return call(
        kernel,
        [
            ((half, packed, 2 * units), jnp.bfloat16),
            ((half, packed, 2 * units), jnp.bfloat16),
            ((half, packed, 2 * units), jnp.bfloat16),
            ((half, packed, 2 * units), jnp.bfloat16),
            ((part_rows, D), jnp.bfloat16),
            ((part_rows, D), jnp.bfloat16),
            ((2, part_rows, D), jnp.bfloat16),
        ],
        25.0,
        [
            pltpu.VMEM((rows, D), jnp.float32),
            pltpu.VMEM((rows, D), jnp.bfloat16),
            pltpu.VMEM((D, rows), jnp.bfloat16),
            pltpu.VMEM((units, D), jnp.float32),
        ],
        limit=60,
        grid=(steps,),
        in_specs=[pl.BlockSpec(memory_space=pltpu.SMEM)]
        + [pl.BlockSpec((part_rows, D), whole, pipeline_mode=once)] * (2 * count)
        + [pl.BlockSpec((rows // gu_count, 2 * TILE), lambda step: (0, step))] * gu_count
        + [
            pl.BlockSpec((D, 2 * TILE), lambda step: (0, step)),
            pl.BlockSpec((TILE, D), lambda step: (step, 0)),
        ],
        out_specs=[
            pl.BlockSpec((half, packed, 2 * units), lambda step: (0, 0, 0), pipeline_mode=once),
            pl.BlockSpec((half, packed, 2 * units), lambda step: (0, 0, 0), pipeline_mode=once),
            pl.BlockSpec((half, packed, 2 * units), lambda step: (0, 0, 0), pipeline_mode=once),
            pl.BlockSpec((half, packed, 2 * units), lambda step: (0, 0, 0), pipeline_mode=once),
            pl.BlockSpec((part_rows, D), whole, pipeline_mode=once),
            pl.BlockSpec((part_rows, D), whole, pipeline_mode=once),
            pl.BlockSpec((2, part_rows, D), lambda step: (0, 0, 0), pipeline_mode=once),
        ],
    )(dp_place.reshape(1).astype(jnp.int32), *gz_parts, *n2_parts, *gu_parts, gate_up_full, down_full)


def norm_back(rows, gain, grad):
    inv_root = inverse_root(rows)
    normal = rows * inv_root
    gain_part = jnp.sum(grad * normal, axis=0, keepdims=True)
    weighted = grad * gain
    inner = jnp.mean(weighted * normal, axis=-1, keepdims=True)
    return gain_part, inv_root * (weighted - normal * inner)


def attention_back(upstream, middle, gain, terms, second_full, queries, kv_blocks, biases, cos_wide, sin_wide):
    count = len(terms)
    rows = middle.shape[0]
    span = rows // 2
    wide = GROUP * span

    def kernel(*refs):
        up_ref, mid_ref, gain_ref = refs[:3]
        term_refs = refs[3 : 3 + count]
        w_ref, q_ref, kv0, kv1, kv2, kv3, bias_ref, cos_ref, sin_ref = refs[3 + count : 12 + count]
        gm_ref, gy_ref, dgain_ref, gq_ref, own_ref, d1, d2, d3, go_ref, dkv = refs[12 + count :]
        kvs = (kv0, kv1, kv2, kv3)
        grad = term_refs[0][...].astype(jnp.float32)
        for term in term_refs[1:]:
            grad = grad + term[...].astype(jnp.float32)
        gain_part, back = norm_back(mid_ref[...], gain_ref[...], grad)
        dgain_ref[...] = gain_part
        grad_middle = up_ref[...].astype(jnp.float32) + back
        gm_ref[...] = grad_middle
        grad_low = grad_middle.astype(jnp.bfloat16)
        gy_ref[...] = grad_low
        for tile in range(D // 128):
            start = KV_WIDTH
            block = dot(grad_low, w_ref[tile * 128 : tile * 128 + 128, start:], NT).astype(jnp.bfloat16)
            for part in range(2):
                head = 2 * tile + part
                place = (head % GROUP) * span
                for half in range(2):
                    go_ref[head // GROUP, half, place : place + span, :] = block[
                        half * span : half * span + span, part * HEAD : part * HEAD + HEAD
                    ]
        for group in range(KV_HEADS):
            key_lanes = slice(group * HEAD, group * HEAD + HEAD)
            value_lanes = slice(KV_WIDTH + group * HEAD, KV_WIDTH + group * HEAD + HEAD)
            keys = [key_part(kvs, half, key_lanes) for half in range(2)]
            values = [key_part(kvs, half, value_lanes) for half in range(2)]
            for half in range(2):
                query = q_ref[group, half] * jnp.bfloat16(SCALE)
                grad_out = go_ref[group, half]
                bias = jnp.concatenate([bias_ref[half]] * GROUP, axis=1)
                use = [half] if half == 0 else [1, 0]
                scores = []
                top = None
                for which in use:
                    score = dot(keys[which], query, NT)
                    if which == half:
                        score = score + bias
                    scores.append(score)
                    best = jnp.max(score, axis=0, keepdims=True)
                    top = best if top is None else jnp.maximum(top, best)
                weights = [jnp.exp(score - top) for score in scores]
                total = sum(jnp.sum(weight, axis=0, keepdims=True) for weight in weights)
                scale = 1.0 / total
                probs = [weight * scale for weight in weights]
                grads = [dot(values[which], grad_out, NT) for which in use]
                inner = sum(
                    jnp.sum(prob * grad_prob, axis=0, keepdims=True)
                    for prob, grad_prob in zip(probs, grads)
                )
                grad_query = None
                for which, prob, grad_prob in zip(use, probs, grads):
                    grad_score = (prob * (grad_prob - inner)).astype(jnp.bfloat16)
                    value_grad = dot(prob.astype(jnp.bfloat16), grad_out)
                    key_grad = dot(grad_score, query)
                    if half == 0:
                        dkv[group, which] = key_grad
                        dkv[KV_HEADS + group, which] = value_grad
                    elif which == 0:
                        dkv[group, which] += key_grad
                        dkv[KV_HEADS + group, which] += value_grad
                    else:
                        dkv[group, which] = key_grad
                        dkv[KV_HEADS + group, which] = value_grad
                    term = dot(keys[which].T, grad_score)
                    grad_query = term if grad_query is None else grad_query + term
                grad_query = grad_query * SCALE
                cos_w = cos_ref[half * span : half * span + span, :]
                sin_w = sin_ref[half * span : half * span + span, :]
                for member in range(GROUP):
                    head = group * GROUP + member
                    piece = grad_query[:, member * span : member * span + span].T
                    pair = jnp.concatenate([piece, piece], axis=1)
                    turned = turn(pair, cos_w, -sin_w)[:, :HEAD]
                    gq_ref[half * span : half * span + span, head * HEAD : head * HEAD + HEAD] = (
                        turned.astype(jnp.bfloat16)
                    )
        for place, out in enumerate((own_ref, d1, d2, d3)):
            for half in range(2):
                block = jnp.concatenate(
                    [dkv[lane, half, place * span : place * span + span, :] for lane in range(2 * KV_HEADS)],
                    axis=1,
                )
                out[half * span : half * span + span, :] = block.astype(out.dtype)

    return call(
        kernel,
        [
            ((rows, D), jnp.float32),
            ((rows, D), jnp.bfloat16),
            ((1, D), jnp.float32),
            ((rows, D), jnp.bfloat16),
            ((rows, 2 * KV_WIDTH), jnp.float32),
        ]
        + [((rows, 2 * KV_WIDTH), jnp.bfloat16)] * 3,
        13.0,
        [
            pltpu.VMEM((KV_HEADS, 2, wide, HEAD), jnp.bfloat16),
            pltpu.VMEM((2 * KV_HEADS, 2, 4 * span, HEAD), jnp.float32),
        ],
    )(upstream, middle, gain, *terms, second_full, queries, *kv_blocks, biases, cos_wide, sin_wide)


def before_back(kv_terms, gq, x, gain, grad_middle, first_full, second_full, cos_wide, sin_wide):
    rows = x.shape[0]
    count = len(kv_terms)

    def kernel(*refs):
        kv_refs = refs[:count]
        gq_ref, x_ref, gain_ref, gm_ref, w1_ref, w2_ref, cos_ref, sin_ref = refs[count : count + 8]
        up_ref, low_ref, gkv_ref, dgain_ref, bias_one, bias_two = refs[count + 8 :]
        grad = kv_refs[0][...].astype(jnp.float32)
        for ref in kv_refs[1:]:
            grad = grad + ref[...].astype(jnp.float32)
        grad_key = turn(grad[:, :KV_WIDTH], cos_ref[...], -sin_ref[...]).astype(jnp.bfloat16)
        grad_value = grad[:, KV_WIDTH:].astype(jnp.bfloat16)
        gkv_ref[:, :KV_WIDTH] = grad_key
        gkv_ref[:, KV_WIDTH:] = grad_value
        grad_query = gq_ref[...]
        bias_one[:, :D] = jnp.sum(grad_query.astype(jnp.float32), axis=0, keepdims=True)
        bias_one[:, D:] = jnp.sum(grad_key.astype(jnp.float32), axis=0, keepdims=True)
        bias_two[...] = jnp.sum(grad_value.astype(jnp.float32), axis=0, keepdims=True)
        grad_normed = (
            dot(grad_query, w1_ref[:, :D], NT)
            + dot(grad_key, w1_ref[:, D:], NT)
            + dot(grad_value, w2_ref[:, :KV_WIDTH], NT)
        )
        gain_part, back = norm_back(x_ref[...], gain_ref[...], grad_normed)
        dgain_ref[...] = gain_part
        upstream = gm_ref[...] + back
        up_ref[...] = upstream
        low_ref[...] = upstream.astype(jnp.bfloat16)

    return call(
        kernel,
        [
            ((rows, D), jnp.float32),
            ((rows, D), jnp.bfloat16),
            ((rows, 2 * KV_WIDTH), jnp.bfloat16),
            ((1, D), jnp.float32),
            ((1, SPLIT), jnp.float32),
            ((1, KV_WIDTH), jnp.float32),
        ],
        2.4,
    )(*kv_terms, gq, x, gain, grad_middle, first_full, second_full, cos_wide, sin_wide)


def unit_pieces(unit_rows, group_count, seq_devices):
    units = unit_rows * group_count
    steps = pl.cdiv(units, TILE)
    pieces = []
    for owner in range(seq_devices):
        for kind in range(2):
            for group in range(group_count):
                unit = group * unit_rows
                stop = unit + unit_rows
                column = kind * units * seq_devices + (group * seq_devices + owner) * unit_rows
                while unit < stop:
                    step = unit // TILE
                    end = min(stop, (step + 1) * TILE)
                    width = TILE if step < steps - 1 else units - (steps - 1) * TILE
                    inside = 2 * step * TILE + kind * width + unit - step * TILE
                    pieces.append((owner, inside, column, end - unit))
                    column += end - unit
                    unit = end
    return pieces


def spread_columns(weight, place, unit_rows, group_count, seq_devices):
    layers, rows, columns = weight.shape
    quarter = columns // seq_devices
    pieces = unit_pieces(unit_rows, group_count, seq_devices)

    def kernel(place_ref, w_ref, *refs):
        outs, wide, narrow = refs[:seq_devices], refs[-2], refs[-1]
        for layer in range(layers):
            wide[...] = w_ref[layer].astype(jnp.float32)
            for owner in range(seq_devices):
                for who, inside, column, width in pieces:
                    if who == owner:
                        narrow[:, inside : inside + width] = wide[:, column : column + width]
                block = narrow[...].astype(jnp.bfloat16)
                for bit in range(seq_devices):

                    @pl.when(place_ref[0] == owner ^ bit)
                    def _():
                        outs[bit][layer] = block

    return call(
        kernel,
        [((layers, rows, quarter), jnp.bfloat16)] * seq_devices,
        2.5,
        [pltpu.VMEM((rows, columns), jnp.float32), pltpu.VMEM((rows, quarter), jnp.float32)],
        in_specs=[pl.BlockSpec(memory_space=pltpu.SMEM), FULL],
        out_specs=[FULL] * seq_devices,
    )(place.reshape(1).astype(jnp.int32), weight)


def collect_columns(blocks, place, unit_rows, group_count):
    count = len(blocks)
    layers, rows, quarter = blocks[0].shape
    pieces = unit_pieces(unit_rows, group_count, count)

    def kernel(place_ref, *refs):
        out_ref, narrow = refs[count:]
        me = place_ref[0]
        for layer in range(layers):
            for owner in range(count):
                for bit in range(count):

                    @pl.when(me == owner ^ bit)
                    def _():
                        narrow[...] = refs[bit][layer].astype(jnp.float32)

                for who, inside, column, width in pieces:
                    if who == owner:
                        out_ref[layer, :, column : column + width] = narrow[:, inside : inside + width]

    return call(
        kernel,
        [((layers, rows, count * quarter), jnp.float32)],
        1.5,
        [pltpu.VMEM((rows, quarter), jnp.float32)],
        in_specs=[pl.BlockSpec(memory_space=pltpu.SMEM)] + [FULL] * count,
        out_specs=[FULL],
    )(place.reshape(1).astype(jnp.int32), *blocks)[0]


def fold(rows, columns):
    high = rows.shape[0] * 128 // columns
    wide = rows.shape[1] // 128
    return jnp.concatenate(
        [
            jnp.concatenate(
                [rows[high * r : high * r + high, 128 * c : 128 * c + 128] for r in range(columns // 128)],
                axis=1,
            )
            for c in range(wide)
        ],
        axis=0,
    )


def unfold(rows, width):
    high = rows.shape[0] * 128 // width
    wide = rows.shape[1] // 128
    return jnp.concatenate(
        [
            jnp.concatenate(
                [rows[high * c : high * c + high, 128 * r : 128 * r + 128] for c in range(width // 128)],
                axis=1,
            )
            for r in range(wide)
        ],
        axis=0,
    )


def pack_rows(blocks, down, place):
    owners = len(blocks)
    layers, rows, columns = blocks[0].shape
    total = owners * rows + down.shape[1] * down.shape[2] // columns

    def kernel(place_ref, down_ref, *refs):
        ins, outs = refs[:owners], refs[owners:]
        for layer in range(layers):
            parts = []
            for owner in range(owners):
                part = ins[0][layer].astype(jnp.float32)
                for bit in range(1, owners):
                    part = jnp.where(
                        place_ref[0] == owner ^ bit, ins[bit][layer].astype(jnp.float32), part
                    )
                parts.append(part)
            parts.append(fold(down_ref[layer].astype(jnp.float32), columns))
            outs[layer][0] = jnp.concatenate(parts, axis=0).astype(jnp.bfloat16)

    return call(
        kernel,
        [((1, total, columns), jnp.bfloat16)] * layers,
        3.0,
        in_specs=[pl.BlockSpec(memory_space=pltpu.SMEM)] + [FULL] * (owners + 1),
        out_specs=[FULL] * layers,
    )(place.reshape(1).astype(jnp.int32), down, *blocks)


def unpack(parts, places, chunk):
    count, total, columns = parts[0].shape
    number = count * len(parts)
    unit_rows = (total - chunk) * columns // D

    def kernel(place_ref, *refs):
        ins, gate_ref, down_ref = refs[: len(parts)], refs[-2], refs[-1]
        for which in range(len(parts)):
            for k in range(count):
                spot = place_ref[which * count + k]
                gate_ref[spot] = ins[which][k, :chunk, :]
                down_ref[spot] = unfold(ins[which][k, chunk:, :].astype(jnp.float32), D).astype(
                    jnp.bfloat16
                )

    gate, down = call(
        kernel,
        [((number, chunk, columns), jnp.bfloat16), ((number, unit_rows, D), jnp.bfloat16)],
        5.0,
        in_specs=[pl.BlockSpec(memory_space=pltpu.SMEM)] + [FULL] * len(parts),
        out_specs=[FULL] * 2,
    )(jnp.stack(places).astype(jnp.int32), *parts)
    return gate.reshape(number * chunk, columns), down.reshape(number * unit_rows, D)


def split_rows(terms, chunk, place, count):
    layers = len(terms)
    total_rows, columns = terms[0][0].shape
    rows = chunk // count
    unit_rows = (total_rows - chunk) * columns // D

    def kernel(place_ref, *refs):
        ins, outs, down_ref = refs[: 2 * layers], refs[2 * layers : -1], refs[-1]
        for layer in range(layers):
            total = ins[2 * layer][...].astype(jnp.float32) + ins[2 * layer + 1][...].astype(
                jnp.float32
            )
            down_ref[layer] = unfold(total[chunk:], D)
            for owner in range(count):
                block = total[owner * rows : owner * rows + rows].astype(jnp.bfloat16)
                for bit in range(count):

                    @pl.when(place_ref[0] == owner ^ bit)
                    def _():
                        outs[bit][layer] = block

    *blocks, down = call(
        kernel,
        [((layers, rows, columns), jnp.bfloat16)] * count
        + [((layers, unit_rows, D), jnp.float32)],
        3.0,
        in_specs=[pl.BlockSpec(memory_space=pltpu.SMEM)] + [FULL] * (2 * layers),
        out_specs=[FULL] * (count + 1),
    )(place.reshape(1).astype(jnp.int32), *[term for pair in terms for term in pair])
    return blocks, down


def assemble(parts, places, chip_rows):
    line, rows, width = parts[0].shape

    def kernel(place_ref, *refs):
        ins = refs[:8]
        first_ref, second_ref, small_ref = refs[8:]
        here, chip, side = place_ref[0] == 0, place_ref[1] == 0, place_ref[2] % 2 == 0
        mine = place_ref[2] // 2
        small = jnp.zeros((rows - chip_rows, width), jnp.float32)
        for spot in range(line):
            halves = []
            for half in range(2):
                pieces = []
                blocks = [ins[4 * half + k][spot].astype(jnp.float32) for k in range(4)]
                for block in blocks:
                    small = small + block[chip_rows:]
                lower = [jnp.where(side, blocks[2 * x], blocks[2 * x + 1]) for x in range(2)]
                upper = [jnp.where(side, blocks[2 * x + 1], blocks[2 * x]) for x in range(2)]
                for pair in (lower, upper):
                    pieces.append(jnp.where(chip, pair[0], pair[1])[:chip_rows])
                    pieces.append(jnp.where(chip, pair[1], pair[0])[:chip_rows])
                halves.append(jnp.concatenate(pieces, axis=0).astype(jnp.bfloat16))
            first_ref[mine ^ spot] = jnp.where(here, halves[0], halves[1])
            second_ref[mine ^ spot] = jnp.where(here, halves[1], halves[0])
        small_ref[...] = small

    first, second, small = call(
        kernel,
        [
            ((line, 4 * chip_rows, width), jnp.bfloat16),
            ((line, 4 * chip_rows, width), jnp.bfloat16),
            ((rows - chip_rows, width), jnp.float32),
        ],
        4.0,
        in_specs=[pl.BlockSpec(memory_space=pltpu.SMEM)] + [FULL] * 8,
        out_specs=[FULL] * 3,
    )(jnp.stack(places).astype(jnp.int32), *parts)
    return first.reshape(-1, width), second.reshape(-1, width), small


def projection_grads(normed, grad_query, grad_kv, mixed, grad_low, gain_one, gain_two, bias_one, bias_two, places, chip_rows, line):
    width = SPLIT

    def kernel(place_ref, n_ref, gq_ref, gkv_ref, mixed_ref, gy_ref, g1_ref, g2_ref, b1_ref, b2_ref, keep0, keep1, send0, send1, pad):
        here, chip, side = place_ref[0] == 0, place_ref[1] == 0, place_ref[2] % 2
        mine = place_ref[2] // 2
        turned = n_ref[...].T
        pad[...] = jnp.zeros_like(pad)
        pad[0:1, :D] = g1_ref[...]
        pad[1:2, :D] = g2_ref[...]
        pad[2:3, :] = b1_ref[...]
        pad[3:4, :KV_WIDTH] = b2_ref[...]
        small = pad[...]
        first = jnp.concatenate(
            [dot(turned, gq_ref[...]), dot(turned, gkv_ref[:, :KV_WIDTH])], axis=1
        )
        second = jnp.concatenate(
            [dot(turned, gkv_ref[:, KV_WIDTH:]), dot(mixed_ref[...], gy_ref[...], TN)], axis=1
        )

        def chunk(part, number):
            rows = part[number * chip_rows : (number + 1) * chip_rows]
            return jnp.concatenate([rows, small], axis=0).astype(jnp.bfloat16)

        for spot in range(line):
            for pair in range(2):
                slot = side ^ pair
                firsts = [chunk(first, 4 * spot + 2 * pair + x) for x in range(2)]
                seconds = [chunk(second, 4 * spot + 2 * pair + x) for x in range(2)]
                keeps = [jnp.where(here, one, two) for one, two in zip(firsts, seconds)]
                sends = [jnp.where(here, two, one) for one, two in zip(firsts, seconds)]
                keep0[slot, mine ^ spot] = jnp.where(chip, keeps[0], keeps[1])
                keep1[slot, mine ^ spot] = jnp.where(chip, keeps[1], keeps[0])
                send0[slot, mine ^ spot] = jnp.where(chip, sends[0], sends[1])
                send1[slot, mine ^ spot] = jnp.where(chip, sends[1], sends[0])

    return call(
        kernel,
        [((2, line, chip_rows + 8, width), jnp.bfloat16)] * 4,
        6.0,
        [pltpu.VMEM((8, width), jnp.float32)],
        in_specs=[pl.BlockSpec(memory_space=pltpu.SMEM)] + [FULL] * 9,
        out_specs=[FULL] * 4,
    )(
        jnp.stack(places).astype(jnp.int32),
        normed,
        grad_query,
        grad_kv,
        mixed,
        grad_low,
        gain_one,
        gain_two,
        bias_one,
        bias_two,
    )


def swap(values, axis, bit):
    size = lax.axis_size(axis)
    return lax.ppermute(values, axis, [(i, i ^ bit) for i in range(size)])


def after(values, *others):
    return lax.optimization_barrier((values,) + tuple(others))[0]


def line_bits():
    bits = [1]
    while 4 * bits[-1] < lax.axis_size("dp"):
        bits.append(2 * bits[-1])
    return bits


def line_gather(values, bits):
    for bit in bits:
        values = jnp.concatenate([values, swap(values, "dp", 2 * bit)], axis=0)
    return values


def line_steps(values, moves):
    return lax.ppermute(
        values, "dp", [(2 * here + side, 2 * there + side) for here, there in moves for side in range(2)]
    )


def cross_middle(values):
    line = lax.axis_size("dp") // 2
    if line == 4:
        return line_steps(values, [(1, 2), (2, 1)])
    return swap(values, "dp", line)


def line_scatter(values, bits):
    for bit in bits[:0:-1]:
        values = add_low(values[:bit], swap(values[bit:], "dp", 2 * bit))
    return [values[0], swap(values[1], "dp", 2)]


def add_low(left, right):
    return (left.astype(jnp.float32) + right.astype(jnp.float32)).astype(jnp.bfloat16)


def group_rows(values, *waited):
    beside = swap(values, "seq", 1)
    across = swap(values, "seq", 2)
    return [values, beside, across, swap(after(across, *waited), "seq", 1)]


def placed(values, offset, width):
    return lax.dynamic_update_slice(jnp.zeros((width,), values.dtype), values, (offset,))


def body(
    tokens,
    cotangent,
    span_order,
    attn_gain,
    joined_weight,
    joined_bias,
    out_weight,
    mlp_gain,
    gate_up_weight,
    down_weight,
):
    seq_count, tok_len, model_width = tokens.shape
    span_len = tok_len // 2
    group_count = lax.axis_size("dp")
    seq_devices = lax.axis_size("seq")
    unit_rows = down_weight.shape[1]
    width_rows = gate_up_weight.shape[1]
    units = group_count * unit_rows
    dp_place = lax.axis_index("dp")
    seq_place = lax.axis_index("seq")
    core = seq_place % 2
    chip_x = seq_place // 2
    device = dp_place * seq_devices + seq_place
    chip_rows = 2 * width_rows
    line = group_count // 2
    side = dp_place % 2
    line_place = dp_place // 2

    order = [lax.dynamic_slice(span_order, (0, seq_place ^ bit), (1, 1))[0, 0] for bit in range(4)]
    inside = jnp.arange(span_len, dtype=jnp.int32)
    own_places = jnp.concatenate(
        [order[0] * span_len + inside, (2 * seq_devices - 1 - order[0]) * span_len + inside]
    )
    half_biases = []
    for half in range(2):
        blocks = []
        for bit in range(4):
            ahead = order[bit] < order[0] if half == 0 else order[bit] > order[0]
            allowed = ahead | ((order[bit] == order[0]) & (inside[:, None] >= inside[None, :]))
            blocks.append(jnp.where(allowed, 0.0, NEGATIVE).astype(jnp.float32))
        half_biases.append(jnp.concatenate(blocks, axis=1))
    biases = jnp.stack(half_biases)
    biases_turned = jnp.swapaxes(biases, 1, 2)
    cos_table, sin_table = rotary_tables(own_places)
    cos_wide = jnp.concatenate([cos_table] * 4, axis=1)
    sin_wide = jnp.concatenate([-sin_table, sin_table] * 2, axis=1)

    def attn_shard(layer):
        first = joined_weight[layer][:, :SPLIT]
        second = jnp.concatenate([joined_weight[layer][:, SPLIT:], out_weight[layer]], axis=1)
        got = swap(jnp.where(core == 0, second, first), "seq", 1)
        mine = jnp.where(core == 0, first, second)
        rows = jnp.where(core == 0, jnp.stack([mine, got]), jnp.stack([got, mine])).reshape(
            chip_rows, -1
        )
        bias_all = placed(joined_bias[layer], device * joined_bias.shape[1], SPLIT + KV_WIDTH)
        extra = jnp.zeros((8, SPLIT), jnp.bfloat16)
        extra = extra.at[0].set(placed(attn_gain[layer], device * width_rows, SPLIT))
        extra = extra.at[1].set(placed(mlp_gain[layer], device * width_rows, SPLIT))
        extra = extra.at[2].set(bias_all[:SPLIT])
        extra = extra.at[3, :KV_WIDTH].set(bias_all[SPLIT:])
        return jnp.concatenate([rows, extra], axis=0)

    def attn_finish(own_side, other_side, *waited):
        parts = [own_side, other_side]
        parts = parts + [swap(after(part, *waited), "seq", 2) for part in parts]
        parts = parts + [swap(part, "seq", 1) for part in parts]
        first_full, second_full, small = assemble(parts, [core, chip_x, dp_place], chip_rows)
        return (
            first_full,
            second_full,
            small[0:1, :model_width],
            small[1:2, :model_width],
            small[2:3],
            small[3:4, :KV_WIDTH],
        )

    bits = line_bits()
    spread = spread_columns(gate_up_weight, seq_place, unit_rows, group_count, seq_devices)
    shards = [attn_shard(layer)[None] for layer in range(LAYERS)]
    gate_blocks = [spread[0]] + [swap(spread[bit], "seq", bit) for bit in range(1, 4)]
    gate_shards = pack_rows(gate_blocks, down_weight, seq_place)
    attn_line = line_gather(after(shards[0], *spread), bits)
    attn_other = swap(after(attn_line, *gate_shards), "dp", 1)
    def outward(crossed):
        if line != 4:
            return crossed
        passed = line_steps(crossed, [(1, 0), (2, 3)])
        return jnp.where((line_place == 1) | (line_place == 2), crossed, passed)

    near = [line_gather(after(gate_shards[0], attn_line), bits[:-1])]
    near.append(line_gather(after(gate_shards[1], near[0]), bits[:-1]))
    near_pair = [swap(after(near[0], attn_other), "dp", 1)]
    crossed = [cross_middle(near[0])]
    far = []
    offsets = [dp_place ^ (2 * k) for k in range(line)]
    half = line // 2
    if line == 4:
        beyond = [jnp.where(line_place < 2, 2 + k, 1 - k) * 2 + side for k in range(2)]
    else:
        beyond = offsets[half:]
    places = offsets[:half] + beyond
    places = [offsets[:half], beyond, [spot ^ 1 for spot in offsets[:half]], [spot ^ 1 for spot in beyond]]
    places = [spot for group in places for spot in group]

    def mlp_finish(layer, far_pair):
        parts = [near[layer], far[layer], near_pair[layer], far_pair]
        return unpack(parts, places, seq_devices * width_rows)

    terms = [tokens.reshape(tok_len, model_width)]
    kept_state = []
    mlp_sets = []
    attn_sets = [attn_finish(attn_line, attn_other)]
    for layer in range(LAYERS):
        first_full, second_full, gain_full, mlp_gain_full, bias_first, bias_second = attn_sets[layer]
        x, normed, queries, own_kv = before_attention(
            terms,
            after(gain_full, *near) if layer == 0 else after(gain_full, near_pair[1]),
            first_full,
            second_full,
            bias_first,
            bias_second,
            cos_wide,
            sin_wide,
        )
        kv_blocks = [own_kv] + [swap(own_kv, "seq", bit) for bit in range(1, 4)]
        waited = (near_pair[0],) if layer == 0 else ()
        mixed, middle, n2 = attention(
            queries, kv_blocks, biases, x, second_full, after(mlp_gain_full, *waited)
        )
        n2_parts = group_rows(n2)
        if layer == 0:
            second_line = line_gather(after(shards[1], own_kv), bits[:1])
            for bit in bits[1:]:
                second_line = line_gather(after(second_line, n2), [bit])
            second_other = swap(after(second_line, n2_parts[3]), "dp", 1)
            far.append(outward(after(crossed[0], n2)))
            far_pair = swap(far[0], "dp", 1)
            crossed.append(cross_middle(after(near[1], n2)))
            attn_sets.append(attn_finish(second_line, second_other, n2_parts[3]))
            near_pair.append(swap(after(near[1], far_pair), "dp", 1))
            n2_parts[0] = after(n2_parts[0], attn_sets[1][2], crossed[1])
        mlp_sets.append(mlp_finish(layer, far_pair))
        gu_near, *outs_near = feed_forward(n2_parts[:2], *mlp_sets[layer])
        if layer + 1 == LAYERS:
            low_parts = group_rows(
                after(cotangent.reshape(tok_len, model_width), n2_parts[3]), gu_near
            )
        gu_far, *outs_far = feed_forward(n2_parts[2:], *mlp_sets[layer])
        if layer == 0:
            far.append(outward(crossed[1]))
            outs_far[0] = after(outs_far[0], far[1])
            far_pair = swap(after(far[1], outs_far[0]), "dp", 1)
        across_sum = add_low(outs_far[0], swap(outs_far[1], "seq", 1))
        terms = [middle, outs_near[0], swap(outs_near[1], "seq", 1)]
        if layer + 1 < LAYERS:
            terms.append(swap(across_sum, "seq", 2))
        kept_state.append((x, normed, queries, kv_blocks, mixed, middle, n2_parts, [gu_near, gu_far]))
    upstream = cotangent.reshape(tok_len, model_width)
    states = [None] * LAYERS
    before = None

    def send_attn(state, pair, *waited):
        near, far, got_near, got_far = state["attn_parts"]
        return swap(after(add_low(far[pair], got_far[pair]), *waited), "seq", 2)

    def sum_attn(state, arrived, *waited):
        near, far, got_near, got_far = state["attn_parts"]
        return [
            (
                near[pair].astype(jnp.float32)
                + got_near[pair].astype(jnp.float32)
                + after(arrived[pair], *waited).astype(jnp.float32)
            ).astype(jnp.bfloat16)
            for pair in range(2)
        ]

    def step_one(state, *waited):
        far_sum = state["far_sum"]
        if line == 4:
            far_sum = add_low(far_sum, after(state["inward"], *waited))
        state["crossed"] = cross_middle(far_sum)
        state["near_sum"] = add_low(state["keep_near"], after(state["near_got"], *waited))

    def step_two(state, *waited):
        near_sum = add_low(state["near_sum"], after(state["crossed"], *waited))
        state["terms"] = line_scatter(near_sum, bits[:-1])

    def finish(states):
        other_side = jnp.concatenate([state["attn_sums"][1] for state in states], axis=1)
        other_side = swap(after(other_side, states[0]["near_got"]), "dp", 1)
        own_side = jnp.concatenate([state["attn_sums"][0] for state in states], axis=1)
        owned = sum(
            term.astype(jnp.float32) for term in line_scatter(add_low(own_side, other_side), bits)
        ).reshape(LAYERS, chip_rows + 8, -1)
        extra = owned[:, chip_rows:]
        halves = owned[:, :chip_rows].reshape(LAYERS, 2, width_rows, -1)
        mine = lax.dynamic_index_in_dim(halves, core, 1, keepdims=False)
        theirs = swap(
            lax.dynamic_index_in_dim(halves, 1 - core, 1, keepdims=False), "seq", 1
        )
        first_own = jnp.where(core == 0, mine, theirs)
        second_own = jnp.where(core == 0, theirs, mine)

        def cut(row, width, stop):
            start = (0, row, device * width)
            return lax.dynamic_slice(extra[:, :, :stop], start, (LAYERS, 1, width))[:, 0]

        gate_rows, down_owned = split_rows(
            [state["terms"] for state in states], seq_devices * width_rows, seq_place, seq_devices
        )
        gate_owned = collect_columns(
            [gate_rows[0]] + [swap(gate_rows[bit], "seq", bit) for bit in range(1, 4)],
            seq_place,
            unit_rows,
            group_count,
        )
        return (
            cut(0, width_rows, model_width),
            jnp.concatenate([first_own, second_own[:, :, :KV_WIDTH]], axis=2),
            cut(2, SPLIT // (group_count * seq_devices), SPLIT),
            cut(3, KV_WIDTH // (group_count * seq_devices), KV_WIDTH),
            second_own[:, :, KV_WIDTH:],
            cut(1, width_rows, model_width),
            gate_owned,
            down_owned,
        )

    for layer in reversed(range(LAYERS)):
        x, normed, queries, kv_blocks, mixed, middle, n2_parts, gu_parts = kept_state[layer]
        first_full, second_full, gain_full, mlp_gain_full, _, _ = attn_sets[layer]
        if before is not None:
            low_parts = group_rows(upstream_low)
            low_parts[0] = after(low_parts[0], *before["attn_parts"][2:])
            attn_sent = [send_attn(before, pair, low_parts[3]) for pair in range(2)]
            last_across = swap(after(across_sum, low_parts[3]), "seq", 2)
        keep_near, keep_far, send_near, send_far, own_out, across_out, pair_out = feed_back(
            low_parts,
            n2_parts,
            gu_parts,
            *mlp_sets[layer],
            dp_place,
            group_count,
        )
        if before is not None:
            pair_out = after(pair_out, last_across, *attn_sent, before["near_got"], before["inward"])
        got = swap(pair_out, "seq", 1)
        out_terms = [own_out, got[0], swap(add_low(across_out, got[1]), "seq", 2)]
        got_far = swap(send_far, "dp", 1)
        near_got = swap(after(send_near, got_far), "dp", 1)
        if before is not None:
            step_one(before, own_out)
            before["attn_sums"] = sum_attn(before, attn_sent, own_out)
        grad_middle, grad_low, mlp_gain_part, grad_query, own_term, *kv_terms = attention_back(
            upstream,
            middle,
            mlp_gain_full,
            out_terms,
            second_full,
            queries,
            kv_blocks,
            biases_turned,
            cos_wide,
            sin_wide,
        )
        kv_terms = [own_term] + [swap(kv_terms[bit - 1], "seq", bit) for bit in range(1, 4)]
        upstream, upstream_low, grad_kv, attn_gain_part, bias_first, bias_second = before_back(
            kv_terms,
            grad_query,
            x,
            gain_full,
            grad_middle,
            first_full,
            second_full,
            cos_wide,
            sin_wide,
        )
        far_sum = add_low(keep_far, after(got_far, upstream))
        state = {
            "layer": layer,
            "far_sum": far_sum,
            "keep_near": keep_near,
            "near_got": near_got,
            "inward": line_steps(far_sum, [(0, 1), (3, 2)]) if line == 4 else far_sum,
        }
        if before is not None:
            step_two(before, far_sum)
        near_x, far_x, near_other, far_other = projection_grads(
            normed,
            grad_query,
            grad_kv,
            mixed,
            grad_low,
            attn_gain_part,
            mlp_gain_part,
            bias_first,
            bias_second,
            [core, chip_x, dp_place],
            chip_rows,
            line,
        )
        got_far_other = swap(far_other, "seq", 1)
        got_near_other = swap(near_other, "seq", 1)
        state["attn_parts"] = (near_x, far_x, got_near_other, got_far_other)
        states[layer] = before = state
    step_one(before)
    step_two(before)
    arrived = [None, send_attn(before, 1)]
    arrived[0] = send_attn(before, 0)
    before["attn_sums"] = sum_attn(before, arrived)
    grads = finish(states)
    terms.append(last_across)
    activations = sum(term.astype(jnp.float32) for term in terms).astype(jnp.bfloat16)
    return (
        activations.reshape(seq_count, tok_len, model_width),
        upstream.reshape(seq_count, tok_len, model_width),
    ) + grads


def solution(mesh):
    in_specs = (
        P("dp", "seq", None),
        P("dp", "seq", None),
        P("dp", None),
        P(None, ("dp", "seq")),
        P(None, ("dp", "seq"), None),
        P(None, ("dp", "seq")),
        P(None, ("dp", "seq"), None),
        P(None, ("dp", "seq")),
        P(None, ("dp", "seq"), None),
        P(None, ("dp", "seq"), None),
    )
    out_specs = (
        P("dp", "seq", None),
        P("dp", "seq", None),
        P(None, ("dp", "seq")),
        P(None, ("dp", "seq"), None),
        P(None, ("dp", "seq")),
        P(None, ("dp", "seq")),
        P(None, ("dp", "seq"), None),
        P(None, ("dp", "seq")),
        P(None, ("dp", "seq"), None),
        P(None, ("dp", "seq"), None),
    )
    return jax.shard_map(body, mesh=mesh, in_specs=in_specs, out_specs=out_specs, check_vma=False)
```

```python
import jax
import jax.numpy as jnp
from jax import lax
from jax.experimental import pallas as pl
from jax.experimental.pallas import tpu as pltpu
from jax.sharding import PartitionSpec as P

D = 896
HEADS = 14
KV_HEADS = 2
HEAD = 64
LAYERS = 2


EPS = 1e-06
THETA = 1000000.0
NEGATIVE = -1e30


def rotary_tables(positions):
    half_head = HEAD // 2
    frequency = THETA ** (-2.0 * jnp.arange(half_head, dtype=jnp.float32) / HEAD)
    angles = positions.astype(jnp.float32)[..., None] * frequency
    return (jnp.cos(angles), jnp.sin(angles))


NT = (((1,), (1,)), ((), ()))
TN = (((0,), (0,)), ((), ()))
FULL = pl.BlockSpec(memory_space=pltpu.VMEM)
SCALE = HEAD ** (-0.5)
GROUP = HEADS // KV_HEADS
KV_WIDTH = KV_HEADS * HEAD
SPLIT = D + KV_WIDTH
TILE = 384


def dot(left, right, dims=(((1,), (0,)), ((), ()))):
    return lax.dot_general(left, right, dims, preferred_element_type=jnp.float32)


def call(kernel, outs, micros, scratch=(), limit=40, **grid):
    return pl.pallas_call(
        kernel,
        out_shape=[jax.ShapeDtypeStruct(shape, kind) for shape, kind in outs],
        scratch_shapes=list(scratch),
        compiler_params=pltpu.CompilerParams(vmem_limit_bytes=limit * 2**20),
        name=kernel.__qualname__.split(".")[0],
        cost_estimate=pl.CostEstimate(
            flops=0, bytes_accessed=int(micros * 4e3), transcendentals=0
        ),
        **grid,
    )


def turn(block, cos_wide, sin_wide):
    lane = lax.broadcasted_iota(jnp.int32, block.shape, 1)
    width = block.shape[1]
    partner = jnp.where(
        lane % HEAD < HEAD // 2,
        pltpu.roll(block, width - HEAD // 2, 1),
        pltpu.roll(block, HEAD // 2, 1),
    )
    return block * cos_wide + partner * sin_wide


def inverse_root(rows):
    return lax.rsqrt(jnp.mean(rows * rows, axis=-1, keepdims=True) + EPS)


def before_attention(terms, gain, first_full, second_full, bias_first, bias_second, cos_wide, sin_wide):
    count = len(terms)
    rows = terms[0].shape[0]
    span = rows // 2

    def kernel(*refs):
        parts = refs[:count]
        gain_ref, first_ref, second_ref, bias_one, bias_two, cos_ref, sin_ref = refs[count : count + 7]
        x_ref, n_ref, q_ref, kv_ref = refs[count + 7 :]
        x = parts[0][...].astype(jnp.float32)
        for part in parts[1:]:
            x = x + part[...].astype(jnp.float32)
        x_ref[...] = x
        normed = (x * inverse_root(x) * gain_ref[...]).astype(jnp.bfloat16)
        n_ref[...] = normed
        cos_w, sin_w = cos_ref[...], sin_ref[...]
        for tile in range(SPLIT // 128):
            lanes = slice(tile * 128, tile * 128 + 128)
            block = dot(normed, first_ref[:, lanes]) + bias_one[:, lanes]
            turned = turn(block, cos_w, sin_w)
            if tile * 128 < D:
                for part in range(2):
                    head = 2 * tile + part
                    piece = turned[:, part * HEAD : part * HEAD + HEAD].astype(jnp.bfloat16)
                    place = (head % GROUP) * span
                    for half in range(2):
                        q_ref[head // GROUP, half, place : place + span, :] = piece[
                            half * span : half * span + span
                        ]
            else:
                kv_ref[:, :KV_WIDTH] = turned.astype(jnp.bfloat16)
        kv_ref[:, KV_WIDTH:] = (
            dot(normed, second_ref[:, :KV_WIDTH]) + bias_two[...]
        ).astype(jnp.bfloat16)

    return call(
        kernel,
        [
            ((rows, D), jnp.float32),
            ((rows, D), jnp.bfloat16),
            ((KV_HEADS, 2, GROUP * span, HEAD), jnp.bfloat16),
            ((rows, 2 * KV_WIDTH), jnp.bfloat16),
        ],
        4.0,
    )(*terms, gain, first_full, second_full, bias_first, bias_second, cos_wide, sin_wide)


def key_part(kv_refs, half, lanes):
    span = kv_refs[0].shape[0] // 2
    return jnp.concatenate(
        [ref[half * span : half * span + span, lanes] for ref in kv_refs], axis=0
    )


def attention(queries, kv_blocks, biases, x, second_full, gain):
    rows = x.shape[0]
    span = rows // 2

    def kernel(q_ref, kv0, kv1, kv2, kv3, bias_ref, x_ref, w_ref, gain_ref, mixed_ref, mid_ref, n_ref):
        kvs = (kv0, kv1, kv2, kv3)
        for group in range(KV_HEADS):
            key_lanes = slice(group * HEAD, group * HEAD + HEAD)
            value_lanes = slice(KV_WIDTH + group * HEAD, KV_WIDTH + group * HEAD + HEAD)
            keys = [key_part(kvs, half, key_lanes) for half in range(2)]
            values = []
            for half in range(2):
                block = key_part(kvs, half, value_lanes)
                values.append(jnp.concatenate([block, jnp.ones_like(block)], axis=1))
            for half in range(2):
                bias = bias_ref[half]
                for member in range(GROUP):
                    query = q_ref[group, half, member * span : member * span + span, :] * jnp.bfloat16(SCALE)
                    near = dot(query, keys[half], NT) + bias
                    top = jnp.max(near, axis=-1, keepdims=True)
                    if half == 1:
                        far = dot(query, keys[0], NT)
                        top = jnp.maximum(top, jnp.max(far, axis=-1, keepdims=True))
                    total = dot(jnp.exp(near - top).astype(jnp.bfloat16), values[half])
                    if half == 1:
                        total = total + dot(jnp.exp(far - top).astype(jnp.bfloat16), values[0])
                    out = total[:, :HEAD] / total[:, HEAD : 2 * HEAD]
                    head = group * GROUP + member
                    mixed_ref[half * span : half * span + span, head * HEAD : head * HEAD + HEAD] = (
                        out.astype(jnp.bfloat16)
                    )
        middle = x_ref[...] + dot(mixed_ref[...], w_ref[:, KV_WIDTH:])
        mid_ref[...] = middle
        n_ref[...] = (middle * inverse_root(middle) * gain_ref[...]).astype(jnp.bfloat16)

    return call(
        kernel,
        [((rows, D), jnp.bfloat16), ((rows, D), jnp.float32), ((rows, D), jnp.bfloat16)],
        10.5,
    )(queries, *kv_blocks, biases, x, second_full, gain)


def feed_forward(parts, gate_up_full, down_full):
    count = len(parts)
    part_rows = parts[0].shape[0]
    rows = count * part_rows
    units = down_full.shape[0]
    steps = pl.cdiv(units, TILE)
    last = units - (steps - 1) * TILE

    def kernel(*refs):
        part_refs = refs[:count]
        w_ref, d_ref, gu_ref = refs[count : count + 3]
        out_refs, total = refs[count + 3 : -1], refs[-1]
        step = pl.program_id(0)
        n2 = jnp.concatenate([ref[...] for ref in part_refs], axis=0)

        @pl.when(step == 0)
        def _():
            total[...] = jnp.zeros_like(total)

        @pl.when(step < steps - 1)
        def _():
            both = dot(n2, w_ref[...])
            gu_ref[...] = both.astype(jnp.bfloat16)
            gate, up = both[:, :TILE], both[:, TILE:]
            hidden = (gate * jax.nn.sigmoid(gate) * up).astype(jnp.bfloat16)
            total[...] += dot(hidden, d_ref[...])

        @pl.when(step == steps - 1)
        def _():
            both = dot(n2, w_ref[:, : 2 * last])
            gu_ref[:, : 2 * last] = both.astype(jnp.bfloat16)
            gate, up = both[:, :last], both[:, last:]
            hidden = (gate * jax.nn.sigmoid(gate) * up).astype(jnp.bfloat16)
            summed = (total[...] + dot(hidden, d_ref[:last, :])).astype(jnp.bfloat16)
            for place in range(count):
                out_refs[place][...] = summed[place * part_rows : place * part_rows + part_rows]

    whole = lambda step: (0, 0)
    return call(
        kernel,
        [((rows, 2 * units), jnp.bfloat16)] + [((part_rows, D), jnp.bfloat16)] * count,
        9.0,
        [pltpu.VMEM((rows, D), jnp.float32)],
        limit=60,
        grid=(steps,),
        in_specs=[pl.BlockSpec((part_rows, D), whole)] * count
        + [
            pl.BlockSpec((D, 2 * TILE), lambda step: (0, step)),
            pl.BlockSpec((TILE, D), lambda step: (step, 0)),
        ],
        out_specs=[
            pl.BlockSpec((rows, 2 * TILE), lambda step: (0, step)),
        ]
        + [pl.BlockSpec((part_rows, D), whole)] * count,
    )(*parts, gate_up_full, down_full)


def far_slot(mine, place, line):
    if line == 4:
        return jnp.where(mine < 2, place - 2, 1 - place)
    return (mine ^ place) - line // 2


def feed_back(gz_parts, n2_parts, gu_parts, gate_up_full, down_full, dp_place, group_count):
    line = group_count // 2
    half = line // 2
    chunk = D // group_count
    count = len(gz_parts)
    gu_count = len(gu_parts)
    part_rows = gz_parts[0].shape[0]
    rows = count * part_rows
    units = down_full.shape[0]
    unit_rows = units // group_count
    packed = chunk + unit_rows * D // (2 * units)
    once = pl.Buffered(1)
    steps = pl.cdiv(units, TILE)
    last = units - (steps - 1) * TILE

    def kernel(*refs):
        place_ref, *refs = refs
        gz_refs = refs[:count]
        n2_refs = refs[count : 2 * count]
        gu_refs = refs[2 * count : 2 * count + gu_count]
        w_ref, d_ref = refs[2 * count + gu_count : 2 * count + gu_count + 2]
        keep_near, keep_far, send_near, send_far, own_ref, across_ref, pair_ref = refs[
            2 * count + gu_count + 2 : 2 * count + gu_count + 9
        ]
        total, gz, n2t, down = refs[-4:]
        side, mine = place_ref[0] % 2, place_ref[0] // 2
        step = pl.program_id(0)

        @pl.when(step == 0)
        def _():
            total[...] = jnp.zeros_like(total)
            for place in range(count):
                here = slice(place * part_rows, place * part_rows + part_rows)
                gz[here, :] = gz_refs[place][...]
                n2t[:, here] = n2_refs[place][...].T

        def write(spot, even, odd, rows, lanes):
            keep = jnp.where(side == 0, even, odd)
            send = jnp.where(side == 0, odd, even)
            slot = mine ^ spot
            beyond = far_slot(mine, spot, line)

            @pl.when(slot < half)
            def _():
                keep_near[slot, rows, lanes] = keep
                send_near[slot, rows, lanes] = send

            @pl.when(slot >= half)
            def _():
                keep_far[beyond, rows, lanes] = keep
                send_far[beyond, rows, lanes] = send

        def work(width):
            gu = jnp.concatenate([ref[:, : 2 * width] for ref in gu_refs], axis=0).astype(jnp.float32)
            gate, up = gu[:, :width], gu[:, width:]
            sig = jax.nn.sigmoid(gate)
            act = gate * sig
            hidden = (act * up).astype(jnp.bfloat16)
            down[pl.ds(pl.multiple_of(step * TILE, 128), width), :] = dot(hidden, gz[...], TN)
            grad = dot(gz[...], d_ref[:width, :], NT)
            d_gate = grad * up * (sig + act * (1.0 - sig))
            d_up = grad * act
            both = jnp.concatenate([d_gate, d_up], axis=1).astype(jnp.bfloat16)
            part = dot(n2t[...], both)
            for spot in range(line):
                even = part[2 * spot * chunk : (2 * spot + 1) * chunk].astype(jnp.bfloat16)
                odd = part[(2 * spot + 1) * chunk : (2 * spot + 2) * chunk].astype(jnp.bfloat16)
                write(spot, even, odd, slice(0, chunk), pl.ds(pl.multiple_of(step * 2 * TILE, 128), 2 * width))

            return dot(both, w_ref[:, : 2 * width], NT)

        @pl.when(step < steps - 1)
        def _():
            total[...] += work(TILE)

        @pl.when(step == steps - 1)
        def _():
            summed = (total[...] + work(last)).astype(jnp.bfloat16)
            for spot in range(line):
                even, odd = (
                    fold(down[place * unit_rows : place * unit_rows + unit_rows, :], 2 * units).astype(
                        jnp.bfloat16
                    )
                    for place in (2 * spot, 2 * spot + 1)
                )
                write(spot, even, odd, slice(chunk, packed), slice(0, 2 * units))
            own_ref[...] = summed[:part_rows]
            pair_ref[0] = summed[part_rows : 2 * part_rows]
            across_ref[...] = summed[2 * part_rows : 3 * part_rows]
            pair_ref[1] = summed[3 * part_rows :]

    whole = lambda step: (0, 0)
    return call(
        kernel,
        [
            ((half, packed, 2 * units), jnp.bfloat16),
            ((half, packed, 2 * units), jnp.bfloat16),
            ((half, packed, 2 * units), jnp.bfloat16),
            ((half, packed, 2 * units), jnp.bfloat16),
            ((part_rows, D), jnp.bfloat16),
            ((part_rows, D), jnp.bfloat16),
            ((2, part_rows, D), jnp.bfloat16),
        ],
        25.0,
        [
            pltpu.VMEM((rows, D), jnp.float32),
            pltpu.VMEM((rows, D), jnp.bfloat16),
            pltpu.VMEM((D, rows), jnp.bfloat16),
            pltpu.VMEM((units, D), jnp.float32),
        ],
        limit=60,
        grid=(steps,),
        in_specs=[pl.BlockSpec(memory_space=pltpu.SMEM)]
        + [pl.BlockSpec((part_rows, D), whole, pipeline_mode=once)] * (2 * count)
        + [pl.BlockSpec((rows // gu_count, 2 * TILE), lambda step: (0, step))] * gu_count
        + [
            pl.BlockSpec((D, 2 * TILE), lambda step: (0, step)),
            pl.BlockSpec((TILE, D), lambda step: (step, 0)),
        ],
        out_specs=[
            pl.BlockSpec((half, packed, 2 * units), lambda step: (0, 0, 0), pipeline_mode=once),
            pl.BlockSpec((half, packed, 2 * units), lambda step: (0, 0, 0), pipeline_mode=once),
            pl.BlockSpec((half, packed, 2 * units), lambda step: (0, 0, 0), pipeline_mode=once),
            pl.BlockSpec((half, packed, 2 * units), lambda step: (0, 0, 0), pipeline_mode=once),
            pl.BlockSpec((part_rows, D), whole, pipeline_mode=once),
            pl.BlockSpec((part_rows, D), whole, pipeline_mode=once),
            pl.BlockSpec((2, part_rows, D), lambda step: (0, 0, 0), pipeline_mode=once),
        ],
    )(dp_place.reshape(1).astype(jnp.int32), *gz_parts, *n2_parts, *gu_parts, gate_up_full, down_full)


def norm_back(rows, gain, grad):
    inv_root = inverse_root(rows)
    normal = rows * inv_root
    gain_part = jnp.sum(grad * normal, axis=0, keepdims=True)
    weighted = grad * gain
    inner = jnp.mean(weighted * normal, axis=-1, keepdims=True)
    return gain_part, inv_root * (weighted - normal * inner)


def attention_back(upstream, middle, gain, terms, second_full, queries, kv_blocks, biases, cos_wide, sin_wide):
    count = len(terms)
    rows = middle.shape[0]
    span = rows // 2
    wide = GROUP * span

    def kernel(*refs):
        up_ref, mid_ref, gain_ref = refs[:3]
        term_refs = refs[3 : 3 + count]
        w_ref, q_ref, kv0, kv1, kv2, kv3, bias_ref, cos_ref, sin_ref = refs[3 + count : 12 + count]
        gm_ref, gy_ref, dgain_ref, gq_ref, own_ref, d1, d2, d3, go_ref, dkv = refs[12 + count :]
        kvs = (kv0, kv1, kv2, kv3)
        grad = term_refs[0][...].astype(jnp.float32)
        for term in term_refs[1:]:
            grad = grad + term[...].astype(jnp.float32)
        gain_part, back = norm_back(mid_ref[...], gain_ref[...], grad)
        dgain_ref[...] = gain_part
        grad_middle = up_ref[...].astype(jnp.float32) + back
        gm_ref[...] = grad_middle
        grad_low = grad_middle.astype(jnp.bfloat16)
        gy_ref[...] = grad_low
        for tile in range(D // 128):
            start = KV_WIDTH
            block = dot(grad_low, w_ref[tile * 128 : tile * 128 + 128, start:], NT).astype(jnp.bfloat16)
            for part in range(2):
                head = 2 * tile + part
                place = (head % GROUP) * span
                for half in range(2):
                    go_ref[head // GROUP, half, place : place + span, :] = block[
                        half * span : half * span + span, part * HEAD : part * HEAD + HEAD
                    ]
        for group in range(KV_HEADS):
            key_lanes = slice(group * HEAD, group * HEAD + HEAD)
            value_lanes = slice(KV_WIDTH + group * HEAD, KV_WIDTH + group * HEAD + HEAD)
            keys = [key_part(kvs, half, key_lanes) for half in range(2)]
            values = [key_part(kvs, half, value_lanes) for half in range(2)]
            for half in range(2):
                query = q_ref[group, half] * jnp.bfloat16(SCALE)
                grad_out = go_ref[group, half]
                bias = jnp.concatenate([bias_ref[half]] * GROUP, axis=1)
                use = [half] if half == 0 else [1, 0]
                scores = []
                top = None
                for which in use:
                    score = dot(keys[which], query, NT)
                    if which == half:
                        score = score + bias
                    scores.append(score)
                    best = jnp.max(score, axis=0, keepdims=True)
                    top = best if top is None else jnp.maximum(top, best)
                weights = [jnp.exp(score - top) for score in scores]
                total = sum(jnp.sum(weight, axis=0, keepdims=True) for weight in weights)
                scale = 1.0 / total
                probs = [weight * scale for weight in weights]
                grads = [dot(values[which], grad_out, NT) for which in use]
                inner = sum(
                    jnp.sum(prob * grad_prob, axis=0, keepdims=True)
                    for prob, grad_prob in zip(probs, grads)
                )
                grad_query = None
                for which, prob, grad_prob in zip(use, probs, grads):
                    grad_score = (prob * (grad_prob - inner)).astype(jnp.bfloat16)
                    value_grad = dot(prob.astype(jnp.bfloat16), grad_out)
                    key_grad = dot(grad_score, query)
                    if half == 0:
                        dkv[group, which] = key_grad
                        dkv[KV_HEADS + group, which] = value_grad
                    elif which == 0:
                        dkv[group, which] += key_grad
                        dkv[KV_HEADS + group, which] += value_grad
                    else:
                        dkv[group, which] = key_grad
                        dkv[KV_HEADS + group, which] = value_grad
                    term = dot(keys[which].T, grad_score)
                    grad_query = term if grad_query is None else grad_query + term
                grad_query = grad_query * SCALE
                cos_w = cos_ref[half * span : half * span + span, :]
                sin_w = sin_ref[half * span : half * span + span, :]
                for member in range(GROUP):
                    head = group * GROUP + member
                    piece = grad_query[:, member * span : member * span + span].T
                    pair = jnp.concatenate([piece, piece], axis=1)
                    turned = turn(pair, cos_w, -sin_w)[:, :HEAD]
                    gq_ref[half * span : half * span + span, head * HEAD : head * HEAD + HEAD] = (
                        turned.astype(jnp.bfloat16)
                    )
        for place, out in enumerate((own_ref, d1, d2, d3)):
            for half in range(2):
                block = jnp.concatenate(
                    [dkv[lane, half, place * span : place * span + span, :] for lane in range(2 * KV_HEADS)],
                    axis=1,
                )
                out[half * span : half * span + span, :] = block.astype(out.dtype)

    return call(
        kernel,
        [
            ((rows, D), jnp.float32),
            ((rows, D), jnp.bfloat16),
            ((1, D), jnp.float32),
            ((rows, D), jnp.bfloat16),
            ((rows, 2 * KV_WIDTH), jnp.float32),
        ]
        + [((rows, 2 * KV_WIDTH), jnp.bfloat16)] * 3,
        13.0,
        [
            pltpu.VMEM((KV_HEADS, 2, wide, HEAD), jnp.bfloat16),
            pltpu.VMEM((2 * KV_HEADS, 2, 4 * span, HEAD), jnp.float32),
        ],
    )(upstream, middle, gain, *terms, second_full, queries, *kv_blocks, biases, cos_wide, sin_wide)


def before_back(kv_terms, gq, x, gain, grad_middle, first_full, second_full, cos_wide, sin_wide):
    rows = x.shape[0]
    count = len(kv_terms)

    def kernel(*refs):
        kv_refs = refs[:count]
        gq_ref, x_ref, gain_ref, gm_ref, w1_ref, w2_ref, cos_ref, sin_ref = refs[count : count + 8]
        up_ref, low_ref, gkv_ref, dgain_ref, bias_one, bias_two = refs[count + 8 :]
        grad = kv_refs[0][...].astype(jnp.float32)
        for ref in kv_refs[1:]:
            grad = grad + ref[...].astype(jnp.float32)
        grad_key = turn(grad[:, :KV_WIDTH], cos_ref[...], -sin_ref[...]).astype(jnp.bfloat16)
        grad_value = grad[:, KV_WIDTH:].astype(jnp.bfloat16)
        gkv_ref[:, :KV_WIDTH] = grad_key
        gkv_ref[:, KV_WIDTH:] = grad_value
        grad_query = gq_ref[...]
        bias_one[:, :D] = jnp.sum(grad_query.astype(jnp.float32), axis=0, keepdims=True)
        bias_one[:, D:] = jnp.sum(grad_key.astype(jnp.float32), axis=0, keepdims=True)
        bias_two[...] = jnp.sum(grad_value.astype(jnp.float32), axis=0, keepdims=True)
        grad_normed = (
            dot(grad_query, w1_ref[:, :D], NT)
            + dot(grad_key, w1_ref[:, D:], NT)
            + dot(grad_value, w2_ref[:, :KV_WIDTH], NT)
        )
        gain_part, back = norm_back(x_ref[...], gain_ref[...], grad_normed)
        dgain_ref[...] = gain_part
        upstream = gm_ref[...] + back
        up_ref[...] = upstream
        low_ref[...] = upstream.astype(jnp.bfloat16)

    return call(
        kernel,
        [
            ((rows, D), jnp.float32),
            ((rows, D), jnp.bfloat16),
            ((rows, 2 * KV_WIDTH), jnp.bfloat16),
            ((1, D), jnp.float32),
            ((1, SPLIT), jnp.float32),
            ((1, KV_WIDTH), jnp.float32),
        ],
        2.4,
    )(*kv_terms, gq, x, gain, grad_middle, first_full, second_full, cos_wide, sin_wide)


def unit_pieces(unit_rows, group_count, seq_devices):
    units = unit_rows * group_count
    steps = pl.cdiv(units, TILE)
    pieces = []
    for owner in range(seq_devices):
        for kind in range(2):
            for group in range(group_count):
                unit = group * unit_rows
                stop = unit + unit_rows
                column = kind * units * seq_devices + (group * seq_devices + owner) * unit_rows
                while unit < stop:
                    step = unit // TILE
                    end = min(stop, (step + 1) * TILE)
                    width = TILE if step < steps - 1 else units - (steps - 1) * TILE
                    inside = 2 * step * TILE + kind * width + unit - step * TILE
                    pieces.append((owner, inside, column, end - unit))
                    column += end - unit
                    unit = end
    return pieces


def spread_columns(weight, place, unit_rows, group_count, seq_devices):
    layers, rows, columns = weight.shape
    quarter = columns // seq_devices
    pieces = unit_pieces(unit_rows, group_count, seq_devices)

    def kernel(place_ref, w_ref, *refs):
        outs, wide, narrow = refs[:seq_devices], refs[-2], refs[-1]
        for layer in range(layers):
            wide[...] = w_ref[layer].astype(jnp.float32)
            for owner in range(seq_devices):
                for who, inside, column, width in pieces:
                    if who == owner:
                        narrow[:, inside : inside + width] = wide[:, column : column + width]
                block = narrow[...].astype(jnp.bfloat16)
                for bit in range(seq_devices):

                    @pl.when(place_ref[0] == owner ^ bit)
                    def _():
                        outs[bit][layer] = block

    return call(
        kernel,
        [((layers, rows, quarter), jnp.bfloat16)] * seq_devices,
        2.5,
        [pltpu.VMEM((rows, columns), jnp.float32), pltpu.VMEM((rows, quarter), jnp.float32)],
        in_specs=[pl.BlockSpec(memory_space=pltpu.SMEM), FULL],
        out_specs=[FULL] * seq_devices,
    )(place.reshape(1).astype(jnp.int32), weight)


def collect_columns(blocks, place, unit_rows, group_count):
    count = len(blocks)
    layers, rows, quarter = blocks[0].shape
    pieces = unit_pieces(unit_rows, group_count, count)

    def kernel(place_ref, *refs):
        out_ref, narrow = refs[count:]
        me = place_ref[0]
        for layer in range(layers):
            for owner in range(count):
                for bit in range(count):

                    @pl.when(me == owner ^ bit)
                    def _():
                        narrow[...] = refs[bit][layer].astype(jnp.float32)

                for who, inside, column, width in pieces:
                    if who == owner:
                        out_ref[layer, :, column : column + width] = narrow[:, inside : inside + width]

    return call(
        kernel,
        [((layers, rows, count * quarter), jnp.float32)],
        1.5,
        [pltpu.VMEM((rows, quarter), jnp.float32)],
        in_specs=[pl.BlockSpec(memory_space=pltpu.SMEM)] + [FULL] * count,
        out_specs=[FULL],
    )(place.reshape(1).astype(jnp.int32), *blocks)[0]


def fold(rows, columns):
    high = rows.shape[0] * 128 // columns
    wide = rows.shape[1] // 128
    return jnp.concatenate(
        [
            jnp.concatenate(
                [rows[high * r : high * r + high, 128 * c : 128 * c + 128] for r in range(columns // 128)],
                axis=1,
            )
            for c in range(wide)
        ],
        axis=0,
    )


def unfold(rows, width):
    high = rows.shape[0] * 128 // width
    wide = rows.shape[1] // 128
    return jnp.concatenate(
        [
            jnp.concatenate(
                [rows[high * c : high * c + high, 128 * r : 128 * r + 128] for c in range(width // 128)],
                axis=1,
            )
            for r in range(wide)
        ],
        axis=0,
    )


def pack_rows(blocks, down, place):
    owners = len(blocks)
    layers, rows, columns = blocks[0].shape
    total = owners * rows + down.shape[1] * down.shape[2] // columns

    def kernel(place_ref, down_ref, *refs):
        ins, outs = refs[:owners], refs[owners:]
        for layer in range(layers):
            parts = []
            for owner in range(owners):
                part = ins[0][layer].astype(jnp.float32)
                for bit in range(1, owners):
                    part = jnp.where(
                        place_ref[0] == owner ^ bit, ins[bit][layer].astype(jnp.float32), part
                    )
                parts.append(part)
            parts.append(fold(down_ref[layer].astype(jnp.float32), columns))
            outs[layer][0] = jnp.concatenate(parts, axis=0).astype(jnp.bfloat16)

    return call(
        kernel,
        [((1, total, columns), jnp.bfloat16)] * layers,
        3.0,
        in_specs=[pl.BlockSpec(memory_space=pltpu.SMEM)] + [FULL] * (owners + 1),
        out_specs=[FULL] * layers,
    )(place.reshape(1).astype(jnp.int32), down, *blocks)


def unpack(parts, places, chunk):
    count, total, columns = parts[0].shape
    number = count * len(parts)
    unit_rows = (total - chunk) * columns // D

    def kernel(place_ref, *refs):
        ins, gate_ref, down_ref = refs[: len(parts)], refs[-2], refs[-1]
        for which in range(len(parts)):
            for k in range(count):
                spot = place_ref[which * count + k]
                gate_ref[spot] = ins[which][k, :chunk, :]
                down_ref[spot] = unfold(ins[which][k, chunk:, :].astype(jnp.float32), D).astype(
                    jnp.bfloat16
                )

    gate, down = call(
        kernel,
        [((number, chunk, columns), jnp.bfloat16), ((number, unit_rows, D), jnp.bfloat16)],
        5.0,
        in_specs=[pl.BlockSpec(memory_space=pltpu.SMEM)] + [FULL] * len(parts),
        out_specs=[FULL] * 2,
    )(jnp.stack(places).astype(jnp.int32), *parts)
    return gate.reshape(number * chunk, columns), down.reshape(number * unit_rows, D)


def split_rows(terms, chunk, place, count):
    layers = len(terms)
    total_rows, columns = terms[0][0].shape
    rows = chunk // count
    unit_rows = (total_rows - chunk) * columns // D

    def kernel(place_ref, *refs):
        ins, outs, down_ref = refs[: 2 * layers], refs[2 * layers : -1], refs[-1]
        for layer in range(layers):
            total = ins[2 * layer][...].astype(jnp.float32) + ins[2 * layer + 1][...].astype(
                jnp.float32
            )
            down_ref[layer] = unfold(total[chunk:], D)
            for owner in range(count):
                block = total[owner * rows : owner * rows + rows].astype(jnp.bfloat16)
                for bit in range(count):

                    @pl.when(place_ref[0] == owner ^ bit)
                    def _():
                        outs[bit][layer] = block

    *blocks, down = call(
        kernel,
        [((layers, rows, columns), jnp.bfloat16)] * count
        + [((layers, unit_rows, D), jnp.float32)],
        3.0,
        in_specs=[pl.BlockSpec(memory_space=pltpu.SMEM)] + [FULL] * (2 * layers),
        out_specs=[FULL] * (count + 1),
    )(place.reshape(1).astype(jnp.int32), *[term for pair in terms for term in pair])
    return blocks, down


def assemble(parts, places, chip_rows):
    line, rows, width = parts[0].shape

    def kernel(place_ref, *refs):
        ins = refs[:8]
        first_ref, second_ref, small_ref = refs[8:]
        here, chip, side = place_ref[0] == 0, place_ref[1] == 0, place_ref[2] % 2 == 0
        mine = place_ref[2] // 2
        small = jnp.zeros((rows - chip_rows, width), jnp.float32)
        for spot in range(line):
            halves = []
            for half in range(2):
                pieces = []
                blocks = [ins[4 * half + k][spot].astype(jnp.float32) for k in range(4)]
                for block in blocks:
                    small = small + block[chip_rows:]
                lower = [jnp.where(side, blocks[2 * x], blocks[2 * x + 1]) for x in range(2)]
                upper = [jnp.where(side, blocks[2 * x + 1], blocks[2 * x]) for x in range(2)]
                for pair in (lower, upper):
                    pieces.append(jnp.where(chip, pair[0], pair[1])[:chip_rows])
                    pieces.append(jnp.where(chip, pair[1], pair[0])[:chip_rows])
                halves.append(jnp.concatenate(pieces, axis=0).astype(jnp.bfloat16))
            first_ref[mine ^ spot] = jnp.where(here, halves[0], halves[1])
            second_ref[mine ^ spot] = jnp.where(here, halves[1], halves[0])
        small_ref[...] = small

    first, second, small = call(
        kernel,
        [
            ((line, 4 * chip_rows, width), jnp.bfloat16),
            ((line, 4 * chip_rows, width), jnp.bfloat16),
            ((rows - chip_rows, width), jnp.float32),
        ],
        4.0,
        in_specs=[pl.BlockSpec(memory_space=pltpu.SMEM)] + [FULL] * 8,
        out_specs=[FULL] * 3,
    )(jnp.stack(places).astype(jnp.int32), *parts)
    return first.reshape(-1, width), second.reshape(-1, width), small


def projection_grads(normed, grad_query, grad_kv, mixed, grad_low, gain_one, gain_two, bias_one, bias_two, places, chip_rows, line):
    width = SPLIT

    def kernel(place_ref, n_ref, gq_ref, gkv_ref, mixed_ref, gy_ref, g1_ref, g2_ref, b1_ref, b2_ref, keep0, keep1, send0, send1, pad):
        here, chip, side = place_ref[0] == 0, place_ref[1] == 0, place_ref[2] % 2
        mine = place_ref[2] // 2
        turned = n_ref[...].T
        pad[...] = jnp.zeros_like(pad)
        pad[0:1, :D] = g1_ref[...]
        pad[1:2, :D] = g2_ref[...]
        pad[2:3, :] = b1_ref[...]
        pad[3:4, :KV_WIDTH] = b2_ref[...]
        small = pad[...]
        first = jnp.concatenate(
            [dot(turned, gq_ref[...]), dot(turned, gkv_ref[:, :KV_WIDTH])], axis=1
        )
        second = jnp.concatenate(
            [dot(turned, gkv_ref[:, KV_WIDTH:]), dot(mixed_ref[...], gy_ref[...], TN)], axis=1
        )

        def chunk(part, number):
            rows = part[number * chip_rows : (number + 1) * chip_rows]
            return jnp.concatenate([rows, small], axis=0).astype(jnp.bfloat16)

        for spot in range(line):
            for pair in range(2):
                slot = side ^ pair
                firsts = [chunk(first, 4 * spot + 2 * pair + x) for x in range(2)]
                seconds = [chunk(second, 4 * spot + 2 * pair + x) for x in range(2)]
                keeps = [jnp.where(here, one, two) for one, two in zip(firsts, seconds)]
                sends = [jnp.where(here, two, one) for one, two in zip(firsts, seconds)]
                keep0[slot, mine ^ spot] = jnp.where(chip, keeps[0], keeps[1])
                keep1[slot, mine ^ spot] = jnp.where(chip, keeps[1], keeps[0])
                send0[slot, mine ^ spot] = jnp.where(chip, sends[0], sends[1])
                send1[slot, mine ^ spot] = jnp.where(chip, sends[1], sends[0])

    return call(
        kernel,
        [((2, line, chip_rows + 8, width), jnp.bfloat16)] * 4,
        6.0,
        [pltpu.VMEM((8, width), jnp.float32)],
        in_specs=[pl.BlockSpec(memory_space=pltpu.SMEM)] + [FULL] * 9,
        out_specs=[FULL] * 4,
    )(
        jnp.stack(places).astype(jnp.int32),
        normed,
        grad_query,
        grad_kv,
        mixed,
        grad_low,
        gain_one,
        gain_two,
        bias_one,
        bias_two,
    )


def swap(values, axis, bit):
    size = lax.axis_size(axis)
    return lax.ppermute(values, axis, [(i, i ^ bit) for i in range(size)])


def after(values, *others):
    return lax.optimization_barrier((values,) + tuple(others))[0]


def line_bits():
    bits = [1]
    while 4 * bits[-1] < lax.axis_size("dp"):
        bits.append(2 * bits[-1])
    return bits


def line_gather(values, bits, *waited):
    for bit in bits:
        values = jnp.concatenate([values, after(swap(values, "dp", 2 * bit), *waited)], axis=0)
    return values


def line_steps(values, moves):
    return lax.ppermute(
        values, "dp", [(2 * here + side, 2 * there + side) for here, there in moves for side in range(2)]
    )


def cross_middle(values):
    line = lax.axis_size("dp") // 2
    if line == 4:
        return line_steps(values, [(1, 2), (2, 1)])
    return swap(values, "dp", line)


def line_scatter(values, bits, *waited):
    for bit in bits[:0:-1]:
        values = add_low(values[:bit], after(swap(values[bit:], "dp", 2 * bit), *waited))
    return [values[0], swap(values[1], "dp", 2)]


def add_low(left, right):
    return (left.astype(jnp.float32) + right.astype(jnp.float32)).astype(jnp.bfloat16)


def group_rows(values, *waited):
    beside = swap(values, "seq", 1)
    across = swap(values, "seq", 2)
    return [values, beside, across, swap(after(across, *waited), "seq", 1)]


def placed(values, offset, width):
    return lax.dynamic_update_slice(jnp.zeros((width,), values.dtype), values, (offset,))


def body(
    tokens,
    cotangent,
    span_order,
    attn_gain,
    joined_weight,
    joined_bias,
    out_weight,
    mlp_gain,
    gate_up_weight,
    down_weight,
):
    seq_count, tok_len, model_width = tokens.shape
    span_len = tok_len // 2
    group_count = lax.axis_size("dp")
    seq_devices = lax.axis_size("seq")
    unit_rows = down_weight.shape[1]
    width_rows = gate_up_weight.shape[1]
    units = group_count * unit_rows
    dp_place = lax.axis_index("dp")
    seq_place = lax.axis_index("seq")
    core = seq_place % 2
    chip_x = seq_place // 2
    device = dp_place * seq_devices + seq_place
    chip_rows = 2 * width_rows
    line = group_count // 2
    side = dp_place % 2
    line_place = dp_place // 2

    order = [lax.dynamic_slice(span_order, (0, seq_place ^ bit), (1, 1))[0, 0] for bit in range(4)]
    inside = jnp.arange(span_len, dtype=jnp.int32)
    own_places = jnp.concatenate(
        [order[0] * span_len + inside, (2 * seq_devices - 1 - order[0]) * span_len + inside]
    )
    half_biases = []
    for half in range(2):
        blocks = []
        for bit in range(4):
            ahead = order[bit] < order[0] if half == 0 else order[bit] > order[0]
            allowed = ahead | ((order[bit] == order[0]) & (inside[:, None] >= inside[None, :]))
            blocks.append(jnp.where(allowed, 0.0, NEGATIVE).astype(jnp.float32))
        half_biases.append(jnp.concatenate(blocks, axis=1))
    biases = jnp.stack(half_biases)
    biases_turned = jnp.swapaxes(biases, 1, 2)
    cos_table, sin_table = rotary_tables(own_places)
    cos_wide = jnp.concatenate([cos_table] * 4, axis=1)
    sin_wide = jnp.concatenate([-sin_table, sin_table] * 2, axis=1)

    def attn_shard(layer):
        first = joined_weight[layer][:, :SPLIT]
        second = jnp.concatenate([joined_weight[layer][:, SPLIT:], out_weight[layer]], axis=1)
        got = swap(jnp.where(core == 0, second, first), "seq", 1)
        mine = jnp.where(core == 0, first, second)
        rows = jnp.where(core == 0, jnp.stack([mine, got]), jnp.stack([got, mine])).reshape(
            chip_rows, -1
        )
        bias_all = placed(joined_bias[layer], device * joined_bias.shape[1], SPLIT + KV_WIDTH)
        extra = jnp.zeros((8, SPLIT), jnp.bfloat16)
        extra = extra.at[0].set(placed(attn_gain[layer], device * width_rows, SPLIT))
        extra = extra.at[1].set(placed(mlp_gain[layer], device * width_rows, SPLIT))
        extra = extra.at[2].set(bias_all[:SPLIT])
        extra = extra.at[3, :KV_WIDTH].set(bias_all[SPLIT:])
        return jnp.concatenate([rows, extra], axis=0)

    def attn_finish(own_side, other_side, *waited, ahead=None):
        parts = [own_side, other_side]
        parts = parts + [swap(after(part, *waited), "seq", 2) for part in parts]
        parts = parts + [swap(after(part, other_side), "seq", 1) for part in parts]
        if ahead is not None:
            parts[1] = after(parts[1], ahead)
        first_full, second_full, small = assemble(parts, [core, chip_x, dp_place], chip_rows)
        return (
            first_full,
            second_full,
            small[0:1, :model_width],
            small[1:2, :model_width],
            small[2:3],
            small[3:4, :KV_WIDTH],
        )

    bits = line_bits()
    spread = spread_columns(gate_up_weight, seq_place, unit_rows, group_count, seq_devices)
    shards = [attn_shard(layer)[None] for layer in range(LAYERS)]
    gate_blocks = [spread[0]] + [swap(spread[bit], "seq", bit) for bit in range(1, 4)]
    gate_shards = pack_rows(gate_blocks, down_weight, seq_place)
    attn_line = line_gather(after(shards[0], *spread), bits)
    attn_other = swap(after(attn_line, *gate_shards), "dp", 1)
    def outward(crossed, *waited):
        if line != 4:
            return crossed
        passed = after(line_steps(crossed, [(1, 0), (2, 3)]), *waited)
        return jnp.where((line_place == 1) | (line_place == 2), crossed, passed)

    near = [line_gather(after(gate_shards[0], attn_line), bits[:-1])]
    near_pair = [swap(after(near[0], attn_other), "dp", 1)]
    crossed = [cross_middle(near[0])]
    far = []
    offsets = [dp_place ^ (2 * k) for k in range(line)]
    half = line // 2
    if line == 4:
        beyond = [jnp.where(line_place < 2, 2 + k, 1 - k) * 2 + side for k in range(2)]
    else:
        beyond = offsets[half:]
    places = offsets[:half] + beyond
    places = [offsets[:half], beyond, [spot ^ 1 for spot in offsets[:half]], [spot ^ 1 for spot in beyond]]
    places = [spot for group in places for spot in group]

    def mlp_finish(layer, far_pair):
        parts = [near[layer], far[layer], near_pair[layer], far_pair]
        return unpack(parts, places, seq_devices * width_rows)

    terms = [tokens.reshape(tok_len, model_width)]
    kept_state = []
    mlp_sets = []
    second_line = line_gather(after(shards[1], attn_other), bits[:1])
    attn_sets = [attn_finish(attn_line, attn_other, ahead=second_line)]
    for bit in bits[1:]:
        second_line = line_gather(second_line, [bit])
    for layer in range(LAYERS):
        first_full, second_full, gain_full, mlp_gain_full, bias_first, bias_second = attn_sets[layer]
        x, normed, queries, own_kv = before_attention(
            terms,
            after(gain_full, near[0], crossed[0], second_line) if layer == 0 else after(gain_full, near_pair[1]),
            first_full,
            second_full,
            bias_first,
            bias_second,
            cos_wide,
            sin_wide,
        )
        kv_blocks = [own_kv] + [swap(own_kv, "seq", bit) for bit in range(1, 4)]
        waited = (near_pair[0],) if layer == 0 else ()
        mixed, middle, n2 = attention(
            queries, kv_blocks, biases, x, second_full, after(mlp_gain_full, *waited)
        )
        if layer + 1 == LAYERS:
            far.append(outward(after(crossed[1], kept_state[0][7][0]), own_kv))
            far_pair = swap(far[1], "dp", 1)
            n2_parts = group_rows(n2, far_pair)
        else:
            n2_parts = group_rows(n2)
        if layer == 0:
            second_other = swap(after(second_line, n2), "dp", 1)
            far.append(outward(crossed[0], n2))
            far_pair = swap(far[0], "dp", 1)
            near.append(line_gather(after(gate_shards[1], n2), bits[:-1], n2_parts[3]))
            crossed.append(cross_middle(near[1]))
            attn_sets.append(attn_finish(second_line, second_other, n2_parts[3]))
            near_pair.append(swap(after(near[1], far_pair), "dp", 1))
        mlp_sets.append(mlp_finish(layer, far_pair))
        gu_near, *outs_near = feed_forward(n2_parts[:2], *mlp_sets[layer])
        if layer == 0:
            n2_parts[2] = after(n2_parts[2], crossed[1], gu_near)
        else:
            low_parts = group_rows(
                after(cotangent.reshape(tok_len, model_width), n2_parts[3]), gu_near
            )
        gu_far, *outs_far = feed_forward(n2_parts[2:], *mlp_sets[layer])
        across_sum = add_low(outs_far[0], swap(outs_far[1], "seq", 1))
        terms = [middle, outs_near[0], swap(outs_near[1], "seq", 1)]
        if layer + 1 < LAYERS:
            terms.append(swap(across_sum, "seq", 2))
        kept_state.append((x, normed, queries, kv_blocks, mixed, middle, n2_parts, [gu_near, gu_far]))
    upstream = cotangent.reshape(tok_len, model_width)
    states = [None] * LAYERS
    before = None

    def send_attn(state, pair, *waited):
        near, far, got_near, got_far = state["attn_parts"]
        return swap(after(add_low(far[pair], got_far[pair]), *waited), "seq", 2)

    def sum_attn(state, arrived, *waited):
        near, far, got_near, got_far = state["attn_parts"]
        return [
            (
                near[pair].astype(jnp.float32)
                + got_near[pair].astype(jnp.float32)
                + after(arrived[pair], *waited).astype(jnp.float32)
            ).astype(jnp.bfloat16)
            for pair in range(2)
        ]

    def step_one(state, *waited):
        far_sum = state["far_sum"]
        if line == 4:
            far_sum = add_low(far_sum, after(state["inward"], *waited))
        state["crossed"] = cross_middle(far_sum)
        state["near_sum"] = add_low(state["keep_near"], after(state["near_got"], *waited))

    def step_two(state, *waited):
        state["near_sum"] = add_low(state["near_sum"], after(state["crossed"], *waited))
        state["terms"] = line_scatter(state["near_sum"], bits[:-1])

    def finish(states):
        other_side = jnp.concatenate([state["attn_sums"][1] for state in states], axis=1)
        other_side = swap(after(other_side, states[0]["near_got"]), "dp", 1)
        own_side = jnp.concatenate([state["attn_sums"][0] for state in states], axis=1)
        owned = sum(
            term.astype(jnp.float32)
            for term in line_scatter(
                add_low(own_side, other_side), bits, states[0]["near_sum"]
            )
        ).reshape(LAYERS, chip_rows + 8, -1)
        extra = owned[:, chip_rows:]
        halves = owned[:, :chip_rows].reshape(LAYERS, 2, width_rows, -1)
        mine = lax.dynamic_index_in_dim(halves, core, 1, keepdims=False)
        theirs = swap(
            lax.dynamic_index_in_dim(halves, 1 - core, 1, keepdims=False), "seq", 1
        )
        first_own = jnp.where(core == 0, mine, theirs)
        second_own = jnp.where(core == 0, theirs, mine)

        def cut(row, width, stop):
            start = (0, row, device * width)
            return lax.dynamic_slice(extra[:, :, :stop], start, (LAYERS, 1, width))[:, 0]

        gate_rows, down_owned = split_rows(
            [state["terms"] for state in states], seq_devices * width_rows, seq_place, seq_devices
        )
        gate_owned = collect_columns(
            [gate_rows[0]] + [swap(gate_rows[bit], "seq", bit) for bit in range(1, 4)],
            seq_place,
            unit_rows,
            group_count,
        )
        return (
            cut(0, width_rows, model_width),
            jnp.concatenate([first_own, second_own[:, :, :KV_WIDTH]], axis=2),
            cut(2, SPLIT // (group_count * seq_devices), SPLIT),
            cut(3, KV_WIDTH // (group_count * seq_devices), KV_WIDTH),
            second_own[:, :, KV_WIDTH:],
            cut(1, width_rows, model_width),
            gate_owned,
            down_owned,
        )

    for layer in reversed(range(LAYERS)):
        x, normed, queries, kv_blocks, mixed, middle, n2_parts, gu_parts = kept_state[layer]
        first_full, second_full, gain_full, mlp_gain_full, _, _ = attn_sets[layer]
        if before is not None:
            low_parts = group_rows(upstream_low)
            low_parts[0] = after(low_parts[0], *before["attn_parts"][2:])
            attn_sent = [send_attn(before, pair, low_parts[3]) for pair in range(2)]
            last_across = swap(after(across_sum, low_parts[3]), "seq", 2)
        keep_near, keep_far, send_near, send_far, own_out, across_out, pair_out = feed_back(
            low_parts,
            n2_parts,
            gu_parts,
            *mlp_sets[layer],
            dp_place,
            group_count,
        )
        if before is not None:
            pair_out = after(pair_out, last_across, *attn_sent, before["near_got"], before["inward"])
        got = swap(pair_out, "seq", 1)
        out_terms = [own_out, got[0], swap(add_low(across_out, got[1]), "seq", 2)]
        got_far = swap(send_far, "dp", 1)
        if before is not None:
            step_one(before, own_out)
            before["attn_sums"] = sum_attn(before, attn_sent, own_out)
        grad_middle, grad_low, mlp_gain_part, grad_query, own_term, *kv_terms = attention_back(
            upstream,
            middle,
            mlp_gain_full,
            out_terms,
            second_full,
            queries,
            kv_blocks,
            biases_turned,
            cos_wide,
            sin_wide,
        )
        kv_terms = [own_term] + [swap(kv_terms[bit - 1], "seq", bit) for bit in range(1, 4)]
        upstream, upstream_low, grad_kv, attn_gain_part, bias_first, bias_second = before_back(
            kv_terms,
            grad_query,
            x,
            gain_full,
            grad_middle,
            first_full,
            second_full,
            cos_wide,
            sin_wide,
        )
        near_got = swap(after(send_near, grad_low), "dp", 1)
        far_sum = add_low(keep_far, after(got_far, upstream if before is None else grad_low))
        state = {
            "layer": layer,
            "far_sum": far_sum,
            "keep_near": keep_near,
            "near_got": near_got,
            "inward": line_steps(far_sum, [(0, 1), (3, 2)]) if line == 4 else far_sum,
        }
        if before is not None:
            step_two(before, far_sum)
        near_x, far_x, near_other, far_other = projection_grads(
            normed,
            grad_query,
            grad_kv,
            mixed,
            grad_low,
            attn_gain_part,
            mlp_gain_part,
            bias_first,
            bias_second,
            [core, chip_x, dp_place],
            chip_rows,
            line,
        )
        got_far_other = swap(far_other, "seq", 1)
        got_near_other = swap(near_other, "seq", 1)
        state["attn_parts"] = (near_x, far_x, got_near_other, got_far_other)
        states[layer] = before = state
    step_one(before)
    step_two(before)
    arrived = [None, send_attn(before, 1)]
    arrived[0] = send_attn(before, 0)
    before["attn_sums"] = sum_attn(before, arrived)
    grads = finish(states)
    terms.append(last_across)
    activations = sum(term.astype(jnp.float32) for term in terms).astype(jnp.bfloat16)
    return (
        activations.reshape(seq_count, tok_len, model_width),
        upstream.reshape(seq_count, tok_len, model_width),
    ) + grads


def solution(mesh):
    in_specs = (
        P("dp", "seq", None),
        P("dp", "seq", None),
        P("dp", None),
        P(None, ("dp", "seq")),
        P(None, ("dp", "seq"), None),
        P(None, ("dp", "seq")),
        P(None, ("dp", "seq"), None),
        P(None, ("dp", "seq")),
        P(None, ("dp", "seq"), None),
        P(None, ("dp", "seq"), None),
    )
    out_specs = (
        P("dp", "seq", None),
        P("dp", "seq", None),
        P(None, ("dp", "seq")),
        P(None, ("dp", "seq"), None),
        P(None, ("dp", "seq")),
        P(None, ("dp", "seq")),
        P(None, ("dp", "seq"), None),
        P(None, ("dp", "seq")),
        P(None, ("dp", "seq"), None),
        P(None, ("dp", "seq"), None),
    )
    return jax.shard_map(body, mesh=mesh, in_specs=in_specs, out_specs=out_specs, check_vma=False)
```

```python
import jax
import jax.numpy as jnp
from jax import lax
from jax.experimental import pallas as pl
from jax.experimental.pallas import tpu as pltpu
from jax.sharding import PartitionSpec as P

D = 896
HEADS = 14
KV_HEADS = 2
HEAD = 64
LAYERS = 2


EPS = 1e-06
THETA = 1000000.0
NEGATIVE = -1e30


def rotary_tables(positions):
    half_head = HEAD // 2
    frequency = THETA ** (-2.0 * jnp.arange(half_head, dtype=jnp.float32) / HEAD)
    angles = positions.astype(jnp.float32)[..., None] * frequency
    return (jnp.cos(angles), jnp.sin(angles))


NT = (((1,), (1,)), ((), ()))
TN = (((0,), (0,)), ((), ()))
FULL = pl.BlockSpec(memory_space=pltpu.VMEM)
SCALE = HEAD ** (-0.5)
GROUP = HEADS // KV_HEADS
KV_WIDTH = KV_HEADS * HEAD
SPLIT = D + KV_WIDTH
TILE = 384


def dot(left, right, dims=(((1,), (0,)), ((), ()))):
    return lax.dot_general(left, right, dims, preferred_element_type=jnp.float32)


def call(kernel, outs, micros, scratch=(), limit=40, **grid):
    return pl.pallas_call(
        kernel,
        out_shape=[jax.ShapeDtypeStruct(shape, kind) for shape, kind in outs],
        scratch_shapes=list(scratch),
        compiler_params=pltpu.CompilerParams(vmem_limit_bytes=limit * 2**20),
        name=kernel.__qualname__.split(".")[0],
        cost_estimate=pl.CostEstimate(
            flops=0, bytes_accessed=int(micros * 4e3), transcendentals=0
        ),
        **grid,
    )


def turn(block, cos_wide, sin_wide):
    lane = lax.broadcasted_iota(jnp.int32, block.shape, 1)
    width = block.shape[1]
    partner = jnp.where(
        lane % HEAD < HEAD // 2,
        pltpu.roll(block, width - HEAD // 2, 1),
        pltpu.roll(block, HEAD // 2, 1),
    )
    return block * cos_wide + partner * sin_wide


def inverse_root(rows):
    return lax.rsqrt(jnp.mean(rows * rows, axis=-1, keepdims=True) + EPS)


def before_attention(terms, gain, first_full, second_full, bias_first, bias_second, cos_wide, sin_wide):
    count = len(terms)
    rows = terms[0].shape[0]
    span = rows // 2

    def kernel(*refs):
        parts = refs[:count]
        gain_ref, first_ref, second_ref, bias_one, bias_two, cos_ref, sin_ref = refs[count : count + 7]
        x_ref, n_ref, q_ref, kv_ref = refs[count + 7 :]
        x = parts[0][...].astype(jnp.float32)
        for part in parts[1:]:
            x = x + part[...].astype(jnp.float32)
        x_ref[...] = x
        normed = (x * inverse_root(x) * gain_ref[...]).astype(jnp.bfloat16)
        n_ref[...] = normed
        cos_w, sin_w = cos_ref[...], sin_ref[...]
        for tile in range(SPLIT // 128):
            lanes = slice(tile * 128, tile * 128 + 128)
            block = dot(normed, first_ref[:, lanes]) + bias_one[:, lanes]
            turned = turn(block, cos_w, sin_w)
            if tile * 128 < D:
                for part in range(2):
                    head = 2 * tile + part
                    piece = turned[:, part * HEAD : part * HEAD + HEAD].astype(jnp.bfloat16)
                    place = (head % GROUP) * span
                    for half in range(2):
                        q_ref[head // GROUP, half, place : place + span, :] = piece[
                            half * span : half * span + span
                        ]
            else:
                kv_ref[:, :KV_WIDTH] = turned.astype(jnp.bfloat16)
        kv_ref[:, KV_WIDTH:] = (
            dot(normed, second_ref[:, :KV_WIDTH]) + bias_two[...]
        ).astype(jnp.bfloat16)

    return call(
        kernel,
        [
            ((rows, D), jnp.float32),
            ((rows, D), jnp.bfloat16),
            ((KV_HEADS, 2, GROUP * span, HEAD), jnp.bfloat16),
            ((rows, 2 * KV_WIDTH), jnp.bfloat16),
        ],
        4.0,
    )(*terms, gain, first_full, second_full, bias_first, bias_second, cos_wide, sin_wide)


def key_part(kv_refs, half, lanes):
    span = kv_refs[0].shape[0] // 2
    return jnp.concatenate(
        [ref[half * span : half * span + span, lanes] for ref in kv_refs], axis=0
    )


def attention(queries, kv_blocks, biases, x, second_full, gain):
    rows = x.shape[0]
    span = rows // 2

    def kernel(q_ref, kv0, kv1, kv2, kv3, bias_ref, x_ref, w_ref, gain_ref, mixed_ref, mid_ref, n_ref):
        kvs = (kv0, kv1, kv2, kv3)
        for group in range(KV_HEADS):
            key_lanes = slice(group * HEAD, group * HEAD + HEAD)
            value_lanes = slice(KV_WIDTH + group * HEAD, KV_WIDTH + group * HEAD + HEAD)
            keys = [key_part(kvs, half, key_lanes) for half in range(2)]
            values = []
            for half in range(2):
                block = key_part(kvs, half, value_lanes)
                values.append(jnp.concatenate([block, jnp.ones_like(block)], axis=1))
            for half in range(2):
                bias = bias_ref[half]
                for member in range(GROUP):
                    query = q_ref[group, half, member * span : member * span + span, :] * jnp.bfloat16(SCALE)
                    near = dot(query, keys[half], NT) + bias
                    top = jnp.max(near, axis=-1, keepdims=True)
                    if half == 1:
                        far = dot(query, keys[0], NT)
                        top = jnp.maximum(top, jnp.max(far, axis=-1, keepdims=True))
                    total = dot(jnp.exp(near - top).astype(jnp.bfloat16), values[half])
                    if half == 1:
                        total = total + dot(jnp.exp(far - top).astype(jnp.bfloat16), values[0])
                    out = total[:, :HEAD] / total[:, HEAD : 2 * HEAD]
                    head = group * GROUP + member
                    mixed_ref[half * span : half * span + span, head * HEAD : head * HEAD + HEAD] = (
                        out.astype(jnp.bfloat16)
                    )
        middle = x_ref[...] + dot(mixed_ref[...], w_ref[:, KV_WIDTH:])
        mid_ref[...] = middle
        n_ref[...] = (middle * inverse_root(middle) * gain_ref[...]).astype(jnp.bfloat16)

    return call(
        kernel,
        [((rows, D), jnp.bfloat16), ((rows, D), jnp.float32), ((rows, D), jnp.bfloat16)],
        10.5,
    )(queries, *kv_blocks, biases, x, second_full, gain)


def feed_forward(parts, gate_up_full, down_full):
    count = len(parts)
    part_rows = parts[0].shape[0]
    rows = count * part_rows
    units = down_full.shape[0]
    steps = pl.cdiv(units, TILE)
    last = units - (steps - 1) * TILE

    def kernel(*refs):
        part_refs = refs[:count]
        w_ref, d_ref, gu_ref = refs[count : count + 3]
        out_refs, total = refs[count + 3 : -1], refs[-1]
        step = pl.program_id(0)
        n2 = jnp.concatenate([ref[...] for ref in part_refs], axis=0)

        @pl.when(step == 0)
        def _():
            total[...] = jnp.zeros_like(total)

        @pl.when(step < steps - 1)
        def _():
            both = dot(n2, w_ref[...])
            gu_ref[...] = both.astype(jnp.bfloat16)
            gate, up = both[:, :TILE], both[:, TILE:]
            hidden = (gate * jax.nn.sigmoid(gate) * up).astype(jnp.bfloat16)
            total[...] += dot(hidden, d_ref[...])

        @pl.when(step == steps - 1)
        def _():
            both = dot(n2, w_ref[:, : 2 * last])
            gu_ref[:, : 2 * last] = both.astype(jnp.bfloat16)
            gate, up = both[:, :last], both[:, last:]
            hidden = (gate * jax.nn.sigmoid(gate) * up).astype(jnp.bfloat16)
            summed = (total[...] + dot(hidden, d_ref[:last, :])).astype(jnp.bfloat16)
            for place in range(count):
                out_refs[place][...] = summed[place * part_rows : place * part_rows + part_rows]

    whole = lambda step: (0, 0)
    return call(
        kernel,
        [((rows, 2 * units), jnp.bfloat16)] + [((part_rows, D), jnp.bfloat16)] * count,
        9.0,
        [pltpu.VMEM((rows, D), jnp.float32)],
        limit=60,
        grid=(steps,),
        in_specs=[pl.BlockSpec((part_rows, D), whole)] * count
        + [
            pl.BlockSpec((D, 2 * TILE), lambda step: (0, step)),
            pl.BlockSpec((TILE, D), lambda step: (step, 0)),
        ],
        out_specs=[
            pl.BlockSpec((rows, 2 * TILE), lambda step: (0, step)),
        ]
        + [pl.BlockSpec((part_rows, D), whole)] * count,
    )(*parts, gate_up_full, down_full)


def far_slot(mine, place, line):
    if line == 4:
        return jnp.where(mine < 2, place - 2, 1 - place)
    return (mine ^ place) - line // 2


def feed_back(gz_parts, n2_parts, gu_parts, gate_up_full, down_full, dp_place, group_count, far_arrays):
    line = group_count // 2
    half = line // 2
    each = half // far_arrays
    chunk = D // group_count
    count = len(gz_parts)
    gu_count = len(gu_parts)
    part_rows = gz_parts[0].shape[0]
    rows = count * part_rows
    units = down_full.shape[0]
    unit_rows = units // group_count
    packed = chunk + unit_rows * D // (2 * units)
    once = pl.Buffered(1)
    steps = pl.cdiv(units, TILE)
    last = units - (steps - 1) * TILE

    def kernel(*refs):
        place_ref, *refs = refs
        gz_refs = refs[:count]
        n2_refs = refs[count : 2 * count]
        gu_refs = refs[2 * count : 2 * count + gu_count]
        w_ref, d_ref = refs[2 * count + gu_count : 2 * count + gu_count + 2]
        outs = refs[2 * count + gu_count + 2 : -4]
        keep_near, send_near, own_ref, across_ref, pair_ref = outs[:5]
        keep_far, send_far = outs[5 : 5 + far_arrays], outs[5 + far_arrays :]
        total, gz, n2t, down = refs[-4:]
        side, mine = place_ref[0] % 2, place_ref[0] // 2
        step = pl.program_id(0)

        @pl.when(step == 0)
        def _():
            total[...] = jnp.zeros_like(total)
            for place in range(count):
                here = slice(place * part_rows, place * part_rows + part_rows)
                gz[here, :] = gz_refs[place][...]
                n2t[:, here] = n2_refs[place][...].T

        def write(spot, even, odd, rows, lanes):
            keep = jnp.where(side == 0, even, odd)
            send = jnp.where(side == 0, odd, even)
            slot = mine ^ spot
            beyond = far_slot(mine, spot, line)

            @pl.when(slot < half)
            def _():
                keep_near[slot, rows, lanes] = keep
                send_near[slot, rows, lanes] = send

            for number in range(far_arrays):

                @pl.when((slot >= half) & (beyond // each == number))
                def _():
                    keep_far[number][beyond % each, rows, lanes] = keep
                    send_far[number][beyond % each, rows, lanes] = send

        def work(width):
            gu = jnp.concatenate([ref[:, : 2 * width] for ref in gu_refs], axis=0).astype(jnp.float32)
            gate, up = gu[:, :width], gu[:, width:]
            sig = jax.nn.sigmoid(gate)
            act = gate * sig
            hidden = (act * up).astype(jnp.bfloat16)
            down[pl.ds(pl.multiple_of(step * TILE, 128), width), :] = dot(hidden, gz[...], TN)
            grad = dot(gz[...], d_ref[:width, :], NT)
            d_gate = grad * up * (sig + act * (1.0 - sig))
            d_up = grad * act
            both = jnp.concatenate([d_gate, d_up], axis=1).astype(jnp.bfloat16)
            part = dot(n2t[...], both)
            for spot in range(line):
                even = part[2 * spot * chunk : (2 * spot + 1) * chunk].astype(jnp.bfloat16)
                odd = part[(2 * spot + 1) * chunk : (2 * spot + 2) * chunk].astype(jnp.bfloat16)
                write(spot, even, odd, slice(0, chunk), pl.ds(pl.multiple_of(step * 2 * TILE, 128), 2 * width))

            return dot(both, w_ref[:, : 2 * width], NT)

        @pl.when(step < steps - 1)
        def _():
            total[...] += work(TILE)

        @pl.when(step == steps - 1)
        def _():
            summed = (total[...] + work(last)).astype(jnp.bfloat16)
            for spot in range(line):
                even, odd = (
                    fold(down[place * unit_rows : place * unit_rows + unit_rows, :], 2 * units).astype(
                        jnp.bfloat16
                    )
                    for place in (2 * spot, 2 * spot + 1)
                )
                write(spot, even, odd, slice(chunk, packed), slice(0, 2 * units))
            own_ref[...] = summed[:part_rows]
            pair_ref[0] = summed[part_rows : 2 * part_rows]
            across_ref[...] = summed[2 * part_rows : 3 * part_rows]
            pair_ref[1] = summed[3 * part_rows :]

    whole = lambda step: (0, 0)
    return call(
        kernel,
        [
            ((half, packed, 2 * units), jnp.bfloat16),
            ((half, packed, 2 * units), jnp.bfloat16),
            ((part_rows, D), jnp.bfloat16),
            ((part_rows, D), jnp.bfloat16),
            ((2, part_rows, D), jnp.bfloat16),
        ]
        + [((each, packed, 2 * units), jnp.bfloat16)] * (2 * far_arrays),
        25.0,
        [
            pltpu.VMEM((rows, D), jnp.float32),
            pltpu.VMEM((rows, D), jnp.bfloat16),
            pltpu.VMEM((D, rows), jnp.bfloat16),
            pltpu.VMEM((units, D), jnp.float32),
        ],
        limit=60,
        grid=(steps,),
        in_specs=[pl.BlockSpec(memory_space=pltpu.SMEM)]
        + [pl.BlockSpec((part_rows, D), whole, pipeline_mode=once)] * (2 * count)
        + [pl.BlockSpec((rows // gu_count, 2 * TILE), lambda step: (0, step))] * gu_count
        + [
            pl.BlockSpec((D, 2 * TILE), lambda step: (0, step)),
            pl.BlockSpec((TILE, D), lambda step: (step, 0)),
        ],
        out_specs=[
            pl.BlockSpec((half, packed, 2 * units), lambda step: (0, 0, 0), pipeline_mode=once),
            pl.BlockSpec((half, packed, 2 * units), lambda step: (0, 0, 0), pipeline_mode=once),
            pl.BlockSpec((part_rows, D), whole, pipeline_mode=once),
            pl.BlockSpec((part_rows, D), whole, pipeline_mode=once),
            pl.BlockSpec((2, part_rows, D), lambda step: (0, 0, 0), pipeline_mode=once),
        ]
        + [pl.BlockSpec((each, packed, 2 * units), lambda step: (0, 0, 0), pipeline_mode=once)]
        * (2 * far_arrays),
    )(dp_place.reshape(1).astype(jnp.int32), *gz_parts, *n2_parts, *gu_parts, gate_up_full, down_full)


def norm_back(rows, gain, grad):
    inv_root = inverse_root(rows)
    normal = rows * inv_root
    gain_part = jnp.sum(grad * normal, axis=0, keepdims=True)
    weighted = grad * gain
    inner = jnp.mean(weighted * normal, axis=-1, keepdims=True)
    return gain_part, inv_root * (weighted - normal * inner)


def attention_back(upstream, middle, gain, terms, second_full, queries, kv_blocks, biases, cos_wide, sin_wide):
    count = len(terms)
    rows = middle.shape[0]
    span = rows // 2
    wide = GROUP * span

    def kernel(*refs):
        up_ref, mid_ref, gain_ref = refs[:3]
        term_refs = refs[3 : 3 + count]
        w_ref, q_ref, kv0, kv1, kv2, kv3, bias_ref, cos_ref, sin_ref = refs[3 + count : 12 + count]
        gm_ref, gy_ref, dgain_ref, gq_ref, own_ref, d1, d2, d3, go_ref, dkv = refs[12 + count :]
        kvs = (kv0, kv1, kv2, kv3)
        grad = term_refs[0][...].astype(jnp.float32)
        for term in term_refs[1:]:
            grad = grad + term[...].astype(jnp.float32)
        gain_part, back = norm_back(mid_ref[...], gain_ref[...], grad)
        dgain_ref[...] = gain_part
        grad_middle = up_ref[...].astype(jnp.float32) + back
        gm_ref[...] = grad_middle
        grad_low = grad_middle.astype(jnp.bfloat16)
        gy_ref[...] = grad_low
        for tile in range(D // 128):
            start = KV_WIDTH
            block = dot(grad_low, w_ref[tile * 128 : tile * 128 + 128, start:], NT).astype(jnp.bfloat16)
            for part in range(2):
                head = 2 * tile + part
                place = (head % GROUP) * span
                for half in range(2):
                    go_ref[head // GROUP, half, place : place + span, :] = block[
                        half * span : half * span + span, part * HEAD : part * HEAD + HEAD
                    ]
        for group in range(KV_HEADS):
            key_lanes = slice(group * HEAD, group * HEAD + HEAD)
            value_lanes = slice(KV_WIDTH + group * HEAD, KV_WIDTH + group * HEAD + HEAD)
            keys = [key_part(kvs, half, key_lanes) for half in range(2)]
            values = [key_part(kvs, half, value_lanes) for half in range(2)]
            for half in range(2):
                query = q_ref[group, half] * jnp.bfloat16(SCALE)
                grad_out = go_ref[group, half]
                bias = jnp.concatenate([bias_ref[half]] * GROUP, axis=1)
                use = [half] if half == 0 else [1, 0]
                scores = []
                top = None
                for which in use:
                    score = dot(keys[which], query, NT)
                    if which == half:
                        score = score + bias
                    scores.append(score)
                    best = jnp.max(score, axis=0, keepdims=True)
                    top = best if top is None else jnp.maximum(top, best)
                weights = [jnp.exp(score - top) for score in scores]
                total = sum(jnp.sum(weight, axis=0, keepdims=True) for weight in weights)
                scale = 1.0 / total
                probs = [weight * scale for weight in weights]
                grads = [dot(values[which], grad_out, NT) for which in use]
                inner = sum(
                    jnp.sum(prob * grad_prob, axis=0, keepdims=True)
                    for prob, grad_prob in zip(probs, grads)
                )
                grad_query = None
                for which, prob, grad_prob in zip(use, probs, grads):
                    grad_score = (prob * (grad_prob - inner)).astype(jnp.bfloat16)
                    value_grad = dot(prob.astype(jnp.bfloat16), grad_out)
                    key_grad = dot(grad_score, query)
                    if half == 0:
                        dkv[group, which] = key_grad
                        dkv[KV_HEADS + group, which] = value_grad
                    elif which == 0:
                        dkv[group, which] += key_grad
                        dkv[KV_HEADS + group, which] += value_grad
                    else:
                        dkv[group, which] = key_grad
                        dkv[KV_HEADS + group, which] = value_grad
                    term = dot(keys[which].T, grad_score)
                    grad_query = term if grad_query is None else grad_query + term
                grad_query = grad_query * SCALE
                cos_w = cos_ref[half * span : half * span + span, :]
                sin_w = sin_ref[half * span : half * span + span, :]
                for member in range(GROUP):
                    head = group * GROUP + member
                    piece = grad_query[:, member * span : member * span + span].T
                    pair = jnp.concatenate([piece, piece], axis=1)
                    turned = turn(pair, cos_w, -sin_w)[:, :HEAD]
                    gq_ref[half * span : half * span + span, head * HEAD : head * HEAD + HEAD] = (
                        turned.astype(jnp.bfloat16)
                    )
        for place, out in enumerate((own_ref, d1, d2, d3)):
            for half in range(2):
                block = jnp.concatenate(
                    [dkv[lane, half, place * span : place * span + span, :] for lane in range(2 * KV_HEADS)],
                    axis=1,
                )
                out[half * span : half * span + span, :] = block.astype(out.dtype)

    return call(
        kernel,
        [
            ((rows, D), jnp.float32),
            ((rows, D), jnp.bfloat16),
            ((1, D), jnp.float32),
            ((rows, D), jnp.bfloat16),
            ((rows, 2 * KV_WIDTH), jnp.float32),
        ]
        + [((rows, 2 * KV_WIDTH), jnp.bfloat16)] * 3,
        13.0,
        [
            pltpu.VMEM((KV_HEADS, 2, wide, HEAD), jnp.bfloat16),
            pltpu.VMEM((2 * KV_HEADS, 2, 4 * span, HEAD), jnp.float32),
        ],
    )(upstream, middle, gain, *terms, second_full, queries, *kv_blocks, biases, cos_wide, sin_wide)


def before_back(kv_terms, gq, x, gain, grad_middle, first_full, second_full, cos_wide, sin_wide):
    rows = x.shape[0]
    count = len(kv_terms)

    def kernel(*refs):
        kv_refs = refs[:count]
        gq_ref, x_ref, gain_ref, gm_ref, w1_ref, w2_ref, cos_ref, sin_ref = refs[count : count + 8]
        up_ref, low_ref, gkv_ref, dgain_ref, bias_one, bias_two = refs[count + 8 :]
        grad = kv_refs[0][...].astype(jnp.float32)
        for ref in kv_refs[1:]:
            grad = grad + ref[...].astype(jnp.float32)
        grad_key = turn(grad[:, :KV_WIDTH], cos_ref[...], -sin_ref[...]).astype(jnp.bfloat16)
        grad_value = grad[:, KV_WIDTH:].astype(jnp.bfloat16)
        gkv_ref[:, :KV_WIDTH] = grad_key
        gkv_ref[:, KV_WIDTH:] = grad_value
        grad_query = gq_ref[...]
        bias_one[:, :D] = jnp.sum(grad_query.astype(jnp.float32), axis=0, keepdims=True)
        bias_one[:, D:] = jnp.sum(grad_key.astype(jnp.float32), axis=0, keepdims=True)
        bias_two[...] = jnp.sum(grad_value.astype(jnp.float32), axis=0, keepdims=True)
        grad_normed = (
            dot(grad_query, w1_ref[:, :D], NT)
            + dot(grad_key, w1_ref[:, D:], NT)
            + dot(grad_value, w2_ref[:, :KV_WIDTH], NT)
        )
        gain_part, back = norm_back(x_ref[...], gain_ref[...], grad_normed)
        dgain_ref[...] = gain_part
        upstream = gm_ref[...] + back
        up_ref[...] = upstream
        low_ref[...] = upstream.astype(jnp.bfloat16)

    return call(
        kernel,
        [
            ((rows, D), jnp.float32),
            ((rows, D), jnp.bfloat16),
            ((rows, 2 * KV_WIDTH), jnp.bfloat16),
            ((1, D), jnp.float32),
            ((1, SPLIT), jnp.float32),
            ((1, KV_WIDTH), jnp.float32),
        ],
        2.4,
    )(*kv_terms, gq, x, gain, grad_middle, first_full, second_full, cos_wide, sin_wide)


def unit_pieces(unit_rows, group_count, seq_devices):
    units = unit_rows * group_count
    steps = pl.cdiv(units, TILE)
    pieces = []
    for owner in range(seq_devices):
        for kind in range(2):
            for group in range(group_count):
                unit = group * unit_rows
                stop = unit + unit_rows
                column = kind * units * seq_devices + (group * seq_devices + owner) * unit_rows
                while unit < stop:
                    step = unit // TILE
                    end = min(stop, (step + 1) * TILE)
                    width = TILE if step < steps - 1 else units - (steps - 1) * TILE
                    inside = 2 * step * TILE + kind * width + unit - step * TILE
                    pieces.append((owner, inside, column, end - unit))
                    column += end - unit
                    unit = end
    return pieces


def spread_columns(weight, place, unit_rows, group_count, seq_devices):
    layers, rows, columns = weight.shape
    quarter = columns // seq_devices
    pieces = unit_pieces(unit_rows, group_count, seq_devices)

    def kernel(place_ref, w_ref, *refs):
        outs, wide, narrow = refs[:seq_devices], refs[-2], refs[-1]
        for layer in range(layers):
            wide[...] = w_ref[layer].astype(jnp.float32)
            for owner in range(seq_devices):
                for who, inside, column, width in pieces:
                    if who == owner:
                        narrow[:, inside : inside + width] = wide[:, column : column + width]
                block = narrow[...].astype(jnp.bfloat16)
                for bit in range(seq_devices):

                    @pl.when(place_ref[0] == owner ^ bit)
                    def _():
                        outs[bit][layer] = block

    return call(
        kernel,
        [((layers, rows, quarter), jnp.bfloat16)] * seq_devices,
        2.5,
        [pltpu.VMEM((rows, columns), jnp.float32), pltpu.VMEM((rows, quarter), jnp.float32)],
        in_specs=[pl.BlockSpec(memory_space=pltpu.SMEM), FULL],
        out_specs=[FULL] * seq_devices,
    )(place.reshape(1).astype(jnp.int32), weight)


def collect_columns(blocks, place, unit_rows, group_count):
    count = len(blocks)
    layers, rows, quarter = blocks[0].shape
    pieces = unit_pieces(unit_rows, group_count, count)

    def kernel(place_ref, *refs):
        out_ref, narrow = refs[count:]
        me = place_ref[0]
        for layer in range(layers):
            for owner in range(count):
                for bit in range(count):

                    @pl.when(me == owner ^ bit)
                    def _():
                        narrow[...] = refs[bit][layer].astype(jnp.float32)

                for who, inside, column, width in pieces:
                    if who == owner:
                        out_ref[layer, :, column : column + width] = narrow[:, inside : inside + width]

    return call(
        kernel,
        [((layers, rows, count * quarter), jnp.float32)],
        1.5,
        [pltpu.VMEM((rows, quarter), jnp.float32)],
        in_specs=[pl.BlockSpec(memory_space=pltpu.SMEM)] + [FULL] * count,
        out_specs=[FULL],
    )(place.reshape(1).astype(jnp.int32), *blocks)[0]


def fold(rows, columns):
    high = rows.shape[0] * 128 // columns
    wide = rows.shape[1] // 128
    return jnp.concatenate(
        [
            jnp.concatenate(
                [rows[high * r : high * r + high, 128 * c : 128 * c + 128] for r in range(columns // 128)],
                axis=1,
            )
            for c in range(wide)
        ],
        axis=0,
    )


def unfold(rows, width):
    high = rows.shape[0] * 128 // width
    wide = rows.shape[1] // 128
    return jnp.concatenate(
        [
            jnp.concatenate(
                [rows[high * c : high * c + high, 128 * r : 128 * r + 128] for c in range(width // 128)],
                axis=1,
            )
            for r in range(wide)
        ],
        axis=0,
    )


def pack_rows(blocks, down, place):
    owners = len(blocks)
    layers, rows, columns = blocks[0].shape
    total = owners * rows + down.shape[1] * down.shape[2] // columns

    def kernel(place_ref, down_ref, *refs):
        ins, outs = refs[:owners], refs[owners:]
        for layer in range(layers):
            parts = []
            for owner in range(owners):
                part = ins[0][layer].astype(jnp.float32)
                for bit in range(1, owners):
                    part = jnp.where(
                        place_ref[0] == owner ^ bit, ins[bit][layer].astype(jnp.float32), part
                    )
                parts.append(part)
            parts.append(fold(down_ref[layer].astype(jnp.float32), columns))
            outs[layer][0] = jnp.concatenate(parts, axis=0).astype(jnp.bfloat16)

    return call(
        kernel,
        [((1, total, columns), jnp.bfloat16)] * layers,
        3.0,
        in_specs=[pl.BlockSpec(memory_space=pltpu.SMEM)] + [FULL] * (owners + 1),
        out_specs=[FULL] * layers,
    )(place.reshape(1).astype(jnp.int32), down, *blocks)


def unpack(parts, places, chunk):
    count, total, columns = parts[0].shape
    number = count * len(parts)
    unit_rows = (total - chunk) * columns // D

    def kernel(place_ref, *refs):
        ins, gate_ref, down_ref = refs[: len(parts)], refs[-2], refs[-1]
        for which in range(len(parts)):
            for k in range(count):
                spot = place_ref[which * count + k]
                gate_ref[spot] = ins[which][k, :chunk, :]
                down_ref[spot] = unfold(ins[which][k, chunk:, :].astype(jnp.float32), D).astype(
                    jnp.bfloat16
                )

    gate, down = call(
        kernel,
        [((number, chunk, columns), jnp.bfloat16), ((number, unit_rows, D), jnp.bfloat16)],
        5.0,
        in_specs=[pl.BlockSpec(memory_space=pltpu.SMEM)] + [FULL] * len(parts),
        out_specs=[FULL] * 2,
    )(jnp.stack(places).astype(jnp.int32), *parts)
    return gate.reshape(number * chunk, columns), down.reshape(number * unit_rows, D)


def split_rows(terms, chunk, place, count):
    layers = len(terms)
    total_rows, columns = terms[0][0].shape
    rows = chunk // count
    unit_rows = (total_rows - chunk) * columns // D

    def kernel(place_ref, *refs):
        ins, outs, down_ref = refs[: 2 * layers], refs[2 * layers : -1], refs[-1]
        for layer in range(layers):
            total = ins[2 * layer][...].astype(jnp.float32) + ins[2 * layer + 1][...].astype(
                jnp.float32
            )
            down_ref[layer] = unfold(total[chunk:], D)
            for owner in range(count):
                block = total[owner * rows : owner * rows + rows].astype(jnp.bfloat16)
                for bit in range(count):

                    @pl.when(place_ref[0] == owner ^ bit)
                    def _():
                        outs[bit][layer] = block

    *blocks, down = call(
        kernel,
        [((layers, rows, columns), jnp.bfloat16)] * count
        + [((layers, unit_rows, D), jnp.float32)],
        3.0,
        in_specs=[pl.BlockSpec(memory_space=pltpu.SMEM)] + [FULL] * (2 * layers),
        out_specs=[FULL] * (count + 1),
    )(place.reshape(1).astype(jnp.int32), *[term for pair in terms for term in pair])
    return blocks, down


def assemble(parts, places, chip_rows):
    line, rows, width = parts[0].shape

    def kernel(place_ref, *refs):
        ins = refs[:8]
        first_ref, second_ref, small_ref = refs[8:]
        here, chip, side = place_ref[0] == 0, place_ref[1] == 0, place_ref[2] % 2 == 0
        mine = place_ref[2] // 2
        small = jnp.zeros((rows - chip_rows, width), jnp.float32)
        for spot in range(line):
            halves = []
            for half in range(2):
                pieces = []
                blocks = [ins[4 * half + k][spot].astype(jnp.float32) for k in range(4)]
                for block in blocks:
                    small = small + block[chip_rows:]
                lower = [jnp.where(side, blocks[2 * x], blocks[2 * x + 1]) for x in range(2)]
                upper = [jnp.where(side, blocks[2 * x + 1], blocks[2 * x]) for x in range(2)]
                for pair in (lower, upper):
                    pieces.append(jnp.where(chip, pair[0], pair[1])[:chip_rows])
                    pieces.append(jnp.where(chip, pair[1], pair[0])[:chip_rows])
                halves.append(jnp.concatenate(pieces, axis=0).astype(jnp.bfloat16))
            first_ref[mine ^ spot] = jnp.where(here, halves[0], halves[1])
            second_ref[mine ^ spot] = jnp.where(here, halves[1], halves[0])
        small_ref[...] = small

    first, second, small = call(
        kernel,
        [
            ((line, 4 * chip_rows, width), jnp.bfloat16),
            ((line, 4 * chip_rows, width), jnp.bfloat16),
            ((rows - chip_rows, width), jnp.float32),
        ],
        4.0,
        in_specs=[pl.BlockSpec(memory_space=pltpu.SMEM)] + [FULL] * 8,
        out_specs=[FULL] * 3,
    )(jnp.stack(places).astype(jnp.int32), *parts)
    return first.reshape(-1, width), second.reshape(-1, width), small


def projection_grads(normed, grad_query, grad_kv, mixed, grad_low, gain_one, gain_two, bias_one, bias_two, places, chip_rows, line):
    width = SPLIT

    def kernel(place_ref, n_ref, gq_ref, gkv_ref, mixed_ref, gy_ref, g1_ref, g2_ref, b1_ref, b2_ref, keep0, keep1, send0, send1, pad):
        here, chip, side = place_ref[0] == 0, place_ref[1] == 0, place_ref[2] % 2
        mine = place_ref[2] // 2
        turned = n_ref[...].T
        pad[...] = jnp.zeros_like(pad)
        pad[0:1, :D] = g1_ref[...]
        pad[1:2, :D] = g2_ref[...]
        pad[2:3, :] = b1_ref[...]
        pad[3:4, :KV_WIDTH] = b2_ref[...]
        small = pad[...]
        first = jnp.concatenate(
            [dot(turned, gq_ref[...]), dot(turned, gkv_ref[:, :KV_WIDTH])], axis=1
        )
        second = jnp.concatenate(
            [dot(turned, gkv_ref[:, KV_WIDTH:]), dot(mixed_ref[...], gy_ref[...], TN)], axis=1
        )

        def chunk(part, number):
            rows = part[number * chip_rows : (number + 1) * chip_rows]
            return jnp.concatenate([rows, small], axis=0).astype(jnp.bfloat16)

        for spot in range(line):
            for pair in range(2):
                slot = side ^ pair
                firsts = [chunk(first, 4 * spot + 2 * pair + x) for x in range(2)]
                seconds = [chunk(second, 4 * spot + 2 * pair + x) for x in range(2)]
                keeps = [jnp.where(here, one, two) for one, two in zip(firsts, seconds)]
                sends = [jnp.where(here, two, one) for one, two in zip(firsts, seconds)]
                keep0[slot, mine ^ spot] = jnp.where(chip, keeps[0], keeps[1])
                keep1[slot, mine ^ spot] = jnp.where(chip, keeps[1], keeps[0])
                send0[slot, mine ^ spot] = jnp.where(chip, sends[0], sends[1])
                send1[slot, mine ^ spot] = jnp.where(chip, sends[1], sends[0])

    return call(
        kernel,
        [((2, line, chip_rows + 8, width), jnp.bfloat16)] * 4,
        6.0,
        [pltpu.VMEM((8, width), jnp.float32)],
        in_specs=[pl.BlockSpec(memory_space=pltpu.SMEM)] + [FULL] * 9,
        out_specs=[FULL] * 4,
    )(
        jnp.stack(places).astype(jnp.int32),
        normed,
        grad_query,
        grad_kv,
        mixed,
        grad_low,
        gain_one,
        gain_two,
        bias_one,
        bias_two,
    )


def swap(values, axis, bit):
    size = lax.axis_size(axis)
    return lax.ppermute(values, axis, [(i, i ^ bit) for i in range(size)])


def after(values, *others):
    return lax.optimization_barrier((values,) + tuple(others))[0]


def line_bits():
    bits = [1]
    while 4 * bits[-1] < lax.axis_size("dp"):
        bits.append(2 * bits[-1])
    return bits


def line_gather(values, bits, *waited):
    for bit in bits:
        values = jnp.concatenate([values, after(swap(values, "dp", 2 * bit), *waited)], axis=0)
    return values


def line_steps(values, moves):
    return lax.ppermute(
        values, "dp", [(2 * here + side, 2 * there + side) for here, there in moves for side in range(2)]
    )


def cross_middle(values):
    line = lax.axis_size("dp") // 2
    if line == 4:
        return line_steps(values, [(1, 2), (2, 1)])
    return swap(values, "dp", line)


def line_scatter(values, bits, *waited):
    for bit in bits[:0:-1]:
        values = add_low(values[:bit], after(swap(values[bit:], "dp", 2 * bit), *waited))
    return [values[0], swap(values[1], "dp", 2)]


def add_low(left, right):
    return (left.astype(jnp.float32) + right.astype(jnp.float32)).astype(jnp.bfloat16)


def group_rows(values, *waited):
    beside = swap(values, "seq", 1)
    across = swap(values, "seq", 2)
    return [values, beside, across, swap(after(across, *waited), "seq", 1)]


def placed(values, offset, width):
    return lax.dynamic_update_slice(jnp.zeros((width,), values.dtype), values, (offset,))


def body(
    tokens,
    cotangent,
    span_order,
    attn_gain,
    joined_weight,
    joined_bias,
    out_weight,
    mlp_gain,
    gate_up_weight,
    down_weight,
):
    seq_count, tok_len, model_width = tokens.shape
    span_len = tok_len // 2
    group_count = lax.axis_size("dp")
    seq_devices = lax.axis_size("seq")
    unit_rows = down_weight.shape[1]
    width_rows = gate_up_weight.shape[1]
    units = group_count * unit_rows
    dp_place = lax.axis_index("dp")
    seq_place = lax.axis_index("seq")
    core = seq_place % 2
    chip_x = seq_place // 2
    device = dp_place * seq_devices + seq_place
    chip_rows = 2 * width_rows
    line = group_count // 2
    side = dp_place % 2
    line_place = dp_place // 2

    order = [lax.dynamic_slice(span_order, (0, seq_place ^ bit), (1, 1))[0, 0] for bit in range(4)]
    inside = jnp.arange(span_len, dtype=jnp.int32)
    own_places = jnp.concatenate(
        [order[0] * span_len + inside, (2 * seq_devices - 1 - order[0]) * span_len + inside]
    )
    half_biases = []
    for half in range(2):
        blocks = []
        for bit in range(4):
            ahead = order[bit] < order[0] if half == 0 else order[bit] > order[0]
            allowed = ahead | ((order[bit] == order[0]) & (inside[:, None] >= inside[None, :]))
            blocks.append(jnp.where(allowed, 0.0, NEGATIVE).astype(jnp.float32))
        half_biases.append(jnp.concatenate(blocks, axis=1))
    biases = jnp.stack(half_biases)
    biases_turned = jnp.swapaxes(biases, 1, 2)
    cos_table, sin_table = rotary_tables(own_places)
    cos_wide = jnp.concatenate([cos_table] * 4, axis=1)
    sin_wide = jnp.concatenate([-sin_table, sin_table] * 2, axis=1)

    def attn_shard(layer):
        first = joined_weight[layer][:, :SPLIT]
        second = jnp.concatenate([joined_weight[layer][:, SPLIT:], out_weight[layer]], axis=1)
        got = swap(jnp.where(core == 0, second, first), "seq", 1)
        mine = jnp.where(core == 0, first, second)
        rows = jnp.where(core == 0, jnp.stack([mine, got]), jnp.stack([got, mine])).reshape(
            chip_rows, -1
        )
        bias_all = placed(joined_bias[layer], device * joined_bias.shape[1], SPLIT + KV_WIDTH)
        extra = jnp.zeros((8, SPLIT), jnp.bfloat16)
        extra = extra.at[0].set(placed(attn_gain[layer], device * width_rows, SPLIT))
        extra = extra.at[1].set(placed(mlp_gain[layer], device * width_rows, SPLIT))
        extra = extra.at[2].set(bias_all[:SPLIT])
        extra = extra.at[3, :KV_WIDTH].set(bias_all[SPLIT:])
        return jnp.concatenate([rows, extra], axis=0)

    def attn_parts(own_side, other_side, *waited):
        parts = [own_side, other_side]
        return parts + [swap(after(part, *waited), "seq", 2) for part in parts]

    def attn_finish(parts):
        other_side = parts[1]
        parts = parts + [swap(after(part, other_side), "seq", 1) for part in parts]
        first_full, second_full, small = assemble(parts, [core, chip_x, dp_place], chip_rows)
        return (
            first_full,
            second_full,
            small[0:1, :model_width],
            small[1:2, :model_width],
            small[2:3],
            small[3:4, :KV_WIDTH],
        )

    bits = line_bits()
    spread = spread_columns(gate_up_weight, seq_place, unit_rows, group_count, seq_devices)
    shards = [attn_shard(layer)[None] for layer in range(LAYERS)]
    gate_blocks = [spread[0]] + [swap(spread[bit], "seq", bit) for bit in range(1, 4)]
    gate_shards = pack_rows(gate_blocks, down_weight, seq_place)
    attn_line = line_gather(after(shards[0], *spread), bits)
    attn_other = swap(after(attn_line, *gate_shards), "dp", 1)
    def outward(crossed, *waited):
        if line != 4:
            return crossed
        passed = after(line_steps(crossed, [(1, 0), (2, 3)]), *waited)
        return jnp.where((line_place == 1) | (line_place == 2), crossed, passed)

    first_parts = attn_parts(attn_line, attn_other)
    near = [line_gather(after(gate_shards[0], attn_other), bits[:-1], first_parts[3])]
    near_pair = [swap(after(near[0], attn_other), "dp", 1)]
    crossed = [cross_middle(near[0])]
    far = []
    offsets = [dp_place ^ (2 * k) for k in range(line)]
    half = line // 2
    if line == 4:
        beyond = [jnp.where(line_place < 2, 2 + k, 1 - k) * 2 + side for k in range(2)]
    else:
        beyond = offsets[half:]
    places = offsets[:half] + beyond
    places = [offsets[:half], beyond, [spot ^ 1 for spot in offsets[:half]], [spot ^ 1 for spot in beyond]]
    places = [spot for group in places for spot in group]

    def mlp_finish(layer, far_pair):
        parts = [near[layer], far[layer], near_pair[layer], far_pair]
        return unpack(parts, places, seq_devices * width_rows)

    terms = [tokens.reshape(tok_len, model_width)]
    kept_state = []
    mlp_sets = []
    attn_sets = [attn_finish(first_parts)]
    for layer in range(LAYERS):
        first_full, second_full, gain_full, mlp_gain_full, bias_first, bias_second = attn_sets[layer]
        if layer == 0:
            second_line = line_gather(after(shards[1], first_full), bits[:1])
        x, normed, queries, own_kv = before_attention(
            terms,
            after(gain_full, near[0], second_line) if layer == 0 else after(gain_full, near_pair[1]),
            first_full,
            second_full,
            bias_first,
            bias_second,
            cos_wide,
            sin_wide,
        )
        kv_blocks = [own_kv] + [swap(own_kv, "seq", bit) for bit in range(1, 4)]
        waited = (near_pair[0],) if layer == 0 else ()
        mixed, middle, n2 = attention(
            queries, kv_blocks, biases, x, second_full, after(mlp_gain_full, *waited)
        )
        if layer + 1 == LAYERS:
            far.append(outward(after(crossed[1], kept_state[0][7][0]), own_kv))
            far_pair = swap(far[1], "dp", 1)
            n2_parts = group_rows(n2, far_pair)
        else:
            n2_parts = group_rows(n2)
        if layer == 0:
            second_line = line_gather(second_line, bits[1:])
            second_other = swap(after(second_line, n2_parts[3]), "dp", 1)
            far.append(outward(after(crossed[0], n2)))
            far_pair = swap(far[0], "dp", 1)
            near.append(line_gather(after(gate_shards[1], n2), bits[:-1], n2_parts[3]))
            crossed.append(cross_middle(near[1]))
            attn_sets.append(attn_finish(attn_parts(second_line, second_other, n2_parts[3])))
            near_pair.append(swap(after(near[1], far_pair), "dp", 1))
        mlp_sets.append(mlp_finish(layer, far_pair))
        gu_near, *outs_near = feed_forward(n2_parts[:2], *mlp_sets[layer])
        if layer == 0:
            n2_parts[2] = after(n2_parts[2], crossed[1], gu_near)
        else:
            low_parts = group_rows(
                after(cotangent.reshape(tok_len, model_width), n2_parts[3]), gu_near
            )
        gu_far, *outs_far = feed_forward(n2_parts[2:], *mlp_sets[layer])
        across_sum = add_low(outs_far[0], swap(outs_far[1], "seq", 1))
        terms = [middle, outs_near[0], swap(outs_near[1], "seq", 1)]
        if layer + 1 < LAYERS:
            terms.append(swap(across_sum, "seq", 2))
        kept_state.append((x, normed, queries, kv_blocks, mixed, middle, n2_parts, [gu_near, gu_far]))
    upstream = cotangent.reshape(tok_len, model_width)
    states = [None] * LAYERS
    before = None

    def send_attn(state, pair, *waited):
        near, far, got_near, got_far = state["attn_parts"]
        return swap(after(add_low(far[pair], got_far[pair]), *waited), "seq", 2)

    def sum_attn(state, arrived, *waited):
        near, far, got_near, got_far = state["attn_parts"]
        return [
            (
                near[pair].astype(jnp.float32)
                + got_near[pair].astype(jnp.float32)
                + after(arrived[pair], *waited).astype(jnp.float32)
            ).astype(jnp.bfloat16)
            for pair in range(2)
        ]

    def step_one(state, *waited):
        far_sum = state["far_sum"]
        if line == 4:
            far_sum = add_low(far_sum, after(state["inward"], *waited))
        state["crossed"] = cross_middle(far_sum)
        state["near_sum"] = add_low(state["keep_near"], after(state["near_got"], *waited))

    def step_two(state, *waited):
        state["near_sum"] = add_low(state["near_sum"], after(state["crossed"], *waited))
        state["terms"] = line_scatter(state["near_sum"], bits[:-1])

    def finish(states):
        state = states[0]
        other_side = swap(after(state["attn_sums"][1], state["near_got"]), "dp", 1)
        state["owned"] = line_scatter(
            add_low(state["attn_sums"][0], other_side), bits, state["near_sum"]
        )
        owned = jnp.stack(
            [sum(term.astype(jnp.float32) for term in state["owned"]) for state in states]
        )
        extra = owned[:, chip_rows:]
        halves = owned[:, :chip_rows].reshape(LAYERS, 2, width_rows, -1)
        mine = lax.dynamic_index_in_dim(halves, core, 1, keepdims=False)
        theirs = swap(
            lax.dynamic_index_in_dim(halves, 1 - core, 1, keepdims=False), "seq", 1
        )
        first_own = jnp.where(core == 0, mine, theirs)
        second_own = jnp.where(core == 0, theirs, mine)

        def cut(row, width, stop):
            start = (0, row, device * width)
            return lax.dynamic_slice(extra[:, :, :stop], start, (LAYERS, 1, width))[:, 0]

        gate_rows, down_owned = split_rows(
            [state["terms"] for state in states], seq_devices * width_rows, seq_place, seq_devices
        )
        gate_owned = collect_columns(
            [gate_rows[0]] + [swap(gate_rows[bit], "seq", bit) for bit in range(1, 4)],
            seq_place,
            unit_rows,
            group_count,
        )
        return (
            cut(0, width_rows, model_width),
            jnp.concatenate([first_own, second_own[:, :, :KV_WIDTH]], axis=2),
            cut(2, SPLIT // (group_count * seq_devices), SPLIT),
            cut(3, KV_WIDTH // (group_count * seq_devices), KV_WIDTH),
            second_own[:, :, KV_WIDTH:],
            cut(1, width_rows, model_width),
            gate_owned,
            down_owned,
        )

    for layer in reversed(range(LAYERS)):
        x, normed, queries, kv_blocks, mixed, middle, n2_parts, gu_parts = kept_state[layer]
        first_full, second_full, gain_full, mlp_gain_full, _, _ = attn_sets[layer]
        if before is not None:
            low_parts = group_rows(upstream_low)
            low_parts[0] = after(low_parts[0], *before["attn_parts"][2:])
            attn_sent = [send_attn(before, pair, low_parts[3]) for pair in range(2)]
            last_across = swap(after(across_sum, low_parts[3]), "seq", 2)
        apart = line == 4 and layer == 0
        keep_near, send_near, own_out, across_out, pair_out, *far_parts = feed_back(
            low_parts,
            n2_parts,
            gu_parts,
            *mlp_sets[layer],
            dp_place,
            group_count,
            2 if apart else 1,
        )
        if before is not None:
            pair_out = after(pair_out, last_across, *attn_sent, before["near_got"], before["inward"])
        got = swap(pair_out, "seq", 1)
        out_terms = [own_out, got[0], swap(add_low(across_out, got[1]), "seq", 2)]
        if apart:
            keep_far, send_far = far_parts[:2], far_parts[2:]
            got_far = [swap(after(send_far[0], got), "dp", 1), swap(send_far[1], "dp", 1)]
            far_sums = [None, add_low(keep_far[1], after(got_far[1], out_terms[2]))]
            inward = [None, line_steps(far_sums[1], [(0, 1), (3, 2)])]
        else:
            keep_far, send_far = far_parts
            got_far = swap(send_far, "dp", 1)
        if before is not None:
            step_one(before, own_out)
            before["attn_sums"] = sum_attn(before, attn_sent, own_out)
        grad_middle, grad_low, mlp_gain_part, grad_query, own_term, *kv_terms = attention_back(
            upstream,
            middle,
            mlp_gain_full,
            out_terms,
            second_full,
            queries,
            kv_blocks,
            biases_turned,
            cos_wide,
            sin_wide,
        )
        if apart:
            kv_terms[0] = after(kv_terms[0], inward[1])
        kv_terms = [own_term] + [swap(kv_terms[bit - 1], "seq", bit) for bit in range(1, 4)]
        upstream, upstream_low, grad_kv, attn_gain_part, bias_first, bias_second = before_back(
            kv_terms,
            grad_query,
            x,
            gain_full,
            grad_middle,
            first_full,
            second_full,
            cos_wide,
            sin_wide,
        )
        near_got = swap(after(send_near, grad_low), "dp", 1)
        if apart:
            across_middle = [None, cross_middle(add_low(far_sums[1], after(inward[1], grad_low)))]
            far_sums[0] = add_low(keep_far[0], after(got_far[0], grad_low))
            inward[0] = after(line_steps(far_sums[0], [(0, 1), (3, 2)]), upstream)
            across_middle[0] = cross_middle(add_low(far_sums[0], inward[0]))
            near_one = add_low(add_low(keep_near[1], near_got[1]), across_middle[1][0])
            near_zero = add_low(add_low(keep_near[0], near_got[0]), across_middle[0][0])
            state = {"near_got": near_got, "near_sum": near_one}
            state["terms"] = [near_zero, swap(near_one, "dp", 2)]
            step_two(before, far_sums[0])
        else:
            far_sum = add_low(keep_far, after(got_far, upstream if before is None else grad_low))
            state = {
                "far_sum": far_sum,
                "keep_near": keep_near,
                "near_got": near_got,
                "inward": line_steps(far_sum, [(0, 1), (3, 2)]) if line == 4 else far_sum,
            }
            if before is not None:
                step_two(before, far_sum)
        if before is not None:
            other_side = swap(after(before["attn_sums"][1], grad_low), "dp", 1)
            attn_pair = add_low(before["attn_sums"][0], after(other_side, upstream))
        near_x, far_x, near_other, far_other = projection_grads(
            normed,
            grad_query,
            grad_kv,
            mixed,
            grad_low,
            attn_gain_part,
            mlp_gain_part,
            bias_first,
            bias_second,
            [core, chip_x, dp_place],
            chip_rows,
            line,
        )
        got_far_other = swap(far_other, "seq", 1)
        got_near_other = swap(near_other, "seq", 1)
        state["attn_parts"] = (near_x, far_x, got_near_other, got_far_other)
        if before is not None:
            before["owned"] = line_scatter(attn_pair, bits, got_far_other)
        states[layer] = before = state
    if line != 4:
        step_one(before)
        step_two(before)
    arrived = [None, send_attn(before, 1)]
    arrived[0] = send_attn(before, 0)
    before["attn_sums"] = sum_attn(before, arrived)
    grads = finish(states)
    terms.append(last_across)
    activations = sum(term.astype(jnp.float32) for term in terms).astype(jnp.bfloat16)
    return (
        activations.reshape(seq_count, tok_len, model_width),
        upstream.reshape(seq_count, tok_len, model_width),
    ) + grads


def solution(mesh):
    in_specs = (
        P("dp", "seq", None),
        P("dp", "seq", None),
        P("dp", None),
        P(None, ("dp", "seq")),
        P(None, ("dp", "seq"), None),
        P(None, ("dp", "seq")),
        P(None, ("dp", "seq"), None),
        P(None, ("dp", "seq")),
        P(None, ("dp", "seq"), None),
        P(None, ("dp", "seq"), None),
    )
    out_specs = (
        P("dp", "seq", None),
        P("dp", "seq", None),
        P(None, ("dp", "seq")),
        P(None, ("dp", "seq"), None),
        P(None, ("dp", "seq")),
        P(None, ("dp", "seq")),
        P(None, ("dp", "seq"), None),
        P(None, ("dp", "seq")),
        P(None, ("dp", "seq"), None),
        P(None, ("dp", "seq"), None),
    )
    return jax.shard_map(body, mesh=mesh, in_specs=in_specs, out_specs=out_specs, check_vma=False)
```

```python
import jax
import jax.numpy as jnp
from jax import lax
from jax.experimental import pallas as pl
from jax.experimental.pallas import tpu as pltpu
from jax.sharding import PartitionSpec as P

D = 896
HEADS = 14
KV_HEADS = 2
HEAD = 64
LAYERS = 2


EPS = 1e-06
THETA = 1000000.0
NEGATIVE = -1e30


def rotary_tables(positions):
    half_head = HEAD // 2
    frequency = THETA ** (-2.0 * jnp.arange(half_head, dtype=jnp.float32) / HEAD)
    angles = positions.astype(jnp.float32)[..., None] * frequency
    return (jnp.cos(angles), jnp.sin(angles))


NT = (((1,), (1,)), ((), ()))
TN = (((0,), (0,)), ((), ()))
FULL = pl.BlockSpec(memory_space=pltpu.VMEM)
SCALE = HEAD ** (-0.5)
GROUP = HEADS // KV_HEADS
KV_WIDTH = KV_HEADS * HEAD
SPLIT = D + KV_WIDTH
TILE = 384


def dot(left, right, dims=(((1,), (0,)), ((), ()))):
    return lax.dot_general(left, right, dims, preferred_element_type=jnp.float32)


def call(kernel, outs, micros, scratch=(), limit=40, **grid):
    return pl.pallas_call(
        kernel,
        out_shape=[jax.ShapeDtypeStruct(shape, kind) for shape, kind in outs],
        scratch_shapes=list(scratch),
        compiler_params=pltpu.CompilerParams(vmem_limit_bytes=limit * 2**20),
        name=kernel.__qualname__.split(".")[0],
        cost_estimate=pl.CostEstimate(
            flops=0, bytes_accessed=int(micros * 4e3), transcendentals=0
        ),
        **grid,
    )


def turn(block, cos_wide, sin_wide):
    lane = lax.broadcasted_iota(jnp.int32, block.shape, 1)
    width = block.shape[1]
    partner = jnp.where(
        lane % HEAD < HEAD // 2,
        pltpu.roll(block, width - HEAD // 2, 1),
        pltpu.roll(block, HEAD // 2, 1),
    )
    return block * cos_wide + partner * sin_wide


def inverse_root(rows):
    return lax.rsqrt(jnp.mean(rows * rows, axis=-1, keepdims=True) + EPS)


def before_attention(terms, gain, first_full, second_full, bias_first, bias_second, cos_wide, sin_wide):
    count = len(terms)
    rows = terms[0].shape[0]
    span = rows // 2

    def kernel(*refs):
        parts = refs[:count]
        gain_ref, first_ref, second_ref, bias_one, bias_two, cos_ref, sin_ref = refs[count : count + 7]
        x_ref, n_ref, q_ref, kv_ref = refs[count + 7 :]
        x = parts[0][...].astype(jnp.float32)
        for part in parts[1:]:
            x = x + part[...].astype(jnp.float32)
        x_ref[...] = x
        normed = (x * inverse_root(x) * gain_ref[...]).astype(jnp.bfloat16)
        n_ref[...] = normed
        cos_w, sin_w = cos_ref[...], sin_ref[...]
        for tile in range(SPLIT // 128):
            lanes = slice(tile * 128, tile * 128 + 128)
            block = dot(normed, first_ref[:, lanes]) + bias_one[:, lanes]
            turned = turn(block, cos_w, sin_w)
            if tile * 128 < D:
                for part in range(2):
                    head = 2 * tile + part
                    piece = turned[:, part * HEAD : part * HEAD + HEAD].astype(jnp.bfloat16)
                    place = (head % GROUP) * span
                    for half in range(2):
                        q_ref[head // GROUP, half, place : place + span, :] = piece[
                            half * span : half * span + span
                        ]
            else:
                kv_ref[:, :KV_WIDTH] = turned.astype(jnp.bfloat16)
        kv_ref[:, KV_WIDTH:] = (
            dot(normed, second_ref[:, :KV_WIDTH]) + bias_two[...]
        ).astype(jnp.bfloat16)

    return call(
        kernel,
        [
            ((rows, D), jnp.float32),
            ((rows, D), jnp.bfloat16),
            ((KV_HEADS, 2, GROUP * span, HEAD), jnp.bfloat16),
            ((rows, 2 * KV_WIDTH), jnp.bfloat16),
        ],
        4.0,
    )(*terms, gain, first_full, second_full, bias_first, bias_second, cos_wide, sin_wide)


def key_part(kv_refs, half, lanes):
    span = kv_refs[0].shape[0] // 2
    return jnp.concatenate(
        [ref[half * span : half * span + span, lanes] for ref in kv_refs], axis=0
    )


def attention(queries, kv_blocks, biases, x, second_full, gain):
    rows = x.shape[0]
    span = rows // 2

    def kernel(q_ref, kv0, kv1, kv2, kv3, bias_ref, x_ref, w_ref, gain_ref, mixed_ref, mid_ref, n_ref):
        kvs = (kv0, kv1, kv2, kv3)
        for group in range(KV_HEADS):
            key_lanes = slice(group * HEAD, group * HEAD + HEAD)
            value_lanes = slice(KV_WIDTH + group * HEAD, KV_WIDTH + group * HEAD + HEAD)
            keys = [key_part(kvs, half, key_lanes) for half in range(2)]
            values = []
            for half in range(2):
                block = key_part(kvs, half, value_lanes)
                values.append(jnp.concatenate([block, jnp.ones_like(block)], axis=1))
            for half in range(2):
                bias = bias_ref[half]
                for member in range(GROUP):
                    query = q_ref[group, half, member * span : member * span + span, :] * jnp.bfloat16(SCALE)
                    near = dot(query, keys[half], NT) + bias
                    top = jnp.max(near, axis=-1, keepdims=True)
                    if half == 1:
                        far = dot(query, keys[0], NT)
                        top = jnp.maximum(top, jnp.max(far, axis=-1, keepdims=True))
                    total = dot(jnp.exp(near - top).astype(jnp.bfloat16), values[half])
                    if half == 1:
                        total = total + dot(jnp.exp(far - top).astype(jnp.bfloat16), values[0])
                    out = total[:, :HEAD] / total[:, HEAD : 2 * HEAD]
                    head = group * GROUP + member
                    mixed_ref[half * span : half * span + span, head * HEAD : head * HEAD + HEAD] = (
                        out.astype(jnp.bfloat16)
                    )
        middle = x_ref[...] + dot(mixed_ref[...], w_ref[:, KV_WIDTH:])
        mid_ref[...] = middle
        n_ref[...] = (middle * inverse_root(middle) * gain_ref[...]).astype(jnp.bfloat16)

    return call(
        kernel,
        [((rows, D), jnp.bfloat16), ((rows, D), jnp.float32), ((rows, D), jnp.bfloat16)],
        10.5,
    )(queries, *kv_blocks, biases, x, second_full, gain)


def feed_forward(parts, gate_up_full, down_full):
    count = len(parts)
    part_rows = parts[0].shape[0]
    rows = count * part_rows
    units = down_full.shape[0]
    steps = pl.cdiv(units, TILE)
    last = units - (steps - 1) * TILE

    def kernel(*refs):
        part_refs = refs[:count]
        w_ref, d_ref, gu_ref = refs[count : count + 3]
        out_refs, total = refs[count + 3 : -1], refs[-1]
        step = pl.program_id(0)
        n2 = jnp.concatenate([ref[...] for ref in part_refs], axis=0)

        @pl.when(step == 0)
        def _():
            total[...] = jnp.zeros_like(total)

        @pl.when(step < steps - 1)
        def _():
            both = dot(n2, w_ref[...])
            gu_ref[...] = both.astype(jnp.bfloat16)
            gate, up = both[:, :TILE], both[:, TILE:]
            hidden = (gate * jax.nn.sigmoid(gate) * up).astype(jnp.bfloat16)
            total[...] += dot(hidden, d_ref[...])

        @pl.when(step == steps - 1)
        def _():
            both = dot(n2, w_ref[:, : 2 * last])
            gu_ref[:, : 2 * last] = both.astype(jnp.bfloat16)
            gate, up = both[:, :last], both[:, last:]
            hidden = (gate * jax.nn.sigmoid(gate) * up).astype(jnp.bfloat16)
            summed = (total[...] + dot(hidden, d_ref[:last, :])).astype(jnp.bfloat16)
            for place in range(count):
                out_refs[place][...] = summed[place * part_rows : place * part_rows + part_rows]

    whole = lambda step: (0, 0)
    return call(
        kernel,
        [((rows, 2 * units), jnp.bfloat16)] + [((part_rows, D), jnp.bfloat16)] * count,
        9.0,
        [pltpu.VMEM((rows, D), jnp.float32)],
        limit=60,
        grid=(steps,),
        in_specs=[pl.BlockSpec((part_rows, D), whole)] * count
        + [
            pl.BlockSpec((D, 2 * TILE), lambda step: (0, step)),
            pl.BlockSpec((TILE, D), lambda step: (step, 0)),
        ],
        out_specs=[
            pl.BlockSpec((rows, 2 * TILE), lambda step: (0, step)),
        ]
        + [pl.BlockSpec((part_rows, D), whole)] * count,
    )(*parts, gate_up_full, down_full)


def far_slot(mine, place, line):
    if line == 4:
        return jnp.where(mine < 2, place - 2, 1 - place)
    return (mine ^ place) - line // 2


def feed_back(gz_parts, n2_parts, gu_parts, gate_up_full, down_full, dp_place, group_count, far_arrays):
    line = group_count // 2
    half = line // 2
    each = half // far_arrays
    chunk = D // group_count
    count = len(gz_parts)
    gu_count = len(gu_parts)
    part_rows = gz_parts[0].shape[0]
    rows = count * part_rows
    units = down_full.shape[0]
    unit_rows = units // group_count
    packed = chunk + unit_rows * D // (2 * units)
    once = pl.Buffered(1)
    steps = pl.cdiv(units, TILE)
    last = units - (steps - 1) * TILE

    def kernel(*refs):
        place_ref, *refs = refs
        gz_refs = refs[:count]
        n2_refs = refs[count : 2 * count]
        gu_refs = refs[2 * count : 2 * count + gu_count]
        w_ref, d_ref = refs[2 * count + gu_count : 2 * count + gu_count + 2]
        outs = refs[2 * count + gu_count + 2 : -4]
        keep_near, send_near, own_ref, across_ref, pair_ref = outs[:5]
        keep_far, send_far = outs[5 : 5 + far_arrays], outs[5 + far_arrays :]
        total, gz, n2t, down = refs[-4:]
        side, mine = place_ref[0] % 2, place_ref[0] // 2
        step = pl.program_id(0)

        @pl.when(step == 0)
        def _():
            total[...] = jnp.zeros_like(total)
            for place in range(count):
                here = slice(place * part_rows, place * part_rows + part_rows)
                gz[here, :] = gz_refs[place][...]
                n2t[:, here] = n2_refs[place][...].T

        def write(spot, even, odd, rows, lanes):
            keep = jnp.where(side == 0, even, odd)
            send = jnp.where(side == 0, odd, even)
            slot = mine ^ spot
            beyond = far_slot(mine, spot, line)

            @pl.when(slot < half)
            def _():
                keep_near[slot, rows, lanes] = keep
                send_near[slot, rows, lanes] = send

            for number in range(far_arrays):

                @pl.when((slot >= half) & (beyond // each == number))
                def _():
                    keep_far[number][beyond % each, rows, lanes] = keep
                    send_far[number][beyond % each, rows, lanes] = send

        def work(width):
            gu = jnp.concatenate([ref[:, : 2 * width] for ref in gu_refs], axis=0).astype(jnp.float32)
            gate, up = gu[:, :width], gu[:, width:]
            sig = jax.nn.sigmoid(gate)
            act = gate * sig
            hidden = (act * up).astype(jnp.bfloat16)
            down[pl.ds(pl.multiple_of(step * TILE, 128), width), :] = dot(hidden, gz[...], TN)
            grad = dot(gz[...], d_ref[:width, :], NT)
            d_gate = grad * up * (sig + act * (1.0 - sig))
            d_up = grad * act
            both = jnp.concatenate([d_gate, d_up], axis=1).astype(jnp.bfloat16)
            part = dot(n2t[...], both)
            for spot in range(line):
                even = part[2 * spot * chunk : (2 * spot + 1) * chunk].astype(jnp.bfloat16)
                odd = part[(2 * spot + 1) * chunk : (2 * spot + 2) * chunk].astype(jnp.bfloat16)
                write(spot, even, odd, slice(0, chunk), pl.ds(pl.multiple_of(step * 2 * TILE, 128), 2 * width))

            return dot(both, w_ref[:, : 2 * width], NT)

        @pl.when(step < steps - 1)
        def _():
            total[...] += work(TILE)

        @pl.when(step == steps - 1)
        def _():
            summed = (total[...] + work(last)).astype(jnp.bfloat16)
            for spot in range(line):
                even, odd = (
                    fold(down[place * unit_rows : place * unit_rows + unit_rows, :], 2 * units).astype(
                        jnp.bfloat16
                    )
                    for place in (2 * spot, 2 * spot + 1)
                )
                write(spot, even, odd, slice(chunk, packed), slice(0, 2 * units))
            own_ref[...] = summed[:part_rows]
            pair_ref[0] = summed[part_rows : 2 * part_rows]
            across_ref[...] = summed[2 * part_rows : 3 * part_rows]
            pair_ref[1] = summed[3 * part_rows :]

    whole = lambda step: (0, 0)
    return call(
        kernel,
        [
            ((half, packed, 2 * units), jnp.bfloat16),
            ((half, packed, 2 * units), jnp.bfloat16),
            ((part_rows, D), jnp.bfloat16),
            ((part_rows, D), jnp.bfloat16),
            ((2, part_rows, D), jnp.bfloat16),
        ]
        + [((each, packed, 2 * units), jnp.bfloat16)] * (2 * far_arrays),
        25.0,
        [
            pltpu.VMEM((rows, D), jnp.float32),
            pltpu.VMEM((rows, D), jnp.bfloat16),
            pltpu.VMEM((D, rows), jnp.bfloat16),
            pltpu.VMEM((units, D), jnp.float32),
        ],
        limit=60,
        grid=(steps,),
        in_specs=[pl.BlockSpec(memory_space=pltpu.SMEM)]
        + [pl.BlockSpec((part_rows, D), whole, pipeline_mode=once)] * (2 * count)
        + [pl.BlockSpec((rows // gu_count, 2 * TILE), lambda step: (0, step))] * gu_count
        + [
            pl.BlockSpec((D, 2 * TILE), lambda step: (0, step)),
            pl.BlockSpec((TILE, D), lambda step: (step, 0)),
        ],
        out_specs=[
            pl.BlockSpec((half, packed, 2 * units), lambda step: (0, 0, 0), pipeline_mode=once),
            pl.BlockSpec((half, packed, 2 * units), lambda step: (0, 0, 0), pipeline_mode=once),
            pl.BlockSpec((part_rows, D), whole, pipeline_mode=once),
            pl.BlockSpec((part_rows, D), whole, pipeline_mode=once),
            pl.BlockSpec((2, part_rows, D), lambda step: (0, 0, 0), pipeline_mode=once),
        ]
        + [pl.BlockSpec((each, packed, 2 * units), lambda step: (0, 0, 0), pipeline_mode=once)]
        * (2 * far_arrays),
    )(dp_place.reshape(1).astype(jnp.int32), *gz_parts, *n2_parts, *gu_parts, gate_up_full, down_full)


def norm_back(rows, gain, grad):
    inv_root = inverse_root(rows)
    normal = rows * inv_root
    gain_part = jnp.sum(grad * normal, axis=0, keepdims=True)
    weighted = grad * gain
    inner = jnp.mean(weighted * normal, axis=-1, keepdims=True)
    return gain_part, inv_root * (weighted - normal * inner)


def attention_back(upstream, middle, gain, terms, second_full, queries, kv_blocks, biases, cos_wide, sin_wide):
    count = len(terms)
    rows = middle.shape[0]
    span = rows // 2
    wide = GROUP * span

    def kernel(*refs):
        up_ref, mid_ref, gain_ref = refs[:3]
        term_refs = refs[3 : 3 + count]
        w_ref, q_ref, kv0, kv1, kv2, kv3, bias_ref, cos_ref, sin_ref = refs[3 + count : 12 + count]
        gm_ref, gy_ref, dgain_ref, gq_ref, own_ref, d1, d2, d3, go_ref, dkv = refs[12 + count :]
        kvs = (kv0, kv1, kv2, kv3)
        grad = term_refs[0][...].astype(jnp.float32)
        for term in term_refs[1:]:
            grad = grad + term[...].astype(jnp.float32)
        gain_part, back = norm_back(mid_ref[...], gain_ref[...], grad)
        dgain_ref[...] = gain_part
        grad_middle = up_ref[...].astype(jnp.float32) + back
        gm_ref[...] = grad_middle
        grad_low = grad_middle.astype(jnp.bfloat16)
        gy_ref[...] = grad_low
        for tile in range(D // 128):
            start = KV_WIDTH
            block = dot(grad_low, w_ref[tile * 128 : tile * 128 + 128, start:], NT).astype(jnp.bfloat16)
            for part in range(2):
                head = 2 * tile + part
                place = (head % GROUP) * span
                for half in range(2):
                    go_ref[head // GROUP, half, place : place + span, :] = block[
                        half * span : half * span + span, part * HEAD : part * HEAD + HEAD
                    ]
        for group in range(KV_HEADS):
            key_lanes = slice(group * HEAD, group * HEAD + HEAD)
            value_lanes = slice(KV_WIDTH + group * HEAD, KV_WIDTH + group * HEAD + HEAD)
            keys = [key_part(kvs, half, key_lanes) for half in range(2)]
            values = [key_part(kvs, half, value_lanes) for half in range(2)]
            for half in range(2):
                query = q_ref[group, half] * jnp.bfloat16(SCALE)
                grad_out = go_ref[group, half]
                bias = jnp.concatenate([bias_ref[half]] * GROUP, axis=1)
                use = [half] if half == 0 else [1, 0]
                scores = []
                top = None
                for which in use:
                    score = dot(keys[which], query, NT)
                    if which == half:
                        score = score + bias
                    scores.append(score)
                    best = jnp.max(score, axis=0, keepdims=True)
                    top = best if top is None else jnp.maximum(top, best)
                weights = [jnp.exp(score - top) for score in scores]
                total = sum(jnp.sum(weight, axis=0, keepdims=True) for weight in weights)
                scale = 1.0 / total
                probs = [weight * scale for weight in weights]
                grads = [dot(values[which], grad_out, NT) for which in use]
                inner = sum(
                    jnp.sum(prob * grad_prob, axis=0, keepdims=True)
                    for prob, grad_prob in zip(probs, grads)
                )
                grad_query = None
                for which, prob, grad_prob in zip(use, probs, grads):
                    grad_score = (prob * (grad_prob - inner)).astype(jnp.bfloat16)
                    value_grad = dot(prob.astype(jnp.bfloat16), grad_out)
                    key_grad = dot(grad_score, query)
                    if half == 0:
                        dkv[group, which] = key_grad
                        dkv[KV_HEADS + group, which] = value_grad
                    elif which == 0:
                        dkv[group, which] += key_grad
                        dkv[KV_HEADS + group, which] += value_grad
                    else:
                        dkv[group, which] = key_grad
                        dkv[KV_HEADS + group, which] = value_grad
                    term = dot(keys[which].T, grad_score)
                    grad_query = term if grad_query is None else grad_query + term
                grad_query = grad_query * SCALE
                cos_w = cos_ref[half * span : half * span + span, :]
                sin_w = sin_ref[half * span : half * span + span, :]
                for member in range(GROUP):
                    head = group * GROUP + member
                    piece = grad_query[:, member * span : member * span + span].T
                    pair = jnp.concatenate([piece, piece], axis=1)
                    turned = turn(pair, cos_w, -sin_w)[:, :HEAD]
                    gq_ref[half * span : half * span + span, head * HEAD : head * HEAD + HEAD] = (
                        turned.astype(jnp.bfloat16)
                    )
        for place, out in enumerate((own_ref, d1, d2, d3)):
            for half in range(2):
                block = jnp.concatenate(
                    [dkv[lane, half, place * span : place * span + span, :] for lane in range(2 * KV_HEADS)],
                    axis=1,
                )
                out[half * span : half * span + span, :] = block.astype(out.dtype)

    return call(
        kernel,
        [
            ((rows, D), jnp.float32),
            ((rows, D), jnp.bfloat16),
            ((1, D), jnp.float32),
            ((rows, D), jnp.bfloat16),
            ((rows, 2 * KV_WIDTH), jnp.float32),
        ]
        + [((rows, 2 * KV_WIDTH), jnp.bfloat16)] * 3,
        13.0,
        [
            pltpu.VMEM((KV_HEADS, 2, wide, HEAD), jnp.bfloat16),
            pltpu.VMEM((2 * KV_HEADS, 2, 4 * span, HEAD), jnp.float32),
        ],
    )(upstream, middle, gain, *terms, second_full, queries, *kv_blocks, biases, cos_wide, sin_wide)


def before_back(kv_terms, gq, x, gain, grad_middle, first_full, second_full, cos_wide, sin_wide):
    rows = x.shape[0]
    count = len(kv_terms)

    def kernel(*refs):
        kv_refs = refs[:count]
        gq_ref, x_ref, gain_ref, gm_ref, w1_ref, w2_ref, cos_ref, sin_ref = refs[count : count + 8]
        up_ref, low_ref, gkv_ref, dgain_ref, bias_one, bias_two = refs[count + 8 :]
        grad = kv_refs[0][...].astype(jnp.float32)
        for ref in kv_refs[1:]:
            grad = grad + ref[...].astype(jnp.float32)
        grad_key = turn(grad[:, :KV_WIDTH], cos_ref[...], -sin_ref[...]).astype(jnp.bfloat16)
        grad_value = grad[:, KV_WIDTH:].astype(jnp.bfloat16)
        gkv_ref[:, :KV_WIDTH] = grad_key
        gkv_ref[:, KV_WIDTH:] = grad_value
        grad_query = gq_ref[...]
        bias_one[:, :D] = jnp.sum(grad_query.astype(jnp.float32), axis=0, keepdims=True)
        bias_one[:, D:] = jnp.sum(grad_key.astype(jnp.float32), axis=0, keepdims=True)
        bias_two[...] = jnp.sum(grad_value.astype(jnp.float32), axis=0, keepdims=True)
        grad_normed = (
            dot(grad_query, w1_ref[:, :D], NT)
            + dot(grad_key, w1_ref[:, D:], NT)
            + dot(grad_value, w2_ref[:, :KV_WIDTH], NT)
        )
        gain_part, back = norm_back(x_ref[...], gain_ref[...], grad_normed)
        dgain_ref[...] = gain_part
        upstream = gm_ref[...] + back
        up_ref[...] = upstream
        low_ref[...] = upstream.astype(jnp.bfloat16)

    return call(
        kernel,
        [
            ((rows, D), jnp.float32),
            ((rows, D), jnp.bfloat16),
            ((rows, 2 * KV_WIDTH), jnp.bfloat16),
            ((1, D), jnp.float32),
            ((1, SPLIT), jnp.float32),
            ((1, KV_WIDTH), jnp.float32),
        ],
        2.4,
    )(*kv_terms, gq, x, gain, grad_middle, first_full, second_full, cos_wide, sin_wide)


def unit_pieces(unit_rows, group_count, seq_devices):
    units = unit_rows * group_count
    steps = pl.cdiv(units, TILE)
    pieces = []
    for owner in range(seq_devices):
        for kind in range(2):
            for group in range(group_count):
                unit = group * unit_rows
                stop = unit + unit_rows
                column = kind * units * seq_devices + (group * seq_devices + owner) * unit_rows
                while unit < stop:
                    step = unit // TILE
                    end = min(stop, (step + 1) * TILE)
                    width = TILE if step < steps - 1 else units - (steps - 1) * TILE
                    inside = 2 * step * TILE + kind * width + unit - step * TILE
                    pieces.append((owner, inside, column, end - unit))
                    column += end - unit
                    unit = end
    return pieces


def spread_columns(weight, place, unit_rows, group_count, seq_devices):
    layers, rows, columns = weight.shape
    quarter = columns // seq_devices
    pieces = unit_pieces(unit_rows, group_count, seq_devices)

    def kernel(place_ref, w_ref, *refs):
        outs, wide, narrow = refs[:seq_devices], refs[-2], refs[-1]
        for layer in range(layers):
            wide[...] = w_ref[layer].astype(jnp.float32)
            for owner in range(seq_devices):
                for who, inside, column, width in pieces:
                    if who == owner:
                        narrow[:, inside : inside + width] = wide[:, column : column + width]
                block = narrow[...].astype(jnp.bfloat16)
                for bit in range(seq_devices):

                    @pl.when(place_ref[0] == owner ^ bit)
                    def _():
                        outs[bit][layer] = block

    return call(
        kernel,
        [((layers, rows, quarter), jnp.bfloat16)] * seq_devices,
        2.5,
        [pltpu.VMEM((rows, columns), jnp.float32), pltpu.VMEM((rows, quarter), jnp.float32)],
        in_specs=[pl.BlockSpec(memory_space=pltpu.SMEM), FULL],
        out_specs=[FULL] * seq_devices,
    )(place.reshape(1).astype(jnp.int32), weight)


def collect_columns(blocks, place, unit_rows, group_count):
    count = len(blocks)
    layers, rows, quarter = blocks[0].shape
    pieces = unit_pieces(unit_rows, group_count, count)

    def kernel(place_ref, *refs):
        out_ref, narrow = refs[count:]
        me = place_ref[0]
        for layer in range(layers):
            for owner in range(count):
                for bit in range(count):

                    @pl.when(me == owner ^ bit)
                    def _():
                        narrow[...] = refs[bit][layer].astype(jnp.float32)

                for who, inside, column, width in pieces:
                    if who == owner:
                        out_ref[layer, :, column : column + width] = narrow[:, inside : inside + width]

    return call(
        kernel,
        [((layers, rows, count * quarter), jnp.float32)],
        1.5,
        [pltpu.VMEM((rows, quarter), jnp.float32)],
        in_specs=[pl.BlockSpec(memory_space=pltpu.SMEM)] + [FULL] * count,
        out_specs=[FULL],
    )(place.reshape(1).astype(jnp.int32), *blocks)[0]


def fold(rows, columns):
    high = rows.shape[0] * 128 // columns
    wide = rows.shape[1] // 128
    return jnp.concatenate(
        [
            jnp.concatenate(
                [rows[high * r : high * r + high, 128 * c : 128 * c + 128] for r in range(columns // 128)],
                axis=1,
            )
            for c in range(wide)
        ],
        axis=0,
    )


def unfold(rows, width):
    high = rows.shape[0] * 128 // width
    wide = rows.shape[1] // 128
    return jnp.concatenate(
        [
            jnp.concatenate(
                [rows[high * c : high * c + high, 128 * r : 128 * r + 128] for c in range(width // 128)],
                axis=1,
            )
            for r in range(wide)
        ],
        axis=0,
    )


def pack_rows(blocks, down, place):
    owners = len(blocks)
    layers, rows, columns = blocks[0].shape
    total = owners * rows + down.shape[1] * down.shape[2] // columns

    def kernel(place_ref, down_ref, *refs):
        ins, outs = refs[:owners], refs[owners:]
        for layer in range(layers):
            parts = []
            for owner in range(owners):
                part = ins[0][layer].astype(jnp.float32)
                for bit in range(1, owners):
                    part = jnp.where(
                        place_ref[0] == owner ^ bit, ins[bit][layer].astype(jnp.float32), part
                    )
                parts.append(part)
            parts.append(fold(down_ref[layer].astype(jnp.float32), columns))
            outs[layer][0] = jnp.concatenate(parts, axis=0).astype(jnp.bfloat16)

    return call(
        kernel,
        [((1, total, columns), jnp.bfloat16)] * layers,
        3.0,
        in_specs=[pl.BlockSpec(memory_space=pltpu.SMEM)] + [FULL] * (owners + 1),
        out_specs=[FULL] * layers,
    )(place.reshape(1).astype(jnp.int32), down, *blocks)


def unpack(parts, places, chunk):
    count, total, columns = parts[0].shape
    number = count * len(parts)
    unit_rows = (total - chunk) * columns // D

    def kernel(place_ref, *refs):
        ins, gate_ref, down_ref = refs[: len(parts)], refs[-2], refs[-1]
        for which in range(len(parts)):
            for k in range(count):
                spot = place_ref[which * count + k]
                gate_ref[spot] = ins[which][k, :chunk, :]
                down_ref[spot] = unfold(ins[which][k, chunk:, :].astype(jnp.float32), D).astype(
                    jnp.bfloat16
                )

    gate, down = call(
        kernel,
        [((number, chunk, columns), jnp.bfloat16), ((number, unit_rows, D), jnp.bfloat16)],
        5.0,
        in_specs=[pl.BlockSpec(memory_space=pltpu.SMEM)] + [FULL] * len(parts),
        out_specs=[FULL] * 2,
    )(jnp.stack(places).astype(jnp.int32), *parts)
    return gate.reshape(number * chunk, columns), down.reshape(number * unit_rows, D)


def split_rows(terms, chunk, place, count):
    layers = len(terms)
    total_rows, columns = terms[0][0].shape
    rows = chunk // count
    unit_rows = (total_rows - chunk) * columns // D

    def kernel(place_ref, *refs):
        ins, outs, down_ref = refs[: 2 * layers], refs[2 * layers : -1], refs[-1]
        for layer in range(layers):
            total = ins[2 * layer][...].astype(jnp.float32) + ins[2 * layer + 1][...].astype(
                jnp.float32
            )
            down_ref[layer] = unfold(total[chunk:], D)
            for owner in range(count):
                block = total[owner * rows : owner * rows + rows].astype(jnp.bfloat16)
                for bit in range(count):

                    @pl.when(place_ref[0] == owner ^ bit)
                    def _():
                        outs[bit][layer] = block

    *blocks, down = call(
        kernel,
        [((layers, rows, columns), jnp.bfloat16)] * count
        + [((layers, unit_rows, D), jnp.float32)],
        3.0,
        in_specs=[pl.BlockSpec(memory_space=pltpu.SMEM)] + [FULL] * (2 * layers),
        out_specs=[FULL] * (count + 1),
    )(place.reshape(1).astype(jnp.int32), *[term for pair in terms for term in pair])
    return blocks, down


def assemble(parts, places, chip_rows):
    line, rows, width = parts[0].shape

    def kernel(place_ref, *refs):
        ins = refs[:8]
        first_ref, second_ref, small_ref = refs[8:]
        here, chip, side = place_ref[0] == 0, place_ref[1] == 0, place_ref[2] % 2 == 0
        mine = place_ref[2] // 2
        small = jnp.zeros((rows - chip_rows, width), jnp.float32)
        for spot in range(line):
            halves = []
            for half in range(2):
                pieces = []
                blocks = [ins[4 * half + k][spot].astype(jnp.float32) for k in range(4)]
                for block in blocks:
                    small = small + block[chip_rows:]
                lower = [jnp.where(side, blocks[2 * x], blocks[2 * x + 1]) for x in range(2)]
                upper = [jnp.where(side, blocks[2 * x + 1], blocks[2 * x]) for x in range(2)]
                for pair in (lower, upper):
                    pieces.append(jnp.where(chip, pair[0], pair[1])[:chip_rows])
                    pieces.append(jnp.where(chip, pair[1], pair[0])[:chip_rows])
                halves.append(jnp.concatenate(pieces, axis=0).astype(jnp.bfloat16))
            first_ref[mine ^ spot] = jnp.where(here, halves[0], halves[1])
            second_ref[mine ^ spot] = jnp.where(here, halves[1], halves[0])
        small_ref[...] = small

    first, second, small = call(
        kernel,
        [
            ((line, 4 * chip_rows, width), jnp.bfloat16),
            ((line, 4 * chip_rows, width), jnp.bfloat16),
            ((rows - chip_rows, width), jnp.float32),
        ],
        4.0,
        in_specs=[pl.BlockSpec(memory_space=pltpu.SMEM)] + [FULL] * 8,
        out_specs=[FULL] * 3,
    )(jnp.stack(places).astype(jnp.int32), *parts)
    return first.reshape(-1, width), second.reshape(-1, width), small


def projection_grads(normed, grad_query, grad_kv, mixed, grad_low, gain_one, gain_two, bias_one, bias_two, places, chip_rows, line):
    width = SPLIT

    def kernel(place_ref, n_ref, gq_ref, gkv_ref, mixed_ref, gy_ref, g1_ref, g2_ref, b1_ref, b2_ref, keep0, keep1, send0, send1, pad):
        here, chip, side = place_ref[0] == 0, place_ref[1] == 0, place_ref[2] % 2
        mine = place_ref[2] // 2
        turned = n_ref[...].T
        pad[...] = jnp.zeros_like(pad)
        pad[0:1, :D] = g1_ref[...]
        pad[1:2, :D] = g2_ref[...]
        pad[2:3, :] = b1_ref[...]
        pad[3:4, :KV_WIDTH] = b2_ref[...]
        small = pad[...]
        first = jnp.concatenate(
            [dot(turned, gq_ref[...]), dot(turned, gkv_ref[:, :KV_WIDTH])], axis=1
        )
        second = jnp.concatenate(
            [dot(turned, gkv_ref[:, KV_WIDTH:]), dot(mixed_ref[...], gy_ref[...], TN)], axis=1
        )

        def chunk(part, number):
            rows = part[number * chip_rows : (number + 1) * chip_rows]
            return jnp.concatenate([rows, small], axis=0).astype(jnp.bfloat16)

        for spot in range(line):
            for pair in range(2):
                slot = side ^ pair
                firsts = [chunk(first, 4 * spot + 2 * pair + x) for x in range(2)]
                seconds = [chunk(second, 4 * spot + 2 * pair + x) for x in range(2)]
                keeps = [jnp.where(here, one, two) for one, two in zip(firsts, seconds)]
                sends = [jnp.where(here, two, one) for one, two in zip(firsts, seconds)]
                keep0[slot, mine ^ spot] = jnp.where(chip, keeps[0], keeps[1])
                keep1[slot, mine ^ spot] = jnp.where(chip, keeps[1], keeps[0])
                send0[slot, mine ^ spot] = jnp.where(chip, sends[0], sends[1])
                send1[slot, mine ^ spot] = jnp.where(chip, sends[1], sends[0])

    return call(
        kernel,
        [((2, line, chip_rows + 8, width), jnp.bfloat16)] * 4,
        6.0,
        [pltpu.VMEM((8, width), jnp.float32)],
        in_specs=[pl.BlockSpec(memory_space=pltpu.SMEM)] + [FULL] * 9,
        out_specs=[FULL] * 4,
    )(
        jnp.stack(places).astype(jnp.int32),
        normed,
        grad_query,
        grad_kv,
        mixed,
        grad_low,
        gain_one,
        gain_two,
        bias_one,
        bias_two,
    )


def swap(values, axis, bit):
    size = lax.axis_size(axis)
    return lax.ppermute(values, axis, [(i, i ^ bit) for i in range(size)])


def after(values, *others):
    return lax.optimization_barrier((values,) + tuple(others))[0]


def line_bits():
    bits = [1]
    while 4 * bits[-1] < lax.axis_size("dp"):
        bits.append(2 * bits[-1])
    return bits


def line_gather(values, bits, *waited):
    for bit in bits:
        values = jnp.concatenate([values, after(swap(values, "dp", 2 * bit), *waited)], axis=0)
    return values


def line_steps(values, moves):
    return lax.ppermute(
        values, "dp", [(2 * here + side, 2 * there + side) for here, there in moves for side in range(2)]
    )


def cross_middle(values):
    line = lax.axis_size("dp") // 2
    if line == 4:
        return line_steps(values, [(1, 2), (2, 1)])
    return swap(values, "dp", line)


def line_scatter(values, bits, *waited):
    for bit in bits[:0:-1]:
        values = add_low(values[:bit], after(swap(values[bit:], "dp", 2 * bit), *waited))
    return [values[0], swap(values[1], "dp", 2)]


def add_low(left, right):
    return (left.astype(jnp.float32) + right.astype(jnp.float32)).astype(jnp.bfloat16)


def group_rows(values, *waited):
    beside = swap(values, "seq", 1)
    across = swap(values, "seq", 2)
    return [values, beside, across, swap(after(across, *waited), "seq", 1)]


def placed(values, offset, width):
    return lax.dynamic_update_slice(jnp.zeros((width,), values.dtype), values, (offset,))


def body(
    tokens,
    cotangent,
    span_order,
    attn_gain,
    joined_weight,
    joined_bias,
    out_weight,
    mlp_gain,
    gate_up_weight,
    down_weight,
):
    seq_count, tok_len, model_width = tokens.shape
    span_len = tok_len // 2
    group_count = lax.axis_size("dp")
    seq_devices = lax.axis_size("seq")
    unit_rows = down_weight.shape[1]
    width_rows = gate_up_weight.shape[1]
    units = group_count * unit_rows
    dp_place = lax.axis_index("dp")
    seq_place = lax.axis_index("seq")
    core = seq_place % 2
    chip_x = seq_place // 2
    device = dp_place * seq_devices + seq_place
    chip_rows = 2 * width_rows
    line = group_count // 2
    side = dp_place % 2
    line_place = dp_place // 2

    order = [lax.dynamic_slice(span_order, (0, seq_place ^ bit), (1, 1))[0, 0] for bit in range(4)]
    inside = jnp.arange(span_len, dtype=jnp.int32)
    own_places = jnp.concatenate(
        [order[0] * span_len + inside, (2 * seq_devices - 1 - order[0]) * span_len + inside]
    )
    half_biases = []
    for half in range(2):
        blocks = []
        for bit in range(4):
            ahead = order[bit] < order[0] if half == 0 else order[bit] > order[0]
            allowed = ahead | ((order[bit] == order[0]) & (inside[:, None] >= inside[None, :]))
            blocks.append(jnp.where(allowed, 0.0, NEGATIVE).astype(jnp.float32))
        half_biases.append(jnp.concatenate(blocks, axis=1))
    biases = jnp.stack(half_biases)
    biases_turned = jnp.swapaxes(biases, 1, 2)
    cos_table, sin_table = rotary_tables(own_places)
    cos_wide = jnp.concatenate([cos_table] * 4, axis=1)
    sin_wide = jnp.concatenate([-sin_table, sin_table] * 2, axis=1)

    def attn_shard(layer):
        first = joined_weight[layer][:, :SPLIT]
        second = jnp.concatenate([joined_weight[layer][:, SPLIT:], out_weight[layer]], axis=1)
        got = swap(jnp.where(core == 0, second, first), "seq", 1)
        mine = jnp.where(core == 0, first, second)
        rows = jnp.where(core == 0, jnp.stack([mine, got]), jnp.stack([got, mine])).reshape(
            chip_rows, -1
        )
        bias_all = placed(joined_bias[layer], device * joined_bias.shape[1], SPLIT + KV_WIDTH)
        extra = jnp.zeros((8, SPLIT), jnp.bfloat16)
        extra = extra.at[0].set(placed(attn_gain[layer], device * width_rows, SPLIT))
        extra = extra.at[1].set(placed(mlp_gain[layer], device * width_rows, SPLIT))
        extra = extra.at[2].set(bias_all[:SPLIT])
        extra = extra.at[3, :KV_WIDTH].set(bias_all[SPLIT:])
        return jnp.concatenate([rows, extra], axis=0)

    def attn_parts(own_side, other_side, *waited):
        parts = [own_side, other_side]
        return parts + [swap(after(part, *waited), "seq", 2) for part in parts]

    def attn_finish(parts):
        other_side = parts[1]
        parts = parts + [swap(after(part, other_side), "seq", 1) for part in parts]
        first_full, second_full, small = assemble(parts, [core, chip_x, dp_place], chip_rows)
        return (
            first_full,
            second_full,
            small[0:1, :model_width],
            small[1:2, :model_width],
            small[2:3],
            small[3:4, :KV_WIDTH],
        )

    bits = line_bits()
    spread = spread_columns(gate_up_weight, seq_place, unit_rows, group_count, seq_devices)
    shards = [attn_shard(layer)[None] for layer in range(LAYERS)]
    gate_blocks = [spread[0]] + [swap(spread[bit], "seq", bit) for bit in range(1, 4)]
    gate_shards = pack_rows(gate_blocks, down_weight, seq_place)
    attn_line = line_gather(after(shards[0], *spread), bits)
    attn_other = swap(after(attn_line, *gate_shards), "dp", 1)
    def outward(crossed, *waited):
        if line != 4:
            return crossed
        passed = after(line_steps(crossed, [(1, 0), (2, 3)]), *waited)
        return jnp.where((line_place == 1) | (line_place == 2), crossed, passed)

    first_parts = attn_parts(attn_line, attn_other)
    near = [line_gather(after(gate_shards[0], attn_other), bits[:-1], first_parts[3])]
    near_pair = [swap(after(near[0], attn_other), "dp", 1)]
    crossed = [cross_middle(near[0])]
    far = []
    offsets = [dp_place ^ (2 * k) for k in range(line)]
    half = line // 2
    if line == 4:
        beyond = [jnp.where(line_place < 2, 2 + k, 1 - k) * 2 + side for k in range(2)]
    else:
        beyond = offsets[half:]
    places = offsets[:half] + beyond
    places = [offsets[:half], beyond, [spot ^ 1 for spot in offsets[:half]], [spot ^ 1 for spot in beyond]]
    places = [spot for group in places for spot in group]

    def mlp_finish(layer, far_pair):
        parts = [near[layer], far[layer], near_pair[layer], far_pair]
        return unpack(parts, places, seq_devices * width_rows)

    terms = [tokens.reshape(tok_len, model_width)]
    kept_state = []
    mlp_sets = []
    attn_sets = [attn_finish(first_parts)]
    for layer in range(LAYERS):
        first_full, second_full, gain_full, mlp_gain_full, bias_first, bias_second = attn_sets[layer]
        if layer == 0:
            second_start = line_gather(after(shards[1], first_full), bits[:1])
            second_line = line_gather(second_start, bits[1:])
        x, normed, queries, own_kv = before_attention(
            terms,
            after(gain_full, near[0], second_start) if layer == 0 else after(gain_full, near_pair[1]),
            first_full,
            second_full,
            bias_first,
            bias_second,
            cos_wide,
            sin_wide,
        )
        kv_blocks = [own_kv] + [swap(own_kv, "seq", bit) for bit in range(1, 4)]
        waited = (near_pair[0], crossed[0], second_line) if layer == 0 else ()
        mixed, middle, n2 = attention(
            queries, kv_blocks, biases, x, second_full, after(mlp_gain_full, *waited)
        )
        if layer + 1 == LAYERS:
            far.append(outward(after(crossed[1], kept_state[0][7][0]), own_kv))
            far_pair = swap(far[1], "dp", 1)
            n2_parts = group_rows(n2, far_pair)
        else:
            n2_parts = group_rows(n2)
        if layer == 0:
            second_other = swap(after(second_line, n2_parts[3]), "dp", 1)
            far.append(outward(crossed[0], n2))
            far_pair = swap(far[0], "dp", 1)
            near.append(line_gather(after(gate_shards[1], n2), bits[:-1], n2_parts[3], far[0]))
            crossed.append(cross_middle(near[1]))
            attn_sets.append(attn_finish(attn_parts(second_line, second_other, n2_parts[3])))
            near_pair.append(swap(after(near[1], far_pair), "dp", 1))
        mlp_sets.append(mlp_finish(layer, far_pair))
        gu_near, *outs_near = feed_forward(n2_parts[:2], *mlp_sets[layer])
        if layer == 0:
            n2_parts[2] = after(n2_parts[2], crossed[1], gu_near)
        else:
            low_parts = group_rows(
                after(cotangent.reshape(tok_len, model_width), n2_parts[3]), gu_near
            )
        gu_far, *outs_far = feed_forward(n2_parts[2:], *mlp_sets[layer])
        across_sum = add_low(outs_far[0], swap(outs_far[1], "seq", 1))
        terms = [middle, outs_near[0], swap(outs_near[1], "seq", 1)]
        if layer + 1 < LAYERS:
            terms.append(swap(across_sum, "seq", 2))
        kept_state.append((x, normed, queries, kv_blocks, mixed, middle, n2_parts, [gu_near, gu_far]))
    upstream = cotangent.reshape(tok_len, model_width)
    states = [None] * LAYERS
    before = None

    def send_attn(state, pair, *waited):
        near, far, got_near, got_far = state["attn_parts"]
        return swap(after(add_low(far[pair], got_far[pair]), *waited), "seq", 2)

    def sum_attn(state, arrived, *waited):
        near, far, got_near, got_far = state["attn_parts"]
        return [
            (
                near[pair].astype(jnp.float32)
                + got_near[pair].astype(jnp.float32)
                + after(arrived[pair], *waited).astype(jnp.float32)
            ).astype(jnp.bfloat16)
            for pair in range(2)
        ]

    def step_one(state, *waited):
        far_sum = state["far_sum"]
        if line == 4:
            far_sum = add_low(far_sum, after(state["inward"], *waited))
        state["crossed"] = cross_middle(far_sum)
        state["near_sum"] = add_low(state["keep_near"], after(state["near_got"], *waited))

    def step_two(state, *waited):
        state["near_sum"] = add_low(state["near_sum"], after(state["crossed"], *waited))
        state["terms"] = line_scatter(state["near_sum"], bits[:-1])

    def finish(states):
        state = states[0]
        other_side = swap(after(state["attn_sums"][1], state["near_got"]), "dp", 1)
        state["owned"] = line_scatter(
            add_low(state["attn_sums"][0], other_side), bits, state["near_sum"]
        )
        owned = jnp.stack(
            [sum(term.astype(jnp.float32) for term in state["owned"]) for state in states]
        )
        extra = owned[:, chip_rows:]
        halves = owned[:, :chip_rows].reshape(LAYERS, 2, width_rows, -1)
        mine = lax.dynamic_index_in_dim(halves, core, 1, keepdims=False)
        theirs = swap(
            lax.dynamic_index_in_dim(halves, 1 - core, 1, keepdims=False), "seq", 1
        )
        first_own = jnp.where(core == 0, mine, theirs)
        second_own = jnp.where(core == 0, theirs, mine)

        def cut(row, width, stop):
            start = (0, row, device * width)
            return lax.dynamic_slice(extra[:, :, :stop], start, (LAYERS, 1, width))[:, 0]

        gate_rows, down_owned = split_rows(
            [state["terms"] for state in states], seq_devices * width_rows, seq_place, seq_devices
        )
        gate_owned = collect_columns(
            [gate_rows[0]] + [swap(gate_rows[bit], "seq", bit) for bit in range(1, 4)],
            seq_place,
            unit_rows,
            group_count,
        )
        return (
            cut(0, width_rows, model_width),
            jnp.concatenate([first_own, second_own[:, :, :KV_WIDTH]], axis=2),
            cut(2, SPLIT // (group_count * seq_devices), SPLIT),
            cut(3, KV_WIDTH // (group_count * seq_devices), KV_WIDTH),
            second_own[:, :, KV_WIDTH:],
            cut(1, width_rows, model_width),
            gate_owned,
            down_owned,
        )

    for layer in reversed(range(LAYERS)):
        x, normed, queries, kv_blocks, mixed, middle, n2_parts, gu_parts = kept_state[layer]
        first_full, second_full, gain_full, mlp_gain_full, _, _ = attn_sets[layer]
        if before is not None:
            low_parts = group_rows(upstream_low)
            low_parts[0] = after(low_parts[0], *before["attn_parts"][2:])
            attn_sent = [send_attn(before, pair, low_parts[3]) for pair in range(2)]
            last_across = swap(after(across_sum, low_parts[3]), "seq", 2)
        apart = line == 4 and layer == 0
        keep_near, send_near, own_out, across_out, pair_out, *far_parts = feed_back(
            low_parts,
            n2_parts,
            gu_parts,
            *mlp_sets[layer],
            dp_place,
            group_count,
            2 if apart else 1,
        )
        if before is not None:
            pair_out = after(pair_out, terms[2], last_across, *attn_sent, before["near_got"], before["inward"])
        got = swap(pair_out, "seq", 1)
        out_terms = [own_out, got[0], swap(add_low(across_out, got[1]), "seq", 2)]
        if apart:
            keep_far, send_far = far_parts[:2], far_parts[2:]
            got_far = [swap(after(send_far[0], got), "dp", 1), swap(send_far[1], "dp", 1)]
            far_sums = [None, add_low(keep_far[1], after(got_far[1], out_terms[2]))]
            inward = [None, line_steps(far_sums[1], [(0, 1), (3, 2)])]
        else:
            keep_far, send_far = far_parts
            got_far = swap(send_far, "dp", 1)
        if before is not None:
            step_one(before, own_out)
            before["attn_sums"] = sum_attn(before, attn_sent, own_out)
        grad_middle, grad_low, mlp_gain_part, grad_query, own_term, *kv_terms = attention_back(
            upstream,
            middle,
            mlp_gain_full,
            out_terms,
            second_full,
            queries,
            kv_blocks,
            biases_turned,
            cos_wide,
            sin_wide,
        )
        if apart:
            kv_terms[0] = after(kv_terms[0], inward[1])
        kv_terms = [own_term] + [swap(kv_terms[bit - 1], "seq", bit) for bit in range(1, 4)]
        upstream, upstream_low, grad_kv, attn_gain_part, bias_first, bias_second = before_back(
            kv_terms,
            grad_query,
            x,
            gain_full,
            grad_middle,
            first_full,
            second_full,
            cos_wide,
            sin_wide,
        )
        near_got = swap(after(send_near, grad_low), "dp", 1)
        if apart:
            across_middle = [None, cross_middle(add_low(far_sums[1], after(inward[1], grad_low)))]
            far_sums[0] = add_low(keep_far[0], after(got_far[0], grad_low))
            inward[0] = after(line_steps(far_sums[0], [(0, 1), (3, 2)]), upstream)
            across_middle[0] = cross_middle(add_low(far_sums[0], inward[0]))
            near_one = add_low(add_low(keep_near[1], near_got[1]), across_middle[1][0])
            near_zero = add_low(add_low(keep_near[0], near_got[0]), across_middle[0][0])
            state = {"near_got": near_got, "near_sum": near_one}
            state["terms"] = [near_zero, swap(near_one, "dp", 2)]
            step_two(before, far_sums[0])
        else:
            far_sum = add_low(keep_far, after(got_far, upstream if before is None else grad_low))
            state = {
                "far_sum": far_sum,
                "keep_near": keep_near,
                "near_got": near_got,
                "inward": line_steps(far_sum, [(0, 1), (3, 2)]) if line == 4 else far_sum,
            }
            if before is not None:
                step_two(before, far_sum)
        if before is not None:
            other_side = swap(after(before["attn_sums"][1], grad_low), "dp", 1)
            attn_pair = add_low(before["attn_sums"][0], after(other_side, upstream))
        near_x, far_x, near_other, far_other = projection_grads(
            normed,
            grad_query,
            grad_kv,
            mixed,
            grad_low,
            attn_gain_part,
            mlp_gain_part,
            bias_first,
            bias_second,
            [core, chip_x, dp_place],
            chip_rows,
            line,
        )
        got_far_other = swap(far_other, "seq", 1)
        got_near_other = swap(near_other, "seq", 1)
        state["attn_parts"] = (near_x, far_x, got_near_other, got_far_other)
        if before is not None:
            before["owned"] = line_scatter(
                attn_pair, bits, state["near_sum"] if apart else got_far_other
            )
        states[layer] = before = state
    if line != 4:
        step_one(before)
        step_two(before)
    arrived = [None, send_attn(before, 1)]
    arrived[0] = send_attn(before, 0)
    before["attn_sums"] = sum_attn(before, arrived)
    grads = finish(states)
    terms.append(last_across)
    activations = sum(term.astype(jnp.float32) for term in terms).astype(jnp.bfloat16)
    return (
        activations.reshape(seq_count, tok_len, model_width),
        upstream.reshape(seq_count, tok_len, model_width),
    ) + grads


def solution(mesh):
    in_specs = (
        P("dp", "seq", None),
        P("dp", "seq", None),
        P("dp", None),
        P(None, ("dp", "seq")),
        P(None, ("dp", "seq"), None),
        P(None, ("dp", "seq")),
        P(None, ("dp", "seq"), None),
        P(None, ("dp", "seq")),
        P(None, ("dp", "seq"), None),
        P(None, ("dp", "seq"), None),
    )
    out_specs = (
        P("dp", "seq", None),
        P("dp", "seq", None),
        P(None, ("dp", "seq")),
        P(None, ("dp", "seq"), None),
        P(None, ("dp", "seq")),
        P(None, ("dp", "seq")),
        P(None, ("dp", "seq"), None),
        P(None, ("dp", "seq")),
        P(None, ("dp", "seq"), None),
        P(None, ("dp", "seq"), None),
    )
    return jax.shard_map(body, mesh=mesh, in_specs=in_specs, out_specs=out_specs, check_vma=False)
```

```python
import jax
import jax.numpy as jnp
from jax import lax
from jax.experimental import pallas as pl
from jax.experimental.pallas import tpu as pltpu
from jax.sharding import PartitionSpec as P

D = 896
HEADS = 14
KV_HEADS = 2
HEAD = 64
LAYERS = 2


EPS = 1e-06
THETA = 1000000.0
NEGATIVE = -1e30


def rotary_tables(positions):
    half_head = HEAD // 2
    frequency = THETA ** (-2.0 * jnp.arange(half_head, dtype=jnp.float32) / HEAD)
    angles = positions.astype(jnp.float32)[..., None] * frequency
    return (jnp.cos(angles), jnp.sin(angles))


NT = (((1,), (1,)), ((), ()))
TN = (((0,), (0,)), ((), ()))
FULL = pl.BlockSpec(memory_space=pltpu.VMEM)
SCALE = HEAD ** (-0.5)
GROUP = HEADS // KV_HEADS
KV_WIDTH = KV_HEADS * HEAD
SPLIT = D + KV_WIDTH
TILE = 384


def dot(left, right, dims=(((1,), (0,)), ((), ()))):
    return lax.dot_general(left, right, dims, preferred_element_type=jnp.float32)


def call(kernel, outs, micros, scratch=(), limit=40, **grid):
    return pl.pallas_call(
        kernel,
        out_shape=[jax.ShapeDtypeStruct(shape, kind) for shape, kind in outs],
        scratch_shapes=list(scratch),
        compiler_params=pltpu.CompilerParams(vmem_limit_bytes=limit * 2**20),
        name=kernel.__qualname__.split(".")[0],
        cost_estimate=pl.CostEstimate(
            flops=0, bytes_accessed=int(micros * 4e3), transcendentals=0
        ),
        **grid,
    )


def turn(block, cos_wide, sin_wide):
    lane = lax.broadcasted_iota(jnp.int32, block.shape, 1)
    width = block.shape[1]
    partner = jnp.where(
        lane % HEAD < HEAD // 2,
        pltpu.roll(block, width - HEAD // 2, 1),
        pltpu.roll(block, HEAD // 2, 1),
    )
    return block * cos_wide + partner * sin_wide


def inverse_root(rows):
    return lax.rsqrt(jnp.mean(rows * rows, axis=-1, keepdims=True) + EPS)


def before_attention(terms, gain, first_full, second_full, bias_first, bias_second, cos_wide, sin_wide):
    count = len(terms)
    rows = terms[0].shape[0]
    span = rows // 2

    def kernel(*refs):
        parts = refs[:count]
        gain_ref, first_ref, second_ref, bias_one, bias_two, cos_ref, sin_ref = refs[count : count + 7]
        x_ref, n_ref, q_ref, kv_ref = refs[count + 7 :]
        x = parts[0][...].astype(jnp.float32)
        for part in parts[1:]:
            x = x + part[...].astype(jnp.float32)
        x_ref[...] = x
        normed = (x * inverse_root(x) * gain_ref[...]).astype(jnp.bfloat16)
        n_ref[...] = normed
        cos_w, sin_w = cos_ref[...], sin_ref[...]
        for tile in range(SPLIT // 128):
            lanes = slice(tile * 128, tile * 128 + 128)
            block = dot(normed, first_ref[:, lanes]) + bias_one[:, lanes]
            turned = turn(block, cos_w, sin_w)
            if tile * 128 < D:
                for part in range(2):
                    head = 2 * tile + part
                    piece = turned[:, part * HEAD : part * HEAD + HEAD].astype(jnp.bfloat16)
                    place = (head % GROUP) * span
                    for half in range(2):
                        q_ref[head // GROUP, half, place : place + span, :] = piece[
                            half * span : half * span + span
                        ]
            else:
                kv_ref[:, :KV_WIDTH] = turned.astype(jnp.bfloat16)
        kv_ref[:, KV_WIDTH:] = (
            dot(normed, second_ref[:, :KV_WIDTH]) + bias_two[...]
        ).astype(jnp.bfloat16)

    return call(
        kernel,
        [
            ((rows, D), jnp.float32),
            ((rows, D), jnp.bfloat16),
            ((KV_HEADS, 2, GROUP * span, HEAD), jnp.bfloat16),
            ((rows, 2 * KV_WIDTH), jnp.bfloat16),
        ],
        4.0,
    )(*terms, gain, first_full, second_full, bias_first, bias_second, cos_wide, sin_wide)


def key_part(kv_refs, half, lanes):
    span = kv_refs[0].shape[0] // 2
    return jnp.concatenate(
        [ref[half * span : half * span + span, lanes] for ref in kv_refs], axis=0
    )


def attention(queries, kv_blocks, biases, x, second_full, gain):
    rows = x.shape[0]
    span = rows // 2

    def kernel(q_ref, kv0, kv1, kv2, kv3, bias_ref, x_ref, w_ref, gain_ref, mixed_ref, mid_ref, n_ref):
        kvs = (kv0, kv1, kv2, kv3)
        for group in range(KV_HEADS):
            key_lanes = slice(group * HEAD, group * HEAD + HEAD)
            value_lanes = slice(KV_WIDTH + group * HEAD, KV_WIDTH + group * HEAD + HEAD)
            keys = [key_part(kvs, half, key_lanes) for half in range(2)]
            values = []
            for half in range(2):
                block = key_part(kvs, half, value_lanes)
                values.append(jnp.concatenate([block, jnp.ones_like(block)], axis=1))
            for half in range(2):
                bias = bias_ref[half]
                for member in range(GROUP):
                    query = q_ref[group, half, member * span : member * span + span, :] * jnp.bfloat16(SCALE)
                    near = dot(query, keys[half], NT) + bias
                    top = jnp.max(near, axis=-1, keepdims=True)
                    if half == 1:
                        far = dot(query, keys[0], NT)
                        top = jnp.maximum(top, jnp.max(far, axis=-1, keepdims=True))
                    total = dot(jnp.exp(near - top).astype(jnp.bfloat16), values[half])
                    if half == 1:
                        total = total + dot(jnp.exp(far - top).astype(jnp.bfloat16), values[0])
                    out = total[:, :HEAD] / total[:, HEAD : 2 * HEAD]
                    head = group * GROUP + member
                    mixed_ref[half * span : half * span + span, head * HEAD : head * HEAD + HEAD] = (
                        out.astype(jnp.bfloat16)
                    )
        middle = x_ref[...] + dot(mixed_ref[...], w_ref[:, KV_WIDTH:])
        mid_ref[...] = middle
        n_ref[...] = (middle * inverse_root(middle) * gain_ref[...]).astype(jnp.bfloat16)

    return call(
        kernel,
        [((rows, D), jnp.bfloat16), ((rows, D), jnp.float32), ((rows, D), jnp.bfloat16)],
        10.5,
    )(queries, *kv_blocks, biases, x, second_full, gain)


def feed_forward(parts, gate_up_full, down_full):
    count = len(parts)
    part_rows = parts[0].shape[0]
    rows = count * part_rows
    units = down_full.shape[0]
    steps = pl.cdiv(units, TILE)
    last = units - (steps - 1) * TILE

    def kernel(*refs):
        part_refs = refs[:count]
        w_ref, d_ref, gu_ref = refs[count : count + 3]
        out_refs, total = refs[count + 3 : -1], refs[-1]
        step = pl.program_id(0)
        n2 = jnp.concatenate([ref[...] for ref in part_refs], axis=0)

        @pl.when(step == 0)
        def _():
            total[...] = jnp.zeros_like(total)

        @pl.when(step < steps - 1)
        def _():
            both = dot(n2, w_ref[...])
            gu_ref[...] = both.astype(jnp.bfloat16)
            gate, up = both[:, :TILE], both[:, TILE:]
            hidden = (gate * jax.nn.sigmoid(gate) * up).astype(jnp.bfloat16)
            total[...] += dot(hidden, d_ref[...])

        @pl.when(step == steps - 1)
        def _():
            both = dot(n2, w_ref[:, : 2 * last])
            gu_ref[:, : 2 * last] = both.astype(jnp.bfloat16)
            gate, up = both[:, :last], both[:, last:]
            hidden = (gate * jax.nn.sigmoid(gate) * up).astype(jnp.bfloat16)
            summed = (total[...] + dot(hidden, d_ref[:last, :])).astype(jnp.bfloat16)
            for place in range(count):
                out_refs[place][...] = summed[place * part_rows : place * part_rows + part_rows]

    whole = lambda step: (0, 0)
    return call(
        kernel,
        [((rows, 2 * units), jnp.bfloat16)] + [((part_rows, D), jnp.bfloat16)] * count,
        9.0,
        [pltpu.VMEM((rows, D), jnp.float32)],
        limit=60,
        grid=(steps,),
        in_specs=[pl.BlockSpec((part_rows, D), whole)] * count
        + [
            pl.BlockSpec((D, 2 * TILE), lambda step: (0, step)),
            pl.BlockSpec((TILE, D), lambda step: (step, 0)),
        ],
        out_specs=[
            pl.BlockSpec((rows, 2 * TILE), lambda step: (0, step)),
        ]
        + [pl.BlockSpec((part_rows, D), whole)] * count,
    )(*parts, gate_up_full, down_full)


def far_slot(mine, place, line):
    if line == 4:
        return jnp.where(mine < 2, place - 2, 1 - place)
    return (mine ^ place) - line // 2


def feed_back(gz_parts, n2_parts, gu_parts, gate_up_full, down_full, dp_place, group_count, far_arrays):
    line = group_count // 2
    half = line // 2
    each = half // far_arrays
    chunk = D // group_count
    count = len(gz_parts)
    gu_count = len(gu_parts)
    part_rows = gz_parts[0].shape[0]
    rows = count * part_rows
    units = down_full.shape[0]
    unit_rows = units // group_count
    packed = chunk + unit_rows * D // (2 * units)
    once = pl.Buffered(1)
    steps = pl.cdiv(units, TILE)
    last = units - (steps - 1) * TILE

    def kernel(*refs):
        place_ref, *refs = refs
        gz_refs = refs[:count]
        n2_refs = refs[count : 2 * count]
        gu_refs = refs[2 * count : 2 * count + gu_count]
        w_ref, d_ref = refs[2 * count + gu_count : 2 * count + gu_count + 2]
        outs = refs[2 * count + gu_count + 2 : -4]
        keep_near, send_near, own_ref, across_ref, pair_ref = outs[:5]
        keep_far, send_far = outs[5 : 5 + far_arrays], outs[5 + far_arrays :]
        total, gz, n2t, down = refs[-4:]
        side, mine = place_ref[0] % 2, place_ref[0] // 2
        step = pl.program_id(0)

        @pl.when(step == 0)
        def _():
            total[...] = jnp.zeros_like(total)
            for place in range(count):
                here = slice(place * part_rows, place * part_rows + part_rows)
                gz[here, :] = gz_refs[place][...]
                n2t[:, here] = n2_refs[place][...].T

        def write(spot, even, odd, rows, lanes):
            keep = jnp.where(side == 0, even, odd)
            send = jnp.where(side == 0, odd, even)
            slot = mine ^ spot
            beyond = far_slot(mine, spot, line)

            @pl.when(slot < half)
            def _():
                keep_near[slot, rows, lanes] = keep
                send_near[slot, rows, lanes] = send

            for number in range(far_arrays):

                @pl.when((slot >= half) & (beyond // each == number))
                def _():
                    keep_far[number][beyond % each, rows, lanes] = keep
                    send_far[number][beyond % each, rows, lanes] = send

        def work(width):
            gu = jnp.concatenate([ref[:, : 2 * width] for ref in gu_refs], axis=0).astype(jnp.float32)
            gate, up = gu[:, :width], gu[:, width:]
            sig = jax.nn.sigmoid(gate)
            act = gate * sig
            hidden = (act * up).astype(jnp.bfloat16)
            down[pl.ds(pl.multiple_of(step * TILE, 128), width), :] = dot(hidden, gz[...], TN)
            grad = dot(gz[...], d_ref[:width, :], NT)
            d_gate = grad * up * (sig + act * (1.0 - sig))
            d_up = grad * act
            both = jnp.concatenate([d_gate, d_up], axis=1).astype(jnp.bfloat16)
            part = dot(n2t[...], both)
            for spot in range(line):
                even = part[2 * spot * chunk : (2 * spot + 1) * chunk].astype(jnp.bfloat16)
                odd = part[(2 * spot + 1) * chunk : (2 * spot + 2) * chunk].astype(jnp.bfloat16)
                write(spot, even, odd, slice(0, chunk), pl.ds(pl.multiple_of(step * 2 * TILE, 128), 2 * width))

            return dot(both, w_ref[:, : 2 * width], NT)

        @pl.when(step < steps - 1)
        def _():
            total[...] += work(TILE)

        @pl.when(step == steps - 1)
        def _():
            summed = (total[...] + work(last)).astype(jnp.bfloat16)
            for spot in range(line):
                even, odd = (
                    fold(down[place * unit_rows : place * unit_rows + unit_rows, :], 2 * units).astype(
                        jnp.bfloat16
                    )
                    for place in (2 * spot, 2 * spot + 1)
                )
                write(spot, even, odd, slice(chunk, packed), slice(0, 2 * units))
            own_ref[...] = summed[:part_rows]
            pair_ref[0] = summed[part_rows : 2 * part_rows]
            across_ref[...] = summed[2 * part_rows : 3 * part_rows]
            pair_ref[1] = summed[3 * part_rows :]

    whole = lambda step: (0, 0)
    return call(
        kernel,
        [
            ((half, packed, 2 * units), jnp.bfloat16),
            ((half, packed, 2 * units), jnp.bfloat16),
            ((part_rows, D), jnp.bfloat16),
            ((part_rows, D), jnp.bfloat16),
            ((2, part_rows, D), jnp.bfloat16),
        ]
        + [((each, packed, 2 * units), jnp.bfloat16)] * (2 * far_arrays),
        25.0,
        [
            pltpu.VMEM((rows, D), jnp.float32),
            pltpu.VMEM((rows, D), jnp.bfloat16),
            pltpu.VMEM((D, rows), jnp.bfloat16),
            pltpu.VMEM((units, D), jnp.float32),
        ],
        limit=60,
        grid=(steps,),
        in_specs=[pl.BlockSpec(memory_space=pltpu.SMEM)]
        + [pl.BlockSpec((part_rows, D), whole, pipeline_mode=once)] * (2 * count)
        + [pl.BlockSpec((rows // gu_count, 2 * TILE), lambda step: (0, step))] * gu_count
        + [
            pl.BlockSpec((D, 2 * TILE), lambda step: (0, step)),
            pl.BlockSpec((TILE, D), lambda step: (step, 0)),
        ],
        out_specs=[
            pl.BlockSpec((half, packed, 2 * units), lambda step: (0, 0, 0), pipeline_mode=once),
            pl.BlockSpec((half, packed, 2 * units), lambda step: (0, 0, 0), pipeline_mode=once),
            pl.BlockSpec((part_rows, D), whole, pipeline_mode=once),
            pl.BlockSpec((part_rows, D), whole, pipeline_mode=once),
            pl.BlockSpec((2, part_rows, D), lambda step: (0, 0, 0), pipeline_mode=once),
        ]
        + [pl.BlockSpec((each, packed, 2 * units), lambda step: (0, 0, 0), pipeline_mode=once)]
        * (2 * far_arrays),
    )(dp_place.reshape(1).astype(jnp.int32), *gz_parts, *n2_parts, *gu_parts, gate_up_full, down_full)


def norm_back(rows, gain, grad):
    inv_root = inverse_root(rows)
    normal = rows * inv_root
    gain_part = jnp.sum(grad * normal, axis=0, keepdims=True)
    weighted = grad * gain
    inner = jnp.mean(weighted * normal, axis=-1, keepdims=True)
    return gain_part, inv_root * (weighted - normal * inner)


def attention_back(upstream, middle, gain, terms, second_full, queries, kv_blocks, biases, cos_wide, sin_wide):
    count = len(terms)
    rows = middle.shape[0]
    span = rows // 2
    wide = GROUP * span

    def kernel(*refs):
        up_ref, mid_ref, gain_ref = refs[:3]
        term_refs = refs[3 : 3 + count]
        w_ref, q_ref, kv0, kv1, kv2, kv3, bias_ref, cos_ref, sin_ref = refs[3 + count : 12 + count]
        gm_ref, gy_ref, dgain_ref, gq_ref, own_ref, d1, d2, d3, go_ref, dkv = refs[12 + count :]
        kvs = (kv0, kv1, kv2, kv3)
        grad = term_refs[0][...].astype(jnp.float32)
        for term in term_refs[1:]:
            grad = grad + term[...].astype(jnp.float32)
        gain_part, back = norm_back(mid_ref[...], gain_ref[...], grad)
        dgain_ref[...] = gain_part
        grad_middle = up_ref[...].astype(jnp.float32) + back
        gm_ref[...] = grad_middle
        grad_low = grad_middle.astype(jnp.bfloat16)
        gy_ref[...] = grad_low
        for tile in range(D // 128):
            start = KV_WIDTH
            block = dot(grad_low, w_ref[tile * 128 : tile * 128 + 128, start:], NT).astype(jnp.bfloat16)
            for part in range(2):
                head = 2 * tile + part
                place = (head % GROUP) * span
                for half in range(2):
                    go_ref[head // GROUP, half, place : place + span, :] = block[
                        half * span : half * span + span, part * HEAD : part * HEAD + HEAD
                    ]
        for group in range(KV_HEADS):
            key_lanes = slice(group * HEAD, group * HEAD + HEAD)
            value_lanes = slice(KV_WIDTH + group * HEAD, KV_WIDTH + group * HEAD + HEAD)
            keys = [key_part(kvs, half, key_lanes) for half in range(2)]
            values = [key_part(kvs, half, value_lanes) for half in range(2)]
            for half in range(2):
                query = q_ref[group, half] * jnp.bfloat16(SCALE)
                grad_out = go_ref[group, half]
                bias = jnp.concatenate([bias_ref[half]] * GROUP, axis=1)
                use = [half] if half == 0 else [1, 0]
                scores = []
                top = None
                for which in use:
                    score = dot(keys[which], query, NT)
                    if which == half:
                        score = score + bias
                    scores.append(score)
                    best = jnp.max(score, axis=0, keepdims=True)
                    top = best if top is None else jnp.maximum(top, best)
                weights = [jnp.exp(score - top) for score in scores]
                total = sum(jnp.sum(weight, axis=0, keepdims=True) for weight in weights)
                scale = 1.0 / total
                probs = [weight * scale for weight in weights]
                grads = [dot(values[which], grad_out, NT) for which in use]
                inner = sum(
                    jnp.sum(prob * grad_prob, axis=0, keepdims=True)
                    for prob, grad_prob in zip(probs, grads)
                )
                grad_query = None
                for which, prob, grad_prob in zip(use, probs, grads):
                    grad_score = (prob * (grad_prob - inner)).astype(jnp.bfloat16)
                    value_grad = dot(prob.astype(jnp.bfloat16), grad_out)
                    key_grad = dot(grad_score, query)
                    if half == 0:
                        dkv[group, which] = key_grad
                        dkv[KV_HEADS + group, which] = value_grad
                    elif which == 0:
                        dkv[group, which] += key_grad
                        dkv[KV_HEADS + group, which] += value_grad
                    else:
                        dkv[group, which] = key_grad
                        dkv[KV_HEADS + group, which] = value_grad
                    term = dot(keys[which].T, grad_score)
                    grad_query = term if grad_query is None else grad_query + term
                grad_query = grad_query * SCALE
                cos_w = cos_ref[half * span : half * span + span, :]
                sin_w = sin_ref[half * span : half * span + span, :]
                for member in range(GROUP):
                    head = group * GROUP + member
                    piece = grad_query[:, member * span : member * span + span].T
                    pair = jnp.concatenate([piece, piece], axis=1)
                    turned = turn(pair, cos_w, -sin_w)[:, :HEAD]
                    gq_ref[half * span : half * span + span, head * HEAD : head * HEAD + HEAD] = (
                        turned.astype(jnp.bfloat16)
                    )
        for place, out in enumerate((own_ref, d1, d2, d3)):
            for half in range(2):
                block = jnp.concatenate(
                    [dkv[lane, half, place * span : place * span + span, :] for lane in range(2 * KV_HEADS)],
                    axis=1,
                )
                out[half * span : half * span + span, :] = block.astype(out.dtype)

    return call(
        kernel,
        [
            ((rows, D), jnp.float32),
            ((rows, D), jnp.bfloat16),
            ((1, D), jnp.float32),
            ((rows, D), jnp.bfloat16),
            ((rows, 2 * KV_WIDTH), jnp.float32),
        ]
        + [((rows, 2 * KV_WIDTH), jnp.bfloat16)] * 3,
        13.0,
        [
            pltpu.VMEM((KV_HEADS, 2, wide, HEAD), jnp.bfloat16),
            pltpu.VMEM((2 * KV_HEADS, 2, 4 * span, HEAD), jnp.float32),
        ],
    )(upstream, middle, gain, *terms, second_full, queries, *kv_blocks, biases, cos_wide, sin_wide)


def before_back(kv_terms, gq, x, gain, grad_middle, first_full, second_full, cos_wide, sin_wide):
    rows = x.shape[0]
    count = len(kv_terms)

    def kernel(*refs):
        kv_refs = refs[:count]
        gq_ref, x_ref, gain_ref, gm_ref, w1_ref, w2_ref, cos_ref, sin_ref = refs[count : count + 8]
        up_ref, low_ref, gkv_ref, dgain_ref, bias_one, bias_two = refs[count + 8 :]
        grad = kv_refs[0][...].astype(jnp.float32)
        for ref in kv_refs[1:]:
            grad = grad + ref[...].astype(jnp.float32)
        grad_key = turn(grad[:, :KV_WIDTH], cos_ref[...], -sin_ref[...]).astype(jnp.bfloat16)
        grad_value = grad[:, KV_WIDTH:].astype(jnp.bfloat16)
        gkv_ref[:, :KV_WIDTH] = grad_key
        gkv_ref[:, KV_WIDTH:] = grad_value
        grad_query = gq_ref[...]
        bias_one[:, :D] = jnp.sum(grad_query.astype(jnp.float32), axis=0, keepdims=True)
        bias_one[:, D:] = jnp.sum(grad_key.astype(jnp.float32), axis=0, keepdims=True)
        bias_two[...] = jnp.sum(grad_value.astype(jnp.float32), axis=0, keepdims=True)
        grad_normed = (
            dot(grad_query, w1_ref[:, :D], NT)
            + dot(grad_key, w1_ref[:, D:], NT)
            + dot(grad_value, w2_ref[:, :KV_WIDTH], NT)
        )
        gain_part, back = norm_back(x_ref[...], gain_ref[...], grad_normed)
        dgain_ref[...] = gain_part
        upstream = gm_ref[...] + back
        up_ref[...] = upstream
        low_ref[...] = upstream.astype(jnp.bfloat16)

    return call(
        kernel,
        [
            ((rows, D), jnp.float32),
            ((rows, D), jnp.bfloat16),
            ((rows, 2 * KV_WIDTH), jnp.bfloat16),
            ((1, D), jnp.float32),
            ((1, SPLIT), jnp.float32),
            ((1, KV_WIDTH), jnp.float32),
        ],
        2.4,
    )(*kv_terms, gq, x, gain, grad_middle, first_full, second_full, cos_wide, sin_wide)


def unit_pieces(unit_rows, group_count, seq_devices):
    units = unit_rows * group_count
    steps = pl.cdiv(units, TILE)
    pieces = []
    for owner in range(seq_devices):
        for kind in range(2):
            for group in range(group_count):
                unit = group * unit_rows
                stop = unit + unit_rows
                column = kind * units * seq_devices + (group * seq_devices + owner) * unit_rows
                while unit < stop:
                    step = unit // TILE
                    end = min(stop, (step + 1) * TILE)
                    width = TILE if step < steps - 1 else units - (steps - 1) * TILE
                    inside = 2 * step * TILE + kind * width + unit - step * TILE
                    pieces.append((owner, inside, column, end - unit))
                    column += end - unit
                    unit = end
    return pieces


def spread_columns(weight, place, unit_rows, group_count, seq_devices):
    layers, rows, columns = weight.shape
    quarter = columns // seq_devices
    pieces = unit_pieces(unit_rows, group_count, seq_devices)

    def kernel(place_ref, w_ref, *refs):
        outs, wide, narrow = refs[:seq_devices], refs[-2], refs[-1]
        for layer in range(layers):
            wide[...] = w_ref[layer].astype(jnp.float32)
            for owner in range(seq_devices):
                for who, inside, column, width in pieces:
                    if who == owner:
                        narrow[:, inside : inside + width] = wide[:, column : column + width]
                block = narrow[...].astype(jnp.bfloat16)
                for bit in range(seq_devices):

                    @pl.when(place_ref[0] == owner ^ bit)
                    def _():
                        outs[bit][layer] = block

    return call(
        kernel,
        [((layers, rows, quarter), jnp.bfloat16)] * seq_devices,
        2.5,
        [pltpu.VMEM((rows, columns), jnp.float32), pltpu.VMEM((rows, quarter), jnp.float32)],
        in_specs=[pl.BlockSpec(memory_space=pltpu.SMEM), FULL],
        out_specs=[FULL] * seq_devices,
    )(place.reshape(1).astype(jnp.int32), weight)


def collect_columns(blocks, place, unit_rows, group_count):
    count = len(blocks)
    layers, rows, quarter = blocks[0].shape
    pieces = unit_pieces(unit_rows, group_count, count)

    def kernel(place_ref, *refs):
        out_ref, narrow = refs[count:]
        me = place_ref[0]
        for layer in range(layers):
            for owner in range(count):
                for bit in range(count):

                    @pl.when(me == owner ^ bit)
                    def _():
                        narrow[...] = refs[bit][layer].astype(jnp.float32)

                for who, inside, column, width in pieces:
                    if who == owner:
                        out_ref[layer, :, column : column + width] = narrow[:, inside : inside + width]

    return call(
        kernel,
        [((layers, rows, count * quarter), jnp.float32)],
        1.5,
        [pltpu.VMEM((rows, quarter), jnp.float32)],
        in_specs=[pl.BlockSpec(memory_space=pltpu.SMEM)] + [FULL] * count,
        out_specs=[FULL],
    )(place.reshape(1).astype(jnp.int32), *blocks)[0]


def fold(rows, columns):
    high = rows.shape[0] * 128 // columns
    wide = rows.shape[1] // 128
    return jnp.concatenate(
        [
            jnp.concatenate(
                [rows[high * r : high * r + high, 128 * c : 128 * c + 128] for r in range(columns // 128)],
                axis=1,
            )
            for c in range(wide)
        ],
        axis=0,
    )


def unfold(rows, width):
    high = rows.shape[0] * 128 // width
    wide = rows.shape[1] // 128
    return jnp.concatenate(
        [
            jnp.concatenate(
                [rows[high * c : high * c + high, 128 * r : 128 * r + 128] for c in range(width // 128)],
                axis=1,
            )
            for r in range(wide)
        ],
        axis=0,
    )


def pack_rows(blocks, down, place):
    owners = len(blocks)
    layers, rows, columns = blocks[0].shape
    total = owners * rows + down.shape[1] * down.shape[2] // columns

    def kernel(place_ref, down_ref, *refs):
        ins, outs = refs[:owners], refs[owners:]
        for layer in range(layers):
            parts = []
            for owner in range(owners):
                part = ins[0][layer].astype(jnp.float32)
                for bit in range(1, owners):
                    part = jnp.where(
                        place_ref[0] == owner ^ bit, ins[bit][layer].astype(jnp.float32), part
                    )
                parts.append(part)
            parts.append(fold(down_ref[layer].astype(jnp.float32), columns))
            outs[layer][0] = jnp.concatenate(parts, axis=0).astype(jnp.bfloat16)

    return call(
        kernel,
        [((1, total, columns), jnp.bfloat16)] * layers,
        3.0,
        in_specs=[pl.BlockSpec(memory_space=pltpu.SMEM)] + [FULL] * (owners + 1),
        out_specs=[FULL] * layers,
    )(place.reshape(1).astype(jnp.int32), down, *blocks)


def unpack(parts, places, chunk):
    count, total, columns = parts[0].shape
    number = count * len(parts)
    unit_rows = (total - chunk) * columns // D

    def kernel(place_ref, *refs):
        ins, gate_ref, down_ref = refs[: len(parts)], refs[-2], refs[-1]
        for which in range(len(parts)):
            for k in range(count):
                spot = place_ref[which * count + k]
                gate_ref[spot] = ins[which][k, :chunk, :]
                down_ref[spot] = unfold(ins[which][k, chunk:, :].astype(jnp.float32), D).astype(
                    jnp.bfloat16
                )

    gate, down = call(
        kernel,
        [((number, chunk, columns), jnp.bfloat16), ((number, unit_rows, D), jnp.bfloat16)],
        5.0,
        in_specs=[pl.BlockSpec(memory_space=pltpu.SMEM)] + [FULL] * len(parts),
        out_specs=[FULL] * 2,
    )(jnp.stack(places).astype(jnp.int32), *parts)
    return gate.reshape(number * chunk, columns), down.reshape(number * unit_rows, D)


def split_rows(terms, chunk, place, count):
    layers = len(terms)
    total_rows, columns = terms[0][0].shape
    rows = chunk // count
    unit_rows = (total_rows - chunk) * columns // D

    def kernel(place_ref, *refs):
        ins, outs, down_ref = refs[: 2 * layers], refs[2 * layers : -1], refs[-1]
        for layer in range(layers):
            total = ins[2 * layer][...].astype(jnp.float32) + ins[2 * layer + 1][...].astype(
                jnp.float32
            )
            down_ref[layer] = unfold(total[chunk:], D)
            for owner in range(count):
                block = total[owner * rows : owner * rows + rows].astype(jnp.bfloat16)
                for bit in range(count):

                    @pl.when(place_ref[0] == owner ^ bit)
                    def _():
                        outs[bit][layer] = block

    *blocks, down = call(
        kernel,
        [((layers, rows, columns), jnp.bfloat16)] * count
        + [((layers, unit_rows, D), jnp.float32)],
        3.0,
        in_specs=[pl.BlockSpec(memory_space=pltpu.SMEM)] + [FULL] * (2 * layers),
        out_specs=[FULL] * (count + 1),
    )(place.reshape(1).astype(jnp.int32), *[term for pair in terms for term in pair])
    return blocks, down


def assemble(parts, places, chip_rows):
    line, rows, width = parts[0].shape

    def kernel(place_ref, *refs):
        ins = refs[:8]
        first_ref, second_ref, small_ref = refs[8:]
        here, chip, side = place_ref[0] == 0, place_ref[1] == 0, place_ref[2] % 2 == 0
        mine = place_ref[2] // 2
        small = jnp.zeros((rows - chip_rows, width), jnp.float32)
        for spot in range(line):
            halves = []
            for half in range(2):
                pieces = []
                blocks = [ins[4 * half + k][spot].astype(jnp.float32) for k in range(4)]
                for block in blocks:
                    small = small + block[chip_rows:]
                lower = [jnp.where(side, blocks[2 * x], blocks[2 * x + 1]) for x in range(2)]
                upper = [jnp.where(side, blocks[2 * x + 1], blocks[2 * x]) for x in range(2)]
                for pair in (lower, upper):
                    pieces.append(jnp.where(chip, pair[0], pair[1])[:chip_rows])
                    pieces.append(jnp.where(chip, pair[1], pair[0])[:chip_rows])
                halves.append(jnp.concatenate(pieces, axis=0).astype(jnp.bfloat16))
            first_ref[mine ^ spot] = jnp.where(here, halves[0], halves[1])
            second_ref[mine ^ spot] = jnp.where(here, halves[1], halves[0])
        small_ref[...] = small

    first, second, small = call(
        kernel,
        [
            ((line, 4 * chip_rows, width), jnp.bfloat16),
            ((line, 4 * chip_rows, width), jnp.bfloat16),
            ((rows - chip_rows, width), jnp.float32),
        ],
        4.0,
        in_specs=[pl.BlockSpec(memory_space=pltpu.SMEM)] + [FULL] * 8,
        out_specs=[FULL] * 3,
    )(jnp.stack(places).astype(jnp.int32), *parts)
    return first.reshape(-1, width), second.reshape(-1, width), small


def projection_grads(normed, grad_query, grad_kv, mixed, grad_low, gain_one, gain_two, bias_one, bias_two, places, chip_rows, line):
    width = SPLIT

    def kernel(place_ref, n_ref, gq_ref, gkv_ref, mixed_ref, gy_ref, g1_ref, g2_ref, b1_ref, b2_ref, keep0, keep1, send0, send1, pad):
        here, chip, side = place_ref[0] == 0, place_ref[1] == 0, place_ref[2] % 2
        mine = place_ref[2] // 2
        turned = n_ref[...].T
        pad[...] = jnp.zeros_like(pad)
        pad[0:1, :D] = g1_ref[...]
        pad[1:2, :D] = g2_ref[...]
        pad[2:3, :] = b1_ref[...]
        pad[3:4, :KV_WIDTH] = b2_ref[...]
        small = pad[...]
        first = jnp.concatenate(
            [dot(turned, gq_ref[...]), dot(turned, gkv_ref[:, :KV_WIDTH])], axis=1
        )
        second = jnp.concatenate(
            [dot(turned, gkv_ref[:, KV_WIDTH:]), dot(mixed_ref[...], gy_ref[...], TN)], axis=1
        )

        def chunk(part, number):
            rows = part[number * chip_rows : (number + 1) * chip_rows]
            return jnp.concatenate([rows, small], axis=0).astype(jnp.bfloat16)

        for spot in range(line):
            for pair in range(2):
                slot = side ^ pair
                firsts = [chunk(first, 4 * spot + 2 * pair + x) for x in range(2)]
                seconds = [chunk(second, 4 * spot + 2 * pair + x) for x in range(2)]
                keeps = [jnp.where(here, one, two) for one, two in zip(firsts, seconds)]
                sends = [jnp.where(here, two, one) for one, two in zip(firsts, seconds)]
                keep0[slot, mine ^ spot] = jnp.where(chip, keeps[0], keeps[1])
                keep1[slot, mine ^ spot] = jnp.where(chip, keeps[1], keeps[0])
                send0[slot, mine ^ spot] = jnp.where(chip, sends[0], sends[1])
                send1[slot, mine ^ spot] = jnp.where(chip, sends[1], sends[0])

    return call(
        kernel,
        [((2, line, chip_rows + 8, width), jnp.bfloat16)] * 4,
        6.0,
        [pltpu.VMEM((8, width), jnp.float32)],
        in_specs=[pl.BlockSpec(memory_space=pltpu.SMEM)] + [FULL] * 9,
        out_specs=[FULL] * 4,
    )(
        jnp.stack(places).astype(jnp.int32),
        normed,
        grad_query,
        grad_kv,
        mixed,
        grad_low,
        gain_one,
        gain_two,
        bias_one,
        bias_two,
    )


def swap(values, axis, bit):
    size = lax.axis_size(axis)
    return lax.ppermute(values, axis, [(i, i ^ bit) for i in range(size)])


def after(values, *others):
    return lax.optimization_barrier((values,) + tuple(others))[0]


def line_bits():
    bits = [1]
    while 4 * bits[-1] < lax.axis_size("dp"):
        bits.append(2 * bits[-1])
    return bits


def line_gather(values, bits, *waited):
    for bit in bits:
        values = jnp.concatenate([values, after(swap(values, "dp", 2 * bit), *waited)], axis=0)
    return values


def line_steps(values, moves):
    return lax.ppermute(
        values, "dp", [(2 * here + side, 2 * there + side) for here, there in moves for side in range(2)]
    )


def cross_middle(values):
    line = lax.axis_size("dp") // 2
    if line == 4:
        return line_steps(values, [(1, 2), (2, 1)])
    return swap(values, "dp", line)


def line_scatter(values, bits, *waited):
    for bit in bits[:0:-1]:
        values = add_low(values[:bit], after(swap(values[bit:], "dp", 2 * bit), *waited))
    return [values[0], swap(values[1], "dp", 2)]


def add_low(left, right):
    return (left.astype(jnp.float32) + right.astype(jnp.float32)).astype(jnp.bfloat16)


def group_rows(values, *waited):
    beside = swap(values, "seq", 1)
    across = swap(values, "seq", 2)
    return [values, beside, across, swap(after(across, *waited), "seq", 1)]


def placed(values, offset, width):
    return lax.dynamic_update_slice(jnp.zeros((width,), values.dtype), values, (offset,))


def body(
    tokens,
    cotangent,
    span_order,
    attn_gain,
    joined_weight,
    joined_bias,
    out_weight,
    mlp_gain,
    gate_up_weight,
    down_weight,
):
    seq_count, tok_len, model_width = tokens.shape
    span_len = tok_len // 2
    group_count = lax.axis_size("dp")
    seq_devices = lax.axis_size("seq")
    unit_rows = down_weight.shape[1]
    width_rows = gate_up_weight.shape[1]
    units = group_count * unit_rows
    dp_place = lax.axis_index("dp")
    seq_place = lax.axis_index("seq")
    core = seq_place % 2
    chip_x = seq_place // 2
    device = dp_place * seq_devices + seq_place
    chip_rows = 2 * width_rows
    line = group_count // 2
    side = dp_place % 2
    line_place = dp_place // 2

    order = [lax.dynamic_slice(span_order, (0, seq_place ^ bit), (1, 1))[0, 0] for bit in range(4)]
    inside = jnp.arange(span_len, dtype=jnp.int32)
    own_places = jnp.concatenate(
        [order[0] * span_len + inside, (2 * seq_devices - 1 - order[0]) * span_len + inside]
    )
    half_biases = []
    for half in range(2):
        blocks = []
        for bit in range(4):
            ahead = order[bit] < order[0] if half == 0 else order[bit] > order[0]
            allowed = ahead | ((order[bit] == order[0]) & (inside[:, None] >= inside[None, :]))
            blocks.append(jnp.where(allowed, 0.0, NEGATIVE).astype(jnp.float32))
        half_biases.append(jnp.concatenate(blocks, axis=1))
    biases = jnp.stack(half_biases)
    biases_turned = jnp.swapaxes(biases, 1, 2)
    cos_table, sin_table = rotary_tables(own_places)
    cos_wide = jnp.concatenate([cos_table] * 4, axis=1)
    sin_wide = jnp.concatenate([-sin_table, sin_table] * 2, axis=1)

    def attn_shard(layer):
        first = joined_weight[layer][:, :SPLIT]
        second = jnp.concatenate([joined_weight[layer][:, SPLIT:], out_weight[layer]], axis=1)
        got = swap(jnp.where(core == 0, second, first), "seq", 1)
        mine = jnp.where(core == 0, first, second)
        rows = jnp.where(core == 0, jnp.stack([mine, got]), jnp.stack([got, mine])).reshape(
            chip_rows, -1
        )
        bias_all = placed(joined_bias[layer], device * joined_bias.shape[1], SPLIT + KV_WIDTH)
        extra = jnp.zeros((8, SPLIT), jnp.bfloat16)
        extra = extra.at[0].set(placed(attn_gain[layer], device * width_rows, SPLIT))
        extra = extra.at[1].set(placed(mlp_gain[layer], device * width_rows, SPLIT))
        extra = extra.at[2].set(bias_all[:SPLIT])
        extra = extra.at[3, :KV_WIDTH].set(bias_all[SPLIT:])
        return jnp.concatenate([rows, extra], axis=0)

    def attn_parts(own_side, other_side, *waited):
        parts = [own_side, other_side]
        return parts + [swap(after(part, *waited), "seq", 2) for part in parts]

    def attn_finish(parts):
        other_side = parts[1]
        parts = parts + [swap(after(part, other_side), "seq", 1) for part in parts]
        first_full, second_full, small = assemble(parts, [core, chip_x, dp_place], chip_rows)
        return (
            first_full,
            second_full,
            small[0:1, :model_width],
            small[1:2, :model_width],
            small[2:3],
            small[3:4, :KV_WIDTH],
        )

    bits = line_bits()
    spread = spread_columns(gate_up_weight, seq_place, unit_rows, group_count, seq_devices)
    shards = [attn_shard(layer)[None] for layer in range(LAYERS)]
    gate_blocks = [spread[0]] + [swap(spread[bit], "seq", bit) for bit in range(1, 4)]
    gate_shards = pack_rows(gate_blocks, down_weight, seq_place)
    attn_line = line_gather(after(shards[0], *spread), bits)
    attn_other = swap(after(attn_line, *gate_shards), "dp", 1)
    def outward(crossed, *waited):
        if line != 4:
            return crossed
        passed = after(line_steps(crossed, [(1, 0), (2, 3)]), *waited)
        return jnp.where((line_place == 1) | (line_place == 2), crossed, passed)

    first_parts = attn_parts(attn_line, attn_other)
    near = [line_gather(after(gate_shards[0], attn_other), bits[:-1], first_parts[3])]
    near_pair = [swap(after(near[0], attn_other), "dp", 1)]
    crossed = [cross_middle(near[0])]
    far = []
    offsets = [dp_place ^ (2 * k) for k in range(line)]
    half = line // 2
    if line == 4:
        beyond = [jnp.where(line_place < 2, 2 + k, 1 - k) * 2 + side for k in range(2)]
    else:
        beyond = offsets[half:]
    places = offsets[:half] + beyond
    places = [offsets[:half], beyond, [spot ^ 1 for spot in offsets[:half]], [spot ^ 1 for spot in beyond]]
    places = [spot for group in places for spot in group]

    def mlp_finish(layer, far_pair):
        parts = [near[layer], far[layer], near_pair[layer], far_pair]
        return unpack(parts, places, seq_devices * width_rows)

    terms = [tokens.reshape(tok_len, model_width)]
    kept_state = []
    mlp_sets = []
    attn_sets = [attn_finish(first_parts)]
    for layer in range(LAYERS):
        first_full, second_full, gain_full, mlp_gain_full, bias_first, bias_second = attn_sets[layer]
        x, normed, queries, own_kv = before_attention(
            terms,
            after(gain_full, near[0]) if layer == 0 else after(gain_full, near_pair[1]),
            first_full,
            second_full,
            bias_first,
            bias_second,
            cos_wide,
            sin_wide,
        )
        kv_blocks = [own_kv] + [swap(own_kv, "seq", bit) for bit in range(1, 4)]
        waited = (near_pair[0],) if layer == 0 else ()
        mixed, middle, n2 = attention(
            queries, kv_blocks, biases, x, second_full, after(mlp_gain_full, *waited)
        )
        if layer + 1 == LAYERS:
            far.append(outward(after(crossed[1], kept_state[0][7][0]), own_kv))
            far_pair = swap(far[1], "dp", 1)
            n2_parts = group_rows(n2, far_pair)
        else:
            far.append(outward(crossed[0], n2))
            far_pair = swap(far[0], "dp", 1)
            n2_parts = group_rows(after(n2, far[0]))
            second_start = line_gather(after(shards[1], n2_parts[2]), bits[:1])
            second_line = line_gather(second_start, bits[1:])
            second_other = swap(after(second_line, n2_parts[3]), "dp", 1)
            near.append(line_gather(after(gate_shards[1], second_start), bits[:-1], n2_parts[3]))
            crossed.append(cross_middle(after(near[1], second_line)))
            attn_sets.append(attn_finish(attn_parts(second_line, second_other, n2_parts[3])))
            near_pair.append(swap(after(near[1], far_pair), "dp", 1))
        mlp_sets.append(mlp_finish(layer, far_pair))
        gu_near, *outs_near = feed_forward(n2_parts[:2], *mlp_sets[layer])
        if layer == 0:
            n2_parts[2] = after(n2_parts[2], crossed[1], gu_near)
        else:
            low_parts = group_rows(
                after(cotangent.reshape(tok_len, model_width), n2_parts[3]), gu_near
            )
        gu_far, *outs_far = feed_forward(n2_parts[2:], *mlp_sets[layer])
        across_sum = add_low(outs_far[0], swap(outs_far[1], "seq", 1))
        terms = [middle, outs_near[0], swap(outs_near[1], "seq", 1)]
        if layer + 1 < LAYERS:
            terms.append(swap(across_sum, "seq", 2))
        kept_state.append((x, normed, queries, kv_blocks, mixed, middle, n2_parts, [gu_near, gu_far]))
    upstream = cotangent.reshape(tok_len, model_width)
    states = [None] * LAYERS
    before = None

    def send_attn(state, pair, *waited):
        near, far, got_near, got_far = state["attn_parts"]
        return swap(after(add_low(far[pair], got_far[pair]), *waited), "seq", 2)

    def sum_attn(state, arrived, *waited):
        near, far, got_near, got_far = state["attn_parts"]
        return [
            (
                near[pair].astype(jnp.float32)
                + got_near[pair].astype(jnp.float32)
                + after(arrived[pair], *waited).astype(jnp.float32)
            ).astype(jnp.bfloat16)
            for pair in range(2)
        ]

    def step_one(state, *waited):
        far_sum = state["far_sum"]
        if line == 4:
            far_sum = add_low(far_sum, after(state["inward"], *waited))
        state["crossed"] = cross_middle(far_sum)
        state["near_sum"] = add_low(state["keep_near"], after(state["near_got"], *waited))

    def step_two(state, *waited):
        state["near_sum"] = add_low(state["near_sum"], after(state["crossed"], *waited))
        state["terms"] = line_scatter(state["near_sum"], bits[:-1])

    def finish(states):
        gate_rows, down_owned = split_rows(
            [state["terms"] for state in states], seq_devices * width_rows, seq_place, seq_devices
        )
        state = states[0]
        other_side = swap(after(state["attn_sums"][1], state["near_got"]), "dp", 1)
        state["owned"] = line_scatter(
            add_low(state["attn_sums"][0], other_side), bits, state["near_sum"]
        )
        owned = jnp.stack(
            [
                state["owned"][0].astype(jnp.float32)
                + after(state["owned"][1], gate_rows[0]).astype(jnp.float32)
                for state in states
            ]
        )
        extra = owned[:, chip_rows:]
        halves = owned[:, :chip_rows].reshape(LAYERS, 2, width_rows, -1)
        mine = lax.dynamic_index_in_dim(halves, core, 1, keepdims=False)
        theirs = swap(
            lax.dynamic_index_in_dim(halves, 1 - core, 1, keepdims=False), "seq", 1
        )
        first_own = jnp.where(core == 0, mine, theirs)
        second_own = jnp.where(core == 0, theirs, mine)

        def cut(row, width, stop):
            start = (0, row, device * width)
            return lax.dynamic_slice(extra[:, :, :stop], start, (LAYERS, 1, width))[:, 0]

        gate_owned = collect_columns(
            [gate_rows[0]] + [swap(gate_rows[bit], "seq", bit) for bit in range(1, 4)],
            seq_place,
            unit_rows,
            group_count,
        )
        return (
            cut(0, width_rows, model_width),
            jnp.concatenate([first_own, second_own[:, :, :KV_WIDTH]], axis=2),
            cut(2, SPLIT // (group_count * seq_devices), SPLIT),
            cut(3, KV_WIDTH // (group_count * seq_devices), KV_WIDTH),
            second_own[:, :, KV_WIDTH:],
            cut(1, width_rows, model_width),
            gate_owned,
            down_owned,
        )

    for layer in reversed(range(LAYERS)):
        x, normed, queries, kv_blocks, mixed, middle, n2_parts, gu_parts = kept_state[layer]
        first_full, second_full, gain_full, mlp_gain_full, _, _ = attn_sets[layer]
        if before is not None:
            low_parts = group_rows(upstream_low)
            low_parts[0] = after(low_parts[0], *before["attn_parts"][2:])
            attn_sent = [send_attn(before, pair, low_parts[3]) for pair in range(2)]
            last_across = swap(after(across_sum, low_parts[3]), "seq", 2)
        apart = line == 4 and layer == 0
        keep_near, send_near, own_out, across_out, pair_out, *far_parts = feed_back(
            low_parts,
            n2_parts,
            gu_parts,
            *mlp_sets[layer],
            dp_place,
            group_count,
            2 if apart else 1,
        )
        if before is not None:
            pair_out = after(pair_out, terms[2], last_across, *attn_sent, before["near_got"], before["inward"])
        got = swap(pair_out, "seq", 1)
        out_terms = [own_out, got[0], swap(add_low(across_out, got[1]), "seq", 2)]
        if apart:
            keep_far, send_far = far_parts[:2], far_parts[2:]
            got_far = [swap(after(send_far[0], got), "dp", 1), swap(send_far[1], "dp", 1)]
            far_sums = [None, add_low(keep_far[1], after(got_far[1], out_terms[2]))]
            inward = [None, line_steps(far_sums[1], [(0, 1), (3, 2)])]
        else:
            keep_far, send_far = far_parts
            got_far = swap(send_far, "dp", 1)
        if before is not None:
            step_one(before, own_out)
            before["attn_sums"] = sum_attn(before, attn_sent, own_out)
        grad_middle, grad_low, mlp_gain_part, grad_query, own_term, *kv_terms = attention_back(
            upstream,
            middle,
            mlp_gain_full,
            out_terms,
            second_full,
            queries,
            kv_blocks,
            biases_turned,
            cos_wide,
            sin_wide,
        )
        if apart:
            kv_terms[0] = after(kv_terms[0], inward[1])
        kv_terms = [own_term] + [swap(kv_terms[bit - 1], "seq", bit) for bit in range(1, 4)]
        upstream, upstream_low, grad_kv, attn_gain_part, bias_first, bias_second = before_back(
            kv_terms,
            grad_query,
            x,
            gain_full,
            grad_middle,
            first_full,
            second_full,
            cos_wide,
            sin_wide,
        )
        near_got = swap(after(send_near, grad_low), "dp", 1)
        if apart:
            across_middle = [None, cross_middle(add_low(far_sums[1], after(inward[1], grad_low)))]
            far_sums[0] = add_low(keep_far[0], after(got_far[0], grad_low))
            inward[0] = after(line_steps(far_sums[0], [(0, 1), (3, 2)]), upstream)
            across_middle[0] = cross_middle(add_low(far_sums[0], inward[0]))
            near_one = add_low(add_low(keep_near[1], near_got[1]), across_middle[1][0])
            near_zero = add_low(add_low(keep_near[0], near_got[0]), across_middle[0][0])
            state = {"near_got": near_got, "near_sum": near_one}
            state["terms"] = [near_zero, swap(near_one, "dp", 2)]
            step_two(before, far_sums[0])
        else:
            far_sum = add_low(keep_far, after(got_far, upstream if before is None else grad_low))
            state = {
                "far_sum": far_sum,
                "keep_near": keep_near,
                "near_got": near_got,
                "inward": line_steps(far_sum, [(0, 1), (3, 2)]) if line == 4 else far_sum,
            }
            if before is not None:
                step_two(before, far_sum)
        if before is not None:
            other_side = swap(after(before["attn_sums"][1], grad_low), "dp", 1)
            attn_pair = add_low(before["attn_sums"][0], after(other_side, upstream))
        near_x, far_x, near_other, far_other = projection_grads(
            normed,
            grad_query,
            grad_kv,
            mixed,
            grad_low,
            attn_gain_part,
            mlp_gain_part,
            bias_first,
            bias_second,
            [core, chip_x, dp_place],
            chip_rows,
            line,
        )
        got_far_other = swap(far_other, "seq", 1)
        got_near_other = swap(near_other, "seq", 1)
        state["attn_parts"] = (near_x, far_x, got_near_other, got_far_other)
        if before is not None:
            before["owned"] = line_scatter(
                attn_pair, bits, state["near_sum"] if apart else got_far_other
            )
        states[layer] = before = state
    if line != 4:
        step_one(before)
        step_two(before)
    arrived = [None, send_attn(before, 1)]
    arrived[0] = send_attn(before, 0)
    before["attn_sums"] = sum_attn(before, arrived)
    grads = finish(states)
    terms.append(last_across)
    activations = sum(term.astype(jnp.float32) for term in terms).astype(jnp.bfloat16)
    return (
        activations.reshape(seq_count, tok_len, model_width),
        upstream.reshape(seq_count, tok_len, model_width),
    ) + grads


def solution(mesh):
    in_specs = (
        P("dp", "seq", None),
        P("dp", "seq", None),
        P("dp", None),
        P(None, ("dp", "seq")),
        P(None, ("dp", "seq"), None),
        P(None, ("dp", "seq")),
        P(None, ("dp", "seq"), None),
        P(None, ("dp", "seq")),
        P(None, ("dp", "seq"), None),
        P(None, ("dp", "seq"), None),
    )
    out_specs = (
        P("dp", "seq", None),
        P("dp", "seq", None),
        P(None, ("dp", "seq")),
        P(None, ("dp", "seq"), None),
        P(None, ("dp", "seq")),
        P(None, ("dp", "seq")),
        P(None, ("dp", "seq"), None),
        P(None, ("dp", "seq")),
        P(None, ("dp", "seq"), None),
        P(None, ("dp", "seq"), None),
    )
    return jax.shard_map(body, mesh=mesh, in_specs=in_specs, out_specs=out_specs, check_vma=False)
```

```python
import jax
import jax.numpy as jnp
from jax import lax
from jax.experimental import pallas as pl
from jax.experimental.pallas import tpu as pltpu
from jax.sharding import PartitionSpec as P

D = 896
HEADS = 14
KV_HEADS = 2
HEAD = 64
LAYERS = 2


EPS = 1e-06
THETA = 1000000.0
NEGATIVE = -1e30


def rotary_tables(positions):
    half_head = HEAD // 2
    frequency = THETA ** (-2.0 * jnp.arange(half_head, dtype=jnp.float32) / HEAD)
    angles = positions.astype(jnp.float32)[..., None] * frequency
    return (jnp.cos(angles), jnp.sin(angles))


NT = (((1,), (1,)), ((), ()))
TN = (((0,), (0,)), ((), ()))
FULL = pl.BlockSpec(memory_space=pltpu.VMEM)
SCALE = HEAD ** (-0.5)
GROUP = HEADS // KV_HEADS
KV_WIDTH = KV_HEADS * HEAD
SPLIT = D + KV_WIDTH
TILE = 384


def dot(left, right, dims=(((1,), (0,)), ((), ()))):
    return lax.dot_general(left, right, dims, preferred_element_type=jnp.float32)


def call(kernel, outs, micros, scratch=(), limit=40, **grid):
    return pl.pallas_call(
        kernel,
        out_shape=[jax.ShapeDtypeStruct(shape, kind) for shape, kind in outs],
        scratch_shapes=list(scratch),
        compiler_params=pltpu.CompilerParams(vmem_limit_bytes=limit * 2**20),
        name=kernel.__qualname__.split(".")[0],
        cost_estimate=pl.CostEstimate(
            flops=0, bytes_accessed=int(micros * 4e3), transcendentals=0
        ),
        **grid,
    )


def turn(block, cos_wide, sin_wide):
    lane = lax.broadcasted_iota(jnp.int32, block.shape, 1)
    width = block.shape[1]
    partner = jnp.where(
        lane % HEAD < HEAD // 2,
        pltpu.roll(block, width - HEAD // 2, 1),
        pltpu.roll(block, HEAD // 2, 1),
    )
    return block * cos_wide + partner * sin_wide


def inverse_root(rows):
    return lax.rsqrt(jnp.mean(rows * rows, axis=-1, keepdims=True) + EPS)


def before_attention(terms, gain, first_full, second_full, bias_first, bias_second, cos_wide, sin_wide):
    count = len(terms)
    rows = terms[0].shape[0]
    span = rows // 2

    def kernel(*refs):
        parts = refs[:count]
        gain_ref, first_ref, second_ref, bias_one, bias_two, cos_ref, sin_ref = refs[count : count + 7]
        x_ref, n_ref, q_ref, kv_ref = refs[count + 7 :]
        x = parts[0][...].astype(jnp.float32)
        for part in parts[1:]:
            x = x + part[...].astype(jnp.float32)
        x_ref[...] = x
        normed = (x * inverse_root(x) * gain_ref[...]).astype(jnp.bfloat16)
        n_ref[...] = normed
        cos_w, sin_w = cos_ref[...], sin_ref[...]
        for tile in range(SPLIT // 128):
            lanes = slice(tile * 128, tile * 128 + 128)
            block = dot(normed, first_ref[:, lanes]) + bias_one[:, lanes]
            turned = turn(block, cos_w, sin_w)
            if tile * 128 < D:
                for part in range(2):
                    head = 2 * tile + part
                    piece = turned[:, part * HEAD : part * HEAD + HEAD].astype(jnp.bfloat16)
                    place = (head % GROUP) * span
                    for half in range(2):
                        q_ref[head // GROUP, half, place : place + span, :] = piece[
                            half * span : half * span + span
                        ]
            else:
                kv_ref[:, :KV_WIDTH] = turned.astype(jnp.bfloat16)
        kv_ref[:, KV_WIDTH:] = (
            dot(normed, second_ref[:, :KV_WIDTH]) + bias_two[...]
        ).astype(jnp.bfloat16)

    return call(
        kernel,
        [
            ((rows, D), jnp.float32),
            ((rows, D), jnp.bfloat16),
            ((KV_HEADS, 2, GROUP * span, HEAD), jnp.bfloat16),
            ((rows, 2 * KV_WIDTH), jnp.bfloat16),
        ],
        4.0,
    )(*terms, gain, first_full, second_full, bias_first, bias_second, cos_wide, sin_wide)


def key_part(kv_refs, half, lanes):
    span = kv_refs[0].shape[0] // 2
    return jnp.concatenate(
        [ref[half * span : half * span + span, lanes] for ref in kv_refs], axis=0
    )


def attention(queries, kv_blocks, biases, x, second_full, gain):
    rows = x.shape[0]
    span = rows // 2

    def kernel(q_ref, kv0, kv1, kv2, kv3, bias_ref, x_ref, w_ref, gain_ref, mixed_ref, mid_ref, n_ref):
        kvs = (kv0, kv1, kv2, kv3)
        for group in range(KV_HEADS):
            key_lanes = slice(group * HEAD, group * HEAD + HEAD)
            value_lanes = slice(KV_WIDTH + group * HEAD, KV_WIDTH + group * HEAD + HEAD)
            keys = [key_part(kvs, half, key_lanes) for half in range(2)]
            values = []
            for half in range(2):
                block = key_part(kvs, half, value_lanes)
                values.append(jnp.concatenate([block, jnp.ones_like(block)], axis=1))
            for half in range(2):
                bias = bias_ref[half]
                for member in range(GROUP):
                    query = q_ref[group, half, member * span : member * span + span, :] * jnp.bfloat16(SCALE)
                    near = dot(query, keys[half], NT) + bias
                    top = jnp.max(near, axis=-1, keepdims=True)
                    if half == 1:
                        far = dot(query, keys[0], NT)
                        top = jnp.maximum(top, jnp.max(far, axis=-1, keepdims=True))
                    total = dot(jnp.exp(near - top).astype(jnp.bfloat16), values[half])
                    if half == 1:
                        total = total + dot(jnp.exp(far - top).astype(jnp.bfloat16), values[0])
                    out = total[:, :HEAD] / total[:, HEAD : 2 * HEAD]
                    head = group * GROUP + member
                    mixed_ref[half * span : half * span + span, head * HEAD : head * HEAD + HEAD] = (
                        out.astype(jnp.bfloat16)
                    )
        middle = x_ref[...] + dot(mixed_ref[...], w_ref[:, KV_WIDTH:])
        mid_ref[...] = middle
        n_ref[...] = (middle * inverse_root(middle) * gain_ref[...]).astype(jnp.bfloat16)

    return call(
        kernel,
        [((rows, D), jnp.bfloat16), ((rows, D), jnp.float32), ((rows, D), jnp.bfloat16)],
        10.5,
    )(queries, *kv_blocks, biases, x, second_full, gain)


def feed_forward(parts, gate_up_full, down_full):
    count = len(parts)
    part_rows = parts[0].shape[0]
    rows = count * part_rows
    units = down_full.shape[0]
    steps = pl.cdiv(units, TILE)
    last = units - (steps - 1) * TILE

    def kernel(*refs):
        part_refs = refs[:count]
        w_ref, d_ref, gu_ref = refs[count : count + 3]
        out_refs, total = refs[count + 3 : -1], refs[-1]
        step = pl.program_id(0)
        n2 = jnp.concatenate([ref[...] for ref in part_refs], axis=0)

        @pl.when(step == 0)
        def _():
            total[...] = jnp.zeros_like(total)

        @pl.when(step < steps - 1)
        def _():
            both = dot(n2, w_ref[...])
            gu_ref[...] = both.astype(jnp.bfloat16)
            gate, up = both[:, :TILE], both[:, TILE:]
            hidden = (gate * jax.nn.sigmoid(gate) * up).astype(jnp.bfloat16)
            total[...] += dot(hidden, d_ref[...])

        @pl.when(step == steps - 1)
        def _():
            both = dot(n2, w_ref[:, : 2 * last])
            gu_ref[:, : 2 * last] = both.astype(jnp.bfloat16)
            gate, up = both[:, :last], both[:, last:]
            hidden = (gate * jax.nn.sigmoid(gate) * up).astype(jnp.bfloat16)
            summed = (total[...] + dot(hidden, d_ref[:last, :])).astype(jnp.bfloat16)
            for place in range(count):
                out_refs[place][...] = summed[place * part_rows : place * part_rows + part_rows]

    whole = lambda step: (0, 0)
    return call(
        kernel,
        [((rows, 2 * units), jnp.bfloat16)] + [((part_rows, D), jnp.bfloat16)] * count,
        9.0,
        [pltpu.VMEM((rows, D), jnp.float32)],
        limit=60,
        grid=(steps,),
        in_specs=[pl.BlockSpec((part_rows, D), whole)] * count
        + [
            pl.BlockSpec((D, 2 * TILE), lambda step: (0, step)),
            pl.BlockSpec((TILE, D), lambda step: (step, 0)),
        ],
        out_specs=[
            pl.BlockSpec((rows, 2 * TILE), lambda step: (0, step)),
        ]
        + [pl.BlockSpec((part_rows, D), whole)] * count,
    )(*parts, gate_up_full, down_full)


def far_slot(mine, place, line):
    if line == 4:
        return jnp.where(mine < 2, place - 2, 1 - place)
    return (mine ^ place) - line // 2


def feed_back(gz_parts, n2_parts, gu_parts, gate_up_full, down_full, dp_place, group_count, far_arrays):
    line = group_count // 2
    half = line // 2
    each = half // far_arrays
    chunk = D // group_count
    count = len(gz_parts)
    gu_count = len(gu_parts)
    part_rows = gz_parts[0].shape[0]
    rows = count * part_rows
    units = down_full.shape[0]
    unit_rows = units // group_count
    packed = chunk + unit_rows * D // (2 * units)
    once = pl.Buffered(1)
    steps = pl.cdiv(units, TILE)
    last = units - (steps - 1) * TILE

    def kernel(*refs):
        place_ref, *refs = refs
        gz_refs = refs[:count]
        n2_refs = refs[count : 2 * count]
        gu_refs = refs[2 * count : 2 * count + gu_count]
        w_ref, d_ref = refs[2 * count + gu_count : 2 * count + gu_count + 2]
        outs = refs[2 * count + gu_count + 2 : -4]
        keep_near, send_near, own_ref, across_ref, pair_ref = outs[:5]
        keep_far, send_far = outs[5 : 5 + far_arrays], outs[5 + far_arrays :]
        total, gz, n2t, down = refs[-4:]
        side, mine = place_ref[0] % 2, place_ref[0] // 2
        step = pl.program_id(0)

        @pl.when(step == 0)
        def _():
            total[...] = jnp.zeros_like(total)
            for place in range(count):
                here = slice(place * part_rows, place * part_rows + part_rows)
                gz[here, :] = gz_refs[place][...]
                n2t[:, here] = n2_refs[place][...].T

        def write(spot, even, odd, rows, lanes):
            keep = jnp.where(side == 0, even, odd)
            send = jnp.where(side == 0, odd, even)
            slot = mine ^ spot
            beyond = far_slot(mine, spot, line)

            @pl.when(slot < half)
            def _():
                keep_near[slot, rows, lanes] = keep
                send_near[slot, rows, lanes] = send

            for number in range(far_arrays):

                @pl.when((slot >= half) & (beyond // each == number))
                def _():
                    keep_far[number][beyond % each, rows, lanes] = keep
                    send_far[number][beyond % each, rows, lanes] = send

        def work(width):
            gu = jnp.concatenate([ref[:, : 2 * width] for ref in gu_refs], axis=0).astype(jnp.float32)
            gate, up = gu[:, :width], gu[:, width:]
            sig = jax.nn.sigmoid(gate)
            act = gate * sig
            hidden = (act * up).astype(jnp.bfloat16)
            down[pl.ds(pl.multiple_of(step * TILE, 128), width), :] = dot(hidden, gz[...], TN)
            grad = dot(gz[...], d_ref[:width, :], NT)
            d_gate = grad * up * (sig + act * (1.0 - sig))
            d_up = grad * act
            both = jnp.concatenate([d_gate, d_up], axis=1).astype(jnp.bfloat16)
            part = dot(n2t[...], both)
            for spot in range(line):
                even = part[2 * spot * chunk : (2 * spot + 1) * chunk].astype(jnp.bfloat16)
                odd = part[(2 * spot + 1) * chunk : (2 * spot + 2) * chunk].astype(jnp.bfloat16)
                write(spot, even, odd, slice(0, chunk), pl.ds(pl.multiple_of(step * 2 * TILE, 128), 2 * width))

            return dot(both, w_ref[:, : 2 * width], NT)

        @pl.when(step < steps - 1)
        def _():
            total[...] += work(TILE)

        @pl.when(step == steps - 1)
        def _():
            summed = (total[...] + work(last)).astype(jnp.bfloat16)
            for spot in range(line):
                even, odd = (
                    fold(down[place * unit_rows : place * unit_rows + unit_rows, :], 2 * units).astype(
                        jnp.bfloat16
                    )
                    for place in (2 * spot, 2 * spot + 1)
                )
                write(spot, even, odd, slice(chunk, packed), slice(0, 2 * units))
            own_ref[...] = summed[:part_rows]
            pair_ref[0] = summed[part_rows : 2 * part_rows]
            across_ref[...] = summed[2 * part_rows : 3 * part_rows]
            pair_ref[1] = summed[3 * part_rows :]

    whole = lambda step: (0, 0)
    return call(
        kernel,
        [
            ((half, packed, 2 * units), jnp.bfloat16),
            ((half, packed, 2 * units), jnp.bfloat16),
            ((part_rows, D), jnp.bfloat16),
            ((part_rows, D), jnp.bfloat16),
            ((2, part_rows, D), jnp.bfloat16),
        ]
        + [((each, packed, 2 * units), jnp.bfloat16)] * (2 * far_arrays),
        25.0,
        [
            pltpu.VMEM((rows, D), jnp.float32),
            pltpu.VMEM((rows, D), jnp.bfloat16),
            pltpu.VMEM((D, rows), jnp.bfloat16),
            pltpu.VMEM((units, D), jnp.float32),
        ],
        limit=60,
        grid=(steps,),
        in_specs=[pl.BlockSpec(memory_space=pltpu.SMEM)]
        + [pl.BlockSpec((part_rows, D), whole, pipeline_mode=once)] * (2 * count)
        + [pl.BlockSpec((rows // gu_count, 2 * TILE), lambda step: (0, step))] * gu_count
        + [
            pl.BlockSpec((D, 2 * TILE), lambda step: (0, step)),
            pl.BlockSpec((TILE, D), lambda step: (step, 0)),
        ],
        out_specs=[
            pl.BlockSpec((half, packed, 2 * units), lambda step: (0, 0, 0), pipeline_mode=once),
            pl.BlockSpec((half, packed, 2 * units), lambda step: (0, 0, 0), pipeline_mode=once),
            pl.BlockSpec((part_rows, D), whole, pipeline_mode=once),
            pl.BlockSpec((part_rows, D), whole, pipeline_mode=once),
            pl.BlockSpec((2, part_rows, D), lambda step: (0, 0, 0), pipeline_mode=once),
        ]
        + [pl.BlockSpec((each, packed, 2 * units), lambda step: (0, 0, 0), pipeline_mode=once)]
        * (2 * far_arrays),
    )(dp_place.reshape(1).astype(jnp.int32), *gz_parts, *n2_parts, *gu_parts, gate_up_full, down_full)


def norm_back(rows, gain, grad):
    inv_root = inverse_root(rows)
    normal = rows * inv_root
    gain_part = jnp.sum(grad * normal, axis=0, keepdims=True)
    weighted = grad * gain
    inner = jnp.mean(weighted * normal, axis=-1, keepdims=True)
    return gain_part, inv_root * (weighted - normal * inner)


def attention_back(upstream, middle, gain, terms, second_full, queries, kv_blocks, biases, cos_wide, sin_wide):
    count = len(terms)
    rows = middle.shape[0]
    span = rows // 2
    wide = GROUP * span

    def kernel(*refs):
        up_ref, mid_ref, gain_ref = refs[:3]
        term_refs = refs[3 : 3 + count]
        w_ref, q_ref, kv0, kv1, kv2, kv3, bias_ref, cos_ref, sin_ref = refs[3 + count : 12 + count]
        gm_ref, gy_ref, dgain_ref, gq_ref, own_ref, d1, d2, d3, go_ref, dkv = refs[12 + count :]
        kvs = (kv0, kv1, kv2, kv3)
        grad = term_refs[0][...].astype(jnp.float32)
        for term in term_refs[1:]:
            grad = grad + term[...].astype(jnp.float32)
        gain_part, back = norm_back(mid_ref[...], gain_ref[...], grad)
        dgain_ref[...] = gain_part
        grad_middle = up_ref[...].astype(jnp.float32) + back
        gm_ref[...] = grad_middle
        grad_low = grad_middle.astype(jnp.bfloat16)
        gy_ref[...] = grad_low
        for tile in range(D // 128):
            start = KV_WIDTH
            block = dot(grad_low, w_ref[tile * 128 : tile * 128 + 128, start:], NT).astype(jnp.bfloat16)
            for part in range(2):
                head = 2 * tile + part
                place = (head % GROUP) * span
                for half in range(2):
                    go_ref[head // GROUP, half, place : place + span, :] = block[
                        half * span : half * span + span, part * HEAD : part * HEAD + HEAD
                    ]
        for group in range(KV_HEADS):
            key_lanes = slice(group * HEAD, group * HEAD + HEAD)
            value_lanes = slice(KV_WIDTH + group * HEAD, KV_WIDTH + group * HEAD + HEAD)
            keys = [key_part(kvs, half, key_lanes) for half in range(2)]
            values = [key_part(kvs, half, value_lanes) for half in range(2)]
            for half in range(2):
                query = q_ref[group, half] * jnp.bfloat16(SCALE)
                grad_out = go_ref[group, half]
                bias = jnp.concatenate([bias_ref[half]] * GROUP, axis=1)
                use = [half] if half == 0 else [1, 0]
                scores = []
                top = None
                for which in use:
                    score = dot(keys[which], query, NT)
                    if which == half:
                        score = score + bias
                    scores.append(score)
                    best = jnp.max(score, axis=0, keepdims=True)
                    top = best if top is None else jnp.maximum(top, best)
                weights = [jnp.exp(score - top) for score in scores]
                total = sum(jnp.sum(weight, axis=0, keepdims=True) for weight in weights)
                scale = 1.0 / total
                probs = [weight * scale for weight in weights]
                grads = [dot(values[which], grad_out, NT) for which in use]
                inner = sum(
                    jnp.sum(prob * grad_prob, axis=0, keepdims=True)
                    for prob, grad_prob in zip(probs, grads)
                )
                grad_query = None
                for which, prob, grad_prob in zip(use, probs, grads):
                    grad_score = (prob * (grad_prob - inner)).astype(jnp.bfloat16)
                    value_grad = dot(prob.astype(jnp.bfloat16), grad_out)
                    key_grad = dot(grad_score, query)
                    if half == 0:
                        dkv[group, which] = key_grad
                        dkv[KV_HEADS + group, which] = value_grad
                    elif which == 0:
                        dkv[group, which] += key_grad
                        dkv[KV_HEADS + group, which] += value_grad
                    else:
                        dkv[group, which] = key_grad
                        dkv[KV_HEADS + group, which] = value_grad
                    term = dot(keys[which].T, grad_score)
                    grad_query = term if grad_query is None else grad_query + term
                grad_query = grad_query * SCALE
                cos_w = cos_ref[half * span : half * span + span, :]
                sin_w = sin_ref[half * span : half * span + span, :]
                for member in range(GROUP):
                    head = group * GROUP + member
                    piece = grad_query[:, member * span : member * span + span].T
                    pair = jnp.concatenate([piece, piece], axis=1)
                    turned = turn(pair, cos_w, -sin_w)[:, :HEAD]
                    gq_ref[half * span : half * span + span, head * HEAD : head * HEAD + HEAD] = (
                        turned.astype(jnp.bfloat16)
                    )
        for place, out in enumerate((own_ref, d1, d2, d3)):
            for half in range(2):
                block = jnp.concatenate(
                    [dkv[lane, half, place * span : place * span + span, :] for lane in range(2 * KV_HEADS)],
                    axis=1,
                )
                out[half * span : half * span + span, :] = block.astype(out.dtype)

    return call(
        kernel,
        [
            ((rows, D), jnp.float32),
            ((rows, D), jnp.bfloat16),
            ((1, D), jnp.float32),
            ((rows, D), jnp.bfloat16),
            ((rows, 2 * KV_WIDTH), jnp.float32),
        ]
        + [((rows, 2 * KV_WIDTH), jnp.bfloat16)] * 3,
        13.0,
        [
            pltpu.VMEM((KV_HEADS, 2, wide, HEAD), jnp.bfloat16),
            pltpu.VMEM((2 * KV_HEADS, 2, 4 * span, HEAD), jnp.float32),
        ],
    )(upstream, middle, gain, *terms, second_full, queries, *kv_blocks, biases, cos_wide, sin_wide)


def before_back(kv_terms, gq, x, gain, grad_middle, first_full, second_full, cos_wide, sin_wide):
    rows = x.shape[0]
    count = len(kv_terms)

    def kernel(*refs):
        kv_refs = refs[:count]
        gq_ref, x_ref, gain_ref, gm_ref, w1_ref, w2_ref, cos_ref, sin_ref = refs[count : count + 8]
        up_ref, low_ref, gkv_ref, dgain_ref, bias_one, bias_two = refs[count + 8 :]
        grad = kv_refs[0][...].astype(jnp.float32)
        for ref in kv_refs[1:]:
            grad = grad + ref[...].astype(jnp.float32)
        grad_key = turn(grad[:, :KV_WIDTH], cos_ref[...], -sin_ref[...]).astype(jnp.bfloat16)
        grad_value = grad[:, KV_WIDTH:].astype(jnp.bfloat16)
        gkv_ref[:, :KV_WIDTH] = grad_key
        gkv_ref[:, KV_WIDTH:] = grad_value
        grad_query = gq_ref[...]
        bias_one[:, :D] = jnp.sum(grad_query.astype(jnp.float32), axis=0, keepdims=True)
        bias_one[:, D:] = jnp.sum(grad_key.astype(jnp.float32), axis=0, keepdims=True)
        bias_two[...] = jnp.sum(grad_value.astype(jnp.float32), axis=0, keepdims=True)
        grad_normed = (
            dot(grad_query, w1_ref[:, :D], NT)
            + dot(grad_key, w1_ref[:, D:], NT)
            + dot(grad_value, w2_ref[:, :KV_WIDTH], NT)
        )
        gain_part, back = norm_back(x_ref[...], gain_ref[...], grad_normed)
        dgain_ref[...] = gain_part
        upstream = gm_ref[...] + back
        up_ref[...] = upstream
        low_ref[...] = upstream.astype(jnp.bfloat16)

    return call(
        kernel,
        [
            ((rows, D), jnp.float32),
            ((rows, D), jnp.bfloat16),
            ((rows, 2 * KV_WIDTH), jnp.bfloat16),
            ((1, D), jnp.float32),
            ((1, SPLIT), jnp.float32),
            ((1, KV_WIDTH), jnp.float32),
        ],
        2.4,
    )(*kv_terms, gq, x, gain, grad_middle, first_full, second_full, cos_wide, sin_wide)


def unit_pieces(unit_rows, group_count, seq_devices):
    units = unit_rows * group_count
    steps = pl.cdiv(units, TILE)
    pieces = []
    for owner in range(seq_devices):
        for kind in range(2):
            for group in range(group_count):
                unit = group * unit_rows
                stop = unit + unit_rows
                column = kind * units * seq_devices + (group * seq_devices + owner) * unit_rows
                while unit < stop:
                    step = unit // TILE
                    end = min(stop, (step + 1) * TILE)
                    width = TILE if step < steps - 1 else units - (steps - 1) * TILE
                    inside = 2 * step * TILE + kind * width + unit - step * TILE
                    pieces.append((owner, inside, column, end - unit))
                    column += end - unit
                    unit = end
    return pieces


def spread_columns(weight, place, unit_rows, group_count, seq_devices):
    layers, rows, columns = weight.shape
    quarter = columns // seq_devices
    pieces = unit_pieces(unit_rows, group_count, seq_devices)

    def kernel(place_ref, w_ref, *refs):
        outs, wide, narrow = refs[:seq_devices], refs[-2], refs[-1]
        for layer in range(layers):
            wide[...] = w_ref[layer].astype(jnp.float32)
            for owner in range(seq_devices):
                for who, inside, column, width in pieces:
                    if who == owner:
                        narrow[:, inside : inside + width] = wide[:, column : column + width]
                block = narrow[...].astype(jnp.bfloat16)
                for bit in range(seq_devices):

                    @pl.when(place_ref[0] == owner ^ bit)
                    def _():
                        outs[bit][layer] = block

    return call(
        kernel,
        [((layers, rows, quarter), jnp.bfloat16)] * seq_devices,
        2.5,
        [pltpu.VMEM((rows, columns), jnp.float32), pltpu.VMEM((rows, quarter), jnp.float32)],
        in_specs=[pl.BlockSpec(memory_space=pltpu.SMEM), FULL],
        out_specs=[FULL] * seq_devices,
    )(place.reshape(1).astype(jnp.int32), weight)


def collect_columns(blocks, place, unit_rows, group_count):
    count = len(blocks)
    layers, rows, quarter = blocks[0].shape
    pieces = unit_pieces(unit_rows, group_count, count)

    def kernel(place_ref, *refs):
        out_ref, narrow = refs[count:]
        me = place_ref[0]
        for layer in range(layers):
            for owner in range(count):
                for bit in range(count):

                    @pl.when(me == owner ^ bit)
                    def _():
                        narrow[...] = refs[bit][layer].astype(jnp.float32)

                for who, inside, column, width in pieces:
                    if who == owner:
                        out_ref[layer, :, column : column + width] = narrow[:, inside : inside + width]

    return call(
        kernel,
        [((layers, rows, count * quarter), jnp.float32)],
        1.5,
        [pltpu.VMEM((rows, quarter), jnp.float32)],
        in_specs=[pl.BlockSpec(memory_space=pltpu.SMEM)] + [FULL] * count,
        out_specs=[FULL],
    )(place.reshape(1).astype(jnp.int32), *blocks)[0]


def fold(rows, columns):
    high = rows.shape[0] * 128 // columns
    wide = rows.shape[1] // 128
    return jnp.concatenate(
        [
            jnp.concatenate(
                [rows[high * r : high * r + high, 128 * c : 128 * c + 128] for r in range(columns // 128)],
                axis=1,
            )
            for c in range(wide)
        ],
        axis=0,
    )


def unfold(rows, width):
    high = rows.shape[0] * 128 // width
    wide = rows.shape[1] // 128
    return jnp.concatenate(
        [
            jnp.concatenate(
                [rows[high * c : high * c + high, 128 * r : 128 * r + 128] for c in range(width // 128)],
                axis=1,
            )
            for r in range(wide)
        ],
        axis=0,
    )


def pack_rows(blocks, down, place):
    owners = len(blocks)
    layers, rows, columns = blocks[0].shape
    total = owners * rows + down.shape[1] * down.shape[2] // columns

    def kernel(place_ref, down_ref, *refs):
        ins, outs = refs[:owners], refs[owners:]
        for layer in range(layers):
            parts = []
            for owner in range(owners):
                part = ins[0][layer].astype(jnp.float32)
                for bit in range(1, owners):
                    part = jnp.where(
                        place_ref[0] == owner ^ bit, ins[bit][layer].astype(jnp.float32), part
                    )
                parts.append(part)
            parts.append(fold(down_ref[layer].astype(jnp.float32), columns))
            outs[layer][0] = jnp.concatenate(parts, axis=0).astype(jnp.bfloat16)

    return call(
        kernel,
        [((1, total, columns), jnp.bfloat16)] * layers,
        3.0,
        in_specs=[pl.BlockSpec(memory_space=pltpu.SMEM)] + [FULL] * (owners + 1),
        out_specs=[FULL] * layers,
    )(place.reshape(1).astype(jnp.int32), down, *blocks)


def unpack(parts, places, chunk):
    count, total, columns = parts[0].shape
    number = count * len(parts)
    unit_rows = (total - chunk) * columns // D

    def kernel(place_ref, *refs):
        ins, gate_ref, down_ref = refs[: len(parts)], refs[-2], refs[-1]
        for which in range(len(parts)):
            for k in range(count):
                spot = place_ref[which * count + k]
                gate_ref[spot] = ins[which][k, :chunk, :]
                down_ref[spot] = unfold(ins[which][k, chunk:, :].astype(jnp.float32), D).astype(
                    jnp.bfloat16
                )

    gate, down = call(
        kernel,
        [((number, chunk, columns), jnp.bfloat16), ((number, unit_rows, D), jnp.bfloat16)],
        5.0,
        in_specs=[pl.BlockSpec(memory_space=pltpu.SMEM)] + [FULL] * len(parts),
        out_specs=[FULL] * 2,
    )(jnp.stack(places).astype(jnp.int32), *parts)
    return gate.reshape(number * chunk, columns), down.reshape(number * unit_rows, D)


def split_rows(terms, chunk, place, count):
    layers = len(terms)
    total_rows, columns = terms[0][0].shape
    rows = chunk // count
    unit_rows = (total_rows - chunk) * columns // D

    def kernel(place_ref, *refs):
        ins, outs, down_ref = refs[: 2 * layers], refs[2 * layers : -1], refs[-1]
        for layer in range(layers):
            total = ins[2 * layer][...].astype(jnp.float32) + ins[2 * layer + 1][...].astype(
                jnp.float32
            )
            down_ref[layer] = unfold(total[chunk:], D)
            for owner in range(count):
                block = total[owner * rows : owner * rows + rows].astype(jnp.bfloat16)
                for bit in range(count):

                    @pl.when(place_ref[0] == owner ^ bit)
                    def _():
                        outs[bit][layer] = block

    *blocks, down = call(
        kernel,
        [((layers, rows, columns), jnp.bfloat16)] * count
        + [((layers, unit_rows, D), jnp.float32)],
        3.0,
        in_specs=[pl.BlockSpec(memory_space=pltpu.SMEM)] + [FULL] * (2 * layers),
        out_specs=[FULL] * (count + 1),
    )(place.reshape(1).astype(jnp.int32), *[term for pair in terms for term in pair])
    return blocks, down


def assemble(parts, places, chip_rows):
    line, rows, width = parts[0].shape

    def kernel(place_ref, *refs):
        ins = refs[:8]
        first_ref, second_ref, small_ref = refs[8:]
        here, chip, side = place_ref[0] == 0, place_ref[1] == 0, place_ref[2] % 2 == 0
        mine = place_ref[2] // 2
        small = jnp.zeros((rows - chip_rows, width), jnp.float32)
        for spot in range(line):
            halves = []
            for half in range(2):
                pieces = []
                blocks = [ins[4 * half + k][spot].astype(jnp.float32) for k in range(4)]
                for block in blocks:
                    small = small + block[chip_rows:]
                lower = [jnp.where(side, blocks[2 * x], blocks[2 * x + 1]) for x in range(2)]
                upper = [jnp.where(side, blocks[2 * x + 1], blocks[2 * x]) for x in range(2)]
                for pair in (lower, upper):
                    pieces.append(jnp.where(chip, pair[0], pair[1])[:chip_rows])
                    pieces.append(jnp.where(chip, pair[1], pair[0])[:chip_rows])
                halves.append(jnp.concatenate(pieces, axis=0).astype(jnp.bfloat16))
            first_ref[mine ^ spot] = jnp.where(here, halves[0], halves[1])
            second_ref[mine ^ spot] = jnp.where(here, halves[1], halves[0])
        small_ref[...] = small

    first, second, small = call(
        kernel,
        [
            ((line, 4 * chip_rows, width), jnp.bfloat16),
            ((line, 4 * chip_rows, width), jnp.bfloat16),
            ((rows - chip_rows, width), jnp.float32),
        ],
        4.0,
        in_specs=[pl.BlockSpec(memory_space=pltpu.SMEM)] + [FULL] * 8,
        out_specs=[FULL] * 3,
    )(jnp.stack(places).astype(jnp.int32), *parts)
    return first.reshape(-1, width), second.reshape(-1, width), small


def projection_grads(normed, grad_query, grad_kv, mixed, grad_low, gain_one, gain_two, bias_one, bias_two, places, chip_rows, line):
    width = SPLIT

    def kernel(place_ref, n_ref, gq_ref, gkv_ref, mixed_ref, gy_ref, g1_ref, g2_ref, b1_ref, b2_ref, keep0, keep1, send0, send1, pad):
        here, chip, side = place_ref[0] == 0, place_ref[1] == 0, place_ref[2] % 2
        mine = place_ref[2] // 2
        turned = n_ref[...].T
        pad[...] = jnp.zeros_like(pad)
        pad[0:1, :D] = g1_ref[...]
        pad[1:2, :D] = g2_ref[...]
        pad[2:3, :] = b1_ref[...]
        pad[3:4, :KV_WIDTH] = b2_ref[...]
        small = pad[...]
        first = jnp.concatenate(
            [dot(turned, gq_ref[...]), dot(turned, gkv_ref[:, :KV_WIDTH])], axis=1
        )
        second = jnp.concatenate(
            [dot(turned, gkv_ref[:, KV_WIDTH:]), dot(mixed_ref[...], gy_ref[...], TN)], axis=1
        )

        def chunk(part, number):
            rows = part[number * chip_rows : (number + 1) * chip_rows]
            return jnp.concatenate([rows, small], axis=0).astype(jnp.bfloat16)

        for spot in range(line):
            for pair in range(2):
                slot = side ^ pair
                firsts = [chunk(first, 4 * spot + 2 * pair + x) for x in range(2)]
                seconds = [chunk(second, 4 * spot + 2 * pair + x) for x in range(2)]
                keeps = [jnp.where(here, one, two) for one, two in zip(firsts, seconds)]
                sends = [jnp.where(here, two, one) for one, two in zip(firsts, seconds)]
                keep0[slot, mine ^ spot] = jnp.where(chip, keeps[0], keeps[1])
                keep1[slot, mine ^ spot] = jnp.where(chip, keeps[1], keeps[0])
                send0[slot, mine ^ spot] = jnp.where(chip, sends[0], sends[1])
                send1[slot, mine ^ spot] = jnp.where(chip, sends[1], sends[0])

    return call(
        kernel,
        [((2, line, chip_rows + 8, width), jnp.bfloat16)] * 4,
        6.0,
        [pltpu.VMEM((8, width), jnp.float32)],
        in_specs=[pl.BlockSpec(memory_space=pltpu.SMEM)] + [FULL] * 9,
        out_specs=[FULL] * 4,
    )(
        jnp.stack(places).astype(jnp.int32),
        normed,
        grad_query,
        grad_kv,
        mixed,
        grad_low,
        gain_one,
        gain_two,
        bias_one,
        bias_two,
    )


def swap(values, axis, bit):
    size = lax.axis_size(axis)
    return lax.ppermute(values, axis, [(i, i ^ bit) for i in range(size)])


def after(values, *others):
    return lax.optimization_barrier((values,) + tuple(others))[0]


def line_bits():
    bits = [1]
    while 4 * bits[-1] < lax.axis_size("dp"):
        bits.append(2 * bits[-1])
    return bits


def line_gather(values, bits, *waited):
    for bit in bits:
        values = jnp.concatenate([values, after(swap(values, "dp", 2 * bit), *waited)], axis=0)
    return values


def line_steps(values, moves):
    return lax.ppermute(
        values, "dp", [(2 * here + side, 2 * there + side) for here, there in moves for side in range(2)]
    )


def cross_middle(values):
    line = lax.axis_size("dp") // 2
    if line == 4:
        return line_steps(values, [(1, 2), (2, 1)])
    return swap(values, "dp", line)


def line_scatter(values, bits, *waited):
    for bit in bits[:0:-1]:
        values = add_low(values[:bit], after(swap(values[bit:], "dp", 2 * bit), *waited))
    return [values[0], swap(values[1], "dp", 2)]


def add_low(left, right):
    return (left.astype(jnp.float32) + right.astype(jnp.float32)).astype(jnp.bfloat16)


def group_rows(values, *waited):
    beside = swap(values, "seq", 1)
    across = swap(values, "seq", 2)
    return [values, beside, across, swap(after(across, *waited), "seq", 1)]


def placed(values, offset, width):
    return lax.dynamic_update_slice(jnp.zeros((width,), values.dtype), values, (offset,))


def body(
    tokens,
    cotangent,
    span_order,
    attn_gain,
    joined_weight,
    joined_bias,
    out_weight,
    mlp_gain,
    gate_up_weight,
    down_weight,
):
    seq_count, tok_len, model_width = tokens.shape
    span_len = tok_len // 2
    group_count = lax.axis_size("dp")
    seq_devices = lax.axis_size("seq")
    unit_rows = down_weight.shape[1]
    width_rows = gate_up_weight.shape[1]
    units = group_count * unit_rows
    dp_place = lax.axis_index("dp")
    seq_place = lax.axis_index("seq")
    core = seq_place % 2
    chip_x = seq_place // 2
    device = dp_place * seq_devices + seq_place
    chip_rows = 2 * width_rows
    line = group_count // 2
    side = dp_place % 2
    line_place = dp_place // 2

    order = [lax.dynamic_slice(span_order, (0, seq_place ^ bit), (1, 1))[0, 0] for bit in range(4)]
    inside = jnp.arange(span_len, dtype=jnp.int32)
    own_places = jnp.concatenate(
        [order[0] * span_len + inside, (2 * seq_devices - 1 - order[0]) * span_len + inside]
    )
    half_biases = []
    for half in range(2):
        blocks = []
        for bit in range(4):
            ahead = order[bit] < order[0] if half == 0 else order[bit] > order[0]
            allowed = ahead | ((order[bit] == order[0]) & (inside[:, None] >= inside[None, :]))
            blocks.append(jnp.where(allowed, 0.0, NEGATIVE).astype(jnp.float32))
        half_biases.append(jnp.concatenate(blocks, axis=1))
    biases = jnp.stack(half_biases)
    biases_turned = jnp.swapaxes(biases, 1, 2)
    cos_table, sin_table = rotary_tables(own_places)
    cos_wide = jnp.concatenate([cos_table] * 4, axis=1)
    sin_wide = jnp.concatenate([-sin_table, sin_table] * 2, axis=1)

    def attn_shard(layer):
        first = joined_weight[layer][:, :SPLIT]
        second = jnp.concatenate([joined_weight[layer][:, SPLIT:], out_weight[layer]], axis=1)
        got = swap(jnp.where(core == 0, second, first), "seq", 1)
        mine = jnp.where(core == 0, first, second)
        rows = jnp.where(core == 0, jnp.stack([mine, got]), jnp.stack([got, mine])).reshape(
            chip_rows, -1
        )
        bias_all = placed(joined_bias[layer], device * joined_bias.shape[1], SPLIT + KV_WIDTH)
        extra = jnp.zeros((8, SPLIT), jnp.bfloat16)
        extra = extra.at[0].set(placed(attn_gain[layer], device * width_rows, SPLIT))
        extra = extra.at[1].set(placed(mlp_gain[layer], device * width_rows, SPLIT))
        extra = extra.at[2].set(bias_all[:SPLIT])
        extra = extra.at[3, :KV_WIDTH].set(bias_all[SPLIT:])
        return jnp.concatenate([rows, extra], axis=0)

    def attn_parts(own_side, other_side, *waited):
        parts = [own_side, other_side]
        return parts + [swap(after(part, *waited), "seq", 2) for part in parts]

    def attn_finish(parts):
        other_side = parts[1]
        parts = parts + [swap(after(part, other_side), "seq", 1) for part in parts]
        first_full, second_full, small = assemble(parts, [core, chip_x, dp_place], chip_rows)
        return (
            first_full,
            second_full,
            small[0:1, :model_width],
            small[1:2, :model_width],
            small[2:3],
            small[3:4, :KV_WIDTH],
        )

    bits = line_bits()
    spread = spread_columns(gate_up_weight, seq_place, unit_rows, group_count, seq_devices)
    shards = [attn_shard(layer)[None] for layer in range(LAYERS)]
    gate_blocks = [spread[0]] + [swap(spread[bit], "seq", bit) for bit in range(1, 4)]
    gate_shards = pack_rows(gate_blocks, down_weight, seq_place)
    attn_line = line_gather(after(shards[0], *spread), bits)
    attn_other = swap(after(attn_line, *gate_shards), "dp", 1)
    def outward(crossed, *waited):
        if line != 4:
            return crossed
        passed = after(line_steps(crossed, [(1, 0), (2, 3)]), *waited)
        return jnp.where((line_place == 1) | (line_place == 2), crossed, passed)

    first_parts = attn_parts(attn_line, attn_other)
    near = [line_gather(after(gate_shards[0], attn_other), bits[:-1], first_parts[3])]
    near_pair = [swap(after(near[0], attn_other), "dp", 1)]
    crossed = [cross_middle(near[0])]
    far = []
    offsets = [dp_place ^ (2 * k) for k in range(line)]
    half = line // 2
    if line == 4:
        beyond = [jnp.where(line_place < 2, 2 + k, 1 - k) * 2 + side for k in range(2)]
    else:
        beyond = offsets[half:]
    places = offsets[:half] + beyond
    places = [offsets[:half], beyond, [spot ^ 1 for spot in offsets[:half]], [spot ^ 1 for spot in beyond]]
    places = [spot for group in places for spot in group]

    def mlp_finish(layer, far_pair):
        parts = [near[layer], far[layer], near_pair[layer], far_pair]
        return unpack(parts, places, seq_devices * width_rows)

    terms = [tokens.reshape(tok_len, model_width)]
    kept_state = []
    mlp_sets = []
    attn_sets = [attn_finish(first_parts)]
    for layer in range(LAYERS):
        first_full, second_full, gain_full, mlp_gain_full, bias_first, bias_second = attn_sets[layer]
        x, normed, queries, own_kv = before_attention(
            terms,
            after(gain_full, near[0]) if layer == 0 else after(gain_full, near_pair[1]),
            first_full,
            second_full,
            bias_first,
            bias_second,
            cos_wide,
            sin_wide,
        )
        kv_blocks = [own_kv] + [swap(own_kv, "seq", bit) for bit in range(1, 4)]
        waited = (near_pair[0],) if layer == 0 else ()
        mixed, middle, n2 = attention(
            queries, kv_blocks, biases, x, second_full, after(mlp_gain_full, *waited)
        )
        if layer + 1 == LAYERS:
            far.append(outward(after(crossed[1], kept_state[0][7][1]), own_kv))
            far_pair = swap(far[1], "dp", 1)
            n2_parts = group_rows(n2, far_pair)
        else:
            far.append(outward(crossed[0], n2))
            far_pair = swap(far[0], "dp", 1)
            n2_parts = group_rows(after(n2, far[0]))
            second_start = line_gather(after(shards[1], far_pair), bits[:1])
            second_line = line_gather(second_start, bits[1:])
            second_other = swap(after(second_line, n2_parts[3]), "dp", 1)
            near.append(line_gather(after(gate_shards[1], far[0]), bits[:-1], n2_parts[3]))
            crossed.append(cross_middle(after(near[1], second_line)))
            attn_sets.append(attn_finish(attn_parts(second_line, second_other, n2_parts[3])))
            near_pair.append(swap(after(near[1], far_pair), "dp", 1))
        mlp_sets.append(mlp_finish(layer, far_pair))
        gu_near, *outs_near = feed_forward(n2_parts[:2], *mlp_sets[layer])
        if layer == 0:
            n2_parts[2] = after(n2_parts[2], gu_near)
        else:
            low_parts = group_rows(
                after(cotangent.reshape(tok_len, model_width), n2_parts[3]), gu_near
            )
        gu_far, *outs_far = feed_forward(n2_parts[2:], *mlp_sets[layer])
        across_sum = add_low(outs_far[0], swap(outs_far[1], "seq", 1))
        terms = [middle, outs_near[0], swap(outs_near[1], "seq", 1)]
        if layer + 1 < LAYERS:
            terms.append(swap(across_sum, "seq", 2))
        kept_state.append((x, normed, queries, kv_blocks, mixed, middle, n2_parts, [gu_near, gu_far]))
    upstream = cotangent.reshape(tok_len, model_width)
    states = [None] * LAYERS
    before = None

    def send_attn(state, pair, *waited):
        near, far, got_near, got_far = state["attn_parts"]
        return swap(after(add_low(far[pair], got_far[pair]), *waited), "seq", 2)

    def sum_attn(state, arrived, *waited):
        near, far, got_near, got_far = state["attn_parts"]
        return [
            (
                near[pair].astype(jnp.float32)
                + got_near[pair].astype(jnp.float32)
                + after(arrived[pair], *waited).astype(jnp.float32)
            ).astype(jnp.bfloat16)
            for pair in range(2)
        ]

    def step_one(state, *waited):
        far_sum = state["far_sum"]
        if line == 4:
            far_sum = add_low(far_sum, after(state["inward"], *waited))
        state["crossed"] = cross_middle(far_sum)
        state["near_sum"] = add_low(state["keep_near"], after(state["near_got"], *waited))

    def step_two(state, *waited):
        state["near_sum"] = add_low(state["near_sum"], after(state["crossed"], *waited))
        state["terms"] = line_scatter(state["near_sum"], bits[:-1])

    def finish(states):
        gate_rows, down_owned = split_rows(
            [state["terms"] for state in states], seq_devices * width_rows, seq_place, seq_devices
        )
        state = states[0]
        other_side = swap(after(state["attn_sums"][1], state["near_got"]), "dp", 1)
        state["owned"] = line_scatter(
            add_low(state["attn_sums"][0], other_side), bits, state["near_sum"]
        )
        owned = jnp.stack(
            [
                state["owned"][0].astype(jnp.float32)
                + after(state["owned"][1], gate_rows[0]).astype(jnp.float32)
                for state in states
            ]
        )
        extra = owned[:, chip_rows:]
        halves = owned[:, :chip_rows].reshape(LAYERS, 2, width_rows, -1)
        mine = lax.dynamic_index_in_dim(halves, core, 1, keepdims=False)
        theirs = swap(
            lax.dynamic_index_in_dim(halves, 1 - core, 1, keepdims=False), "seq", 1
        )
        first_own = jnp.where(core == 0, mine, theirs)
        second_own = jnp.where(core == 0, theirs, mine)

        def cut(row, width, stop):
            start = (0, row, device * width)
            return lax.dynamic_slice(extra[:, :, :stop], start, (LAYERS, 1, width))[:, 0]

        gate_owned = collect_columns(
            [gate_rows[0]] + [swap(gate_rows[bit], "seq", bit) for bit in range(1, 4)],
            seq_place,
            unit_rows,
            group_count,
        )
        return (
            cut(0, width_rows, model_width),
            jnp.concatenate([first_own, second_own[:, :, :KV_WIDTH]], axis=2),
            cut(2, SPLIT // (group_count * seq_devices), SPLIT),
            cut(3, KV_WIDTH // (group_count * seq_devices), KV_WIDTH),
            second_own[:, :, KV_WIDTH:],
            cut(1, width_rows, model_width),
            gate_owned,
            down_owned,
        )

    for layer in reversed(range(LAYERS)):
        x, normed, queries, kv_blocks, mixed, middle, n2_parts, gu_parts = kept_state[layer]
        first_full, second_full, gain_full, mlp_gain_full, _, _ = attn_sets[layer]
        if before is not None:
            low_parts = group_rows(upstream_low)
            low_parts[0] = after(low_parts[0], *before["attn_parts"][2:])
            attn_sent = [send_attn(before, pair, low_parts[3]) for pair in range(2)]
            last_across = swap(after(across_sum, low_parts[3]), "seq", 2)
        apart = line == 4 and layer == 0
        keep_near, send_near, own_out, across_out, pair_out, *far_parts = feed_back(
            low_parts,
            n2_parts,
            gu_parts,
            *mlp_sets[layer],
            dp_place,
            group_count,
            2 if apart else 1,
        )
        if before is not None:
            pair_out = after(pair_out, terms[2], last_across, *attn_sent, before["near_got"], before["inward"])
        got = swap(pair_out, "seq", 1)
        out_terms = [own_out, got[0], swap(add_low(across_out, got[1]), "seq", 2)]
        if apart:
            keep_far, send_far = far_parts[:2], far_parts[2:]
            got_far = [swap(after(send_far[0], got), "dp", 1), swap(send_far[1], "dp", 1)]
            far_sums = [None, add_low(keep_far[1], after(got_far[1], out_terms[2]))]
            inward = [None, line_steps(far_sums[1], [(0, 1), (3, 2)])]
        else:
            keep_far, send_far = far_parts
            got_far = swap(send_far, "dp", 1)
        if before is not None:
            step_one(before, own_out)
            before["attn_sums"] = sum_attn(before, attn_sent, own_out)
        grad_middle, grad_low, mlp_gain_part, grad_query, own_term, *kv_terms = attention_back(
            upstream,
            middle,
            mlp_gain_full,
            out_terms,
            second_full,
            queries,
            kv_blocks,
            biases_turned,
            cos_wide,
            sin_wide,
        )
        if apart:
            kv_terms[0] = after(kv_terms[0], inward[1])
        kv_terms = [own_term] + [swap(kv_terms[bit - 1], "seq", bit) for bit in range(1, 4)]
        upstream, upstream_low, grad_kv, attn_gain_part, bias_first, bias_second = before_back(
            kv_terms,
            grad_query,
            x,
            gain_full,
            grad_middle,
            first_full,
            second_full,
            cos_wide,
            sin_wide,
        )
        near_got = swap(after(send_near, grad_low), "dp", 1)
        if apart:
            across_middle = [None, cross_middle(add_low(far_sums[1], after(inward[1], grad_low)))]
            far_sums[0] = add_low(keep_far[0], after(got_far[0], grad_low))
            inward[0] = after(line_steps(far_sums[0], [(0, 1), (3, 2)]), upstream)
            across_middle[0] = cross_middle(add_low(far_sums[0], inward[0]))
            near_one = add_low(add_low(keep_near[1], near_got[1]), across_middle[1][0])
            near_zero = add_low(add_low(keep_near[0], near_got[0]), across_middle[0][0])
            state = {"near_got": near_got, "near_sum": near_one}
            state["terms"] = [near_zero, swap(near_one, "dp", 2)]
            step_two(before, far_sums[0])
        else:
            far_sum = add_low(keep_far, after(got_far, upstream if before is None else grad_low))
            state = {
                "far_sum": far_sum,
                "keep_near": keep_near,
                "near_got": near_got,
                "inward": line_steps(far_sum, [(0, 1), (3, 2)]) if line == 4 else far_sum,
            }
            if before is not None:
                step_two(before, far_sum)
        if before is not None:
            other_side = swap(after(before["attn_sums"][1], grad_low), "dp", 1)
            attn_pair = add_low(before["attn_sums"][0], after(other_side, upstream))
        near_x, far_x, near_other, far_other = projection_grads(
            normed,
            grad_query,
            grad_kv,
            mixed,
            grad_low,
            attn_gain_part,
            mlp_gain_part,
            bias_first,
            bias_second,
            [core, chip_x, dp_place],
            chip_rows,
            line,
        )
        got_far_other = swap(far_other, "seq", 1)
        got_near_other = swap(near_other, "seq", 1)
        state["attn_parts"] = (near_x, far_x, got_near_other, got_far_other)
        if before is not None:
            before["owned"] = line_scatter(
                attn_pair, bits, state["near_sum"] if apart else got_far_other
            )
        states[layer] = before = state
    if line != 4:
        step_one(before)
        step_two(before)
    arrived = [None, send_attn(before, 1)]
    arrived[0] = send_attn(before, 0)
    before["attn_sums"] = sum_attn(before, arrived)
    grads = finish(states)
    terms.append(last_across)
    activations = sum(term.astype(jnp.float32) for term in terms).astype(jnp.bfloat16)
    return (
        activations.reshape(seq_count, tok_len, model_width),
        upstream.reshape(seq_count, tok_len, model_width),
    ) + grads


def solution(mesh):
    in_specs = (
        P("dp", "seq", None),
        P("dp", "seq", None),
        P("dp", None),
        P(None, ("dp", "seq")),
        P(None, ("dp", "seq"), None),
        P(None, ("dp", "seq")),
        P(None, ("dp", "seq"), None),
        P(None, ("dp", "seq")),
        P(None, ("dp", "seq"), None),
        P(None, ("dp", "seq"), None),
    )
    out_specs = (
        P("dp", "seq", None),
        P("dp", "seq", None),
        P(None, ("dp", "seq")),
        P(None, ("dp", "seq"), None),
        P(None, ("dp", "seq")),
        P(None, ("dp", "seq")),
        P(None, ("dp", "seq"), None),
        P(None, ("dp", "seq")),
        P(None, ("dp", "seq"), None),
        P(None, ("dp", "seq"), None),
    )
    return jax.shard_map(body, mesh=mesh, in_specs=in_specs, out_specs=out_specs, check_vma=False)
```
